32 devices in a mesh: rows: 16 (over z, y, x), blk: 2 (over core).
Axes of the slice: x: 2, y: 2, z: 4, core: 2. Of those that a mesh axis runs over, the one named last changes fastest.
Arguments:
- tokens: bfloat16 [16, 1024, 768], P('rows', 'blk'), may hold values from -6 to 6
- segments: int32 [16, 1024], P('rows'), may hold values from 0 to 1024, as said below
- w_qkv: bfloat16 [768, 2304], P(('rows', 'blk')), may hold values from -0.21875 to 0.21875
- w_out: bfloat16 [768, 768], P(('rows', 'blk')), may hold values from -1.25 to 1.25
- ln1_gain: bfloat16 [768], P(('rows', 'blk')), may hold values from 0.5 to 1.5
- ln1_bias: bfloat16 [768], P(('rows', 'blk')), may hold values from -1.796875 to 1.796875
- w_gate_up: bfloat16 [768, 6144], P(('rows', 'blk')), may hold values from -0.21875 to 0.21875
- w_down: bfloat16 [3072, 768], P(('rows', 'blk')), may hold values from -0.109375 to 0.109375
- ln2_gain: bfloat16 [768], P(('rows', 'blk')), may hold values from 0.5 to 1.5
- ln2_bias: bfloat16 [768], P(('rows', 'blk')), may hold values from -1.796875 to 1.796875
- out_grad: bfloat16 [16, 1024, 768], P('rows', 'blk'), may hold values from -6 to 6
Outputs:
- output: bfloat16 [16, 1024, 768], P('rows', 'blk')
- tokens_grad: bfloat16 [16, 1024, 768], P('rows', 'blk')
- w_qkv_grad: float32 [768, 2304], P(('rows', 'blk'))
- w_out_grad: float32 [768, 768], P(('rows', 'blk'))
- ln1_gain_grad: float32 [768], P(('rows', 'blk'))
- ln1_bias_grad: float32 [768], P(('rows', 'blk'))
- w_gate_up_grad: float32 [768, 6144], P(('rows', 'blk'))
- w_down_grad: float32 [3072, 768], P(('rows', 'blk'))
- ln2_gain_grad: float32 [768], P(('rows', 'blk'))
- ln2_bias_grad: float32 [768], P(('rows', 'blk'))
- stats: float32 [4], replicated
The draws below stay inside these ranges and needn't reach their ends.
Inputs may be any that keep to these rules, and one draw needn't show every extreme that they name: `segments`: each packed row is a run of fragments labelled 0, 1, 2, ... in order, each of at most 512 positions (all but the last one before the padding at least 128), one of them exactly 512, followed by 1 to 255 padding positions labelled 1024.
All inputs are finite; a program needn't handle non-finite values.
Results may differ from the reference program's by a relative error of at most 0.014.
Values may be sent and summed in bfloat16 or wider, within the bound.
A program may use at most 192 MiB of HBM per device.

```python
import math
import jax
import jax.numpy as jnp
from jax import lax

D = 768
HEADS = 12
FF = 3072
FRAG = 512
TOK_DEV = 512
SEQ = 1024
ROWS = 16


def draw_segments(key, part):
    key = jax.random.fold_in(key, 11)
    size_key, pick_key, short_key, pad_key = jax.random.split(key, 4)
    count = SEQ // (FRAG // 4) + 2
    pieces = jax.random.randint(size_key, (ROWS, count), FRAG // 4, FRAG + 1)
    chosen = jax.random.randint(pick_key, (ROWS, 1), 0, 2)
    shorter = jax.random.randint(short_key, (ROWS, 1), FRAG // 4, FRAG // 2 + 1)
    index = jnp.arange(count, dtype=jnp.int32)[None, :]
    pieces = jnp.where(index == chosen, FRAG, pieces)
    pieces = jnp.where((index == 0) & (chosen == 1), shorter, pieces)
    ends = jnp.cumsum(pieces, 1)
    padding = jax.random.randint(pad_key, (ROWS, 1), 1, TOK_DEV // 2)
    places = jnp.arange(SEQ, dtype=jnp.int32)[None, :]
    labels = jnp.sum((places[:, :, None] >= ends[:, None, :]).astype(jnp.int32), -1)
    return jnp.where(places >= SEQ - padding, SEQ, labels).astype(jnp.int32)


def block_levels(own_key, extent, cuts, smallest, largest):
    loudness = 1.0
    for axis_at, parts in cuts:
        steps = jax.random.uniform(jax.random.fold_in(jax.random.fold_in(own_key, 6), axis_at), (parts,), jnp.float32, smallest / len(cuts), largest / len(cuts))
        loudness = loudness * jnp.repeat(jnp.exp(steps), extent[axis_at] // parts).reshape((-1,) + (1,) * (len(extent) - 1 - axis_at))
    return loudness


def scatter_about(own_key, shape, scale, bound, cuts=(), kind=jnp.bfloat16):
    factor_of = block_levels(own_key, shape, cuts, -0.22, 0.18) if cuts else 1.0
    drawn = jax.random.normal(own_key, shape, jnp.float32) * scale * factor_of
    return jnp.minimum(jnp.maximum(drawn, -bound), bound).astype(kind)


def setup_inputs(seed: int = 0) -> dict:
    key_list = jax.random.split(jax.random.key(seed), 12)
    return {
        "tokens": scatter_about(key_list[0], (ROWS, SEQ, D), 1.0, 6.0, ((0, 16), (1, 2))),
        "segments": draw_segments(jax.random.fold_in(key_list[11], 71), 0),
        "w_qkv": scatter_about(key_list[2], (D, 3 * D), D ** -0.5, 0.21875, ((0, 32),)),
        "w_out": scatter_about(key_list[3], (D, D), (D // 32) ** -0.5, 1.25, ((0, 32),)),
        "ln1_gain": jnp.clip(1.0 + 0.1 * jax.random.normal(key_list[4], (D,), jnp.float32), 0.5, 1.5).astype(jnp.bfloat16),
        "ln1_bias": scatter_about(key_list[5], (D,), 0.3, 1.796875, ((0, 32),)),
        "w_gate_up": scatter_about(key_list[6], (D, 2 * FF), D ** -0.5, 0.21875, ((0, 32),)),
        "w_down": scatter_about(key_list[7], (FF, D), FF ** -0.5, 0.109375, ((0, 32),)),
        "ln2_gain": jnp.clip(1.0 + 0.1 * jax.random.normal(key_list[8], (D,), jnp.float32), 0.5, 1.5).astype(jnp.bfloat16),
        "ln2_bias": scatter_about(key_list[9], (D,), 0.3, 1.796875, ((0, 32),)),
        "out_grad": scatter_about(key_list[10], (ROWS, SEQ, D), 1.0, 6.0, ((0, 16), (1, 2))),
    }


@jax.custom_vjp
def low(v):
    return lax.optimization_barrier(v.astype(jnp.bfloat16)).astype(jnp.float32)

@jax.custom_vjp
def low_back(v):
    return v

def low_keep(v):
    return (low(v), None)

def low_pass(kept, grad):
    return (grad,)

def back_keep(v):
    return (v, None)

def back_low(kept, grad):
    return (low(grad),)
low.defvjp(low_keep, low_pass)
low_back.defvjp(back_keep, back_low)
ln_eps = 1e-12
masked_score = -1e+30

def product(left, right):
    return jnp.dot(left, right, precision=lax.Precision.HIGHEST, preferred_element_type=jnp.float32)

def layer_norm(resid, gain, bias):
    mean = lax.optimization_barrier(jnp.mean(resid, -1, keepdims=True))
    centred = resid - mean
    spread = lax.optimization_barrier(jnp.mean(centred * centred, -1, keepdims=True))
    return centred * lax.rsqrt(spread + ln_eps) * gain + bias

def geglu(gate_up):
    half = gate_up.shape[-1] // 2
    return jax.nn.gelu(gate_up[:, :half], approximate=False) * gate_up[:, half:]

def head_slopes(heads):
    order = jnp.arange(1, heads + 1, dtype=jnp.float32)
    return jnp.exp2(-8.0 * order / heads)

def permitted(labels_q, labels_k, pos_q, pos_k, pad_label):
    same_piece = (labels_q[:, None] == labels_k[None, :]) & (labels_k[None, :] != pad_label)
    return same_piece | (pos_q[:, None] == pos_k[None, :])

def row_pass(inputs, labels, weights):
    w_qkv, w_out, gain_one, bias_one, w_gate_up, w_down, gain_two, bias_two = weights
    seq_len, width = inputs.shape
    heads = HEADS
    depth = width // heads
    qkv = low(low_back(product(inputs, w_qkv)))

    def heads_first(matrix):
        return matrix.reshape(seq_len, heads, depth).transpose(1, 0, 2)
    query = heads_first(qkv[:, :width])
    key = heads_first(qkv[:, width:2 * width])
    value = heads_first(qkv[:, 2 * width:])
    slopes = head_slopes(heads)
    positions = jnp.arange(seq_len, dtype=jnp.int32)
    block_rows = math.gcd(seq_len, 512)

    def attend(index):
        start = index * block_rows
        q_blk = lax.dynamic_slice_in_dim(query, start, block_rows, 1)
        q_pos = lax.dynamic_slice_in_dim(positions, start, block_rows, 0)
        q_lab = lax.dynamic_slice_in_dim(labels, start, block_rows, 0)
        raw = jnp.einsum('hqd,hkd->hqk', q_blk, key, precision=lax.Precision.HIGHEST, preferred_element_type=jnp.float32) * depth ** (-0.5)
        distance = jnp.abs(q_pos[:, None] - positions[None, :]).astype(jnp.float32)
        raw = low_back(raw - slopes[:, None, None] * distance[None])
        logits = jnp.where(permitted(q_lab, labels, q_pos, positions, seq_len)[None], raw, masked_score)
        top = lax.optimization_barrier(jnp.max(logits, -1, keepdims=True))
        lse = top + jnp.log(lax.optimization_barrier(jnp.sum(jnp.exp(logits - top), -1, keepdims=True)))
        probs = low(jnp.exp(logits - lse))
        return jnp.einsum('hqk,hkd->hqd', probs, value, precision=lax.Precision.HIGHEST, preferred_element_type=jnp.float32)
    blocks = lax.map(jax.checkpoint(attend), jnp.arange(seq_len // block_rows, dtype=jnp.int32))
    attended = low(low_back(blocks.transpose(0, 2, 1, 3).reshape(seq_len, width)))
    branch_a = low_back(product(attended, w_out))
    hidden1 = layer_norm(inputs + branch_a, gain_one, bias_one)
    gate_up = low_back(product(low(hidden1), w_gate_up))
    act = low(geglu(gate_up))
    branch_f = low_back(product(act, w_down))
    result = layer_norm(hidden1 + branch_f, gain_two, bias_two)
    valid = (labels != seq_len).astype(inputs.dtype)[:, None]
    squares = jnp.stack([jnp.sum(valid * term * term) for term in (inputs, branch_a, hidden1, branch_f)])
    return (result, squares)

def reference(tokens, segments, w_qkv, w_out, ln1_gain, ln1_bias, w_gate_up, w_down, ln2_gain, ln2_bias, out_grad):
    floats = tuple((arr.astype(jnp.float32) for arr in (tokens, w_qkv, w_out, ln1_gain, ln1_bias, w_gate_up, w_down, ln2_gain, ln2_bias)))

    def whole(inputs, *weights):

        def single(x_row, lab_row):
            return row_pass(x_row, lab_row, weights)
        checked = jax.checkpoint(single)

        def step(total, row):
            out_row, squares = checked(row[0], row[1])
            return (total + squares, out_row)
        total, outs = lax.scan(step, jnp.zeros((4,), jnp.float32), (inputs, segments))
        return (outs, total)
    outs, pullback, total = jax.vjp(whole, *floats, has_aux=True)
    grads = pullback(out_grad.astype(jnp.float32))
    count = jnp.sum((segments != SEQ).astype(jnp.float32))
    stats = jnp.sqrt(total / (count * D))
    return (outs.astype(jnp.bfloat16), grads[0].astype(jnp.bfloat16), grads[1], grads[2], grads[3], grads[4], grads[5], grads[6], grads[7], grads[8], stats)
```

```python
import jax
import jax.numpy as jnp
from jax import lax
from jax.experimental import pallas as pl
from jax.experimental.pallas import tpu as pltpu
from jax.sharding import PartitionSpec as P

MESH = pl.DeviceIdType.MESH


class Place:
    def __init__(self):
        r, self.c = lax.axis_index("rows"), lax.axis_index("blk")
        self.x, self.y, self.z = r % 2, (r // 2) % 2, r // 4
        self.sib = (r, 1 - self.c)
        self.xn = (self.at(0, "x"), self.c)
        self.yn = (self.at(0, "y"), self.c)
        self.zn = {k: (self.at(k, "o"), self.c) for k in (1, 2, 3)}

    def plane(self, k):
        z, low = self.z % 2, self.z // 2
        if k % 2:
            z = 1 - z
        if k // 2:
            low = 1 - low
        return low * 2 + z

    def at(self, k, j):
        x = 1 - self.x if j in "xd" else self.x
        y = 1 - self.y if j in "yd" else self.y
        return self.plane(k) * 4 + y * 2 + x

    def greet(self):
        barrier = pltpu.get_barrier_semaphore()
        peers = [self.sib, self.xn, self.yn] + [self.zn[k] for k in (1, 2, 3)]
        for peer in peers:
            pl.semaphore_signal(barrier, inc=1, device_id=peer, device_id_type=MESH)
        pl.semaphore_wait(barrier, len(peers))


class Copies:
    def __init__(self, send, recv):
        self.send, self.recv, self.open = send, recv, []

    def put(self, src, dst, slot, peer):
        copy = pltpu.make_async_remote_copy(
            src_ref=src, dst_ref=dst, send_sem=self.send.at[slot], recv_sem=self.recv.at[slot],
            device_id=peer, device_id_type=MESH,
        )
        copy.start()
        self.open.append(copy)

    def got(self, dst, slot, peer):
        pltpu.make_async_remote_copy(
            src_ref=dst, dst_ref=dst, send_sem=self.send.at[slot], recv_sem=self.recv.at[slot],
            device_id=peer, device_id_type=MESH,
        ).wait_recv()

    def drain(self):
        for copy in self.open:
            copy.wait_send()
        self.open = []


class Gather:
    def __init__(self, place, copies, base, own, out):
        self.p, self.cp, self.base, self.own, self.out = place, copies, base, own, out

    def slot(self, kind, k, j="o"):
        start = {"z": -1, "x": 3, "y": 7, "d": 11, "s": 15}[kind]
        return self.base + start + (4 * k + "oxyd".index(j) if kind == "s" else k)

    def block(self, k, j):
        return self.out(self.p.c, self.p.at(k, j))

    def push(self, src, k, j):
        self.cp.put(src, self.block(k, j), self.slot("s", k, j), self.p.sib)

    def own_z(self):
        for k in (1, 2, 3):
            self.cp.put(self.own, self.block(0, "o"), self.slot("z", k), self.p.zn[k])

    def own_xy(self):
        self.spread(self.own, 0)

    def spread(self, src, k):
        dst = self.block(k, "o")
        self.cp.put(src, dst, self.slot("x", k), self.p.xn)
        self.cp.put(src, dst, self.slot("y", k), self.p.yn)
        self.push(src, k, "o")

    def from_z(self, k):
        block = self.block(k, "o")
        self.cp.got(block, self.slot("z", k), self.p.zn[k])
        self.spread(block, k)

    def from_xy(self, k):
        x, y = self.block(k, "x"), self.block(k, "y")
        self.cp.got(x, self.slot("x", k), self.p.xn)
        if k >= 2:
            self.cp.put(x, x, self.slot("d", k), self.p.yn)
        self.push(x, k, "x")
        self.cp.got(y, self.slot("y", k), self.p.yn)
        if k < 2:
            self.cp.put(y, y, self.slot("d", k), self.p.xn)
        self.push(y, k, "y")

    def from_d(self, k):
        block = self.block(k, "d")
        self.cp.got(block, self.slot("d", k), self.p.xn)
        self.push(block, k, "d")

    def from_sib(self):
        for k in range(4):
            for j in "oxyd":
                block = self.out(1 - self.p.c, self.p.at(k, j))
                self.cp.got(block, self.slot("s", k, j), self.p.sib)


def low_add(left, right):
    return left + right


class Scatter:
    def __init__(self, place, copies, base, local, grad, own, sib, rly, xin, yin, out, zin):
        self.p, self.cp, self.base, self.local, self.grad = place, copies, base, local, grad
        self.own, self.sib, self.rly, self.xin, self.yin, self.out, self.zin = own, sib, rly, xin, yin, out, zin

    def slot(self, kind, k):
        return self.base + {"s": 0, "r": 4, "x": 8, "y": 12, "z": 15}[kind] + k

    def load(self, k):
        four = pl.ds(self.p.plane(k) * 4, 4)
        return pltpu.make_async_copy(self.grad(self.p.c, four), self.own.at[four], self.local.at[self.base + k])

    def begin(self, k):
        four = pl.ds(self.p.plane(k) * 4, 4)
        self.cp.put(self.grad(1 - self.p.c, four), self.sib.at[four], self.slot("s", k), self.p.sib)
        self.load(k).start()

    def pair(self, k):
        p = self.p
        four = pl.ds(p.plane(k) * 4, 4)
        self.load(k).wait()
        self.cp.got(self.sib.at[four], self.slot("s", k), p.sib)
        d, x, y = p.at(k, "d"), p.at(k, "x"), p.at(k, "y")
        self.own[d] = low_add(self.own[d], self.sib[d])
        self.cp.put(self.own.at[d], self.rly.at[k], self.slot("r", k), p.xn if k < 2 else p.yn)
        if k < 2:
            self.own[x] = low_add(self.own[x], self.sib[x])
            self.cp.put(self.own.at[x], self.xin.at[k], self.slot("x", k), p.xn)
        else:
            self.own[y] = low_add(self.own[y], self.sib[y])
            self.cp.put(self.own.at[y], self.yin.at[k], self.slot("y", k), p.yn)

    def relay(self, k):
        p = self.p
        x, y = p.at(k, "x"), p.at(k, "y")
        self.cp.got(self.rly.at[k], self.slot("r", k), p.xn)
        if k < 2:
            self.own[y] = low_add(low_add(self.own[y], self.sib[y]), self.rly[k])
            self.cp.put(self.own.at[y], self.yin.at[k], self.slot("y", k), p.yn)
        else:
            self.own[x] = low_add(low_add(self.own[x], self.sib[x]), self.rly[k])
            self.cp.put(self.own.at[x], self.xin.at[k], self.slot("x", k), p.xn)

    def plane(self, k):
        p = self.p
        o = p.at(k, "o")
        self.cp.got(self.xin.at[k], self.slot("x", k), p.xn)
        self.cp.got(self.yin.at[k], self.slot("y", k), p.yn)
        wide = jnp.float32
        total = (self.own[o].astype(wide) + self.sib[o].astype(wide)) + (
            self.xin[k].astype(wide) + self.yin[k].astype(wide)
        )
        self.out[k] = total.astype(jnp.bfloat16)
        if k:
            self.cp.put(self.out.at[k], self.zin.at[k - 1], self.slot("z", k), p.zn[k])

    def total(self):
        for k in (1, 2, 3):
            self.cp.got(self.zin.at[k - 1], self.slot("z", k), self.p.zn[k])
        wide = jnp.float32
        return (self.out[0].astype(wide) + self.zin[0].astype(wide)) + (
            self.zin[1].astype(wide) + self.zin[2].astype(wide)
        )


rows_chip = 48
gather_slots, scatter_slots = 31, 19


def gather_kernel(a_shard, g_shard, d_own, a_full, g_full, d_full, a_pair, g_pair, a_own, g_own, pair_sem, send, recv, local):
    place = Place()
    place.greet()
    c = place.c
    pairs = Copies(pair_sem.at[0], pair_sem.at[1])
    for i, (shard, other) in enumerate(((a_shard, a_pair), (g_shard, g_pair))):
        pairs.put(shard.at[1 - c], other, i, place.sib)
    copies = Copies(send, recv)
    a_out = lambda half, r: a_full.at[half, r]
    g_out = lambda half, r: g_full.at[half, r]
    d_out = lambda half, r: d_full.at[r, half]
    mats = [
        Gather(place, copies, 0, a_own, a_out),
        Gather(place, copies, gather_slots, g_own, g_out),
        Gather(place, copies, 2 * gather_slots, d_own, d_out),
    ]
    att, gat, dow = mats

    def assemble(shard, other, own, i):
        pairs.got(other, i, place.sib)
        mine = shard[c, :24, :].astype(jnp.float32)
        theirs = other[:24, :].astype(jnp.float32)
        first = c == 0
        top = jnp.where(first, mine, theirs)
        low = jnp.where(first, theirs, mine)
        own[...] = jnp.concatenate([top, low], 0).astype(jnp.bfloat16)

    kept = [pltpu.make_async_copy(m.own, m.block(0, "o"), local.at[i]) for i, m in enumerate(mats)]
    assemble(a_shard, a_pair, a_own, 0)
    att.own_z()
    att.own_xy()
    kept[0].start()
    assemble(g_shard, g_pair, g_own, 1)
    gat.own_z()
    dow.own_z()
    kept[1].start()
    kept[2].start()
    for k in (1, 2, 3):
        att.from_z(k)
    for k in range(4):
        att.from_xy(k)
    gat.own_xy()
    for k in (1, 2, 3):
        gat.from_z(k)
    for k in range(4):
        att.from_d(k)
    for k in range(4):
        gat.from_xy(k)
    dow.own_xy()
    for k in (1, 2, 3):
        dow.from_z(k)
    for k in range(4):
        gat.from_d(k)
    for k in range(4):
        dow.from_xy(k)
    for k in range(4):
        dow.from_d(k)
    for m in mats:
        m.from_sib()
    for copy in kept:
        copy.wait()
    pairs.drain()
    copies.drain()


def gather_weights(a_shard, g_shard, d_shard):
    half_a, half_g = a_shard.shape[-1], g_shard.shape[-1]
    low = jnp.bfloat16
    return pl.pallas_call(
        gather_kernel,
        out_shape=(
            jax.ShapeDtypeStruct((2, 16, rows_chip, half_a), low),
            jax.ShapeDtypeStruct((2, 16, rows_chip, half_g), low),
            jax.ShapeDtypeStruct((16, 2) + d_shard.shape, low),
        ),
        in_specs=[pl.BlockSpec(memory_space=pltpu.VMEM)] * 3,
        out_specs=(pl.BlockSpec(memory_space=pl.ANY),) * 3,
        scratch_shapes=[
            pltpu.VMEM(a_shard.shape[1:], low),
            pltpu.VMEM(g_shard.shape[1:], low),
            pltpu.VMEM((rows_chip, half_a), low),
            pltpu.VMEM((rows_chip, half_g), low),
            pltpu.SemaphoreType.DMA((2, 2)),
            pltpu.SemaphoreType.DMA((3 * gather_slots,)),
            pltpu.SemaphoreType.DMA((3 * gather_slots,)),
            pltpu.SemaphoreType.DMA((3,)),
        ],
        compiler_params=pltpu.CompilerParams(
            collective_id=0, has_side_effects=True, vmem_limit_bytes=32 * 2**20
        ),
        name="gather_weights",
    )(a_shard, g_shard, d_shard)


def scatter_kernel(
    a_grad, g_grad, d_grad, small, qkv_out, wout_out, gu_out, down_out, small_out, *scratch
):
    place = Place()
    place.greet()
    c = place.c
    bufs, (a_sum, g_sum, a_fin, g_fin, small_buf, send, recv, local, fin_sem) = scratch[:21], scratch[21:]
    copies = Copies(send, recv)
    last = Copies(fin_sem.at[0], fin_sem.at[1])
    a_at = lambda half, four: a_grad.at[half, four]
    g_at = lambda half, four: g_grad.at[half, four]
    d_at = lambda half, four: d_grad.at[four, half]
    mats = [
        Scatter(place, copies, i * scatter_slots, local, at, *bufs[7 * i : 7 * i + 7])
        for i, at in enumerate((g_at, d_at, a_at))
    ]
    order = [(m, k) for m in mats for k in (3, 2, 1, 0)]
    depth = 3
    steps = ["begin", "pair", "relay", "plane"]
    hops = ((place.sib, 0), (place.xn, 1), (place.yn, 2))

    def exchange(i):
        peer, slot = hops[i]
        last.put(small_buf.at[i], small_buf.at[4 + i], slot, peer)

    def combine(i):
        peer, slot = hops[i]
        last.got(small_buf.at[4 + i], slot, peer)
        small_buf[i + 1] = small_buf[i] + small_buf[4 + i]

    small_buf[0] = small[...]
    exchange(0)
    for t in range(len(order) + depth):
        for s, name in enumerate(steps):
            if 0 <= t - s < len(order):
                m, k = order[t - s]
                getattr(m, name)(k)
        if 1 <= t <= 3:
            combine(t - 1)
            if t < 3:
                exchange(t)
            else:
                for k in (1, 2, 3):
                    last.put(small_buf.at[3], small_buf.at[6 + k], 2 + k, place.zn[k])
    for k in (1, 2, 3):
        last.got(small_buf.at[6 + k], 2 + k, place.zn[k])
    small_out[...] = (small_buf[3] + small_buf[7]) + (small_buf[8] + small_buf[9])
    gate, down, att = mats
    down_out[...] = down.total()
    g_sum[...] = gate.total()
    mine, theirs = pl.ds(pl.multiple_of(24 * c, 8), 24), pl.ds(pl.multiple_of(24 - 24 * c, 8), 24)
    last.put(g_sum.at[theirs], g_fin, 6, place.sib)
    a_sum[...] = att.total()
    last.put(a_sum.at[theirs], a_fin, 7, place.sib)
    first = c == 0
    last.got(g_fin, 6, place.sib)
    last.got(a_fin, 7, place.sib)
    half_g = g_fin.shape[1]
    gu_out[:, :half_g] = jnp.where(first, g_sum[mine], g_fin[...])
    gu_out[:, half_g:] = jnp.where(first, g_fin[...], g_sum[mine])
    left = jnp.where(first, a_sum[mine], a_fin[...])
    right = jnp.where(first, a_fin[...], a_sum[mine])
    cut = qkv_out.shape[1] - left.shape[1]
    qkv_out[:, : left.shape[1]] = left
    qkv_out[:, left.shape[1] :] = right[:, :cut]
    wout_out[...] = right[:, cut:]
    copies.drain()
    last.drain()


def scatter_grads(a_grad, g_grad, d_grad, small):
    low = jnp.bfloat16
    bufs = []
    for rows, half in ((rows_chip, g_grad.shape[-1]), d_grad.shape[2:], (rows_chip, a_grad.shape[-1])):
        for count in (16, 16, 4, 4, 4, 4, 3):
            bufs.append(pltpu.VMEM((count, rows, half), low))
    half_a, half_g = a_grad.shape[-1], g_grad.shape[-1]
    width = d_grad.shape[-1]
    wide = jnp.float32
    return pl.pallas_call(
        scatter_kernel,
        out_shape=(
            jax.ShapeDtypeStruct((24, 3 * width), wide),
            jax.ShapeDtypeStruct((24, width), wide),
            jax.ShapeDtypeStruct((24, 2 * half_g), wide),
            jax.ShapeDtypeStruct(d_grad.shape[2:], wide),
            jax.ShapeDtypeStruct(small.shape, wide),
        ),
        in_specs=[pl.BlockSpec(memory_space=pl.ANY)] * 3 + [pl.BlockSpec(memory_space=pltpu.VMEM)],
        out_specs=(pl.BlockSpec(memory_space=pltpu.VMEM),) * 5,
        scratch_shapes=bufs
        + [
            pltpu.VMEM((rows_chip, half_a), wide),
            pltpu.VMEM((rows_chip, half_g), wide),
            pltpu.VMEM((24, half_a), wide),
            pltpu.VMEM((24, half_g), wide),
            pltpu.VMEM((10,) + small.shape, wide),
            pltpu.SemaphoreType.DMA((3 * scatter_slots,)),
            pltpu.SemaphoreType.DMA((3 * scatter_slots,)),
            pltpu.SemaphoreType.DMA((3 * scatter_slots,)),
            pltpu.SemaphoreType.DMA((2, 8)),
        ],
        compiler_params=pltpu.CompilerParams(
            collective_id=1, has_side_effects=True, vmem_limit_bytes=60 * 2**20
        ),
        name="scatter_grads",
    )(a_grad, g_grad, d_grad, small)


HEADS = 12


ln_eps = 1e-12
masked_score = -1e30
group_heads = 2
lane_width = 128


def extended(cells, sides, width):
    for axis, dim in sides:
        count = lax.axis_size(axis)
        ends = count - 1
        head = lax.slice_in_dim(cells, 0, width, axis=dim)
        tail = lax.slice_in_dim(cells, cells.shape[dim] - width, cells.shape[dim], axis=dim)
        cells = jnp.concatenate(
            [
                lax.ppermute(tail, axis, [(i, (i + 1) % count) for i in range(ends)]),
                cells,
                lax.ppermute(head, axis, [((i + 1) % count, i) for i in range(ends)]),
            ],
            axis=dim,
        )
    return cells


def layer_norm(resid, gain, bias):
    mean = jnp.mean(resid, -1, keepdims=True)
    centred = resid - mean
    spread = jnp.mean(centred * centred, -1, keepdims=True)
    return centred * lax.rsqrt(spread + ln_eps) * gain + bias


def geglu(gate_up):
    half = gate_up.shape[-1] // 2
    return jax.nn.gelu(gate_up[:, :half], approximate=False) * gate_up[:, half:]


def head_slopes(heads):
    order = jnp.arange(1, heads + 1, dtype=jnp.float32)
    return jnp.exp2(-8.0 * order / heads)


def permitted(labels_q, labels_k, pos_q, pos_k, pad_label):
    same_piece = (labels_q[:, None] == labels_k[None, :]) & (labels_k[None, :] != pad_label)
    return same_piece | (pos_q[:, None] == pos_k[None, :])


def times_transposed(left, right):
    return lax.dot_general(
        left, right, (((1,), (1,)), ((), ())), preferred_element_type=jnp.float32
    )


def transposed_times(left, right):
    return lax.dot_general(
        left, right, (((0,), (0,)), ((), ())), preferred_element_type=jnp.float32
    )


def split_heads(matrix, heads):
    count, width = matrix.shape
    return matrix.reshape(count, heads // group_heads, group_heads, width // heads).transpose(
        1, 2, 0, 3
    )


def merge_heads(groups):
    number, size, count, depth = groups.shape
    return groups.transpose(2, 0, 1, 3).reshape(count, number * size * depth)


def lane_rows(matrix):
    return matrix.reshape(-1, lane_width)


def owner_rows(flat, whole_rows, columns, owners):
    return flat.reshape(whole_rows // owners, columns)


def group_scores(q_grp, k_grp, slope_grp, distance, allowed):
    scale = q_grp.shape[-1] ** (-0.5)
    raw = jnp.einsum("gqd,gkd->gqk", q_grp, k_grp, preferred_element_type=jnp.float32) * scale
    raw = raw - slope_grp[:, None, None] * distance[None]
    return jnp.where(allowed[None], raw, masked_score)


def body(
    tokens,
    segments,
    w_qkv,
    w_out,
    ln1_gain,
    ln1_bias,
    w_gate_up,
    w_down,
    ln2_gain,
    ln2_bias,
    out_grad,
):
    inputs = tokens[0]
    tok_rows, width = inputs.shape
    heads = HEADS
    owners = lax.axis_size(("rows", "blk"))
    labels = segments[0]
    seq_len = labels.shape[0]
    first = lax.axis_index("blk") * tok_rows
    query_pos = first + jnp.arange(tok_rows, dtype=jnp.int32)
    window_pos = first - tok_rows + jnp.arange(3 * tok_rows, dtype=jnp.int32)
    query_labels = lax.dynamic_slice_in_dim(labels, first, tok_rows, 0)
    padded_labels = jnp.pad(labels, (tok_rows, tok_rows), constant_values=seq_len)
    window_labels = lax.dynamic_slice_in_dim(padded_labels, first, 3 * tok_rows, 0)
    slope_groups = head_slopes(heads).reshape(heads // group_heads, group_heads)
    allowed = permitted(query_labels, window_labels, query_pos, window_pos, seq_len)
    distance = jnp.abs(query_pos[:, None] - window_pos[None, :]).astype(jnp.float32)
    gathered = gathered_weights(w_qkv, w_out, ln1_gain, ln1_bias, w_gate_up, w_down, ln2_gain, ln2_bias)
    wqkv_full, wout_full, wgu_full, wdown_full, gain_one, bias_one, gain_two, bias_two = gathered
    qkv = jnp.dot(inputs, wqkv_full, preferred_element_type=jnp.float32).astype(jnp.bfloat16)
    query = qkv[:, :width]
    window_kv = extended(qkv[:, width:], (("blk", 0),), tok_rows)
    q_groups = split_heads(query, heads)
    k_groups = split_heads(window_kv[:, :width], heads)
    v_groups = split_heads(window_kv[:, width:], heads)

    def forward_group(parts):
        q_grp, k_grp, v_grp, slope_grp = parts
        logits = group_scores(q_grp, k_grp, slope_grp, distance, allowed)
        top = jnp.max(logits, -1, keepdims=True)
        lse = top + jnp.log(jnp.sum(jnp.exp(logits - top), -1, keepdims=True))
        probs = jnp.exp(logits - lse).astype(jnp.bfloat16)
        mixed = jnp.einsum("gqk,gkd->gqd", probs, v_grp, preferred_element_type=jnp.float32)
        return (mixed, lse[..., 0])

    mixed_groups, lse_groups = lax.map(forward_group, (q_groups, k_groups, v_groups, slope_groups))
    attended = merge_heads(mixed_groups).astype(jnp.bfloat16)
    branch_a = jnp.dot(attended, wout_full, preferred_element_type=jnp.float32)
    inputs_float = inputs.astype(jnp.float32)
    resid_one = inputs_float + branch_a
    hidden1, norm_one_back = jax.vjp(
        layer_norm, resid_one, gain_one.astype(jnp.float32), bias_one.astype(jnp.float32)
    )
    hidden1_low = hidden1.astype(jnp.bfloat16)
    gate_up = jnp.dot(hidden1_low, wgu_full, preferred_element_type=jnp.float32)
    act, glu_back = jax.vjp(geglu, gate_up)
    act_low = act.astype(jnp.bfloat16)
    branch_f = jnp.dot(act_low, wdown_full, preferred_element_type=jnp.float32)
    final, norm_two_back = jax.vjp(
        layer_norm, hidden1 + branch_f, gain_two.astype(jnp.float32), bias_two.astype(jnp.float32)
    )
    output = final.astype(jnp.bfloat16)[None]
    valid = (query_labels != seq_len).astype(jnp.float32)[:, None]
    squares = jnp.stack(
        [jnp.sum(valid * term * term) for term in (inputs_float, branch_a, hidden1, branch_f)]
    )
    d_resid_two, d_gain_two, d_bias_two = norm_two_back(out_grad[0].astype(jnp.float32))
    d_branch_f = d_resid_two.astype(jnp.bfloat16)
    wgu_back, wdown_back, wqkv_back, wout_back = wgu_full, wdown_full, wqkv_full, wout_full
    d_act = times_transposed(d_branch_f, wdown_back)
    (d_gate_up,) = glu_back(d_act)
    d_gate_up_low = d_gate_up.astype(jnp.bfloat16)
    grad_down = transposed_times(act_low, d_branch_f)
    grad_gate_up = transposed_times(hidden1_low, d_gate_up_low)
    d_hidden1 = d_resid_two + times_transposed(d_gate_up_low, wgu_back)
    d_resid_one, d_gain_one, d_bias_one = norm_one_back(d_hidden1)
    d_branch_a = d_resid_one.astype(jnp.bfloat16)
    grad_out = transposed_times(attended, d_branch_a)
    d_attended = times_transposed(d_branch_a, wout_back).astype(jnp.bfloat16)
    do_groups = split_heads(d_attended, heads)
    scale = width // heads
    scale = scale ** (-0.5)

    def backward_group(parts):
        q_grp, k_grp, v_grp, slope_grp, do_grp, lse_grp = parts
        logits = group_scores(q_grp, k_grp, slope_grp, distance, allowed)
        probs = jnp.exp(logits - lse_grp[..., None])
        dprob = jnp.einsum("gqd,gkd->gqk", do_grp, v_grp, preferred_element_type=jnp.float32)
        delta = jnp.sum(probs * dprob, -1, keepdims=True)
        dlogit = (probs * (dprob - delta)).astype(jnp.bfloat16)
        dq = jnp.einsum("gqk,gkd->gqd", dlogit, k_grp, preferred_element_type=jnp.float32) * scale
        dk = jnp.einsum("gqk,gqd->gkd", dlogit, q_grp, preferred_element_type=jnp.float32) * scale
        dv = jnp.einsum(
            "gqk,gqd->gkd", probs.astype(jnp.bfloat16), do_grp, preferred_element_type=jnp.float32
        )
        return (dq, dk, dv)

    dq_groups, dk_groups, dv_groups = lax.map(
        backward_group, (q_groups, k_groups, v_groups, slope_groups, do_groups, lse_groups)
    )
    kv_terms = jnp.concatenate([merge_heads(dk_groups), merge_heads(dv_groups)], 1)
    outward = jnp.concatenate([kv_terms[:tok_rows], kv_terms[2 * tok_rows :]], 0)
    received = extended(outward.astype(jnp.bfloat16), (("blk", 0),), tok_rows).astype(outward.dtype)
    kv_own = kv_terms[tok_rows : 2 * tok_rows] + received[:tok_rows] + received[3 * tok_rows :]
    d_qkv = jnp.concatenate(
        [merge_heads(dq_groups).astype(jnp.bfloat16), kv_own.astype(jnp.bfloat16)], 1
    )
    grad_qkv = transposed_times(inputs, d_qkv)
    tokens_grad = (d_resid_one + times_transposed(d_qkv, wqkv_back)).astype(jnp.bfloat16)[None]
    parts, vectors, square_sums, valid_count = summed_grads(
        grad_qkv, grad_out, grad_gate_up, grad_down,
        (d_gain_one, d_bias_one, d_gain_two, d_bias_two), squares, jnp.sum(valid),
    )
    stats = jnp.sqrt(square_sums / (valid_count * width))
    return (
        output, tokens_grad, parts[0], parts[1], vectors[0], vectors[1],
        parts[2], parts[3], vectors[2], vectors[3], stats,
    )


def on_chip_grid():
    return lax.axis_size("rows") == 16 and lax.axis_size("blk") == 2


def gathered_weights(w_qkv, w_out, ln1_gain, ln1_bias, w_gate_up, w_down, ln2_gain, ln2_bias):
    vectors = (ln1_gain, ln1_bias, ln2_gain, ln2_bias)
    both = ("rows", "blk")
    if not on_chip_grid():
        mats = [lax.all_gather(w, both, axis=0, tiled=True) for w in (w_qkv, w_out, w_gate_up, w_down)]
        table = lax.all_gather(jnp.stack(vectors, 1), both, axis=0, tiled=True)
        return (*mats, *(table[:, i] for i in range(4)))
    width = w_out.shape[1]
    rows = w_out.shape[0]
    table = jnp.pad(jnp.stack(vectors, 1), ((0, 0), (0, lane_width - 4)))
    left = jnp.concatenate([w_qkv[:, : 2 * width], table], 1)
    right = jnp.concatenate([w_qkv[:, 2 * width :], w_out, jnp.zeros_like(table)], 1)
    spare = ((0, 0), (0, 32 - rows), (0, 0))
    a_shard = jnp.pad(jnp.stack([left, right]), spare)
    ff = w_gate_up.shape[1] // 2
    g_shard = jnp.pad(jnp.stack([w_gate_up[:, :ff], w_gate_up[:, ff:]]), spare)
    a_full, g_full, d_full = gather_weights(a_shard, g_shard, w_down)
    a_left, a_right = a_full.reshape(2, width, -1)
    wqkv = jnp.concatenate([a_left[:, : 2 * width], a_right[:, :width]], 1)
    wout = a_right[:, width : 2 * width]
    wgu = jnp.concatenate([*g_full.reshape(2, width, ff)], 1)
    columns = (a_left[:, 2 * width + i] for i in range(4))
    return (wqkv, wout, wgu, d_full.reshape(-1, width), *columns)


def summed_grads(grad_qkv, grad_out, grad_gate_up, grad_down, vectors, squares, count):
    both = ("rows", "blk")
    width = grad_out.shape[1]
    owners = lax.axis_size(both)
    if not on_chip_grid():
        parts = [
            lax.psum_scatter(g, both, scatter_dimension=0, tiled=True)
            for g in (grad_qkv, grad_out, grad_gate_up, grad_down)
        ]
        vectors = [lax.psum_scatter(v, both, scatter_dimension=0, tiled=True) for v in vectors]
        return (parts, vectors, *lax.psum((squares, count), both))
    low = jnp.bfloat16
    left = grad_qkv[:, : 2 * width]
    right = jnp.concatenate([grad_qkv[:, 2 * width :], grad_out], 1)
    ff = grad_gate_up.shape[1] // 2
    chips = lambda m: m.astype(low).reshape(16, -1, m.shape[1])
    a_grad = jnp.stack([chips(left), chips(right)])
    g_grad = jnp.stack([chips(grad_gate_up[:, :ff]), chips(grad_gate_up[:, ff:])])
    d_grad = grad_down.astype(low).reshape(16, 2, -1, width)
    flat = jnp.concatenate([*vectors, squares, count[None]])
    small = jnp.pad(flat, (0, 32 * lane_width - flat.shape[0])).reshape(32, lane_width)
    *parts, small = scatter_grads(a_grad, g_grad, d_grad, small)
    flat = small.reshape(-1)
    me = lax.axis_index("rows") * 2 + lax.axis_index("blk")
    share = width // owners
    mine = [lax.dynamic_slice_in_dim(flat, i * width + me * share, share) for i in range(4)]
    return (parts, mine, flat[4 * width : 4 * width + 4], flat[4 * width + 4])


def solution(mesh):
    placed = (
        P("rows", "blk", None),
        P("rows", None),
        P(("rows", "blk"), None),
        P(("rows", "blk"), None),
        P(("rows", "blk")),
        P(("rows", "blk")),
        P(("rows", "blk"), None),
        P(("rows", "blk"), None),
        P(("rows", "blk")),
        P(("rows", "blk")),
        P("rows", "blk", None),
    )
    return jax.shard_map(
        body,
        mesh=mesh,
        in_specs=placed,
        out_specs=(
            P("rows", "blk", None),
            P("rows", "blk", None),
            P(("rows", "blk"), None),
            P(("rows", "blk"), None),
            P(("rows", "blk")),
            P(("rows", "blk")),
            P(("rows", "blk"), None),
            P(("rows", "blk"), None),
            P(("rows", "blk")),
            P(("rows", "blk")),
            P(),
        ),
        check_vma=False,
    )
```

```python
import jax
import jax.numpy as jnp
from jax import lax
from jax.experimental import pallas as pl
from jax.experimental.pallas import tpu as pltpu
from jax.sharding import PartitionSpec as P

HEADS = 12


ln_eps = 1e-12
far = 1e33
lane_width = 128


def times_transposed(left, right):
    return lax.dot_general(
        left, right, (((1,), (1,)), ((), ())), preferred_element_type=jnp.float32
    )


def transposed_times(left, right):
    return lax.dot_general(
        left, right, (((0,), (0,)), ((), ())), preferred_element_type=jnp.float32
    )


MESH = pl.DeviceIdType.MESH


class Place:
    def __init__(self):
        r, self.c = lax.axis_index("rows"), lax.axis_index("blk")
        self.x, self.y, self.z = r % 2, (r // 2) % 2, r // 4
        self.sib = (r, 1 - self.c)
        self.xn = (self.at(0, "x"), self.c)
        self.yn = (self.at(0, "y"), self.c)
        self.zn = {k: (self.at(k, "o"), self.c) for k in (1, 2, 3)}

    def plane(self, k):
        z, low = self.z % 2, self.z // 2
        if k % 2:
            z = 1 - z
        if k // 2:
            low = 1 - low
        return low * 2 + z

    def at(self, k, j):
        x = 1 - self.x if j in "xd" else self.x
        y = 1 - self.y if j in "yd" else self.y
        return self.plane(k) * 4 + y * 2 + x

    def greet(self):
        barrier = pltpu.get_barrier_semaphore()
        peers = [self.sib, self.xn, self.yn] + [self.zn[k] for k in (1, 2, 3)]
        for peer in peers:
            pl.semaphore_signal(barrier, inc=1, device_id=peer, device_id_type=MESH)
        pl.semaphore_wait(barrier, len(peers))


class Copies:
    def __init__(self, send, recv):
        self.send, self.recv, self.open = send, recv, []

    def put(self, src, dst, slot, peer):
        copy = pltpu.make_async_remote_copy(
            src_ref=src, dst_ref=dst, send_sem=self.send.at[slot], recv_sem=self.recv.at[slot],
            device_id=peer, device_id_type=MESH,
        )
        copy.start()
        self.open.append(copy)

    def got(self, dst, slot, peer):
        pltpu.make_async_remote_copy(
            src_ref=dst, dst_ref=dst, send_sem=self.send.at[slot], recv_sem=self.recv.at[slot],
            device_id=peer, device_id_type=MESH,
        ).wait_recv()

    def drain(self):
        for copy in self.open:
            copy.wait_send()
        self.open = []


class Gather:
    def __init__(self, place, copies, base, own, out):
        self.p, self.cp, self.base, self.own, self.out = place, copies, base, own, out

    def slot(self, kind, k, j="o"):
        start = {"z": -1, "x": 3, "y": 7, "d": 11, "s": 15}[kind]
        return self.base + start + (4 * k + "oxyd".index(j) if kind == "s" else k)

    def block(self, k, j):
        return self.out(self.p.c, self.p.at(k, j))

    def push(self, src, k, j):
        self.cp.put(src, self.block(k, j), self.slot("s", k, j), self.p.sib)

    def own_z(self):
        for k in (1, 2, 3):
            self.cp.put(self.own, self.block(0, "o"), self.slot("z", k), self.p.zn[k])

    def own_xy(self):
        self.spread(self.own, 0)

    def spread(self, src, k):
        dst = self.block(k, "o")
        self.cp.put(src, dst, self.slot("x", k), self.p.xn)
        self.cp.put(src, dst, self.slot("y", k), self.p.yn)
        self.push(src, k, "o")

    def from_z(self, k):
        block = self.block(k, "o")
        self.cp.got(block, self.slot("z", k), self.p.zn[k])
        self.spread(block, k)

    def from_xy(self, k):
        x, y = self.block(k, "x"), self.block(k, "y")
        self.cp.got(x, self.slot("x", k), self.p.xn)
        if k >= 2:
            self.cp.put(x, x, self.slot("d", k), self.p.yn)
        self.push(x, k, "x")
        self.cp.got(y, self.slot("y", k), self.p.yn)
        if k < 2:
            self.cp.put(y, y, self.slot("d", k), self.p.xn)
        self.push(y, k, "y")

    def from_d(self, k):
        block = self.block(k, "d")
        self.cp.got(block, self.slot("d", k), self.p.xn)
        self.push(block, k, "d")

    def from_sib(self):
        for k in range(4):
            for j in "oxyd":
                block = self.out(1 - self.p.c, self.p.at(k, j))
                self.cp.got(block, self.slot("s", k, j), self.p.sib)


def low_add(left, right):
    return left + right


class Scatter:
    def __init__(self, place, copies, base, local, grad, own, sib, rly, xin, yin, out, zin):
        self.p, self.cp, self.base, self.local, self.grad = place, copies, base, local, grad
        self.own, self.sib, self.rly, self.xin, self.yin, self.out, self.zin = own, sib, rly, xin, yin, out, zin

    def slot(self, kind, k):
        return self.base + {"s": 0, "r": 4, "x": 8, "y": 12, "z": 15}[kind] + k

    def load(self, k):
        four = pl.ds(self.p.plane(k) * 4, 4)
        return pltpu.make_async_copy(self.grad(self.p.c, four), self.own.at[four], self.local.at[self.base + k])

    def begin(self, k):
        four = pl.ds(self.p.plane(k) * 4, 4)
        self.cp.put(self.grad(1 - self.p.c, four), self.sib.at[four], self.slot("s", k), self.p.sib)
        self.load(k).start()

    def pair(self, k):
        p = self.p
        four = pl.ds(p.plane(k) * 4, 4)
        self.load(k).wait()
        self.cp.got(self.sib.at[four], self.slot("s", k), p.sib)
        d, x, y = p.at(k, "d"), p.at(k, "x"), p.at(k, "y")
        self.own[d] = low_add(self.own[d], self.sib[d])
        self.cp.put(self.own.at[d], self.rly.at[k], self.slot("r", k), p.xn if k < 2 else p.yn)
        if k < 2:
            self.own[x] = low_add(self.own[x], self.sib[x])
            self.cp.put(self.own.at[x], self.xin.at[k], self.slot("x", k), p.xn)
        else:
            self.own[y] = low_add(self.own[y], self.sib[y])
            self.cp.put(self.own.at[y], self.yin.at[k], self.slot("y", k), p.yn)

    def relay(self, k):
        p = self.p
        x, y = p.at(k, "x"), p.at(k, "y")
        self.cp.got(self.rly.at[k], self.slot("r", k), p.xn)
        if k < 2:
            self.own[y] = low_add(low_add(self.own[y], self.sib[y]), self.rly[k])
            self.cp.put(self.own.at[y], self.yin.at[k], self.slot("y", k), p.yn)
        else:
            self.own[x] = low_add(low_add(self.own[x], self.sib[x]), self.rly[k])
            self.cp.put(self.own.at[x], self.xin.at[k], self.slot("x", k), p.xn)

    def plane(self, k):
        p = self.p
        o = p.at(k, "o")
        self.cp.got(self.xin.at[k], self.slot("x", k), p.xn)
        self.cp.got(self.yin.at[k], self.slot("y", k), p.yn)
        wide = jnp.float32
        total = (self.own[o].astype(wide) + self.sib[o].astype(wide)) + (
            self.xin[k].astype(wide) + self.yin[k].astype(wide)
        )
        self.out[k] = total.astype(jnp.bfloat16)
        if k:
            self.cp.put(self.out.at[k], self.zin.at[k - 1], self.slot("z", k), p.zn[k])

    def total(self):
        for k in (1, 2, 3):
            self.cp.got(self.zin.at[k - 1], self.slot("z", k), self.p.zn[k])
        wide = jnp.float32
        return (self.out[0].astype(wide) + self.zin[0].astype(wide)) + (
            self.zin[1].astype(wide) + self.zin[2].astype(wide)
        )


rows_chip = 48
gather_slots, scatter_slots = 31, 19


def gather_kernel(a_shard, g_shard, d_own, a_full, g_full, d_full, a_pair, g_pair, a_own, g_own, pair_sem, send, recv, local):
    place = Place()
    place.greet()
    c = place.c
    pairs = Copies(pair_sem.at[0], pair_sem.at[1])
    for i, (shard, other) in enumerate(((a_shard, a_pair), (g_shard, g_pair))):
        pairs.put(shard.at[1 - c], other, i, place.sib)
    copies = Copies(send, recv)
    a_out = lambda half, r: a_full.at[half, r]
    g_out = lambda half, r: g_full.at[half, r]
    d_out = lambda half, r: d_full.at[r, half]
    mats = [
        Gather(place, copies, 0, a_own, a_out),
        Gather(place, copies, gather_slots, g_own, g_out),
        Gather(place, copies, 2 * gather_slots, d_own, d_out),
    ]
    att, gat, dow = mats

    def assemble(shard, other, own, i):
        pairs.got(other, i, place.sib)
        mine = shard[c, :24, :].astype(jnp.float32)
        theirs = other[:24, :].astype(jnp.float32)
        first = c == 0
        top = jnp.where(first, mine, theirs)
        low = jnp.where(first, theirs, mine)
        own[...] = jnp.concatenate([top, low], 0).astype(jnp.bfloat16)

    kept = [pltpu.make_async_copy(m.own, m.block(0, "o"), local.at[i]) for i, m in enumerate(mats)]
    assemble(a_shard, a_pair, a_own, 0)
    att.own_z()
    att.own_xy()
    kept[0].start()
    assemble(g_shard, g_pair, g_own, 1)
    gat.own_z()
    dow.own_z()
    kept[1].start()
    kept[2].start()
    for k in (1, 2, 3):
        att.from_z(k)
    for k in range(4):
        att.from_xy(k)
    gat.own_xy()
    for k in (1, 2, 3):
        gat.from_z(k)
    for k in range(4):
        att.from_d(k)
    for k in range(4):
        gat.from_xy(k)
    dow.own_xy()
    for k in (1, 2, 3):
        dow.from_z(k)
    for k in range(4):
        gat.from_d(k)
    for k in range(4):
        dow.from_xy(k)
    for k in range(4):
        dow.from_d(k)
    for m in mats:
        m.from_sib()
    for copy in kept:
        copy.wait()
    pairs.drain()
    copies.drain()


def gather_weights(a_shard, g_shard, d_shard):
    half_a, half_g = a_shard.shape[-1], g_shard.shape[-1]
    low = jnp.bfloat16
    return pl.pallas_call(
        gather_kernel,
        out_shape=(
            jax.ShapeDtypeStruct((2, 16, rows_chip, half_a), low),
            jax.ShapeDtypeStruct((2, 16, rows_chip, half_g), low),
            jax.ShapeDtypeStruct((16, 2) + d_shard.shape, low),
        ),
        in_specs=[pl.BlockSpec(memory_space=pltpu.VMEM)] * 3,
        out_specs=(pl.BlockSpec(memory_space=pl.ANY),) * 3,
        scratch_shapes=[
            pltpu.VMEM(a_shard.shape[1:], low),
            pltpu.VMEM(g_shard.shape[1:], low),
            pltpu.VMEM((rows_chip, half_a), low),
            pltpu.VMEM((rows_chip, half_g), low),
            pltpu.SemaphoreType.DMA((2, 2)),
            pltpu.SemaphoreType.DMA((3 * gather_slots,)),
            pltpu.SemaphoreType.DMA((3 * gather_slots,)),
            pltpu.SemaphoreType.DMA((3,)),
        ],
        compiler_params=pltpu.CompilerParams(
            collective_id=0, has_side_effects=True, vmem_limit_bytes=32 * 2**20
        ),
        name="gather_weights",
    )(a_shard, g_shard, d_shard)


def scatter_kernel(
    a_grad, g_grad, d_grad, small, qkv_out, wout_out, gu_out, down_out, small_out, *scratch
):
    place = Place()
    place.greet()
    c = place.c
    bufs, (a_sum, g_sum, a_fin, g_fin, small_buf, send, recv, local, fin_sem) = scratch[:21], scratch[21:]
    copies = Copies(send, recv)
    last = Copies(fin_sem.at[0], fin_sem.at[1])
    a_at = lambda half, four: a_grad.at[half, four]
    g_at = lambda half, four: g_grad.at[half, four]
    d_at = lambda half, four: d_grad.at[four, half]
    mats = [
        Scatter(place, copies, i * scatter_slots, local, at, *bufs[7 * i : 7 * i + 7])
        for i, at in enumerate((g_at, d_at, a_at))
    ]
    order = [(m, k) for m in mats for k in (3, 2, 1, 0)]
    depth = 3
    steps = ["begin", "pair", "relay", "plane"]
    hops = ((place.sib, 0), (place.xn, 1), (place.yn, 2))

    def exchange(i):
        peer, slot = hops[i]
        last.put(small_buf.at[i], small_buf.at[4 + i], slot, peer)

    def combine(i):
        peer, slot = hops[i]
        last.got(small_buf.at[4 + i], slot, peer)
        small_buf[i + 1] = small_buf[i] + small_buf[4 + i]

    small_buf[0] = small[...]
    exchange(0)
    for t in range(len(order) + depth):
        for s, name in enumerate(steps):
            if 0 <= t - s < len(order):
                m, k = order[t - s]
                getattr(m, name)(k)
        if 1 <= t <= 3:
            combine(t - 1)
            if t < 3:
                exchange(t)
            else:
                for k in (1, 2, 3):
                    last.put(small_buf.at[3], small_buf.at[6 + k], 2 + k, place.zn[k])
    for k in (1, 2, 3):
        last.got(small_buf.at[6 + k], 2 + k, place.zn[k])
    small_out[...] = (small_buf[3] + small_buf[7]) + (small_buf[8] + small_buf[9])
    gate, down, att = mats
    down_out[...] = down.total()
    g_sum[...] = gate.total()
    mine, theirs = pl.ds(pl.multiple_of(24 * c, 8), 24), pl.ds(pl.multiple_of(24 - 24 * c, 8), 24)
    last.put(g_sum.at[theirs], g_fin, 6, place.sib)
    a_sum[...] = att.total()
    last.put(a_sum.at[theirs], a_fin, 7, place.sib)
    first = c == 0
    last.got(g_fin, 6, place.sib)
    last.got(a_fin, 7, place.sib)
    half_g = g_fin.shape[1]
    gu_out[:, :half_g] = jnp.where(first, g_sum[mine], g_fin[...])
    gu_out[:, half_g:] = jnp.where(first, g_fin[...], g_sum[mine])
    left = jnp.where(first, a_sum[mine], a_fin[...])
    right = jnp.where(first, a_fin[...], a_sum[mine])
    cut = qkv_out.shape[1] - left.shape[1]
    qkv_out[:, : left.shape[1]] = left
    qkv_out[:, left.shape[1] :] = right[:, :cut]
    wout_out[...] = right[:, cut:]
    copies.drain()
    last.drain()


def scatter_grads(a_grad, g_grad, d_grad, small):
    low = jnp.bfloat16
    bufs = []
    for rows, half in ((rows_chip, g_grad.shape[-1]), d_grad.shape[2:], (rows_chip, a_grad.shape[-1])):
        for count in (16, 16, 4, 4, 4, 4, 3):
            bufs.append(pltpu.VMEM((count, rows, half), low))
    half_a, half_g = a_grad.shape[-1], g_grad.shape[-1]
    width = d_grad.shape[-1]
    wide = jnp.float32
    return pl.pallas_call(
        scatter_kernel,
        out_shape=(
            jax.ShapeDtypeStruct((24, 3 * width), wide),
            jax.ShapeDtypeStruct((24, width), wide),
            jax.ShapeDtypeStruct((24, 2 * half_g), wide),
            jax.ShapeDtypeStruct(d_grad.shape[2:], wide),
            jax.ShapeDtypeStruct(small.shape, wide),
        ),
        in_specs=[pl.BlockSpec(memory_space=pl.ANY)] * 3 + [pl.BlockSpec(memory_space=pltpu.VMEM)],
        out_specs=(pl.BlockSpec(memory_space=pltpu.VMEM),) * 5,
        scratch_shapes=bufs
        + [
            pltpu.VMEM((rows_chip, half_a), wide),
            pltpu.VMEM((rows_chip, half_g), wide),
            pltpu.VMEM((24, half_a), wide),
            pltpu.VMEM((24, half_g), wide),
            pltpu.VMEM((10,) + small.shape, wide),
            pltpu.SemaphoreType.DMA((3 * scatter_slots,)),
            pltpu.SemaphoreType.DMA((3 * scatter_slots,)),
            pltpu.SemaphoreType.DMA((3 * scatter_slots,)),
            pltpu.SemaphoreType.DMA((2, 8)),
        ],
        compiler_params=pltpu.CompilerParams(
            collective_id=1, has_side_effects=True, vmem_limit_bytes=60 * 2**20
        ),
        name="scatter_grads",
    )(a_grad, g_grad, d_grad, small)


def dot(left, right, dims=((1,), (0,))):
    return lax.dot_general(left, right, (dims, ((), ())), preferred_element_type=jnp.float32)


def row_mean(values):
    return jnp.mean(values, -1, keepdims=True)


def normalized(resid):
    centred = resid - row_mean(resid)
    inverse = lax.rsqrt(row_mean(centred * centred) + ln_eps)
    return centred * inverse, inverse


def norm_back(grad, gain, norm, inverse):
    e = grad * gain
    return inverse * (e - row_mean(e) - norm * row_mean(e * norm))


def column_sum(values):
    return jnp.sum(values, 0, keepdims=True)


def ffn_kernel(
    tokens, attended, w_out, vectors, valid, out_grad, w_gu, w_down,
    output, d_resid_one, d_att, grad_out, grad_gu, grad_down, small,
    hid, hid_low, hid_t, norm_one, inv_one, slope_gate, slope_up, act, total, d_hid, d_branch,
):
    i = pl.program_id(0)
    tiles = pl.num_programs(0) // 2
    low = jnp.bfloat16
    wide = jnp.float32

    @pl.when(i == 0)
    def _():
        branch = dot(attended[...], w_out[0])
        toks = tokens[...].astype(wide)
        norm, inverse = normalized(toks + branch)
        norm_one[...] = norm
        inv_one[...] = inverse
        hidden = norm * vectors[0:1, :] + vectors[1:2, :]
        hid[...] = hidden
        hid_low[...] = hidden.astype(low)
        hid_t[...] = hidden.T.astype(low)
        mask = valid[...]
        small[4:5, :] = column_sum(mask * toks * toks)
        small[5:6, :] = column_sum(mask * branch * branch)
        small[6:7, :] = column_sum(mask * hidden * hidden)
        small[8:16, :] = jnp.zeros((8, small.shape[1]), wide)
        small[8:9, :] = jnp.broadcast_to(jnp.sum(mask, 0, keepdims=True), (1, small.shape[1]))
        total[...] = jnp.zeros_like(total)

    @pl.when(i < tiles)
    def _():
        h = hid_low[...]
        gate = dot(h, w_gu[0])
        up = dot(h, w_gu[1])
        cdf = 0.5 + 0.5 * lax.erf(gate * 0.7071067811865476)
        glu = gate * cdf
        density = 0.3989422804014327 * jnp.exp(-0.5 * gate * gate)
        slope_up[i] = glu
        slope_gate[i] = up * (cdf + gate * density)
        a = (glu * up).astype(low)
        act[i] = a
        total[...] += dot(a, w_down[...])

    @pl.when(i == tiles - 1)
    def _():
        branch = total[...]
        mask = valid[...]
        small[7:8, :] = column_sum(mask * branch * branch)
        norm, inverse = normalized(hid[...] + branch)
        gain = vectors[2:3, :]
        output[...] = (norm * gain + vectors[3:4, :]).astype(low)
        grad = out_grad[...].astype(wide)
        small[2:3, :] = column_sum(grad * norm)
        small[3:4, :] = column_sum(grad)
        back = norm_back(grad, gain, norm, inverse)
        d_hid[...] = back
        d_branch[...] = back.astype(low)

    @pl.when(i >= tiles)
    def _():
        j = i - tiles
        db = d_branch[...]
        grad_down[...] = dot(act[j].T, db).astype(low)
        d_act = dot(db, w_down[...], ((1,), (1,)))
        d_gate = (d_act * slope_gate[j]).astype(low)
        d_up = (d_act * slope_up[j]).astype(low)
        h_t = hid_t[...]
        grad_gu[0] = dot(h_t, d_gate).astype(low)
        grad_gu[1] = dot(h_t, d_up).astype(low)
        d_hid[...] += dot(d_gate, w_gu[0], ((1,), (1,))) + dot(d_up, w_gu[1], ((1,), (1,)))

    @pl.when(i == 2 * tiles - 1)
    def _():
        grad = d_hid[...]
        norm = norm_one[...]
        small[0:1, :] = column_sum(grad * norm)
        small[1:2, :] = column_sum(grad)
        back = norm_back(grad, vectors[0:1, :], norm, inv_one[...])
        d_resid_one[...] = back
        db = back.astype(low)
        grad_out[...] = dot(attended[...].T, db).astype(low)
        d_att[...] = dot(db, w_out[0], ((1,), (1,))).astype(low)


def ffn(tokens, attended, a_full, vectors, valid, out_grad, w_gu, w_down):
    rows, width = tokens.shape
    ff = w_down.shape[0]
    tile = 512
    tiles = ff // tile
    low, wide = jnp.bfloat16, jnp.float32
    whole = lambda *shape: pl.BlockSpec(shape, lambda i: (0,) * len(shape))
    at = lambda i: jnp.where(i < tiles, i, i - tiles)
    late = lambda i: jnp.maximum(i - tiles, 0)
    return pl.pallas_call(
        ffn_kernel,
        grid=(2 * tiles,),
        out_shape=(
            jax.ShapeDtypeStruct((rows, width), low),
            jax.ShapeDtypeStruct((rows, width), wide),
            jax.ShapeDtypeStruct((rows, width), low),
            jax.ShapeDtypeStruct((width, width), low),
            jax.ShapeDtypeStruct((2, width, ff), low),
            jax.ShapeDtypeStruct((ff, width), low),
            jax.ShapeDtypeStruct((16, width), wide),
        ),
        in_specs=[
            whole(rows, width),
            whole(rows, width),
            pl.BlockSpec((1, width, width), lambda i: (1, 0, 1)),
            whole(8, width),
            whole(rows, 1),
            whole(rows, width),
            pl.BlockSpec((2, width, tile), lambda i: (0, 0, at(i))),
            pl.BlockSpec((tile, width), lambda i: (at(i), 0)),
        ],
        out_specs=(
            whole(rows, width),
            whole(rows, width),
            whole(rows, width),
            whole(width, width),
            pl.BlockSpec((2, width, tile), lambda i: (0, 0, late(i))),
            pl.BlockSpec((tile, width), lambda i: (late(i), 0)),
            whole(16, width),
        ),
        scratch_shapes=[
            pltpu.VMEM((rows, width), wide),
            pltpu.VMEM((rows, width), low),
            pltpu.VMEM((width, rows), low),
            pltpu.VMEM((rows, width), wide),
            pltpu.VMEM((rows, 1), wide),
            pltpu.VMEM((tiles, rows, tile), wide),
            pltpu.VMEM((tiles, rows, tile), wide),
            pltpu.VMEM((tiles, rows, tile), low),
            pltpu.VMEM((rows, width), wide),
            pltpu.VMEM((rows, width), wide),
            pltpu.VMEM((rows, width), low),
        ],
        compiler_params=pltpu.CompilerParams(vmem_limit_bytes=60 * 2**20),
        cost_estimate=pl.CostEstimate(
            flops=2 * rows * width * (9 * ff + 3 * width), bytes_accessed=18 * ff * width, transcendentals=2 * rows * ff
        ),
        name="feed_forward",
    )(tokens, attended, a_full, vectors, valid, out_grad, w_gu, w_down)


def half_of(block, axis, second):
    place = lax.broadcasted_iota(jnp.int32, block.shape, axis)
    depth = block.shape[axis] // 2
    keep = place >= depth if second else place < depth
    return jnp.where(keep, block, jnp.zeros_like(block))


def attend_kernel(heads, q, k, v, span, attended, lse, out_t, q_t, v_t):
    low = jnp.bfloat16
    rows, width = q.shape
    lanes = lane_width
    depth = width // heads
    chunk = 256

    q_t[...] = (q[...].astype(jnp.float32) * depth**-0.5).T.astype(low)
    v_t[...] = v[...].astype(jnp.float32).T.astype(low)

    @pl.loop(0, heads // 2)
    def _(pair):
        at = pl.ds(pl.multiple_of(pair * lanes, lanes), lanes)
        keys = k[:, at]
        for h in (0, 1):
            slope = jnp.exp2(jnp.full((1, 1), -8.0 / heads, jnp.float32) * (2 * pair + h + 1).astype(jnp.float32))
            values_t = v_t[pl.ds(pl.multiple_of(pair * lanes + h * depth, depth), depth), :]
            for c in range(rows // chunk):
                here = pl.ds(c * chunk, chunk)
                logits = dot(keys, half_of(q_t[at, here], 0, h)) - slope * span[:, here]
                top = jnp.max(logits, 0, keepdims=True)
                weights = jnp.exp(logits - top)
                norm = jnp.sum(weights, 0, keepdims=True)
                lse[pl.ds(2 * pair + h, 1), here] = top + jnp.log(norm)
                mixed = dot(values_t, weights.astype(low))
                out_t[pl.ds(pl.multiple_of(pair * lanes + h * depth, depth), depth), here] = mixed / norm

    attended[...] = out_t[...].T.astype(low)


def attend(q, k, v, span, heads):
    rows, width = q.shape
    keys = k.shape[0]
    low, wide = jnp.bfloat16, jnp.float32
    return pl.pallas_call(
        lambda *refs: attend_kernel(heads, *refs),
        out_shape=(
            jax.ShapeDtypeStruct((rows, width), low),
            jax.ShapeDtypeStruct((16, rows), wide),
        ),
        in_specs=[pl.BlockSpec(memory_space=pltpu.VMEM)] * 4,
        out_specs=(pl.BlockSpec(memory_space=pltpu.VMEM),) * 2,
        scratch_shapes=[
            pltpu.VMEM((width, rows), wide),
            pltpu.VMEM((width, rows), low),
            pltpu.VMEM((width, keys), low),
        ],
        compiler_params=pltpu.CompilerParams(vmem_limit_bytes=60 * 2**20),
        cost_estimate=pl.CostEstimate(flops=4 * rows * keys * width, bytes_accessed=8 * keys * width, transcendentals=heads * rows * keys),
        name="attend",
    )(q, k, v, span)


def attend_back_kernel(heads, q, k, v, span, lse, att, d_att, dq, dk, dv, q_t, k_t, do_t, dq_t, delta, dk_sum, dv_sum):
    low, wide = jnp.bfloat16, jnp.float32
    rows, width = q.shape
    lanes = lane_width
    depth = width // heads
    chunk = 256
    scale = depth**-0.5

    q_t[...] = (q[...].astype(wide) * scale).T.astype(low)
    k_t[...] = k[...].astype(wide).T.astype(low)
    do_wide = d_att[...].astype(wide)
    do_t[...] = do_wide.T.astype(low)
    both_t = (do_wide * att[...].astype(wide)).T
    delta[...] = jnp.sum(both_t.reshape(heads, depth, rows), 1)

    @pl.loop(0, heads // 2)
    def _(pair):
        at = pl.ds(pl.multiple_of(pair * lanes, lanes), lanes)
        keys, values = k[:, at], v[:, at]
        for c in range(rows // chunk):
            here = pl.ds(c * chunk, chunk)
            q_here = (q[here, at].astype(wide) * scale).astype(low)
            do_here = d_att[here, at]
            dk_part, dv_part = None, None
            for h in (0, 1):
                head = 2 * pair + h
                own = pl.ds(pl.multiple_of(pair * lanes + h * depth, depth), depth)
                slope = jnp.exp2(jnp.full((1, 1), -8.0 / heads, jnp.float32) * (head + 1).astype(wide))
                logits = dot(keys, half_of(q_t[at, here], 0, h)) - slope * span[:, here]
                probs = jnp.exp(logits - lse[pl.ds(head, 1), here])
                d_probs = dot(values, half_of(do_t[at, here], 0, h))
                d_logits = (probs * (d_probs - delta[pl.ds(head, 1), here])).astype(low)
                dv_term = dot(probs.astype(low), half_of(do_here, 1, h))
                dk_term = dot(d_logits, half_of(q_here, 1, h))
                dv_part = dv_term if dv_part is None else dv_part + dv_term
                dk_part = dk_term if dk_part is None else dk_part + dk_term
                dq_t[own, here] = dot(k_t[own, :], d_logits) * scale
            if c == 0:
                dk_sum[...] = dk_part
                dv_sum[...] = dv_part
            else:
                dk_sum[...] += dk_part
                dv_sum[...] += dv_part
        dk[:, at] = dk_sum[...].astype(dk.dtype)
        dv[:, at] = dv_sum[...].astype(dv.dtype)

    dq[...] = dq_t[...].T.astype(low)


def attend_back(q, k, v, span, lse, att, d_att, heads):
    rows, width = q.shape
    keys = k.shape[0]
    low, wide = jnp.bfloat16, jnp.float32
    return pl.pallas_call(
        lambda *refs: attend_back_kernel(heads, *refs),
        out_shape=(
            jax.ShapeDtypeStruct((rows, width), low),
            jax.ShapeDtypeStruct((keys, width), wide),
            jax.ShapeDtypeStruct((keys, width), wide),
        ),
        in_specs=[pl.BlockSpec(memory_space=pltpu.VMEM)] * 7,
        out_specs=(pl.BlockSpec(memory_space=pltpu.VMEM),) * 3,
        scratch_shapes=[
            pltpu.VMEM((width, rows), low),
            pltpu.VMEM((width, keys), low),
            pltpu.VMEM((width, rows), low),
            pltpu.VMEM((width, rows), wide),
            pltpu.VMEM((heads, rows), wide),
            pltpu.VMEM((keys, lane_width), wide),
            pltpu.VMEM((keys, lane_width), wide),
        ],
        compiler_params=pltpu.CompilerParams(vmem_limit_bytes=60 * 2**20),
        cost_estimate=pl.CostEstimate(flops=10 * rows * keys * width, bytes_accessed=16 * keys * width, transcendentals=heads * rows * keys),
        name="attend_back",
    )(q, k, v, span, lse, att, d_att)


def window(cells, width):
    count = lax.axis_size("blk")
    if count == 2:
        other = lax.ppermute(cells, "blk", [(0, 1), (1, 0)])
        first = lax.axis_index("blk") == 0
        return jnp.concatenate([jnp.where(first, cells, other), jnp.where(first, other, cells)], 0)
    before = lax.ppermute(cells, "blk", [(i, i + 1) for i in range(count - 1)])
    after = lax.ppermute(cells, "blk", [(i + 1, i) for i in range(count - 1)])
    return jnp.concatenate([before, cells, after], 0)


def window_back(terms, width):
    count = lax.axis_size("blk")
    low = jnp.bfloat16
    if count == 2:
        first = lax.axis_index("blk") == 0
        upper, lower = terms[:width], terms[width:]
        other = lax.ppermute(jnp.where(first, lower, upper).astype(low), "blk", [(0, 1), (1, 0)])
        return jnp.where(first, upper, lower) + other.astype(terms.dtype)
    before = lax.ppermute(terms[2 * width :].astype(low), "blk", [(i, i + 1) for i in range(count - 1)])
    after = lax.ppermute(terms[:width].astype(low), "blk", [(i + 1, i) for i in range(count - 1)])
    return terms[width : 2 * width] + before.astype(terms.dtype) + after.astype(terms.dtype)


def key_spans(labels, first, tok_rows):
    seq_len = labels.shape[0]
    query_pos = first + jnp.arange(tok_rows, dtype=jnp.int32)
    query_labels = lax.dynamic_slice_in_dim(labels, first, tok_rows, 0)
    if seq_len == 2 * tok_rows:
        key_pos, key_labels = jnp.arange(seq_len, dtype=jnp.int32), labels
    else:
        key_pos = first - tok_rows + jnp.arange(3 * tok_rows, dtype=jnp.int32)
        padded = jnp.pad(labels, (tok_rows, tok_rows), constant_values=seq_len)
        key_labels = lax.dynamic_slice_in_dim(padded, first, 3 * tok_rows, 0)
    same = (key_labels[:, None] == query_labels[None, :]) & (key_labels[:, None] != seq_len)
    gap = jnp.abs(key_pos[:, None] - query_pos[None, :])
    return jnp.where(same | (gap == 0), gap.astype(jnp.float32), far)


def on_chip_grid():
    return lax.axis_size("rows") == 16 and lax.axis_size("blk") == 2


def gathered_weights(w_qkv, w_out, ln1_gain, ln1_bias, w_gate_up, w_down, ln2_gain, ln2_bias):
    rows, width = w_out.shape
    ff = w_gate_up.shape[1] // 2
    table = jnp.stack((ln1_gain, ln1_bias, ln2_gain, ln2_bias), 1)
    table = jnp.pad(table, ((0, 0), (0, lane_width - 4)))
    left = jnp.concatenate([w_qkv[:, : 2 * width], table], 1)
    right = jnp.concatenate([w_qkv[:, 2 * width :], w_out, jnp.zeros_like(table)], 1)
    a_shard = jnp.stack([left, right])
    g_shard = jnp.stack([w_gate_up[:, :ff], w_gate_up[:, ff:]])
    if not on_chip_grid():
        both = ("rows", "blk")
        return (
            lax.all_gather(a_shard, both, axis=1, tiled=True),
            lax.all_gather(g_shard, both, axis=1, tiled=True),
            lax.all_gather(w_down, both, axis=0, tiled=True),
        )
    spare = ((0, 0), (0, 32 - rows), (0, 0))
    a_full, g_full, d_full = gather_weights(jnp.pad(a_shard, spare), jnp.pad(g_shard, spare), w_down)
    return a_full.reshape(2, width, -1), g_full.reshape(2, width, ff), d_full.reshape(-1, width)


def summed_grads(a_grad, g_grad, d_grad, small):
    both = ("rows", "blk")
    width = d_grad.shape[1]
    if not on_chip_grid():
        share = lambda g, axis: lax.psum_scatter(g.astype(jnp.float32), both, scatter_dimension=axis, tiled=True)
        left, right = share(a_grad, 1)
        gate, up = share(g_grad, 1)
        cut = right.shape[1] - width
        return (
            jnp.concatenate([left, right[:, :cut]], 1), right[:, cut:],
            jnp.concatenate([gate, up], 1), share(d_grad, 0), lax.psum(small, both),
        )
    split = lambda g: g.reshape(2, 16, rows_chip, g.shape[2])
    return scatter_grads(split(a_grad), split(g_grad), d_grad.reshape(16, 2, -1, width), small)


def body(
    tokens, segments, w_qkv, w_out, ln1_gain, ln1_bias, w_gate_up, w_down, ln2_gain, ln2_bias, out_grad,
):
    inputs, labels = tokens[0], segments[0]
    tok_rows, width = inputs.shape
    low, wide = jnp.bfloat16, jnp.float32
    both = ("rows", "blk")
    first = lax.axis_index("blk") * tok_rows
    span = key_spans(labels, first, tok_rows)
    valid = (lax.dynamic_slice_in_dim(labels, first, tok_rows, 0) != labels.shape[0]).astype(wide)[:, None]
    a_full, w_gu, w_dn = gathered_weights(
        w_qkv, w_out, ln1_gain, ln1_bias, w_gate_up, w_down, ln2_gain, ln2_bias
    )
    vectors = jnp.pad(a_full[0, :, 2 * width : 2 * width + 4].astype(wide).T, ((0, 4), (0, 0)))
    w_qk, w_v = a_full[0, :, : 2 * width], a_full[1, :, :width]
    qk = jnp.dot(inputs, w_qk, preferred_element_type=wide).astype(low)
    v = jnp.dot(inputs, w_v, preferred_element_type=wide).astype(low)
    query = qk[:, :width]
    kv = window(jnp.concatenate([qk[:, width:], v], 1), tok_rows)
    keys, values = kv[:, :width], kv[:, width:]
    attended, lse = attend(query, keys, values, span, HEADS)
    output, d_resid_one, d_att, grad_out, g_grad, d_grad, small = ffn(
        inputs, attended, a_full, vectors, valid, out_grad[0], w_gu, w_dn
    )
    dq, dk, dv = attend_back(query, keys, values, span, lse, attended, d_att, HEADS)
    dkv = window_back(jnp.concatenate([dk, dv], 1), tok_rows)
    d_qk = jnp.concatenate([dq, dkv[:, :width].astype(low)], 1)
    d_v = dkv[:, width:].astype(low)
    grad_qk = transposed_times(inputs, d_qk).astype(low)
    grad_v = transposed_times(inputs, d_v).astype(low)
    d_tokens = d_resid_one + times_transposed(d_qk, w_qk) + times_transposed(d_v, w_v)
    a_grad = jnp.stack([grad_qk, jnp.concatenate([grad_v, grad_out], 1)])
    *parts, small = summed_grads(a_grad, g_grad, d_grad, small)
    share = width // lax.axis_size(both)
    mine = lax.axis_index(both) * share
    rows = lax.dynamic_slice_in_dim(small[:4], mine, share, 1)
    stats = jnp.sqrt(jnp.sum(small[4:8], 1) / (small[8, 0] * width))
    return (
        output[None], d_tokens.astype(low)[None], parts[0], parts[1], rows[0], rows[1],
        parts[2], parts[3], rows[2], rows[3], stats,
    )


def solution(mesh):
    placed = (
        P("rows", "blk", None),
        P("rows", None),
        P(("rows", "blk"), None),
        P(("rows", "blk"), None),
        P(("rows", "blk")),
        P(("rows", "blk")),
        P(("rows", "blk"), None),
        P(("rows", "blk"), None),
        P(("rows", "blk")),
        P(("rows", "blk")),
        P("rows", "blk", None),
    )
    return jax.shard_map(
        body,
        mesh=mesh,
        in_specs=placed,
        out_specs=(
            P("rows", "blk", None),
            P("rows", "blk", None),
            P(("rows", "blk"), None),
            P(("rows", "blk"), None),
            P(("rows", "blk")),
            P(("rows", "blk")),
            P(("rows", "blk"), None),
            P(("rows", "blk"), None),
            P(("rows", "blk")),
            P(("rows", "blk")),
            P(),
        ),
        check_vma=False,
    )
```

```python
import jax
import jax.numpy as jnp
from jax import lax
from jax.experimental import pallas as pl
from jax.experimental.pallas import tpu as pltpu
from jax.sharding import PartitionSpec as P

HEADS = 12


ln_eps = 1e-12
far = 1e33
lane_width = 128


def times_transposed(left, right):
    return lax.dot_general(
        left, right, (((1,), (1,)), ((), ())), preferred_element_type=jnp.float32
    )


def transposed_times(left, right):
    return lax.dot_general(
        left, right, (((0,), (0,)), ((), ())), preferred_element_type=jnp.float32
    )


MESH = pl.DeviceIdType.MESH


class Place:
    def __init__(self):
        r, self.c = lax.axis_index("rows"), lax.axis_index("blk")
        self.x, self.y, self.z = r % 2, (r // 2) % 2, r // 4
        self.sib = (r, 1 - self.c)
        self.xn = (self.at(0, "x"), self.c)
        self.yn = (self.at(0, "y"), self.c)
        self.zn = {k: (self.at(k, "o"), self.c) for k in (1, 2, 3)}

    def plane(self, k):
        z, low = self.z % 2, self.z // 2
        if k % 2:
            z = 1 - z
        if k // 2:
            low = 1 - low
        return low * 2 + z

    def at(self, k, j):
        x = 1 - self.x if j in "xd" else self.x
        y = 1 - self.y if j in "yd" else self.y
        return self.plane(k) * 4 + y * 2 + x

    def greet(self):
        barrier = pltpu.get_barrier_semaphore()
        peers = [self.sib, self.xn, self.yn] + [self.zn[k] for k in (1, 2, 3)]
        for peer in peers:
            pl.semaphore_signal(barrier, inc=1, device_id=peer, device_id_type=MESH)
        pl.semaphore_wait(barrier, len(peers))


class Copies:
    def __init__(self, send, recv):
        self.send, self.recv, self.open = send, recv, []

    def of(self, src, dst, slot, peer):
        return pltpu.make_async_remote_copy(
            src_ref=src, dst_ref=dst, send_sem=self.send.at[slot], recv_sem=self.recv.at[slot],
            device_id=peer, device_id_type=MESH,
        )

    def put(self, src, dst, slot, peer, like=None):
        self.of(src, dst, slot, peer).start()
        self.open.append((like or (lambda: dst), slot))

    def got(self, dst, slot, peer):
        self.of(dst, dst, slot, peer).wait_recv()

    def drain(self, peer):
        for like, slot in self.open:
            self.of(like(), like(), slot, peer).wait_send()
        self.open = []


class Gather:
    def __init__(self, place, copies, base, own, out):
        self.p, self.cp, self.base, self.own, self.out = place, copies, base, own, out

    def slot(self, kind, k, j="o"):
        start = {"z": -1, "x": 3, "y": 7, "d": 11, "s": 15}[kind]
        return self.base + start + (4 * k + "oxyd".index(j) if kind == "s" else k)

    def block(self, k, j):
        return self.out(self.p.c, self.p.at(k, j))

    def send(self, src, dst, slot, peer):
        self.cp.put(src, dst, slot, peer, lambda: self.own)

    def push(self, src, k, j):
        self.send(src, self.block(k, j), self.slot("s", k, j), self.p.sib)

    def to_z(self, k):
        if k:
            self.send(self.own, self.block(0, "o"), self.slot("z", k), self.p.zn[k])

    def spread(self, src, k):
        dst = self.block(k, "o")
        self.send(src, dst, self.slot("x", k), self.p.xn)
        self.send(src, dst, self.slot("y", k), self.p.yn)
        self.push(src, k, "o")

    def from_z(self, k):
        if k == 0:
            self.spread(self.own, 0)
            return
        block = self.block(k, "o")
        self.cp.got(block, self.slot("z", k), self.p.zn[k])
        self.spread(block, k)

    def from_xy(self, k):
        x, y = self.block(k, "x"), self.block(k, "y")
        self.cp.got(x, self.slot("x", k), self.p.xn)
        if k == 2:
            self.send(x, x, self.slot("d", k), self.p.yn)
        self.cp.got(y, self.slot("y", k), self.p.yn)
        if k == 0:
            self.send(y, y, self.slot("d", k), self.p.xn)
        self.push(x, k, "x")
        self.push(y, k, "y")

    def from_even(self, k):
        if k % 2 == 0:
            self.from_d(k)

    def from_odd(self, k):
        if k % 2:
            self.from_d(k)

    def from_d(self, k):
        block = self.block(k, "d")
        self.cp.got(block, self.slot("d", k), self.p.xn)
        if k % 2 == 0:
            self.send(block, block, self.slot("d", k + 1), self.p.zn[1])
        self.push(block, k, "d")

    def from_sib(self):
        for k in range(4):
            for j in "oxyd":
                block = self.out(1 - self.p.c, self.p.at(k, j))
                self.cp.got(block, self.slot("s", k, j), self.p.sib)


class Scatter:
    def __init__(self, place, copies, base, give, own, sib, rly, dia, xin, yin, zin, load=None):
        self.p, self.cp, self.base, self.give, self.own, self.load = place, copies, base, give, own, load
        self.sib, self.rly, self.dia, self.xin, self.yin, self.zin = sib, rly, dia, xin, yin, zin

    def slot(self, kind, k):
        return self.base + {"s": 0, "r": 4, "d": 5, "x": 8, "y": 12, "z": 15}[kind] + k

    def four(self, k):
        return pl.ds(self.p.plane(k) * 4, 4)

    def begin(self, k):
        four = self.four(k)
        self.cp.put(self.give(four), self.sib.at[four], self.slot("s", k), self.p.sib, lambda: self.sib.at[pl.ds(0, 4)])
        if self.load is not None:
            self.load(four, self.base + k).start()

    def to_x(self, own, k):
        self.cp.put(own, self.xin.at[k], self.slot("x", k), self.p.xn, lambda: self.xin.at[k])

    def to_y(self, own, k):
        self.cp.put(own, self.yin.at[k], self.slot("y", k), self.p.yn, lambda: self.yin.at[k])

    def both(self, k, j, *more):
        at = self.p.at(k, j)
        own = self.own(at)
        total = own[...] + self.sib[at]
        for ref in more:
            total = total + ref[...]
        own[...] = total
        return own

    def pair(self, k):
        four = self.four(k)
        if self.load is not None:
            self.load(four, self.base + k).wait()
        self.cp.got(self.sib.at[four], self.slot("s", k), self.p.sib)
        if k % 2:
            i = k // 2
            dia = lambda: self.dia.at[i]
            self.cp.put(self.both(k, "d"), dia(), self.slot("d", 2 * i), self.p.zn[1], dia)
        if k != 2:
            self.to_x(self.both(k, "x"), k)
        if k != 0:
            self.to_y(self.both(k, "y"), k)

    def diag(self, k):
        if k % 2:
            return
        i = k // 2
        self.cp.got(self.dia.at[i], self.slot("d", k), self.p.zn[1])
        own = self.both(k, "d", self.dia.at[i])
        peer = self.p.xn if k == 0 else self.p.yn
        self.cp.put(own, self.rly.at[i], self.slot("r", k), peer, lambda: self.rly.at[i])

    def relay(self, k):
        if k % 2:
            return
        i = k // 2
        self.cp.got(self.rly.at[i], self.slot("r", k), self.p.xn)
        if k == 0:
            self.to_y(self.both(k, "y", self.rly.at[i]), k)
        else:
            self.to_x(self.both(k, "x", self.rly.at[i]), k)

    def plane(self, k):
        p = self.p
        at = p.at(k, "o")
        self.cp.got(self.xin.at[k], self.slot("x", k), p.xn)
        self.cp.got(self.yin.at[k], self.slot("y", k), p.yn)
        wide = jnp.float32
        own = self.own(at)
        total = (own[...].astype(wide) + self.sib[at].astype(wide)) + (
            self.xin[k].astype(wide) + self.yin[k].astype(wide)
        )
        own[...] = total.astype(jnp.bfloat16)
        if k:
            self.cp.put(own, self.zin.at[k - 1], self.slot("z", k), p.zn[k], lambda: self.zin.at[k - 1])

    def total(self):
        for k in (1, 2, 3):
            self.cp.got(self.zin.at[k - 1], self.slot("z", k), self.p.zn[k])
        wide = jnp.float32
        own = self.own(self.p.at(0, "o"))
        return (own[...].astype(wide) + self.zin[0].astype(wide)) + (
            self.zin[1].astype(wide) + self.zin[2].astype(wide)
        )


class Steps:
    def __init__(self, items, stages):
        self.items, self.stages = items, stages

    def __call__(self, t):
        for name, lag in self.stages:
            if 0 <= t - lag < len(self.items):
                matrix, planes = self.items[t - lag]
                for k in planes:
                    getattr(matrix, name)(k)

    def count(self):
        return len(self.items) + max(lag for _, lag in self.stages)


gather_stages = (("to_z", -2), ("from_z", 0), ("from_xy", 1), ("from_even", 2), ("from_odd", 3))
scatter_stages = (("begin", -2), ("pair", 0), ("diag", 1), ("relay", 2), ("plane", 3))
near_far, far_near = ((0, 1), (2, 3)), ((3, 2), (1, 0))


rows_chip = 48
gather_slots, scatter_slots = 31, 19


def gather_kernel(a_shard, g_shard, d_own, a_full, g_full, d_full, a_pair, g_pair, a_own, g_own, pair_sem, send, recv, local):
    place = Place()
    place.greet()
    c = place.c
    pairs = Copies(pair_sem.at[0], pair_sem.at[1])
    for i, (shard, other) in enumerate(((a_shard, a_pair), (g_shard, g_pair))):
        pairs.put(shard.at[1 - c], other, i, place.sib)
    copies = Copies(send, recv)
    half_g = g_full.shape[3] // 2
    outs = [
        lambda half, r: a_full.at[half, r],
        lambda half, r: g_full.at[half, r, :, :half_g],
        lambda half, r: g_full.at[half, r, :, half_g:],
        lambda half, r: d_full.at[r, half],
    ]
    owns = [a_own, g_own.at[:, :half_g], g_own.at[:, half_g:], d_own]
    mats = [Gather(place, copies, i * gather_slots, own, out) for i, (own, out) in enumerate(zip(owns, outs))]

    def assemble(shard, other, own, i):
        pairs.got(other, i, place.sib)
        mine = shard[c, :24, :].astype(jnp.float32)
        theirs = other[:24, :].astype(jnp.float32)
        first = c == 0
        top = jnp.where(first, mine, theirs)
        low = jnp.where(first, theirs, mine)
        own[...] = jnp.concatenate([top, low], 0).astype(jnp.bfloat16)

    kept = [pltpu.make_async_copy(m.own, m.block(0, "o"), local.at[i]) for i, m in enumerate(mats)]
    assemble(a_shard, a_pair, a_own, 0)
    steps = Steps([(m, planes) for m in mats for planes in near_far], gather_stages)
    steps(-2)
    steps(-1)
    kept[0].start()
    assemble(g_shard, g_pair, g_own, 1)
    for copy in kept[1:]:
        copy.start()
    for t in range(steps.count()):
        steps(t)
    for m in mats:
        m.from_sib()
    for copy in kept:
        copy.wait()
    pairs.drain(place.sib)
    copies.drain(place.sib)


def gather_weights(a_shard, g_shard, d_shard):
    half_a, half_g = a_shard.shape[-1], g_shard.shape[-1]
    low = jnp.bfloat16
    return pl.pallas_call(
        gather_kernel,
        out_shape=(
            jax.ShapeDtypeStruct((2, 16, rows_chip, half_a), low),
            jax.ShapeDtypeStruct((2, 16, rows_chip, half_g), low),
            jax.ShapeDtypeStruct((16, 2) + d_shard.shape, low),
        ),
        in_specs=[pl.BlockSpec(memory_space=pltpu.VMEM)] * 3,
        out_specs=(pl.BlockSpec(memory_space=pl.ANY),) * 3,
        scratch_shapes=[
            pltpu.VMEM(a_shard.shape[1:], low),
            pltpu.VMEM(g_shard.shape[1:], low),
            pltpu.VMEM((rows_chip, half_a), low),
            pltpu.VMEM((rows_chip, half_g), low),
            pltpu.SemaphoreType.DMA((2, 2)),
            pltpu.SemaphoreType.DMA((4 * gather_slots,)),
            pltpu.SemaphoreType.DMA((4 * gather_slots,)),
            pltpu.SemaphoreType.DMA((4,)),
        ],
        compiler_params=pltpu.CompilerParams(
            collective_id=0, has_side_effects=True, vmem_limit_bytes=32 * 2**20
        ),
        name="gather_weights",
    )(a_shard, g_shard, d_shard)


def dot(left, right, dims=((1,), (0,))):
    return lax.dot_general(left, right, (dims, ((), ())), preferred_element_type=jnp.float32)


def row_mean(values):
    return jnp.mean(values, -1, keepdims=True)


def normalized(resid):
    centred = resid - row_mean(resid)
    inverse = lax.rsqrt(row_mean(centred * centred) + ln_eps)
    return centred * inverse, inverse


def norm_back(grad, gain, norm, inverse):
    e = grad * gain
    return inverse * (e - row_mean(e) - norm * row_mean(e * norm))


def column_sum(values):
    return jnp.sum(values, 0, keepdims=True)


def ffn_kernel(
    tokens, attended, w_out, vectors, valid, out_grad, w_gu, w_down,
    output, d_resid_one, d_att, grad_out, grad_gu, grad_down, small,
    hid, hid_low, hid_t, norm_one, inv_one, slope_gate, slope_up, act, total, d_hid, d_branch,
):
    i = pl.program_id(0)
    tiles = pl.num_programs(0) // 2
    low = jnp.bfloat16
    wide = jnp.float32

    @pl.when(i == 0)
    def _():
        branch = dot(attended[...], w_out[0])
        toks = tokens[...].astype(wide)
        norm, inverse = normalized(toks + branch)
        norm_one[...] = norm
        inv_one[...] = inverse
        hidden = norm * vectors[0:1, :] + vectors[1:2, :]
        hid[...] = hidden
        hid_low[...] = hidden.astype(low)
        hid_t[...] = hidden.T.astype(low)
        mask = valid[...]
        small[4:5, :] = column_sum(mask * toks * toks)
        small[5:6, :] = column_sum(mask * branch * branch)
        small[6:7, :] = column_sum(mask * hidden * hidden)
        small[8:16, :] = jnp.zeros((8, small.shape[1]), wide)
        small[8:9, :] = jnp.broadcast_to(jnp.sum(mask, 0, keepdims=True), (1, small.shape[1]))
        total[...] = jnp.zeros_like(total)

    @pl.when(i < tiles)
    def _():
        h = hid_low[...]
        gate = dot(h, w_gu[0])
        up = dot(h, w_gu[1])
        cdf = 0.5 + 0.5 * lax.erf(gate * 0.7071067811865476)
        glu = gate * cdf
        density = 0.3989422804014327 * jnp.exp(-0.5 * gate * gate)
        slope_up[i] = glu
        slope_gate[i] = up * (cdf + gate * density)
        a = (glu * up).astype(low)
        act[i] = a
        total[...] += dot(a, w_down[...])

    @pl.when(i == tiles - 1)
    def _():
        branch = total[...]
        mask = valid[...]
        small[7:8, :] = column_sum(mask * branch * branch)
        norm, inverse = normalized(hid[...] + branch)
        gain = vectors[2:3, :]
        output[...] = (norm * gain + vectors[3:4, :]).astype(low)
        grad = out_grad[...].astype(wide)
        small[2:3, :] = column_sum(grad * norm)
        small[3:4, :] = column_sum(grad)
        back = norm_back(grad, gain, norm, inverse)
        d_hid[...] = back
        d_branch[...] = back.astype(low)

    @pl.when(i >= tiles)
    def _():
        j = i - tiles
        db = d_branch[...]
        grad_down[...] = dot(act[j].T, db).astype(low)
        d_act = dot(db, w_down[...], ((1,), (1,)))
        d_gate = (d_act * slope_gate[j]).astype(low)
        d_up = (d_act * slope_up[j]).astype(low)
        h_t = hid_t[...]
        grad_gu[0] = dot(h_t, d_gate).astype(low)
        grad_gu[1] = dot(h_t, d_up).astype(low)
        d_hid[...] += dot(d_gate, w_gu[0], ((1,), (1,))) + dot(d_up, w_gu[1], ((1,), (1,)))

    @pl.when(i == 2 * tiles - 1)
    def _():
        grad = d_hid[...]
        norm = norm_one[...]
        small[0:1, :] = column_sum(grad * norm)
        small[1:2, :] = column_sum(grad)
        back = norm_back(grad, vectors[0:1, :], norm, inv_one[...])
        d_resid_one[...] = back
        db = back.astype(low)
        grad_out[...] = dot(attended[...].T, db).astype(low)
        d_att[...] = dot(db, w_out[0], ((1,), (1,))).astype(low)


def ffn(tokens, attended, a_full, vectors, valid, out_grad, w_gu, w_down):
    rows, width = tokens.shape
    ff = w_down.shape[0]
    tile = 512
    tiles = ff // tile
    low, wide = jnp.bfloat16, jnp.float32
    whole = lambda *shape: pl.BlockSpec(shape, lambda i: (0,) * len(shape))
    at = lambda i: jnp.where(i < tiles, i, i - tiles)
    late = lambda i: jnp.maximum(i - tiles, 0)
    return pl.pallas_call(
        ffn_kernel,
        grid=(2 * tiles,),
        out_shape=(
            jax.ShapeDtypeStruct((rows, width), low),
            jax.ShapeDtypeStruct((rows, width), wide),
            jax.ShapeDtypeStruct((rows, width), low),
            jax.ShapeDtypeStruct((width, width), low),
            jax.ShapeDtypeStruct((2, width, ff), low),
            jax.ShapeDtypeStruct((ff, width), low),
            jax.ShapeDtypeStruct((16, width), wide),
        ),
        in_specs=[
            whole(rows, width),
            whole(rows, width),
            pl.BlockSpec((1, width, width), lambda i: (1, 0, 1)),
            whole(8, width),
            whole(rows, 1),
            whole(rows, width),
            pl.BlockSpec((2, width, tile), lambda i: (0, 0, at(i))),
            pl.BlockSpec((tile, width), lambda i: (at(i), 0)),
        ],
        out_specs=(
            whole(rows, width),
            whole(rows, width),
            whole(rows, width),
            whole(width, width),
            pl.BlockSpec((2, width, tile), lambda i: (0, 0, late(i))),
            pl.BlockSpec((tile, width), lambda i: (late(i), 0)),
            whole(16, width),
        ),
        scratch_shapes=[
            pltpu.VMEM((rows, width), wide),
            pltpu.VMEM((rows, width), low),
            pltpu.VMEM((width, rows), low),
            pltpu.VMEM((rows, width), wide),
            pltpu.VMEM((rows, 1), wide),
            pltpu.VMEM((tiles, rows, tile), wide),
            pltpu.VMEM((tiles, rows, tile), wide),
            pltpu.VMEM((tiles, rows, tile), low),
            pltpu.VMEM((rows, width), wide),
            pltpu.VMEM((rows, width), wide),
            pltpu.VMEM((rows, width), low),
        ],
        compiler_params=pltpu.CompilerParams(vmem_limit_bytes=60 * 2**20),
        cost_estimate=pl.CostEstimate(
            flops=2 * rows * width * (9 * ff + 3 * width), bytes_accessed=18 * ff * width, transcendentals=2 * rows * ff
        ),
        name="feed_forward",
    )(tokens, attended, a_full, vectors, valid, out_grad, w_gu, w_down)


def half_of(block, axis, second):
    place = lax.broadcasted_iota(jnp.int32, block.shape, axis)
    depth = block.shape[axis] // 2
    keep = place >= depth if second else place < depth
    return jnp.where(keep, block, jnp.zeros_like(block))


def attend_kernel(heads, q, k, v, span, attended, lse, out_t, q_t, v_t):
    low = jnp.bfloat16
    rows, width = q.shape
    lanes = lane_width
    depth = width // heads
    chunk = 256

    q_t[...] = (q[...].astype(jnp.float32) * depth**-0.5).T.astype(low)
    v_t[...] = v[...].astype(jnp.float32).T.astype(low)

    @pl.loop(0, heads // 2)
    def _(pair):
        at = pl.ds(pl.multiple_of(pair * lanes, lanes), lanes)
        keys = k[:, at]
        for h in (0, 1):
            slope = jnp.exp2(jnp.full((1, 1), -8.0 / heads, jnp.float32) * (2 * pair + h + 1).astype(jnp.float32))
            values_t = v_t[pl.ds(pl.multiple_of(pair * lanes + h * depth, depth), depth), :]
            for c in range(rows // chunk):
                here = pl.ds(c * chunk, chunk)
                logits = dot(keys, half_of(q_t[at, here], 0, h)) - slope * span[:, here]
                top = jnp.max(logits, 0, keepdims=True)
                weights = jnp.exp(logits - top)
                norm = jnp.sum(weights, 0, keepdims=True)
                lse[pl.ds(2 * pair + h, 1), here] = top + jnp.log(norm)
                mixed = dot(values_t, weights.astype(low))
                out_t[pl.ds(pl.multiple_of(pair * lanes + h * depth, depth), depth), here] = mixed / norm

    attended[...] = out_t[...].T.astype(low)


def attend(q, k, v, span, heads):
    rows, width = q.shape
    keys = k.shape[0]
    low, wide = jnp.bfloat16, jnp.float32
    return pl.pallas_call(
        lambda *refs: attend_kernel(heads, *refs),
        out_shape=(
            jax.ShapeDtypeStruct((rows, width), low),
            jax.ShapeDtypeStruct((16, rows), wide),
        ),
        in_specs=[pl.BlockSpec(memory_space=pltpu.VMEM)] * 4,
        out_specs=(pl.BlockSpec(memory_space=pltpu.VMEM),) * 2,
        scratch_shapes=[
            pltpu.VMEM((width, rows), wide),
            pltpu.VMEM((width, rows), low),
            pltpu.VMEM((width, keys), low),
        ],
        compiler_params=pltpu.CompilerParams(vmem_limit_bytes=60 * 2**20),
        cost_estimate=pl.CostEstimate(flops=4 * rows * keys * width, bytes_accessed=8 * keys * width, transcendentals=heads * rows * keys),
        name="attend",
    )(q, k, v, span)


def attend_back_pair(pair, heads, q, k, v, span, lse, att, d_att, dq, dk_sum, dv_sum):
    low, wide = jnp.bfloat16, jnp.float32
    rows, width = q.shape
    lanes = lane_width
    depth = width // heads
    chunk = 256
    scale = depth**-0.5
    at = pl.ds(pl.multiple_of(pair * lanes, lanes), lanes)
    keys, values = k[:, at], v[:, at]
    keys_t = keys.astype(wide).T.astype(low)
    for c in range(rows // chunk):
        here = pl.ds(c * chunk, chunk)
        q_wide = q[here, at].astype(wide) * scale
        do_here = d_att[here, at]
        do_wide = do_here.astype(wide)
        q_here = q_wide.astype(low)
        q_t, do_t = q_wide.T.astype(low), do_wide.T.astype(low)
        both_t = (do_wide * att[here, at].astype(wide)).T
        dk_part, dv_part, dq_parts = None, None, []
        for h in (0, 1):
            head = 2 * pair + h
            own = slice(h * depth, (h + 1) * depth)
            slope = jnp.exp2(jnp.full((1, 1), -8.0 / heads, wide) * (head + 1).astype(wide))
            delta = jnp.sum(both_t[own], 0, keepdims=True)
            logits = dot(keys, half_of(q_t, 0, h)) - slope * span[:, here]
            probs = jnp.exp(logits - lse[pl.ds(head, 1), here])
            d_probs = dot(values, half_of(do_t, 0, h))
            d_logits = (probs * (d_probs - delta)).astype(low)
            dv_term = dot(probs.astype(low), half_of(do_here, 1, h))
            dk_term = dot(d_logits, half_of(q_here, 1, h))
            dv_part = dv_term if dv_part is None else dv_part + dv_term
            dk_part = dk_term if dk_part is None else dk_part + dk_term
            dq_parts.append(dot(keys_t[own], d_logits) * scale)
        if c == 0:
            dk_sum[...] = dk_part
            dv_sum[...] = dv_part
        else:
            dk_sum[...] += dk_part
            dv_sum[...] += dv_part
        dq[here, at] = jnp.concatenate(dq_parts, 0).T.astype(low)


def attend_back_kernel(heads, q, k, v, span, lse, att, d_att, dq, dk, dv, dk_sum, dv_sum):
    @pl.loop(0, heads // 2)
    def _(pair):
        attend_back_pair(pair, heads, q, k, v, span, lse, att, d_att, dq, dk_sum, dv_sum)
        at = pl.ds(pl.multiple_of(pair * lane_width, lane_width), lane_width)
        dk[:, at] = dk_sum[...]
        dv[:, at] = dv_sum[...]


def attend_back(q, k, v, span, lse, att, d_att, heads):
    rows, width = q.shape
    keys = k.shape[0]
    low, wide = jnp.bfloat16, jnp.float32
    return pl.pallas_call(
        lambda *refs: attend_back_kernel(heads, *refs),
        out_shape=(
            jax.ShapeDtypeStruct((rows, width), low),
            jax.ShapeDtypeStruct((keys, width), wide),
            jax.ShapeDtypeStruct((keys, width), wide),
        ),
        in_specs=[pl.BlockSpec(memory_space=pltpu.VMEM)] * 7,
        out_specs=(pl.BlockSpec(memory_space=pltpu.VMEM),) * 3,
        scratch_shapes=[
            pltpu.VMEM((keys, lane_width), wide),
            pltpu.VMEM((keys, lane_width), wide),
        ],
        compiler_params=pltpu.CompilerParams(vmem_limit_bytes=60 * 2**20),
        cost_estimate=pl.CostEstimate(flops=10 * rows * keys * width, bytes_accessed=16 * keys * width, transcendentals=heads * rows * keys),
        name="attend_back",
    )(q, k, v, span, lse, att, d_att)


def back_kernel(
    heads, tokens, q, k, v, span, lse, att, d_att, d_resid_one, grad_out, a_full, g_grad, d_grad, small,
    d_tokens, qkv_out, wout_out, gu_out, down_out, small_out, *scratch,
):
    place = Place()
    place.greet()
    c = place.c
    low, wide = jnp.bfloat16, jnp.float32
    tok_rows, width = tokens.shape
    pairs = heads // 2
    bufs, rest = scratch[:27], scratch[27:]
    a_grad, dq, dkv_own, dkv_out, dkv_in, g_sum, a_sum, g_fin, a_fin, small_buf, send, recv, local, pair_sem, fin_sem, in_sem = rest
    copies = Copies(send, recv)
    last = Copies(fin_sem.at[0], fin_sem.at[1])
    half_g = g_grad.shape[3] // 2

    def scatter(i, source, own, sib, *more):
        return Scatter(
            place, copies, i * scatter_slots, lambda four: source(1 - c, four), lambda at: own.at[at], sib, *more,
            load=lambda four, slot: pltpu.make_async_copy(source(c, four), own.at[four], local.at[slot]),
        )

    down = scatter(0, lambda half, four: d_grad.at[four, half], *bufs[:7])
    gate = scatter(1, lambda half, four: g_grad.at[half, four, :, :half_g], *bufs[7:14])
    rest = scatter(2, lambda half, four: g_grad.at[half, four, :, half_g:], *bufs[14:21])
    proj = Scatter(
        place, copies, 3 * scatter_slots, lambda four: a_grad.at[1 - c, four], lambda at: a_grad.at[c, at], *bufs[21:]
    )
    chunks = Steps([(m, planes) for m in (down, gate, rest, proj) for planes in far_near], scatter_stages)
    hops = ((place.sib, 0), (place.xn, 1), (place.yn, 2))

    def exchange(i):
        peer, slot = hops[i]
        last.put(small_buf.at[i], small_buf.at[4 + i], slot, peer, lambda: small_buf.at[4 + i])

    def combine(i):
        peer, slot = hops[i]
        last.got(small_buf.at[4 + i], slot, peer)
        small_buf[i + 1] = small_buf[i] + small_buf[4 + i]

    def spread():
        for z in (1, 2, 3):
            last.put(small_buf.at[3], small_buf.at[6 + z], 2 + z, place.zn[z], lambda z=z: small_buf.at[6 + z])

    chunks(-2)
    chunks(-1)
    small_buf[0] = small[...]
    exchange(0)

    def steps(pair):
        for i in range(3):

            @pl.when(pair == 2 * i + 1)
            def _(i=i):
                chunks(i + 1)
                combine(i)
                if i < 2:
                    exchange(i + 1)
                else:
                    spread()

    half = lambda side: pl.ds(pl.multiple_of(side * tok_rows, tok_rows), tok_rows)

    def send_dkv(pair):
        return pltpu.make_async_remote_copy(
            src_ref=dkv_out.at[pair], dst_ref=dkv_in.at[pair], send_sem=pair_sem.at[0, pair],
            recv_sem=pair_sem.at[1, pair], device_id=place.sib, device_id_type=MESH,
        )

    def attention(q_v, k_v, v_v, span_v, att_v, datt_v, dk_sum, dv_sum):
        loads = [
            pltpu.make_async_copy(src, dst, in_sem.at[i])
            for i, (src, dst) in enumerate(
                ((q, q_v), (k, k_v), (v, v_v), (span, span_v), (att, att_v), (d_att, datt_v))
            )
        ]
        for copy in loads:
            copy.start()
        chunks(0)
        for copy in loads:
            copy.wait()

        @pl.loop(0, pairs)
        def _(pair):
            attend_back_pair(
                pair, heads, q_v, k_v, v_v, span_v, lse, att_v, datt_v, dq, dk_sum, dv_sum
            )
            for i, part in enumerate((dk_sum, dv_sum)):
                dkv_own[pair, i] = part[half(c), :]
                dkv_out[pair, i] = part[half(1 - c), :].astype(low)
            send_dkv(pair).start()
            steps(pair)

    block = lambda *shape: pltpu.VMEM(shape, low)
    key_rows = k.shape[0]
    pl.run_scoped(
        attention, block(*q.shape), block(*k.shape), block(*v.shape), pltpu.VMEM(span.shape, wide),
        block(*att.shape), block(*d_att.shape), pltpu.VMEM((key_rows, lane_width), wide),
        pltpu.VMEM((key_rows, lane_width), wide),
    )

    def finish(w_left, w_right, resid, x_t, d_k, d_v):
        loads = [
            pltpu.make_async_copy(a_full.at[0, :, : 2 * width], w_left, in_sem.at[0]),
            pltpu.make_async_copy(a_full.at[1, :, :width], w_right, in_sem.at[1]),
            pltpu.make_async_copy(d_resid_one, resid, in_sem.at[2]),
            pltpu.make_async_copy(grad_out, a_grad.at[1, :, :, width:], in_sem.at[3]),
        ]
        for copy in loads:
            copy.start()
        x_t[...] = tokens[...].astype(wide).T.astype(low)
        for pair in range(pairs):
            send_dkv(pair).wait_recv()
            at = slice(pair * lane_width, (pair + 1) * lane_width)
            d_k[:, at] = (dkv_own[pair, 0] + dkv_in[pair, 0].astype(wide)).astype(low)
            d_v[:, at] = (dkv_own[pair, 1] + dkv_in[pair, 1].astype(wide)).astype(low)
        tile = width // 2
        for side, at, src in ((0, 0, dq), (0, width, d_k), (1, 0, d_v)):
            for part in range(2):
                cols = slice(part * tile, (part + 1) * tile)
                term = dot(x_t[...], src[:, cols]).astype(low)
                a_grad[side, :, :, at + part * tile : at + (part + 1) * tile] = term.reshape(16, rows_chip, tile)
        loads[3].wait()
        chunks(4)
        for copy in loads[:3]:
            copy.wait()
        total = resid[...] + dot(dq[...], w_left[:, :width], ((1,), (1,)))
        chunks(5)
        total += dot(d_k[...], w_left[:, width:], ((1,), (1,))) + dot(d_v[...], w_right[...], ((1,), (1,)))
        d_tokens[...] = total.astype(low)

    pl.run_scoped(
        finish, block(width, 2 * width), block(width, width), pltpu.VMEM((tok_rows, width), wide),
        block(width, tok_rows), block(tok_rows, width), block(tok_rows, width),
    )
    for z in (1, 2, 3):
        last.got(small_buf.at[6 + z], 2 + z, place.zn[z])
    small_out[...] = (small_buf[3] + small_buf[7]) + (small_buf[8] + small_buf[9])
    mine, theirs = pl.ds(pl.multiple_of(24 * c, 8), 24), pl.ds(pl.multiple_of(24 - 24 * c, 8), 24)
    chunks(6)
    down_out[...] = down.total()
    chunks(7)
    g_sum[0] = gate.total()
    last.put(g_sum.at[0, theirs], g_fin.at[0], 6, place.sib, lambda: g_fin.at[0])
    chunks(8)
    chunks(9)
    g_sum[1] = rest.total()
    last.put(g_sum.at[1, theirs], g_fin.at[1], 8, place.sib, lambda: g_fin.at[1])
    chunks(10)
    first = c == 0
    for i, slot in ((0, 6), (1, 8)):
        last.got(g_fin.at[i], slot, place.sib)
        own, other = g_sum[i, mine], g_fin[i]
        gu_out[:, i * half_g : (i + 1) * half_g] = jnp.where(first, own, other)
        gu_out[:, (i + 2) * half_g : (i + 3) * half_g] = jnp.where(first, other, own)
    a_sum[...] = proj.total()
    last.put(a_sum.at[theirs], a_fin, 7, place.sib, lambda: a_fin)
    last.got(a_fin, 7, place.sib)
    left = jnp.where(first, a_sum[mine], a_fin[...])
    right = jnp.where(first, a_fin[...], a_sum[mine])
    qkv_out[:, : 2 * width] = left
    qkv_out[:, 2 * width :] = right[:, :width]
    wout_out[...] = right[:, width:]

    @pl.loop(0, pairs)
    def _(pair):
        send_dkv(pair).wait_send()

    copies.drain(place.sib)
    last.drain(place.sib)


def back(heads, tokens, q, k, v, span, lse, att, d_att, d_resid_one, grad_out, a_full, g_grad, d_grad, small):
    low, wide = jnp.bfloat16, jnp.float32
    tok_rows, width = tokens.shape
    half_g, half_a = g_grad.shape[-1], 2 * width
    pairs = heads // 2
    d_rows = d_grad.shape[2]
    bufs = []
    shapes = ((d_rows, width), (rows_chip, half_g // 2), (rows_chip, half_g // 2), (rows_chip, half_a))
    for i, (rows, half) in enumerate(shapes):
        counts = (16, 16, 2, 2, 4, 4, 3)[i == 3 :]
        bufs += [pltpu.VMEM((count, rows, half), low) for count in counts]
    vmem, hbm = pl.BlockSpec(memory_space=pltpu.VMEM), pl.BlockSpec(memory_space=pl.ANY)
    keys = k.shape[0]
    dma = lambda *shape: pltpu.SemaphoreType.DMA(shape)
    return pl.pallas_call(
        lambda *refs: back_kernel(heads, *refs),
        out_shape=(
            jax.ShapeDtypeStruct((tok_rows, width), low),
            jax.ShapeDtypeStruct((24, 3 * width), wide),
            jax.ShapeDtypeStruct((24, width), wide),
            jax.ShapeDtypeStruct((24, 2 * half_g), wide),
            jax.ShapeDtypeStruct((d_rows, width), wide),
            jax.ShapeDtypeStruct(small.shape, wide),
        ),
        in_specs=[vmem, hbm, hbm, hbm, hbm, vmem] + [hbm] * 7 + [vmem],
        out_specs=(vmem,) * 6,
        scratch_shapes=bufs
        + [
            pltpu.VMEM((2, 16, rows_chip, half_a), low),
            pltpu.VMEM((tok_rows, width), low),
            pltpu.VMEM((pairs, 2, tok_rows, lane_width), wide),
            pltpu.VMEM((pairs, 2, tok_rows, lane_width), low),
            pltpu.VMEM((pairs, 2, tok_rows, lane_width), low),
            pltpu.VMEM((2, rows_chip, half_g // 2), wide),
            pltpu.VMEM((rows_chip, half_a), wide),
            pltpu.VMEM((2, 24, half_g // 2), wide),
            pltpu.VMEM((24, half_a), wide),
            pltpu.VMEM((10,) + small.shape, wide),
            dma(4 * scatter_slots),
            dma(4 * scatter_slots),
            dma(4 * scatter_slots),
            dma(2, pairs),
            dma(2, 9),
            dma(6),
        ],
        compiler_params=pltpu.CompilerParams(
            collective_id=1, has_side_effects=True, vmem_limit_bytes=62 * 2**20
        ),
        cost_estimate=pl.CostEstimate(
            flops=10 * tok_rows * keys * width, bytes_accessed=40 * width * width, transcendentals=heads * tok_rows * keys
        ),
        name="attention_back_and_sums",
    )(tokens, q, k, v, span, lse, att, d_att, d_resid_one, grad_out, a_full, g_grad, d_grad, small)


def window(cells, width):
    count = lax.axis_size("blk")
    if count == 2:
        other = lax.ppermute(cells, "blk", [(0, 1), (1, 0)])
        first = lax.axis_index("blk") == 0
        return jnp.concatenate([jnp.where(first, cells, other), jnp.where(first, other, cells)], 0)
    before = lax.ppermute(cells, "blk", [(i, i + 1) for i in range(count - 1)])
    after = lax.ppermute(cells, "blk", [(i + 1, i) for i in range(count - 1)])
    return jnp.concatenate([before, cells, after], 0)


def window_back(terms, width):
    count = lax.axis_size("blk")
    low = jnp.bfloat16
    if count == 2:
        first = lax.axis_index("blk") == 0
        upper, lower = terms[:width], terms[width:]
        other = lax.ppermute(jnp.where(first, lower, upper).astype(low), "blk", [(0, 1), (1, 0)])
        return jnp.where(first, upper, lower) + other.astype(terms.dtype)
    before = lax.ppermute(terms[2 * width :].astype(low), "blk", [(i, i + 1) for i in range(count - 1)])
    after = lax.ppermute(terms[:width].astype(low), "blk", [(i + 1, i) for i in range(count - 1)])
    return terms[width : 2 * width] + before.astype(terms.dtype) + after.astype(terms.dtype)


def key_spans(labels, first, tok_rows):
    seq_len = labels.shape[0]
    query_pos = first + jnp.arange(tok_rows, dtype=jnp.int32)
    query_labels = lax.dynamic_slice_in_dim(labels, first, tok_rows, 0)
    if seq_len == 2 * tok_rows:
        key_pos, key_labels = jnp.arange(seq_len, dtype=jnp.int32), labels
    else:
        key_pos = first - tok_rows + jnp.arange(3 * tok_rows, dtype=jnp.int32)
        padded = jnp.pad(labels, (tok_rows, tok_rows), constant_values=seq_len)
        key_labels = lax.dynamic_slice_in_dim(padded, first, 3 * tok_rows, 0)
    same = (key_labels[:, None] == query_labels[None, :]) & (key_labels[:, None] != seq_len)
    gap = jnp.abs(key_pos[:, None] - query_pos[None, :])
    return jnp.where(same | (gap == 0), gap.astype(jnp.float32), far)


def on_chip_grid():
    return lax.axis_size("rows") == 16 and lax.axis_size("blk") == 2


def gathered_weights(w_qkv, w_out, ln1_gain, ln1_bias, w_gate_up, w_down, ln2_gain, ln2_bias):
    rows, width = w_out.shape
    ff = w_gate_up.shape[1] // 2
    table = jnp.stack((ln1_gain, ln1_bias, ln2_gain, ln2_bias), 1)
    table = jnp.pad(table, ((0, 0), (0, lane_width - 4)))
    left = jnp.concatenate([w_qkv[:, : 2 * width], table], 1)
    right = jnp.concatenate([w_qkv[:, 2 * width :], w_out, jnp.zeros_like(table)], 1)
    a_shard = jnp.stack([left, right])
    g_shard = jnp.stack([w_gate_up[:, :ff], w_gate_up[:, ff:]])
    if not on_chip_grid():
        both = ("rows", "blk")
        return (
            lax.all_gather(a_shard, both, axis=1, tiled=True),
            lax.all_gather(g_shard, both, axis=1, tiled=True),
            lax.all_gather(w_down, both, axis=0, tiled=True),
        )
    spare = ((0, 0), (0, 32 - rows), (0, 0))
    a_full, g_full, d_full = gather_weights(jnp.pad(a_shard, spare), jnp.pad(g_shard, spare), w_down)
    return a_full.reshape(2, width, -1), g_full.reshape(2, width, ff), d_full.reshape(-1, width)


def back_and_sums(heads, tokens, q, k, v, span, lse, att, d_att, d_resid_one, grad_out, a_full, g_grad, d_grad, small):
    both = ("rows", "blk")
    tok_rows, width = tokens.shape
    if on_chip_grid():
        split = lambda g: g.reshape(2, 16, rows_chip, g.shape[2])
        return back(
            heads, tokens, q, k, v, span, lse, att, d_att, d_resid_one, grad_out.reshape(16, rows_chip, width),
            a_full, split(g_grad), d_grad.reshape(16, 2, -1, width), small,
        )
    low = jnp.bfloat16
    dq, dk, dv = attend_back(q, k, v, span, lse, att, d_att, heads)
    dkv = window_back(jnp.concatenate([dk, dv], 1), tok_rows)
    d_qk = jnp.concatenate([dq, dkv[:, :width].astype(low)], 1)
    d_v = dkv[:, width:].astype(low)
    grad_qkv = transposed_times(tokens, jnp.concatenate([d_qk, d_v], 1))
    d_tokens = d_resid_one + times_transposed(d_qk, a_full[0, :, : 2 * width])
    d_tokens = d_tokens + times_transposed(d_v, a_full[1, :, :width])
    share = lambda g, axis: lax.psum_scatter(g.astype(jnp.float32), both, scatter_dimension=axis, tiled=True)
    gate, up = share(g_grad, 1)
    return (
        d_tokens.astype(low), share(grad_qkv, 0), share(grad_out, 0), jnp.concatenate([gate, up], 1),
        share(d_grad, 0), lax.psum(small, both),
    )


def body(
    tokens, segments, w_qkv, w_out, ln1_gain, ln1_bias, w_gate_up, w_down, ln2_gain, ln2_bias, out_grad,
):
    inputs, labels = tokens[0], segments[0]
    tok_rows, width = inputs.shape
    low, wide = jnp.bfloat16, jnp.float32
    both = ("rows", "blk")
    first = lax.axis_index("blk") * tok_rows
    span = key_spans(labels, first, tok_rows)
    valid = (lax.dynamic_slice_in_dim(labels, first, tok_rows, 0) != labels.shape[0]).astype(wide)[:, None]
    a_full, w_gu, w_dn = gathered_weights(
        w_qkv, w_out, ln1_gain, ln1_bias, w_gate_up, w_down, ln2_gain, ln2_bias
    )
    vectors = jnp.pad(a_full[0, :, 2 * width : 2 * width + 4].astype(wide).T, ((0, 4), (0, 0)))
    w_qk, w_v = a_full[0, :, : 2 * width], a_full[1, :, :width]
    qk = jnp.dot(inputs, w_qk, preferred_element_type=wide).astype(low)
    v = jnp.dot(inputs, w_v, preferred_element_type=wide).astype(low)
    query = qk[:, :width]
    kv = window(jnp.concatenate([qk[:, width:], v], 1), tok_rows)
    keys, values = kv[:, :width], kv[:, width:]
    attended, lse = attend(query, keys, values, span, HEADS)
    output, d_resid_one, d_att, grad_out, g_grad, d_grad, small = ffn(
        inputs, attended, a_full, vectors, valid, out_grad[0], w_gu, w_dn
    )
    d_tokens, *parts, small = back_and_sums(
        HEADS, inputs, query, keys, values, span, lse, attended, d_att, d_resid_one, grad_out, a_full, g_grad, d_grad, small
    )
    share = width // lax.axis_size(both)
    mine = lax.axis_index(both) * share
    rows = lax.dynamic_slice_in_dim(small[:4], mine, share, 1)
    stats = jnp.sqrt(jnp.sum(small[4:8], 1) / (small[8, 0] * width))
    return (
        output[None], d_tokens[None], parts[0], parts[1], rows[0], rows[1],
        parts[2], parts[3], rows[2], rows[3], stats,
    )


def solution(mesh):
    placed = (
        P("rows", "blk", None),
        P("rows", None),
        P(("rows", "blk"), None),
        P(("rows", "blk"), None),
        P(("rows", "blk")),
        P(("rows", "blk")),
        P(("rows", "blk"), None),
        P(("rows", "blk"), None),
        P(("rows", "blk")),
        P(("rows", "blk")),
        P("rows", "blk", None),
    )
    return jax.shard_map(
        body,
        mesh=mesh,
        in_specs=placed,
        out_specs=(
            P("rows", "blk", None),
            P("rows", "blk", None),
            P(("rows", "blk"), None),
            P(("rows", "blk"), None),
            P(("rows", "blk")),
            P(("rows", "blk")),
            P(("rows", "blk"), None),
            P(("rows", "blk"), None),
            P(("rows", "blk")),
            P(("rows", "blk")),
            P(),
        ),
        check_vma=False,
    )
```

```python
import jax
import jax.numpy as jnp
from jax import lax
from jax.experimental import pallas as pl
from jax.experimental.pallas import tpu as pltpu
from jax.sharding import PartitionSpec as P

HEADS = 12


ln_eps = 1e-12
far = 1e33
lane_width = 128


def times_transposed(left, right):
    return lax.dot_general(
        left, right, (((1,), (1,)), ((), ())), preferred_element_type=jnp.float32
    )


def transposed_times(left, right):
    return lax.dot_general(
        left, right, (((0,), (0,)), ((), ())), preferred_element_type=jnp.float32
    )


MESH = pl.DeviceIdType.MESH


class Place:
    def __init__(self):
        r, self.c = lax.axis_index("rows"), lax.axis_index("blk")
        self.x, self.y, self.z = r % 2, (r // 2) % 2, r // 4
        self.sib = (r, 1 - self.c)
        self.xn = (self.at(0, "x"), self.c)
        self.yn = (self.at(0, "y"), self.c)
        self.zn = {k: (self.at(k, "o"), self.c) for k in (1, 2, 3)}

    def plane(self, k):
        z, low = self.z % 2, self.z // 2
        if k % 2:
            z = 1 - z
        if k // 2:
            low = 1 - low
        return low * 2 + z

    def at(self, k, j):
        x = 1 - self.x if j in "xd" else self.x
        y = 1 - self.y if j in "yd" else self.y
        return self.plane(k) * 4 + y * 2 + x

    def greet(self):
        barrier = pltpu.get_barrier_semaphore()
        peers = [self.sib, self.xn, self.yn] + [self.zn[k] for k in (1, 2, 3)]
        for peer in peers:
            pl.semaphore_signal(barrier, inc=1, device_id=peer, device_id_type=MESH)
        pl.semaphore_wait(barrier, len(peers))


class Copies:
    def __init__(self, send, recv):
        self.send, self.recv, self.open = send, recv, []

    def of(self, src, dst, slot, peer):
        return pltpu.make_async_remote_copy(
            src_ref=src, dst_ref=dst, send_sem=self.send.at[slot], recv_sem=self.recv.at[slot],
            device_id=peer, device_id_type=MESH,
        )

    def put(self, src, dst, slot, peer, like=None):
        self.of(src, dst, slot, peer).start()
        self.open.append((like or (lambda: dst), slot))

    def got(self, dst, slot, peer):
        self.of(dst, dst, slot, peer).wait_recv()

    def drain(self, peer):
        for like, slot in self.open:
            self.of(like(), like(), slot, peer).wait_send()
        self.open = []


class Gather:
    def __init__(self, place, copies, base, out):
        self.p, self.cp, self.base, self.out = place, copies, base, out

    def slot(self, kind, k, j="o"):
        start = {"z": -1, "x": 3, "y": 7, "d": 11, "s": 15}[kind]
        return self.base + start + (4 * k + "oxyd".index(j) if kind == "s" else k)

    def block(self, k, j):
        return self.out(self.p.c, self.p.at(k, j))

    def send(self, src, dst, slot, peer):
        self.cp.put(src, dst, slot, peer, lambda: self.out(0, 0))

    def push(self, src, k, j):
        self.send(src, self.block(k, j), self.slot("s", k, j), self.p.sib)

    def to_z(self, k):
        if k:
            self.send(self.block(0, "o"), self.block(0, "o"), self.slot("z", k), self.p.zn[k])

    def spread(self, src, k):
        dst = self.block(k, "o")
        self.send(src, dst, self.slot("x", k), self.p.xn)
        self.send(src, dst, self.slot("y", k), self.p.yn)
        self.push(src, k, "o")

    def from_z(self, k):
        if k == 0:
            self.spread(self.block(0, "o"), 0)
            return
        block = self.block(k, "o")
        self.cp.got(block, self.slot("z", k), self.p.zn[k])
        self.spread(block, k)

    def from_xy(self, k):
        x, y = self.block(k, "x"), self.block(k, "y")
        self.cp.got(x, self.slot("x", k), self.p.xn)
        if k == 2:
            self.send(x, x, self.slot("d", k), self.p.yn)
        self.cp.got(y, self.slot("y", k), self.p.yn)
        if k == 0:
            self.send(y, y, self.slot("d", k), self.p.xn)
        self.push(x, k, "x")
        self.push(y, k, "y")

    def from_even(self, k):
        if k % 2 == 0:
            self.from_d(k)

    def from_odd(self, k):
        if k % 2:
            self.from_d(k)

    def from_d(self, k):
        block = self.block(k, "d")
        self.cp.got(block, self.slot("d", k), self.p.xn)
        if k % 2 == 0:
            self.send(block, block, self.slot("d", k + 1), self.p.zn[1])
        self.push(block, k, "d")

    def from_sib(self):
        for k in range(4):
            for j in "oxyd":
                block = self.out(1 - self.p.c, self.p.at(k, j))
                self.cp.got(block, self.slot("s", k, j), self.p.sib)


class Scatter:
    def __init__(self, place, copies, gives, base, give, own, sib, rly, dia, xin, yin, zin):
        self.p, self.cp, self.gives, self.base, self.give, self.own = place, copies, gives, base, give, own
        self.sib, self.rly, self.dia, self.xin, self.yin, self.zin = sib, rly, dia, xin, yin, zin

    def slot(self, kind, k):
        return self.base + {"s": 0, "r": 4, "d": 5, "x": 8, "y": 12, "z": 15}[kind] + k

    def four(self, k):
        return pl.ds(self.p.plane(k) * 4, 4)

    def begin(self, k):
        four = self.four(k)
        self.gives.put(self.give(four), self.sib.at[four], self.slot("s", k), self.p.sib, lambda: self.sib.at[pl.ds(0, 4)])

    def to_x(self, own, k):
        self.cp.put(own, self.xin.at[k], self.slot("x", k), self.p.xn, lambda: self.xin.at[k])

    def to_y(self, own, k):
        self.cp.put(own, self.yin.at[k], self.slot("y", k), self.p.yn, lambda: self.yin.at[k])

    def both(self, k, j, *more):
        at = self.p.at(k, j)
        own = self.own(at)
        total = own[...] + self.sib[at]
        for ref in more:
            total = total + ref[...]
        own[...] = total
        return own

    def pair(self, k):
        four = self.four(k)
        self.cp.got(self.sib.at[four], self.slot("s", k), self.p.sib)
        if k % 2:
            i = k // 2
            dia = lambda: self.dia.at[i]
            self.cp.put(self.both(k, "d"), dia(), self.slot("d", 2 * i), self.p.zn[1], dia)
        if k != 2:
            self.to_x(self.both(k, "x"), k)
        if k != 0:
            self.to_y(self.both(k, "y"), k)

    def diag(self, k):
        if k % 2:
            return
        i = k // 2
        self.cp.got(self.dia.at[i], self.slot("d", k), self.p.zn[1])
        own = self.both(k, "d", self.dia.at[i])
        peer = self.p.xn if k == 0 else self.p.yn
        self.cp.put(own, self.rly.at[i], self.slot("r", k), peer, lambda: self.rly.at[i])

    def relay(self, k):
        if k % 2:
            return
        i = k // 2
        self.cp.got(self.rly.at[i], self.slot("r", k), self.p.xn)
        if k == 0:
            self.to_y(self.both(k, "y", self.rly.at[i]), k)
        else:
            self.to_x(self.both(k, "x", self.rly.at[i]), k)

    def plane(self, k):
        p = self.p
        at = p.at(k, "o")
        self.cp.got(self.xin.at[k], self.slot("x", k), p.xn)
        self.cp.got(self.yin.at[k], self.slot("y", k), p.yn)
        wide = jnp.float32
        own = self.own(at)
        total = (own[...].astype(wide) + self.sib[at].astype(wide)) + (
            self.xin[k].astype(wide) + self.yin[k].astype(wide)
        )
        own[...] = total.astype(jnp.bfloat16)
        if k:
            self.cp.put(own, self.zin.at[k - 1], self.slot("z", k), p.zn[k], lambda: self.zin.at[k - 1])

    def total(self):
        for k in (1, 2, 3):
            self.cp.got(self.zin.at[k - 1], self.slot("z", k), self.p.zn[k])
        wide = jnp.float32
        own = self.own(self.p.at(0, "o"))
        return (own[...].astype(wide) + self.zin[0].astype(wide)) + (
            self.zin[1].astype(wide) + self.zin[2].astype(wide)
        )


class Steps:
    def __init__(self, items, stages):
        self.items, self.stages = items, stages

    def __call__(self, t):
        for name, lag in self.stages:
            if 0 <= t - lag < len(self.items):
                matrix, planes = self.items[t - lag]
                for k in planes:
                    getattr(matrix, name)(k)

    def count(self):
        return len(self.items) + max(lag for _, lag in self.stages)


gather_stages = (("to_z", -2), ("from_z", 0), ("from_xy", 1), ("from_even", 2), ("from_odd", 3))
scatter_stages = (("pair", 0), ("diag", 1), ("relay", 2), ("plane", 3))
near_far, far_near = ((0, 1), (2, 3)), ((3, 2), (1, 0))


rows_chip = 48
gather_slots, scatter_slots = 31, 19


def dot(left, right, dims=((1,), (0,))):
    return lax.dot_general(left, right, (dims, ((), ())), preferred_element_type=jnp.float32)


def row_mean(values):
    return jnp.mean(values, -1, keepdims=True)


def normalized(resid):
    centred = resid - row_mean(resid)
    inverse = lax.rsqrt(row_mean(centred * centred) + ln_eps)
    return centred * inverse, inverse


def norm_back(grad, gain, norm, inverse):
    e = grad * gain
    return inverse * (e - row_mean(e) - norm * row_mean(e * norm))


def column_sum(values):
    return jnp.sum(values, 0, keepdims=True)


def ffn_kernel(
    tokens, attended, w_out, vectors, valid, out_grad, w_gu, w_down,
    output, d_resid_one, d_att, grad_out, grad_gu, grad_down, small,
    hid, hid_low, hid_t, norm_one, inv_one, slope_gate, slope_up, act, total, d_hid, d_branch,
):
    i = pl.program_id(0)
    tiles = pl.num_programs(0) // 2
    low = jnp.bfloat16
    wide = jnp.float32

    @pl.when(i == 0)
    def _():
        branch = dot(attended[...], w_out[0])
        toks = tokens[...].astype(wide)
        norm, inverse = normalized(toks + branch)
        norm_one[...] = norm
        inv_one[...] = inverse
        hidden = norm * vectors[0:1, :] + vectors[1:2, :]
        hid[...] = hidden
        hid_low[...] = hidden.astype(low)
        hid_t[...] = hidden.T.astype(low)
        mask = valid[...]
        small[4:5, :] = column_sum(mask * toks * toks)
        small[5:6, :] = column_sum(mask * branch * branch)
        small[6:7, :] = column_sum(mask * hidden * hidden)
        small[8:16, :] = jnp.zeros((8, small.shape[1]), wide)
        small[8:9, :] = jnp.broadcast_to(jnp.sum(mask, 0, keepdims=True), (1, small.shape[1]))
        total[...] = jnp.zeros_like(total)

    @pl.when(i < tiles)
    def _():
        h = hid_low[...]
        gate = dot(h, w_gu[0])
        up = dot(h, w_gu[1])
        cdf = 0.5 + 0.5 * lax.erf(gate * 0.7071067811865476)
        glu = gate * cdf
        density = 0.3989422804014327 * jnp.exp(-0.5 * gate * gate)
        slope_up[i] = glu
        slope_gate[i] = up * (cdf + gate * density)
        a = (glu * up).astype(low)
        act[i] = a
        total[...] += dot(a, w_down[...])

    @pl.when(i == tiles - 1)
    def _():
        branch = total[...]
        mask = valid[...]
        small[7:8, :] = column_sum(mask * branch * branch)
        norm, inverse = normalized(hid[...] + branch)
        gain = vectors[2:3, :]
        output[...] = (norm * gain + vectors[3:4, :]).astype(low)
        grad = out_grad[...].astype(wide)
        small[2:3, :] = column_sum(grad * norm)
        small[3:4, :] = column_sum(grad)
        back = norm_back(grad, gain, norm, inverse)
        d_hid[...] = back
        d_branch[...] = back.astype(low)

    @pl.when(i >= tiles)
    def _():
        j = i - tiles
        db = d_branch[...]
        grad_down[...] = dot(act[j].T, db).astype(low)
        d_act = dot(db, w_down[...], ((1,), (1,)))
        d_gate = (d_act * slope_gate[j]).astype(low)
        d_up = (d_act * slope_up[j]).astype(low)
        h_t = hid_t[...]
        grad_gu[0] = dot(h_t, d_gate).astype(low)
        grad_gu[1] = dot(h_t, d_up).astype(low)
        d_hid[...] += dot(d_gate, w_gu[0], ((1,), (1,))) + dot(d_up, w_gu[1], ((1,), (1,)))

    @pl.when(i == 2 * tiles - 1)
    def _():
        grad = d_hid[...]
        norm = norm_one[...]
        small[0:1, :] = column_sum(grad * norm)
        small[1:2, :] = column_sum(grad)
        back = norm_back(grad, vectors[0:1, :], norm, inv_one[...])
        d_resid_one[...] = back
        db = back.astype(low)
        grad_out[...] = dot(attended[...].T, db).astype(low)
        d_att[...] = dot(db, w_out[0], ((1,), (1,))).astype(low)


def ffn(tokens, attended, a_full, vectors, valid, out_grad, w_gu, w_down):
    rows, width = tokens.shape
    ff = w_down.shape[0]
    tile = 512
    tiles = ff // tile
    low, wide = jnp.bfloat16, jnp.float32
    whole = lambda *shape: pl.BlockSpec(shape, lambda i: (0,) * len(shape))
    at = lambda i: jnp.where(i < tiles, i, i - tiles)
    late = lambda i: jnp.maximum(i - tiles, 0)
    return pl.pallas_call(
        ffn_kernel,
        grid=(2 * tiles,),
        out_shape=(
            jax.ShapeDtypeStruct((rows, width), low),
            jax.ShapeDtypeStruct((rows, width), wide),
            jax.ShapeDtypeStruct((rows, width), low),
            jax.ShapeDtypeStruct((width, width), low),
            jax.ShapeDtypeStruct((2, width, ff), low),
            jax.ShapeDtypeStruct((ff, width), low),
            jax.ShapeDtypeStruct((16, width), wide),
        ),
        in_specs=[
            whole(rows, width),
            whole(rows, width),
            pl.BlockSpec((1, width, width), lambda i: (1, 0, 1)),
            whole(8, width),
            whole(rows, 1),
            whole(rows, width),
            pl.BlockSpec((2, width, tile), lambda i: (0, 0, at(i))),
            pl.BlockSpec((tile, width), lambda i: (at(i), 0)),
        ],
        out_specs=(
            whole(rows, width),
            whole(rows, width),
            whole(rows, width),
            whole(width, width),
            pl.BlockSpec((2, width, tile), lambda i: (0, 0, late(i))),
            pl.BlockSpec((tile, width), lambda i: (late(i), 0)),
            whole(16, width),
        ),
        scratch_shapes=[
            pltpu.VMEM((rows, width), wide),
            pltpu.VMEM((rows, width), low),
            pltpu.VMEM((width, rows), low),
            pltpu.VMEM((rows, width), wide),
            pltpu.VMEM((rows, 1), wide),
            pltpu.VMEM((tiles, rows, tile), wide),
            pltpu.VMEM((tiles, rows, tile), wide),
            pltpu.VMEM((tiles, rows, tile), low),
            pltpu.VMEM((rows, width), wide),
            pltpu.VMEM((rows, width), wide),
            pltpu.VMEM((rows, width), low),
        ],
        compiler_params=pltpu.CompilerParams(vmem_limit_bytes=60 * 2**20),
        cost_estimate=pl.CostEstimate(
            flops=2 * rows * width * (9 * ff + 3 * width), bytes_accessed=18 * ff * width, transcendentals=2 * rows * ff
        ),
        name="feed_forward",
    )(tokens, attended, a_full, vectors, valid, out_grad, w_gu, w_down)


def half_of(block, axis, second):
    place = lax.broadcasted_iota(jnp.int32, block.shape, axis)
    depth = block.shape[axis] // 2
    keep = place >= depth if second else place < depth
    return jnp.where(keep, block, jnp.zeros_like(block))


def attend_kernel(heads, q, k, v, span, attended, lse):
    @pl.loop(0, heads // 2)
    def _(pair):
        attend_pair(pair, heads, q, k, v, span, lse, attended)


def attend(q, k, v, span, heads):
    rows, width = q.shape
    keys = k.shape[0]
    low, wide = jnp.bfloat16, jnp.float32
    return pl.pallas_call(
        lambda *refs: attend_kernel(heads, *refs),
        out_shape=(
            jax.ShapeDtypeStruct((rows, width), low),
            jax.ShapeDtypeStruct((16, rows), wide),
        ),
        in_specs=[pl.BlockSpec(memory_space=pltpu.VMEM)] * 4,
        out_specs=(pl.BlockSpec(memory_space=pltpu.VMEM),) * 2,
        compiler_params=pltpu.CompilerParams(vmem_limit_bytes=60 * 2**20),
        cost_estimate=pl.CostEstimate(flops=4 * rows * keys * width, bytes_accessed=8 * keys * width, transcendentals=heads * rows * keys),
        name="attend",
    )(q, k, v, span)


def attend_back_pair(pair, heads, q, k, v, span, lse, att, d_att, dq, dk_sum, dv_sum):
    low, wide = jnp.bfloat16, jnp.float32
    rows, width = q.shape
    lanes = lane_width
    depth = width // heads
    chunk = 256
    scale = depth**-0.5
    at = pl.ds(pl.multiple_of(pair * lanes, lanes), lanes)
    keys, values = k[:, at], v[:, at]
    keys_t = keys.astype(wide).T.astype(low)
    for c in range(rows // chunk):
        here = pl.ds(c * chunk, chunk)
        q_wide = q[here, at].astype(wide)
        do_here = d_att[here, at]
        do_wide = do_here.astype(wide)
        q_here = q_wide.astype(low)
        q_t, do_t = q_wide.T.astype(low), do_wide.T.astype(low)
        both_t = (do_wide * att[here, at].astype(wide)).T
        dk_part, dv_part, dq_parts = None, None, []
        for h in (0, 1):
            head = 2 * pair + h
            own = slice(h * depth, (h + 1) * depth)
            slope = jnp.exp2(jnp.full((1, 1), -8.0 / heads, wide) * (head + 1).astype(wide))
            delta = jnp.sum(both_t[own], 0, keepdims=True)
            logits = dot(keys, half_of(q_t, 0, h)) - slope * span[:, here]
            probs = jnp.exp(logits - lse[pl.ds(head, 1), here])
            d_probs = dot(values, half_of(do_t, 0, h))
            d_logits = (probs * (d_probs - delta)).astype(low)
            dv_term = dot(probs.astype(low), half_of(do_here, 1, h))
            dk_term = dot(d_logits, half_of(q_here, 1, h))
            dv_part = dv_term if dv_part is None else dv_part + dv_term
            dk_part = dk_term if dk_part is None else dk_part + dk_term
            dq_parts.append(dot(keys_t[own], d_logits) * scale)
        if c == 0:
            dk_sum[...] = dk_part
            dv_sum[...] = dv_part
        else:
            dk_sum[...] += dk_part
            dv_sum[...] += dv_part
        dq[here, at] = jnp.concatenate(dq_parts, 0).T.astype(low)


def attend_back_kernel(heads, q, k, v, span, lse, att, d_att, dq, dk, dv, dk_sum, dv_sum):
    @pl.loop(0, heads // 2)
    def _(pair):
        attend_back_pair(pair, heads, q, k, v, span, lse, att, d_att, dq, dk_sum, dv_sum)
        at = pl.ds(pl.multiple_of(pair * lane_width, lane_width), lane_width)
        dk[:, at] = dk_sum[...]
        dv[:, at] = dv_sum[...]


def attend_back(q, k, v, span, lse, att, d_att, heads):
    rows, width = q.shape
    keys = k.shape[0]
    low, wide = jnp.bfloat16, jnp.float32
    return pl.pallas_call(
        lambda *refs: attend_back_kernel(heads, *refs),
        out_shape=(
            jax.ShapeDtypeStruct((rows, width), low),
            jax.ShapeDtypeStruct((keys, width), wide),
            jax.ShapeDtypeStruct((keys, width), wide),
        ),
        in_specs=[pl.BlockSpec(memory_space=pltpu.VMEM)] * 7,
        out_specs=(pl.BlockSpec(memory_space=pltpu.VMEM),) * 3,
        scratch_shapes=[
            pltpu.VMEM((keys, lane_width), wide),
            pltpu.VMEM((keys, lane_width), wide),
        ],
        compiler_params=pltpu.CompilerParams(vmem_limit_bytes=60 * 2**20),
        cost_estimate=pl.CostEstimate(flops=10 * rows * keys * width, bytes_accessed=16 * keys * width, transcendentals=heads * rows * keys),
        name="attend_back",
    )(q, k, v, span, lse, att, d_att)


def attend_pair(pair, heads, q, k, v, span, lse, attended):
    low, wide = jnp.bfloat16, jnp.float32
    rows, width = q.shape
    lanes = lane_width
    depth = width // heads
    chunk = 256
    at = pl.ds(pl.multiple_of(pair * lanes, lanes), lanes)
    keys = k[:, at]
    values_t = v[:, at].astype(wide).T.astype(low)
    for c in range(rows // chunk):
        here = pl.ds(c * chunk, chunk)
        q_t = q[here, at].astype(wide).T.astype(low)
        parts = []
        for h in (0, 1):
            head = 2 * pair + h
            slope = jnp.exp2(jnp.full((1, 1), -8.0 / heads, wide) * (head + 1).astype(wide))
            logits = dot(keys, half_of(q_t, 0, h)) - slope * span[:, here]
            top = jnp.max(logits, 0, keepdims=True)
            weights = jnp.exp(logits - top)
            norm = jnp.sum(weights, 0, keepdims=True)
            lse[pl.ds(head, 1), here] = top + jnp.log(norm)
            parts.append(dot(values_t[h * depth : (h + 1) * depth], weights.astype(low)) / norm)
        attended[here, at] = jnp.concatenate(parts, 0).T.astype(low)


def fore_kernel(
    heads, tokens, a_shard, g_shard, d_shard, valid, span, out_grad,
    a_full, g_full, d_full, q_out, k_out, v_out, att_out, hid_t_out, norm_out, inv_out, gate_out, up_out, act_out,
    output_out, d_hid_out, d_branch_out, lse, vectors, small,
    w_a, w_g, w_d, a_pair, g_pair, q, k, v, att, span_v, grad_v, hid, hid_low, hid_t, norm_one, inv_one,
    slope_gate, slope_up, act, output, d_hid, d_branch, pair_sem, send, recv, in_sem, out_sem,
):
    place = Place()
    place.greet()
    c = place.c
    low, wide = jnp.bfloat16, jnp.float32
    tok_rows, width = tokens.shape
    ff = w_g.shape[3]
    half_g = ff // 2
    pairs = heads // 2
    loads = [pltpu.make_async_copy(src, dst, in_sem.at[i]) for i, (src, dst) in enumerate(((span, span_v), (out_grad, grad_v)))]
    for copy in loads:
        copy.start()
    swaps = Copies(pair_sem.at[0], pair_sem.at[1])
    for i, (shard, other) in enumerate(((a_shard, a_pair), (g_shard, g_pair))):
        swaps.put(shard.at[1 - c], other, i, place.sib)
    copies = Copies(send, recv)
    outs = [
        lambda half, r: w_a.at[half, r],
        lambda half, r: w_g.at[half, r, :, :half_g],
        lambda half, r: w_g.at[half, r, :, half_g:],
        lambda half, r: w_d.at[r, half],
    ]
    mats = [Gather(place, copies, i * gather_slots, out) for i, out in enumerate(outs)]
    steps = Steps([(m, planes) for m in mats for planes in near_far], gather_stages)
    me = place.at(0, "o")

    def assemble(shard, other, full, i):
        swaps.got(other, i, place.sib)
        mine = shard[c, :24, :].astype(wide)
        theirs = other[:24, :].astype(wide)
        first = c == 0
        top = jnp.where(first, mine, theirs)
        rest = jnp.where(first, theirs, mine)
        full[c, me] = jnp.concatenate([top, rest], 0).astype(low)

    assemble(a_shard, a_pair, w_a, 0)
    steps(-2)
    steps(-1)
    assemble(g_shard, g_pair, w_g, 1)
    w_d[me, c] = d_shard[...]
    for t in range(5):
        steps(t)
    mats[0].from_sib()
    saved = []

    def save(src, dst):
        copy = pltpu.make_async_copy(src, dst, out_sem.at[len(saved)])
        copy.start()
        saved.append((src, dst))

    save(w_a, a_full)
    part = lambda half, at, size: w_a[half, :, :, at : at + size].reshape(width, size)
    vectors[...] = part(0, 2 * width, lane_width).astype(wide).T[:8]
    x = tokens[...]
    half = pl.ds(pl.multiple_of(c * tok_rows, tok_rows), tok_rows)
    k[half, :] = dot(x, part(0, width, width)).astype(low)
    swaps.put(k.at[half], k.at[half], 2, place.sib, lambda: k.at[pl.ds(0, tok_rows)])
    v[half, :] = dot(x, part(1, 0, width)).astype(low)
    swaps.put(v.at[half], v.at[half], 3, place.sib, lambda: v.at[pl.ds(0, tok_rows)])
    depth = width // heads
    q[...] = dot(x, part(0, 0, width)).astype(low) * depth**-0.5
    steps(5)
    other = pl.ds(pl.multiple_of((1 - c) * tok_rows, tok_rows), tok_rows)
    swaps.got(k.at[other], 2, place.sib)
    swaps.got(v.at[other], 3, place.sib)
    save(q, q_out)
    save(k, k_out)
    save(v, v_out)
    loads[0].wait()

    @pl.loop(0, pairs)
    def _(pair):
        attend_pair(pair, heads, q, k, v, span_v, lse, att)
        for i in range(3):

            @pl.when(pair == 2 * i + 1)
            def _(i=i):
                steps(6 + i)

    save(att, att_out)
    branch = dot(att[...], part(1, width, width))
    toks = x.astype(wide)
    norm, inverse = normalized(toks + branch)
    norm_one[...] = norm
    inv_one[...] = jnp.broadcast_to(inverse, inv_one.shape)
    hidden = norm * vectors[0:1, :] + vectors[1:2, :]
    hid[...] = hidden
    hid_low[...] = hidden.astype(low)
    hid_t[...] = hidden.T.astype(low)
    save(hid_t, hid_t_out)
    save(norm_one, norm_out)
    save(inv_one, inv_out)
    mask = valid[...]
    small[0:4, :] = jnp.zeros((4, width), wide)
    small[4:5, :] = column_sum(mask * toks * toks)
    small[5:6, :] = column_sum(mask * branch * branch)
    small[6:7, :] = column_sum(mask * hidden * hidden)
    small[8:16, :] = jnp.zeros((8, width), wide)
    small[8:9, :] = jnp.broadcast_to(jnp.sum(mask, 0, keepdims=True), (1, width))
    tile = 512

    def glu(j):
        cols = pl.ds(pl.multiple_of(j * tile, tile), tile)
        h = hid_low[...]
        gate = dot(h, w_g[0, :, :, cols].reshape(width, tile))
        up = dot(h, w_g[1, :, :, cols].reshape(width, tile))
        cdf = 0.5 + 0.5 * lax.erf(gate * 0.7071067811865476)
        mixed = gate * cdf
        density = 0.3989422804014327 * jnp.exp(-0.5 * gate * gate)
        slope_up[:, cols] = mixed.astype(low)
        slope_gate[:, cols] = (up * (cdf + gate * density)).astype(low)
        act[:, cols] = (mixed * up).astype(low)

    mats[1].from_sib()

    @pl.loop(0, half_g // tile)
    def _(j):
        glu(j)

    steps(9)
    mats[2].from_sib()
    save(w_g, g_full)

    @pl.loop(half_g // tile, ff // tile)
    def _(j):
        glu(j)

    save(slope_gate, gate_out)
    save(slope_up, up_out)
    save(act, act_out)
    steps(10)
    mats[3].from_sib()
    save(w_d, d_full)
    d_hid[...] = jnp.zeros_like(d_hid)
    chips = 4
    deep = 2 * chips * w_d.shape[2]

    @pl.loop(0, 16 // chips)
    def _(j):
        cols = pl.ds(pl.multiple_of(j * deep, deep), deep)
        d_hid[...] += dot(act[:, cols], w_d[pl.ds(j * chips, chips)].reshape(deep, width))

    branch = d_hid[...]
    small[7:8, :] = column_sum(mask * branch * branch)
    norm, inverse = normalized(hid[...] + branch)
    gain = vectors[2:3, :]
    output[...] = (norm * gain + vectors[3:4, :]).astype(low)
    save(output, output_out)
    loads[1].wait()
    grad = grad_v[...].astype(wide)
    small[2:3, :] = column_sum(grad * norm)
    small[3:4, :] = column_sum(grad)
    back = norm_back(grad, gain, norm, inverse)
    d_hid[...] = back
    d_branch[...] = back.astype(low)
    save(d_hid, d_hid_out)
    save(d_branch, d_branch_out)
    for i, (src, dst) in enumerate(saved):
        pltpu.make_async_copy(src, dst, out_sem.at[i]).wait()
    swaps.drain(place.sib)
    copies.drain(place.sib)


def fore(heads, tokens, a_shard, g_shard, d_shard, valid, span, out_grad):
    low, wide = jnp.bfloat16, jnp.float32
    rows, width = tokens.shape
    half_a, ff = a_shard.shape[-1], g_shard.shape[-1]
    keys = span.shape[0]
    vmem, hbm = pl.BlockSpec(memory_space=pltpu.VMEM), pl.BlockSpec(memory_space=pl.ANY)
    dma = lambda *shape: pltpu.SemaphoreType.DMA(shape)
    shape = jax.ShapeDtypeStruct
    w_a, w_g, w_d = (2, 16, rows_chip, half_a), (2, 16, rows_chip, ff), (16, 2) + d_shard.shape
    stored = [
        (w_a, low), (w_g, low), (w_d, low), ((rows, width), low), ((keys, width), low), ((keys, width), low),
        ((rows, width), low), ((width, rows), low), ((rows, width), wide), ((rows, lane_width), wide),
        ((rows, ff), low), ((rows, ff), low), ((rows, ff), low), ((rows, width), low), ((rows, width), wide),
        ((rows, width), low),
    ]
    block = lambda *dims: pltpu.VMEM(dims, low)
    block_wide = lambda *dims: pltpu.VMEM(dims, wide)
    return pl.pallas_call(
        lambda *refs: fore_kernel(heads, *refs),
        out_shape=tuple(shape(dims, kind) for dims, kind in stored)
        + (shape((16, rows), wide), shape((8, width), wide), shape((16, width), wide)),
        in_specs=[vmem] * 5 + [hbm] * 2,
        out_specs=(hbm,) * len(stored) + (vmem,) * 3,
        scratch_shapes=[
            block(*w_a), block(*w_g), block(*w_d), block(*a_shard.shape[1:]), block(*g_shard.shape[1:]),
            block(rows, width), block(keys, width), block(keys, width), block(rows, width),
            block_wide(keys, rows), block(rows, width), block_wide(rows, width), block(rows, width),
            block(width, rows), block_wide(rows, width), block_wide(rows, lane_width),
            block(rows, ff), block(rows, ff), block(rows, ff), block(rows, width), block_wide(rows, width),
            block(rows, width), dma(2, 4), dma(4 * gather_slots), dma(4 * gather_slots), dma(2), dma(len(stored)),
        ],
        compiler_params=pltpu.CompilerParams(
            collective_id=0, has_side_effects=True, vmem_limit_bytes=62 * 2**20
        ),
        name="gather_and_forward",
    )(tokens, a_shard, g_shard, d_shard, valid, span, out_grad)


def back_kernel(
    heads, tokens, q, k, v, span, att, hid_t, norm, inv, gate, up, act, d_hid, d_branch, a_full, g_full, d_full,
    lse, vectors, small, d_tokens, qkv_out, wout_out, gu_out, down_out, small_out, *scratch,
):
    place = Place()
    place.greet()
    c = place.c
    first = c == 0
    low, wide = jnp.bfloat16, jnp.float32
    tok_rows, width = tokens.shape
    ff = gate.shape[1]
    pairs = heads // 2
    bufs, rest = scratch[:27], scratch[27:]
    a_grad, dkv_in, resid, d_att, g_sum, a_sum, g_fin, a_fin, small_buf, send, recv, pair_sem, fin_sem, in_sem, tile_sem = rest
    copies = Copies(send, recv)
    gives = Copies(send, recv)
    last = Copies(fin_sem.at[0], fin_sem.at[1])
    half_g = ff // 2

    def scatter(i, own, *more):
        give = lambda four: None
        return Scatter(place, copies, gives, i * scatter_slots, give, lambda at: own.at[at], *more)

    down, left, right = (scatter(i, *bufs[7 * i : 7 * i + 7]) for i in range(3))
    proj = Scatter(
        place, copies, copies, 3 * scatter_slots, lambda four: a_grad.at[1 - c, four],
        lambda at: a_grad.at[c, at], *bufs[21:],
    )
    chunks = Steps([(m, planes) for m in (down, left, right, proj) for planes in far_near], scatter_stages)
    planes = (3, 2, 1, 0)
    hops = ((place.sib, 0), (place.xn, 1), (place.yn, 2))

    def exchange(i):
        peer, slot = hops[i]
        last.put(small_buf.at[i], small_buf.at[4 + i], slot, peer, lambda: small_buf.at[4 + i])

    def combine(i):
        peer, slot = hops[i]
        last.got(small_buf.at[4 + i], slot, peer)
        small_buf[i + 1] = small_buf[i] + small_buf[4 + i]

    def spread():
        for z in (1, 2, 3):
            last.put(small_buf.at[3], small_buf.at[6 + z], 2 + z, place.zn[z], lambda z=z: small_buf.at[6 + z])

    tile = 256

    def feed_forward(give_d, give_g, act_v, db, ht, w_gu, w_dn, gate_v, up_v, att_v, norm_v, inv_v, w_out):
        down.give = lambda four: give_d.at[four]
        left.give = right.give = lambda four: give_g.at[four]
        load = lambda i, src, dst: pltpu.make_async_copy(src, dst, in_sem.at[i])
        loads = [
            load(0, d_branch, db), load(1, hid_t, ht), load(2, d_hid, resid), load(3, att, att_v),
            load(4, norm, norm_v), load(5, inv, inv_v), load(6, a_full.at[1, :, :, width : 2 * width], w_out),
        ]

        def act_load(i, z):
            cols = pl.ds(pl.multiple_of(place.plane(z) * width, width), width)
            return load(7 + i % 2, act.at[:, cols], act_v.at[i % 2])

        def fetch(j):
            slot = j % 2
            cols = pl.ds(pl.multiple_of(j * tile, tile), tile)
            return [
                pltpu.make_async_copy(g_full.at[:, :, :, cols], w_gu.at[slot], tile_sem.at[0, slot]),
                pltpu.make_async_copy(d_full.at[cols], w_dn.at[slot], tile_sem.at[1, slot]),
                pltpu.make_async_copy(gate.at[:, cols], gate_v.at[slot], tile_sem.at[2, slot]),
                pltpu.make_async_copy(up.at[:, cols], up_v.at[slot], tile_sem.at[3, slot]),
            ]

        loads[0].start()
        act_load(0, planes[0]).start()
        act_load(1, planes[1]).start()
        for copy in loads[1:] + fetch(0):
            copy.start()
        loads[0].wait()
        own_d = bufs[0]
        for i, z in enumerate(planes):
            act_load(i, z).wait()
            term = dot(act_v[i % 2].T, db[...]).astype(low).reshape(4, 2, d_shard_rows(width, ff), width)
            if i < 2:
                act_load(i + 2, planes[i + 2]).start()
            four = pl.ds(place.plane(z) * 4, 4)
            own_d[four] = jnp.where(first, term[:, 0], term[:, 1])
            give_d[four] = jnp.where(first, term[:, 1], term[:, 0])
            down.begin(z)
        chunks(0)
        for copy in loads[1:3]:
            copy.wait()

        def tiles(begin, own_g):
            @pl.loop(begin, begin + half_g // tile)
            def _(j):
                slot = j % 2
                for copy in fetch(j):
                    copy.wait()

                @pl.when(j + 1 < ff // tile)
                def _():
                    for copy in fetch(j + 1):
                        copy.start()

                d_act = dot(db[...], w_dn[slot], ((1,), (1,)))
                d_gate = (d_act * gate_v[slot].astype(wide)).astype(low)
                d_up = (d_act * up_v[slot].astype(wide)).astype(low)
                resid[...] += dot(d_gate, w_gu[slot, 0].reshape(width, tile), ((1,), (1,))) + dot(
                    d_up, w_gu[slot, 1].reshape(width, tile), ((1,), (1,))
                )
                cols = pl.ds(pl.multiple_of((j - begin) * tile, tile), tile)
                mine = dot(ht[...], jnp.where(first, d_gate, d_up)).astype(low)
                own_g[:, :, cols] = mine.reshape(16, rows_chip, tile)
                other = dot(ht[...], jnp.where(first, d_up, d_gate)).astype(low)
                give_g[:, :, cols] = other.reshape(16, rows_chip, tile)

        tiles(0, bufs[7])
        for z in planes:
            left.begin(z)
        chunks(1)
        gives.drain(place.sib)
        tiles(half_g // tile, bufs[14])
        for z in planes:
            right.begin(z)
        chunks(2)
        for copy in loads[3:]:
            copy.wait()
        grad = resid[...]
        unit = norm_v[...]
        small_buf[0] = small[...]
        small_buf[0, 0:1, :] = column_sum(grad * unit)
        small_buf[0, 1:2, :] = column_sum(grad)
        exchange(0)
        back = norm_back(grad, vectors[0:1, :], unit, inv_v[:, 0:1])
        resid[...] = back
        d_one = back.astype(low)
        d_att[...] = dot(d_one, w_out[...].reshape(width, width), ((1,), (1,))).astype(low)
        a_grad[1, :, :, width:] = dot(att_v[...].T, d_one).astype(low).reshape(16, rows_chip, width)
        gives.drain(place.sib)

    block = lambda *dims: pltpu.VMEM(dims, low)
    block_wide = lambda *dims: pltpu.VMEM(dims, wide)
    pl.run_scoped(
        feed_forward, block(*bufs[0].shape), block(*bufs[7].shape), block(2, tok_rows, width),
        block(tok_rows, width), block(width, tok_rows), block(2, 2, 16, rows_chip, tile), block(2, tile, width),
        block(2, tok_rows, tile), block(2, tok_rows, tile), block(tok_rows, width), block_wide(tok_rows, width),
        block_wide(tok_rows, lane_width), block(16, rows_chip, width),
    )

    half = lambda side: pl.ds(pl.multiple_of(side * tok_rows, tok_rows), tok_rows)

    def attention_part(dq, dkv_own, dkv_out):
        def send_dkv(pair):
            return pltpu.make_async_remote_copy(
                src_ref=dkv_out.at[pair], dst_ref=dkv_in.at[pair], send_sem=pair_sem.at[0, pair],
                recv_sem=pair_sem.at[1, pair], device_id=place.sib, device_id_type=MESH,
            )

        def attention(q_v, k_v, v_v, span_v, att_v, dk_sum, dv_sum):
            loads = [
                pltpu.make_async_copy(src, dst, in_sem.at[i])
                for i, (src, dst) in enumerate(((q, q_v), (k, k_v), (v, v_v), (span, span_v), (att, att_v)))
            ]
            for copy in loads:
                copy.start()
            for copy in loads:
                copy.wait()

            @pl.loop(0, pairs)
            def _(pair):
                attend_back_pair(pair, heads, q_v, k_v, v_v, span_v, lse, att_v, d_att, dq, dk_sum, dv_sum)
                for i, part in enumerate((dk_sum, dv_sum)):
                    dkv_own[pair, i] = part[half(c), :]
                    dkv_out[pair, i] = part[half(1 - c), :].astype(low)
                send_dkv(pair).start()
                for i in range(3):

                    @pl.when(pair == 2 * i)
                    def _(i=i):
                        chunks(3 + i)
                        combine(i)
                        if i < 2:
                            exchange(i + 1)
                        else:
                            spread()

        key_rows = k.shape[0]
        pl.run_scoped(
            attention, block(*q.shape), block(*k.shape), block(*v.shape), block_wide(*span.shape), block(*att.shape),
            block_wide(key_rows, lane_width), block_wide(key_rows, lane_width),
        )

        def finish(w_left, w_right, x, d_k, d_v):
            loads = [
                pltpu.make_async_copy(src, dst, in_sem.at[i])
                for i, (src, dst) in enumerate(
                    (
                        (tokens, x),
                        (a_full.at[0, :, :, : 2 * width], w_left),
                        (a_full.at[1, :, :, :width], w_right),
                    )
                )
            ]
            for copy in loads:
                copy.start()
            for pair in range(pairs):
                send_dkv(pair).wait_recv()
                at = slice(pair * lane_width, (pair + 1) * lane_width)
                d_k[:, at] = (dkv_own[pair, 0] + dkv_in[pair, 0].astype(wide)).astype(low)
                d_v[:, at] = (dkv_own[pair, 1] + dkv_in[pair, 1].astype(wide)).astype(low)
            loads[0].wait()
            x_t = x[...].T
            size = width // 2
            for side, at, src in ((0, 0, dq), (0, width, d_k), (1, 0, d_v)):
                for part in range(2):
                    term = dot(x_t, src[:, part * size : (part + 1) * size]).astype(low)
                    here = at + part * size
                    a_grad[side, :, :, here : here + size] = term.reshape(16, rows_chip, size)
            for z in planes:
                proj.begin(z)
            for copy in loads[1:]:
                copy.wait()
            w_q = w_left[:, :, :width].reshape(width, width)
            total = resid[...] + dot(dq[...], w_q, ((1,), (1,)))
            chunks(6)
            w_k = w_left[:, :, width:].reshape(width, width)
            total += dot(d_k[...], w_k, ((1,), (1,)))
            total += dot(d_v[...], w_right[...].reshape(width, width), ((1,), (1,)))
            d_tokens[...] = total.astype(low)

        pl.run_scoped(
            finish, block(16, rows_chip, 2 * width), block(16, rows_chip, width), block(tok_rows, width),
            block(tok_rows, width), block(tok_rows, width),
        )

        @pl.loop(0, pairs)
        def _(pair):
            send_dkv(pair).wait_send()

    pl.run_scoped(
        attention_part, block(tok_rows, width), block_wide(pairs, 2, tok_rows, lane_width),
        block(pairs, 2, tok_rows, lane_width),
    )
    for z in (1, 2, 3):
        last.got(small_buf.at[6 + z], 2 + z, place.zn[z])
    small_out[...] = (small_buf[3] + small_buf[7]) + (small_buf[8] + small_buf[9])
    mine, theirs = pl.ds(pl.multiple_of(24 * c, 8), 24), pl.ds(pl.multiple_of(24 - 24 * c, 8), 24)
    down_out[...] = down.total()
    chunks(7)
    g_sum[0] = left.total()
    last.put(g_sum.at[0, theirs], g_fin.at[0], 6, place.sib, lambda: g_fin.at[0])
    chunks(8)
    chunks(9)
    g_sum[1] = right.total()
    last.put(g_sum.at[1, theirs], g_fin.at[1], 8, place.sib, lambda: g_fin.at[1])
    chunks(10)
    for i, slot in ((0, 6), (1, 8)):
        last.got(g_fin.at[i], slot, place.sib)
        own, other = g_sum[i, mine], g_fin[i]
        gu_out[:, i * half_g : (i + 1) * half_g] = jnp.where(first, own, other)
        gu_out[:, (i + 2) * half_g : (i + 3) * half_g] = jnp.where(first, other, own)
    a_sum[...] = proj.total()
    last.put(a_sum.at[theirs], a_fin, 7, place.sib, lambda: a_fin)
    last.got(a_fin, 7, place.sib)
    qkv_out[:, : 2 * width] = jnp.where(first, a_sum[mine], a_fin[...])
    side = jnp.where(first, a_fin[...], a_sum[mine])
    qkv_out[:, 2 * width :] = side[:, :width]
    wout_out[...] = side[:, width:]
    copies.drain(place.sib)
    last.drain(place.sib)


def d_shard_rows(width, ff):
    return ff // 32


def back(heads, tokens, q, k, v, span, att, hid_t, norm, inv, gate, up, act, d_hid, d_branch, a_full, g_full, d_full, lse, vectors, small):
    low, wide = jnp.bfloat16, jnp.float32
    tok_rows, width = tokens.shape
    ff = gate.shape[1]
    half_g, half_a = ff // 2, 2 * width
    pairs = heads // 2
    d_rows = d_shard_rows(width, ff)
    bufs = []
    for i, (rows, half) in enumerate(((d_rows, width), (rows_chip, half_g), (rows_chip, half_g), (rows_chip, half_a))):
        bufs += [pltpu.VMEM((count, rows, half), low) for count in (16, 16, 2, 2, 4, 4, 3)[i == 3 :]]
    vmem, hbm = pl.BlockSpec(memory_space=pltpu.VMEM), pl.BlockSpec(memory_space=pl.ANY)
    dma = lambda *shape: pltpu.SemaphoreType.DMA(shape)
    shape = jax.ShapeDtypeStruct
    return pl.pallas_call(
        lambda *refs: back_kernel(heads, *refs),
        out_shape=(
            shape((tok_rows, width), low), shape((24, 3 * width), wide), shape((24, width), wide),
            shape((24, 2 * ff), wide), shape((d_rows, width), wide), shape(small.shape, wide),
        ),
        in_specs=[hbm] * 17 + [vmem] * 3,
        out_specs=(vmem,) * 6,
        scratch_shapes=bufs
        + [
            pltpu.VMEM((2, 16, rows_chip, half_a), low),
            pltpu.VMEM((pairs, 2, tok_rows, lane_width), low),
            pltpu.VMEM((tok_rows, width), wide),
            pltpu.VMEM((tok_rows, width), low),
            pltpu.VMEM((2, rows_chip, half_g), wide),
            pltpu.VMEM((rows_chip, half_a), wide),
            pltpu.VMEM((2, 24, half_g), wide),
            pltpu.VMEM((24, half_a), wide),
            pltpu.VMEM((10,) + small.shape, wide),
            dma(4 * scatter_slots),
            dma(4 * scatter_slots),
            dma(2, pairs),
            dma(2, 9),
            dma(9),
            dma(4, 2),
        ],
        compiler_params=pltpu.CompilerParams(
            collective_id=1, has_side_effects=True, vmem_limit_bytes=63 * 2**20
        ),
        name="backward_and_sums",
    )(tokens, q, k, v, span, att, hid_t, norm, inv, gate, up, act, d_hid, d_branch, a_full, g_full, d_full, lse, vectors, small)


def window(cells, width):
    count = lax.axis_size("blk")
    before = lax.ppermute(cells, "blk", [(i, i + 1) for i in range(count - 1)])
    after = lax.ppermute(cells, "blk", [(i + 1, i) for i in range(count - 1)])
    return jnp.concatenate([before, cells, after], 0)


def window_back(terms, width):
    count = lax.axis_size("blk")
    low = jnp.bfloat16
    before = lax.ppermute(terms[2 * width :].astype(low), "blk", [(i, i + 1) for i in range(count - 1)])
    after = lax.ppermute(terms[:width].astype(low), "blk", [(i + 1, i) for i in range(count - 1)])
    return terms[width : 2 * width] + before.astype(terms.dtype) + after.astype(terms.dtype)


def key_spans(labels, first, tok_rows):
    seq_len = labels.shape[0]
    query_pos = first + jnp.arange(tok_rows, dtype=jnp.int32)
    query_labels = lax.dynamic_slice_in_dim(labels, first, tok_rows, 0)
    if seq_len == 2 * tok_rows:
        key_pos, key_labels = jnp.arange(seq_len, dtype=jnp.int32), labels
    else:
        key_pos = first - tok_rows + jnp.arange(3 * tok_rows, dtype=jnp.int32)
        padded = jnp.pad(labels, (tok_rows, tok_rows), constant_values=seq_len)
        key_labels = lax.dynamic_slice_in_dim(padded, first, 3 * tok_rows, 0)
    same = (key_labels[:, None] == query_labels[None, :]) & (key_labels[:, None] != seq_len)
    gap = jnp.abs(key_pos[:, None] - query_pos[None, :])
    return jnp.where(same | (gap == 0), gap.astype(jnp.float32), far)


def on_chip_grid():
    return lax.axis_size("rows") == 16 and lax.axis_size("blk") == 2


def packed_shards(w_qkv, w_out, ln1_gain, ln1_bias, w_gate_up, ln2_gain, ln2_bias):
    width = w_out.shape[1]
    ff = w_gate_up.shape[1] // 2
    table = jnp.stack((ln1_gain, ln1_bias, ln2_gain, ln2_bias), 1)
    table = jnp.pad(table, ((0, 0), (0, lane_width - 4)))
    left = jnp.concatenate([w_qkv[:, : 2 * width], table], 1)
    right = jnp.concatenate([w_qkv[:, 2 * width :], w_out, jnp.zeros_like(table)], 1)
    return jnp.stack([left, right]), jnp.stack([w_gate_up[:, :ff], w_gate_up[:, ff:]])


def on_grid(tokens, a_shard, g_shard, w_down, span, valid, out_grad):
    spare = ((0, 0), (0, 32 - a_shard.shape[1]), (0, 0))
    (
        a_full, g_full, d_full, q, k, v, att, hid_t, norm, inv, gate, up, act, output, d_hid, d_branch, lse, vectors, small,
    ) = fore(HEADS, tokens, jnp.pad(a_shard, spare), jnp.pad(g_shard, spare), w_down, valid, span, out_grad)
    d_full = d_full.reshape(-1, tokens.shape[1])
    return output, *back(
        HEADS, tokens, q, k, v, span, att, hid_t, norm, inv, gate, up, act, d_hid, d_branch, a_full, g_full, d_full, lse,
        vectors, small,
    )


def on_any(tokens, a_shard, g_shard, w_down, span, valid, out_grad):
    both = ("rows", "blk")
    tok_rows, width = tokens.shape
    low, wide = jnp.bfloat16, jnp.float32
    a_full = lax.all_gather(a_shard, both, axis=1, tiled=True)
    w_gu = lax.all_gather(g_shard, both, axis=1, tiled=True)
    w_dn = lax.all_gather(w_down, both, axis=0, tiled=True)
    vectors = jnp.pad(a_full[0, :, 2 * width : 2 * width + 4].astype(wide).T, ((0, 4), (0, 0)))
    w_qk, w_v = a_full[0, :, : 2 * width], a_full[1, :, :width]
    qk = jnp.dot(tokens, w_qk, preferred_element_type=wide).astype(low)
    v = jnp.dot(tokens, w_v, preferred_element_type=wide).astype(low)
    query = qk[:, :width] * (width // HEADS) ** -0.5
    kv = window(jnp.concatenate([qk[:, width:], v], 1), tok_rows)
    keys, values = kv[:, :width], kv[:, width:]
    attended, lse = attend(query, keys, values, span, HEADS)
    output, d_resid_one, d_att, grad_out, g_grad, d_grad, small = ffn(
        tokens, attended, a_full, vectors, valid, out_grad, w_gu, w_dn
    )
    dq, dk, dv = attend_back(query, keys, values, span, lse, attended, d_att, HEADS)
    dkv = window_back(jnp.concatenate([dk, dv], 1), tok_rows)
    d_qk = jnp.concatenate([dq, dkv[:, :width].astype(low)], 1)
    d_v = dkv[:, width:].astype(low)
    grad_qkv = transposed_times(tokens, jnp.concatenate([d_qk, d_v], 1))
    d_tokens = d_resid_one + times_transposed(d_qk, w_qk) + times_transposed(d_v, w_v)
    share = lambda g, axis: lax.psum_scatter(g.astype(wide), both, scatter_dimension=axis, tiled=True)
    gate, up = share(g_grad, 1)
    return (
        output, d_tokens.astype(low), share(grad_qkv, 0), share(grad_out, 0), jnp.concatenate([gate, up], 1),
        share(d_grad, 0), lax.psum(small, both),
    )


def body(
    tokens, segments, w_qkv, w_out, ln1_gain, ln1_bias, w_gate_up, w_down, ln2_gain, ln2_bias, out_grad,
):
    inputs, labels = tokens[0], segments[0]
    tok_rows, width = inputs.shape
    both = ("rows", "blk")
    first = lax.axis_index("blk") * tok_rows
    span = key_spans(labels, first, tok_rows)
    here = lax.dynamic_slice_in_dim(labels, first, tok_rows, 0)
    valid = (here != labels.shape[0]).astype(jnp.float32)[:, None]
    a_shard, g_shard = packed_shards(w_qkv, w_out, ln1_gain, ln1_bias, w_gate_up, ln2_gain, ln2_bias)
    run = on_grid if on_chip_grid() else on_any
    output, d_tokens, *parts, small = run(inputs, a_shard, g_shard, w_down, span, valid, out_grad[0])
    share = width // lax.axis_size(both)
    mine = lax.axis_index(both) * share
    rows = lax.dynamic_slice_in_dim(small[:4], mine, share, 1)
    stats = jnp.sqrt(jnp.sum(small[4:8], 1) / (small[8, 0] * width))
    return (
        output[None], d_tokens[None], parts[0], parts[1], rows[0], rows[1],
        parts[2], parts[3], rows[2], rows[3], stats,
    )


def solution(mesh):
    placed = (
        P("rows", "blk", None),
        P("rows", None),
        P(("rows", "blk"), None),
        P(("rows", "blk"), None),
        P(("rows", "blk")),
        P(("rows", "blk")),
        P(("rows", "blk"), None),
        P(("rows", "blk"), None),
        P(("rows", "blk")),
        P(("rows", "blk")),
        P("rows", "blk", None),
    )
    return jax.shard_map(
        body,
        mesh=mesh,
        in_specs=placed,
        out_specs=(
            P("rows", "blk", None),
            P("rows", "blk", None),
            P(("rows", "blk"), None),
            P(("rows", "blk"), None),
            P(("rows", "blk")),
            P(("rows", "blk")),
            P(("rows", "blk"), None),
            P(("rows", "blk"), None),
            P(("rows", "blk")),
            P(("rows", "blk")),
            P(),
        ),
        check_vma=False,
    )
```

```python
import jax
import jax.numpy as jnp
from jax import lax
from jax.experimental import pallas as pl
from jax.experimental.pallas import tpu as pltpu
from jax.sharding import PartitionSpec as P

HEADS = 12


ln_eps = 1e-12
far = 1e33
lane_width = 128


def times_transposed(left, right):
    return lax.dot_general(
        left, right, (((1,), (1,)), ((), ())), preferred_element_type=jnp.float32
    )


def transposed_times(left, right):
    return lax.dot_general(
        left, right, (((0,), (0,)), ((), ())), preferred_element_type=jnp.float32
    )


MESH = pl.DeviceIdType.MESH


class Place:
    def __init__(self):
        r, self.c = lax.axis_index("rows"), lax.axis_index("blk")
        self.x, self.y, self.z = r % 2, (r // 2) % 2, r // 4
        self.sib = (r, 1 - self.c)
        self.xn = (self.at(0, "x"), self.c)
        self.yn = (self.at(0, "y"), self.c)
        self.zn = {k: (self.at(k, "o"), self.c) for k in (1, 2, 3)}

    def plane(self, k):
        z, low = self.z % 2, self.z // 2
        if k % 2:
            z = 1 - z
        if k // 2:
            low = 1 - low
        return low * 2 + z

    def at(self, k, j):
        x = 1 - self.x if j in "xd" else self.x
        y = 1 - self.y if j in "yd" else self.y
        return self.plane(k) * 4 + y * 2 + x

    def greet(self):
        self.barrier = pltpu.get_barrier_semaphore()
        for peer in (self.sib, self.xn, self.yn, *self.zn.values()):
            pl.semaphore_signal(self.barrier, inc=1, device_id=peer, device_id_type=MESH)

    def meet(self):
        pl.semaphore_wait(self.barrier, 6)


class Copies:
    def __init__(self, send, recv):
        self.send, self.recv, self.open = send, recv, []

    def of(self, src, dst, slot, peer):
        return pltpu.make_async_remote_copy(
            src_ref=src, dst_ref=dst, send_sem=self.send.at[slot], recv_sem=self.recv.at[slot],
            device_id=peer, device_id_type=MESH,
        )

    def put(self, src, dst, slot, peer, like=None):
        self.of(src, dst, slot, peer).start()
        self.open.append((like or (lambda: dst), slot))

    def got(self, dst, slot, peer):
        self.of(dst, dst, slot, peer).wait_recv()

    def drain(self, peer):
        for like, slot in self.open:
            self.of(like(), like(), slot, peer).wait_send()
        self.open = []


class Gather:
    def __init__(self, place, copies, base, out):
        self.p, self.cp, self.base, self.out = place, copies, base, out

    def slot(self, kind, k, j="o"):
        start = {"z": -1, "x": 3, "y": 7, "d": 11, "s": 15}[kind]
        return self.base + start + (4 * k + "oxyd".index(j) if kind == "s" else k)

    def block(self, k, j):
        return self.out(self.p.c, self.p.at(k, j))

    def send(self, src, dst, slot, peer):
        self.cp.put(src, dst, slot, peer, lambda: self.out(0, 0))

    def push(self, src, k, j):
        self.send(src, self.block(k, j), self.slot("s", k, j), self.p.sib)

    def to_z(self):
        for k in (1, 2):
            self.send(self.block(0, "o"), self.block(0, "o"), self.slot("z", k), self.p.zn[k])

    def to_xy(self):
        self.spread(self.block(0, "o"), 0)

    def spread(self, src, k):
        dst = self.block(k, "o")
        self.send(src, dst, self.slot("x", k), self.p.xn)
        self.send(src, dst, self.slot("y", k), self.p.yn)
        self.push(src, k, "o")

    def from_z(self, k):
        block = self.block(k, "o")
        self.cp.got(block, self.slot("z", k), self.p.zn[k])
        if k == 2:
            self.send(block, block, self.slot("z", 3), self.p.zn[1])
        self.spread(block, k)

    @staticmethod
    def schedule(mats):
        work = [(mats[0].to_z,)] + [(m.to_xy,) for m in mats[:3]]
        for i, m in enumerate(mats):
            before = mats[i - 1] if i else None
            work.append((m.from_z, 1))
            if i + 1 < len(mats):
                work.append((mats[i + 1].to_z,))
            if before:
                work.append((before.from_xy, 3))
            work += [(m.from_xy, 0), (m.from_z, 2)]
            if before:
                work.append((before.from_d, 2))
            if i + 3 < len(mats):
                work.append((mats[i + 3].to_xy,))
            work += [(m.from_xy, 1), (m.from_z, 3)]
            if before:
                work.append((before.from_d, 1))
            work.append((m.from_d, 0))
            if before:
                work.append((before.from_d, 3))
            work.append((m.from_xy, 2))
        last = mats[-1]
        return work + [(last.from_xy, 3), (last.from_d, 2), (last.from_d, 1), (last.from_d, 3)]

    def from_xy(self, k):
        x, y = self.block(k, "x"), self.block(k, "y")
        self.cp.got(x, self.slot("x", k), self.p.xn)
        if k == 2:
            self.send(x, x, self.slot("d", k), self.p.yn)
        self.cp.got(y, self.slot("y", k), self.p.yn)
        if k == 0:
            self.send(y, y, self.slot("d", k), self.p.xn)
        self.push(x, k, "x")
        self.push(y, k, "y")

    def from_d(self, k):
        block = self.block(k, "d")
        self.cp.got(block, self.slot("d", k), self.p.xn)
        if k % 2 == 0:
            self.send(block, block, self.slot("d", k + 1), self.p.zn[1])
        self.push(block, k, "d")

    def from_sib(self):
        for k in range(4):
            for j in "oxyd":
                block = self.out(1 - self.p.c, self.p.at(k, j))
                self.cp.got(block, self.slot("s", k, j), self.p.sib)


class Scatter:
    def __init__(self, place, copies, gives, base, give, own, sib, rly, dia, xin, yin, zin):
        self.p, self.cp, self.gives, self.base, self.give, self.own = place, copies, gives, base, give, own
        self.sib, self.rly, self.dia, self.xin, self.yin, self.zin = sib, rly, dia, xin, yin, zin

    def slot(self, kind, k):
        return self.base + {"s": 0, "r": 4, "d": 5, "x": 8, "y": 12, "z": 15}[kind] + k

    def four(self, k):
        return pl.ds(self.p.plane(k) * 4, 4)

    def begin(self, k):
        four = self.four(k)
        self.gives.put(self.give(four), self.sib.at[four], self.slot("s", k), self.p.sib, lambda: self.sib.at[pl.ds(0, 4)])

    def to_x(self, own, k):
        self.cp.put(own, self.xin.at[k], self.slot("x", k), self.p.xn, lambda: self.xin.at[k])

    def to_y(self, own, k):
        self.cp.put(own, self.yin.at[k], self.slot("y", k), self.p.yn, lambda: self.yin.at[k])

    def both(self, k, j, *more):
        at = self.p.at(k, j)
        own = self.own(at)
        total = own[...] + self.sib[at]
        for ref in more:
            total = total + ref[...]
        own[...] = total
        return own

    def pair(self, k):
        four = self.four(k)
        self.cp.got(self.sib.at[four], self.slot("s", k), self.p.sib)
        if k % 2:
            i = k // 2
            dia = lambda: self.dia.at[i]
            self.cp.put(self.both(k, "d"), dia(), self.slot("d", 2 * i), self.p.zn[1], dia)
        if k != 2:
            self.to_x(self.both(k, "x"), k)
        if k != 0:
            self.to_y(self.both(k, "y"), k)

    def diag(self, k):
        if k % 2:
            return
        i = k // 2
        self.cp.got(self.dia.at[i], self.slot("d", k), self.p.zn[1])
        own = self.both(k, "d", self.dia.at[i])
        peer = self.p.xn if k == 0 else self.p.yn
        self.cp.put(own, self.rly.at[i], self.slot("r", k), peer, lambda: self.rly.at[i])

    def relay(self, k):
        if k % 2:
            return
        i = k // 2
        self.cp.got(self.rly.at[i], self.slot("r", k), self.p.xn)
        if k == 0:
            self.to_y(self.both(k, "y", self.rly.at[i]), k)
        else:
            self.to_x(self.both(k, "x", self.rly.at[i]), k)

    def plane(self, k):
        p = self.p
        at = p.at(k, "o")
        self.cp.got(self.xin.at[k], self.slot("x", k), p.xn)
        self.cp.got(self.yin.at[k], self.slot("y", k), p.yn)
        wide = jnp.float32
        own = self.own(at)
        total = (own[...].astype(wide) + self.sib[at].astype(wide)) + (
            self.xin[k].astype(wide) + self.yin[k].astype(wide)
        )
        own[...] = total.astype(jnp.bfloat16)
        if k % 2:
            self.to_z(own, k, 1)

    def to_z(self, own, k, step):
        self.cp.put(own, self.zin.at[k - 1], self.slot("z", k), self.p.zn[step], lambda: self.zin.at[k - 1])

    def cross(self):
        self.cp.got(self.zin.at[2], self.slot("z", 3), self.p.zn[1])
        own = self.own(self.p.at(2, "o"))
        own[...] = own[...] + self.zin[2]
        self.to_z(own, 2, 2)

    def all(self, name, *planes):
        for k in planes:
            getattr(self, name)(k)

    def first(self):
        self.all("pair", 3, 1)

    def rest(self):
        self.all("pair", 2, 0)

    def diags(self):
        self.all("diag", 2, 0)

    def relays(self):
        self.all("relay", 2, 0)

    def odd(self):
        self.all("plane", 3, 1)

    def even(self):
        self.all("plane", 2, 0)
        self.cross()

    def total(self):
        for k in (1, 2):
            self.cp.got(self.zin.at[k - 1], self.slot("z", k), self.p.zn[k])
        wide = jnp.float32
        own = self.own(self.p.at(0, "o"))
        return own[...].astype(wide) + (self.zin[0].astype(wide) + self.zin[1].astype(wide))


rows_chip = 48
gather_slots, scatter_slots = 31, 19


def dot(left, right, dims=((1,), (0,))):
    return lax.dot_general(left, right, (dims, ((), ())), preferred_element_type=jnp.float32)


def row_mean(values):
    return jnp.mean(values, -1, keepdims=True)


def normalized(resid):
    centred = resid - row_mean(resid)
    inverse = lax.rsqrt(row_mean(centred * centred) + ln_eps)
    return centred * inverse, inverse


def norm_back(grad, gain, norm, inverse):
    e = grad * gain
    return inverse * (e - row_mean(e) - norm * row_mean(e * norm))


def column_sum(values):
    return jnp.sum(values, 0, keepdims=True)


def ffn_kernel(
    tokens, attended, w_out, vectors, valid, out_grad, w_gu, w_down,
    output, d_resid_one, d_att, grad_out, grad_gu, grad_down, small,
    hid, hid_low, hid_t, norm_one, inv_one, slope_gate, slope_up, act, total, d_hid, d_branch,
):
    i = pl.program_id(0)
    tiles = pl.num_programs(0) // 2
    low = jnp.bfloat16
    wide = jnp.float32

    @pl.when(i == 0)
    def _():
        branch = dot(attended[...], w_out[0])
        toks = tokens[...].astype(wide)
        norm, inverse = normalized(toks + branch)
        norm_one[...] = norm
        inv_one[...] = inverse
        hidden = norm * vectors[0:1, :] + vectors[1:2, :]
        hid[...] = hidden
        hid_low[...] = hidden.astype(low)
        hid_t[...] = hidden.T.astype(low)
        mask = valid[...]
        small[4:5, :] = column_sum(mask * toks * toks)
        small[5:6, :] = column_sum(mask * branch * branch)
        small[6:7, :] = column_sum(mask * hidden * hidden)
        small[8:16, :] = jnp.zeros((8, small.shape[1]), wide)
        small[8:9, :] = jnp.broadcast_to(jnp.sum(mask, 0, keepdims=True), (1, small.shape[1]))
        total[...] = jnp.zeros_like(total)

    @pl.when(i < tiles)
    def _():
        h = hid_low[...]
        gate = dot(h, w_gu[0])
        up = dot(h, w_gu[1])
        cdf = 0.5 + 0.5 * lax.erf(gate * 0.7071067811865476)
        glu = gate * cdf
        density = 0.3989422804014327 * jnp.exp(-0.5 * gate * gate)
        slope_up[i] = glu
        slope_gate[i] = up * (cdf + gate * density)
        a = (glu * up).astype(low)
        act[i] = a
        total[...] += dot(a, w_down[...])

    @pl.when(i == tiles - 1)
    def _():
        branch = total[...]
        mask = valid[...]
        small[7:8, :] = column_sum(mask * branch * branch)
        norm, inverse = normalized(hid[...] + branch)
        gain = vectors[2:3, :]
        output[...] = (norm * gain + vectors[3:4, :]).astype(low)
        grad = out_grad[...].astype(wide)
        small[2:3, :] = column_sum(grad * norm)
        small[3:4, :] = column_sum(grad)
        back = norm_back(grad, gain, norm, inverse)
        d_hid[...] = back
        d_branch[...] = back.astype(low)

    @pl.when(i >= tiles)
    def _():
        j = i - tiles
        db = d_branch[...]
        grad_down[...] = dot(act[j].T, db).astype(low)
        d_act = dot(db, w_down[...], ((1,), (1,)))
        d_gate = (d_act * slope_gate[j]).astype(low)
        d_up = (d_act * slope_up[j]).astype(low)
        h_t = hid_t[...]
        grad_gu[0] = dot(h_t, d_gate).astype(low)
        grad_gu[1] = dot(h_t, d_up).astype(low)
        d_hid[...] += dot(d_gate, w_gu[0], ((1,), (1,))) + dot(d_up, w_gu[1], ((1,), (1,)))

    @pl.when(i == 2 * tiles - 1)
    def _():
        grad = d_hid[...]
        norm = norm_one[...]
        small[0:1, :] = column_sum(grad * norm)
        small[1:2, :] = column_sum(grad)
        back = norm_back(grad, vectors[0:1, :], norm, inv_one[...])
        d_resid_one[...] = back
        db = back.astype(low)
        grad_out[...] = dot(attended[...].T, db).astype(low)
        d_att[...] = dot(db, w_out[0], ((1,), (1,))).astype(low)


def ffn(tokens, attended, a_full, vectors, valid, out_grad, w_gu, w_down):
    rows, width = tokens.shape
    ff = w_down.shape[0]
    tile = 512
    tiles = ff // tile
    low, wide = jnp.bfloat16, jnp.float32
    whole = lambda *shape: pl.BlockSpec(shape, lambda i: (0,) * len(shape))
    at = lambda i: jnp.where(i < tiles, i, i - tiles)
    late = lambda i: jnp.maximum(i - tiles, 0)
    return pl.pallas_call(
        ffn_kernel,
        grid=(2 * tiles,),
        out_shape=(
            jax.ShapeDtypeStruct((rows, width), low),
            jax.ShapeDtypeStruct((rows, width), wide),
            jax.ShapeDtypeStruct((rows, width), low),
            jax.ShapeDtypeStruct((width, width), low),
            jax.ShapeDtypeStruct((2, width, ff), low),
            jax.ShapeDtypeStruct((ff, width), low),
            jax.ShapeDtypeStruct((16, width), wide),
        ),
        in_specs=[
            whole(rows, width),
            whole(rows, width),
            pl.BlockSpec((1, width, width), lambda i: (1, 0, 1)),
            whole(8, width),
            whole(rows, 1),
            whole(rows, width),
            pl.BlockSpec((2, width, tile), lambda i: (0, 0, at(i))),
            pl.BlockSpec((tile, width), lambda i: (at(i), 0)),
        ],
        out_specs=(
            whole(rows, width),
            whole(rows, width),
            whole(rows, width),
            whole(width, width),
            pl.BlockSpec((2, width, tile), lambda i: (0, 0, late(i))),
            pl.BlockSpec((tile, width), lambda i: (late(i), 0)),
            whole(16, width),
        ),
        scratch_shapes=[
            pltpu.VMEM((rows, width), wide),
            pltpu.VMEM((rows, width), low),
            pltpu.VMEM((width, rows), low),
            pltpu.VMEM((rows, width), wide),
            pltpu.VMEM((rows, 1), wide),
            pltpu.VMEM((tiles, rows, tile), wide),
            pltpu.VMEM((tiles, rows, tile), wide),
            pltpu.VMEM((tiles, rows, tile), low),
            pltpu.VMEM((rows, width), wide),
            pltpu.VMEM((rows, width), wide),
            pltpu.VMEM((rows, width), low),
        ],
        compiler_params=pltpu.CompilerParams(vmem_limit_bytes=60 * 2**20),
        cost_estimate=pl.CostEstimate(
            flops=2 * rows * width * (9 * ff + 3 * width), bytes_accessed=18 * ff * width, transcendentals=2 * rows * ff
        ),
        name="feed_forward",
    )(tokens, attended, a_full, vectors, valid, out_grad, w_gu, w_down)


def half_of(block, axis, second):
    place = lax.broadcasted_iota(jnp.int32, block.shape, axis)
    depth = block.shape[axis] // 2
    keep = place >= depth if second else place < depth
    return jnp.where(keep, block, jnp.zeros_like(block))


def attend_kernel(heads, q, k, v, span, attended, lse):
    @pl.loop(0, heads // 2)
    def _(pair):
        attend_pair(pair, heads, q, k, v, span, lse, attended)


def attend(q, k, v, span, heads):
    rows, width = q.shape
    keys = k.shape[0]
    low, wide = jnp.bfloat16, jnp.float32
    return pl.pallas_call(
        lambda *refs: attend_kernel(heads, *refs),
        out_shape=(
            jax.ShapeDtypeStruct((rows, width), low),
            jax.ShapeDtypeStruct((16, rows), wide),
        ),
        in_specs=[pl.BlockSpec(memory_space=pltpu.VMEM)] * 4,
        out_specs=(pl.BlockSpec(memory_space=pltpu.VMEM),) * 2,
        compiler_params=pltpu.CompilerParams(vmem_limit_bytes=60 * 2**20),
        cost_estimate=pl.CostEstimate(flops=4 * rows * keys * width, bytes_accessed=8 * keys * width, transcendentals=heads * rows * keys),
        name="attend",
    )(q, k, v, span)


def attend_back_pair(pair, heads, q, k, v, span, lse, att, d_att, dq, dk_sum, dv_sum):
    low, wide = jnp.bfloat16, jnp.float32
    rows, width = q.shape
    lanes = lane_width
    depth = width // heads
    chunk = 256
    scale = depth**-0.5
    at = pl.ds(pl.multiple_of(pair * lanes, lanes), lanes)
    keys, values = k[:, at], v[:, at]
    keys_t = keys.astype(wide).T.astype(low)
    for c in range(rows // chunk):
        here = pl.ds(c * chunk, chunk)
        q_wide = q[here, at].astype(wide)
        do_here = d_att[here, at]
        do_wide = do_here.astype(wide)
        q_here = q_wide.astype(low)
        q_t, do_t = q_wide.T.astype(low), do_wide.T.astype(low)
        both_t = (do_wide * att[here, at].astype(wide)).T
        dk_part, dv_part, dq_parts = None, None, []
        for h in (0, 1):
            head = 2 * pair + h
            own = slice(h * depth, (h + 1) * depth)
            slope = jnp.exp2(jnp.full((1, 1), -8.0 / heads, wide) * (head + 1).astype(wide))
            delta = jnp.sum(both_t[own], 0, keepdims=True)
            logits = dot(keys, half_of(q_t, 0, h)) - slope * span[:, here]
            probs = jnp.exp(logits - lse[pl.ds(head, 1), here])
            d_probs = dot(values, half_of(do_t, 0, h))
            d_logits = (probs * (d_probs - delta)).astype(low)
            dv_term = dot(probs.astype(low), half_of(do_here, 1, h))
            dk_term = dot(d_logits, half_of(q_here, 1, h))
            dv_part = dv_term if dv_part is None else dv_part + dv_term
            dk_part = dk_term if dk_part is None else dk_part + dk_term
            dq_parts.append(dot(keys_t[own], d_logits) * scale)
        if c == 0:
            dk_sum[...] = dk_part
            dv_sum[...] = dv_part
        else:
            dk_sum[...] += dk_part
            dv_sum[...] += dv_part
        dq[here, at] = jnp.concatenate(dq_parts, 0).T.astype(low)


def attend_back_kernel(heads, q, k, v, span, lse, att, d_att, dq, dk, dv, dk_sum, dv_sum):
    @pl.loop(0, heads // 2)
    def _(pair):
        attend_back_pair(pair, heads, q, k, v, span, lse, att, d_att, dq, dk_sum, dv_sum)
        at = pl.ds(pl.multiple_of(pair * lane_width, lane_width), lane_width)
        dk[:, at] = dk_sum[...]
        dv[:, at] = dv_sum[...]


def attend_back(q, k, v, span, lse, att, d_att, heads):
    rows, width = q.shape
    keys = k.shape[0]
    low, wide = jnp.bfloat16, jnp.float32
    return pl.pallas_call(
        lambda *refs: attend_back_kernel(heads, *refs),
        out_shape=(
            jax.ShapeDtypeStruct((rows, width), low),
            jax.ShapeDtypeStruct((keys, width), wide),
            jax.ShapeDtypeStruct((keys, width), wide),
        ),
        in_specs=[pl.BlockSpec(memory_space=pltpu.VMEM)] * 7,
        out_specs=(pl.BlockSpec(memory_space=pltpu.VMEM),) * 3,
        scratch_shapes=[
            pltpu.VMEM((keys, lane_width), wide),
            pltpu.VMEM((keys, lane_width), wide),
        ],
        compiler_params=pltpu.CompilerParams(vmem_limit_bytes=60 * 2**20),
        cost_estimate=pl.CostEstimate(flops=10 * rows * keys * width, bytes_accessed=16 * keys * width, transcendentals=heads * rows * keys),
        name="attend_back",
    )(q, k, v, span, lse, att, d_att)


def attend_pair(pair, heads, q, k, v, span, lse, attended):
    low, wide = jnp.bfloat16, jnp.float32
    rows, width = q.shape
    lanes = lane_width
    depth = width // heads
    chunk = 256
    at = pl.ds(pl.multiple_of(pair * lanes, lanes), lanes)
    keys = k[:, at]
    values_t = v[:, at].astype(wide).T.astype(low)
    for c in range(rows // chunk):
        here = pl.ds(c * chunk, chunk)
        q_t = q[here, at].astype(wide).T.astype(low)
        parts = []
        for h in (0, 1):
            head = 2 * pair + h
            slope = jnp.exp2(jnp.full((1, 1), -8.0 / heads, wide) * (head + 1).astype(wide))
            logits = dot(keys, half_of(q_t, 0, h)) - slope * span[:, here]
            top = jnp.max(logits, 0, keepdims=True)
            weights = jnp.exp(logits - top)
            norm = jnp.sum(weights, 0, keepdims=True)
            lse[pl.ds(head, 1), here] = top + jnp.log(norm)
            parts.append(dot(values_t[h * depth : (h + 1) * depth], weights.astype(low)) / norm)
        attended[here, at] = jnp.concatenate(parts, 0).T.astype(low)


def fore_kernel(
    heads, tokens, labels, w_qkv, w_out, w_gu, d_shard, norms, out_grad,
    a_full, g_full, d_full, q_out, k_out, v_out, att_out, hid_t_out, norm_out, inv_out, gate_out, up_out, act_out,
    output_out, d_hid_out, d_branch_out, span_out, lse, vectors, small,
    w_a, w_g, w_d, a_give, g_give, a_pair, g_pair, turned, q, k, v, att, span_v, grad_v, hid, hid_low, hid_t, norm_one, inv_one,
    slope_gate, slope_up, act, output, d_hid, d_branch, pair_sem, send, recv, in_sem, out_sem,
):
    place = Place()
    place.greet()
    c = place.c
    low, wide = jnp.bfloat16, jnp.float32
    tok_rows, width = tokens.shape
    ff = w_g.shape[3]
    half_g = ff // 2
    pairs = heads // 2
    load = pltpu.make_async_copy(out_grad, grad_v, in_sem.at[0])
    load.start()
    core_one = c == 1
    turned[...] = jnp.zeros_like(turned)
    turned[0:4, 0 : norms.shape[1]] = norms[...].astype(wide)
    table = turned[...].T[: norms.shape[1]].astype(low)
    left = jnp.concatenate([w_qkv[:, : 2 * width], table], 1)
    right = jnp.concatenate([w_qkv[:, 2 * width :], w_out[...], jnp.zeros_like(table)], 1)
    gate, up = w_gu[:, :ff], w_gu[:, ff:]
    rows = w_qkv.shape[0]
    a_give[:rows, :] = jnp.where(core_one, left, right)
    g_give[:rows, :] = jnp.where(core_one, gate, up)
    swaps = Copies(pair_sem.at[0], pair_sem.at[1])
    place.meet()
    for i, (give, other) in enumerate(((a_give, a_pair), (g_give, g_pair))):
        swaps.put(give, other, i, place.sib)
    copies = Copies(send, recv)
    outs = [
        lambda half, r: w_a.at[half, r],
        lambda half, r: w_g.at[half, r, :, :half_g],
        lambda half, r: w_g.at[half, r, :, half_g:],
        lambda half, r: w_d.at[r, half],
    ]
    mats = [Gather(place, copies, i * gather_slots, out) for i, out in enumerate(outs)]
    first, second, third, fourth = mats
    me = place.at(0, "o")

    def assemble(mine, other, full, i):
        swaps.got(other, i, place.sib)
        mine = mine.astype(wide)
        theirs = other[:rows, :].astype(wide)
        top = jnp.where(core_one, theirs, mine)
        rest = jnp.where(core_one, mine, theirs)
        full[c, me] = jnp.concatenate([top, rest], 0).astype(low)

    work = Gather.schedule(mats)

    def go(count):
        for step, *plane in work[:count]:
            step(*plane)
        del work[:count]

    def upto(matrix):
        done = [i for i, (step, *_) in enumerate(work) if step == matrix.from_d]
        go(done[-1] + 1 if done else 0)

    assemble(jnp.where(core_one, right, left), a_pair, w_a, 0)
    go(2)
    assemble(jnp.where(core_one, up, gate), g_pair, w_g, 1)
    w_d[me, c] = d_shard[...]
    seq_len = labels.shape[1]
    label_row = labels[...].astype(wide)
    label_column = jnp.broadcast_to(label_row, (lane_width, seq_len)).T[:, 0:1]
    half = pl.ds(pl.multiple_of(c * tok_rows, tok_rows), tok_rows)
    same = (label_column == labels[:, half].astype(wide)) & (label_column != seq_len)
    key_at = lax.broadcasted_iota(jnp.int32, span_v.shape, 0)
    gap = jnp.abs(key_at - lax.broadcasted_iota(jnp.int32, span_v.shape, 1) - c * tok_rows)
    span_v[...] = jnp.where(same | (gap == 0), gap.astype(wide), far)
    mask = jnp.broadcast_to(labels[:, half].astype(wide), (lane_width, tok_rows)).T[:, 0:1]
    mask = (mask != seq_len).astype(wide)
    upto(first)
    first.from_sib()
    saved = []

    def save(src, dst):
        copy = pltpu.make_async_copy(src, dst, out_sem.at[len(saved)])
        copy.start()
        saved.append((src, dst))

    save(w_a, a_full)
    save(span_v, span_out)
    part = lambda half, at, size: w_a[half, :, :, at : at + size].reshape(width, size)
    vectors[...] = part(0, 2 * width, lane_width).astype(wide).T[:8]
    x = tokens[...]
    k[half, :] = dot(x, part(0, width, width)).astype(low)
    swaps.put(k.at[half], k.at[half], 2, place.sib, lambda: k.at[pl.ds(0, tok_rows)])
    v[half, :] = dot(x, part(1, 0, width)).astype(low)
    swaps.put(v.at[half], v.at[half], 3, place.sib, lambda: v.at[pl.ds(0, tok_rows)])
    depth = width // heads
    q[...] = dot(x, part(0, 0, width)).astype(low) * depth**-0.5
    go(3)
    other = pl.ds(pl.multiple_of((1 - c) * tok_rows, tok_rows), tok_rows)
    swaps.got(k.at[other], 2, place.sib)
    swaps.got(v.at[other], 3, place.sib)
    save(q, q_out)
    save(k, k_out)
    save(v, v_out)

    shares = (4, 4, 4, 4, 3, 3)
    todo = []
    for count in shares:
        todo.append(work[:count])
        del work[:count]

    @pl.loop(0, pairs)
    def _(pair):
        attend_pair(pair, heads, q, k, v, span_v, lse, att)
        for at, steps in enumerate(todo):

            @pl.when(pair == at)
            def _(steps=steps):
                for step, *plane in steps:
                    step(*plane)

    save(att, att_out)
    branch = dot(att[...], part(1, width, width))
    toks = x.astype(wide)
    norm, inverse = normalized(toks + branch)
    norm_one[...] = norm
    inv_one[...] = jnp.broadcast_to(inverse, inv_one.shape)
    hidden = norm * vectors[0:1, :] + vectors[1:2, :]
    hid[...] = hidden
    hid_low[...] = hidden.astype(low)
    hid_t[...] = hidden.T.astype(low)
    save(hid_t, hid_t_out)
    save(norm_one, norm_out)
    save(inv_one, inv_out)
    small[0:4, :] = jnp.zeros((4, width), wide)
    small[4:5, :] = column_sum(mask * toks * toks)
    small[5:6, :] = column_sum(mask * branch * branch)
    small[6:7, :] = column_sum(mask * hidden * hidden)
    small[8:16, :] = jnp.zeros((8, width), wide)
    small[8:9, :] = jnp.broadcast_to(jnp.sum(mask, 0, keepdims=True), (1, width))
    tile = 512

    def glu(j):
        cols = pl.ds(pl.multiple_of(j * tile, tile), tile)
        h = hid_low[...]
        gate = dot(h, w_g[0, :, :, cols].reshape(width, tile))
        up = dot(h, w_g[1, :, :, cols].reshape(width, tile))
        cdf = 0.5 + 0.5 * lax.erf(gate * 0.7071067811865476)
        mixed = gate * cdf
        density = 0.3989422804014327 * jnp.exp(-0.5 * gate * gate)
        slope_up[:, cols] = mixed.astype(low)
        slope_gate[:, cols] = (up * (cdf + gate * density)).astype(low)
        act[:, cols] = (mixed * up).astype(low)

    upto(second)
    second.from_sib()
    save(w_g.at[:, :, :, :half_g], g_full.at[:, :, :, :half_g])

    @pl.loop(0, half_g // tile)
    def _(j):
        glu(j)

    upto(third)
    third.from_sib()
    save(w_g.at[:, :, :, half_g:], g_full.at[:, :, :, half_g:])
    for src, dst in ((slope_gate, gate_out), (slope_up, up_out), (act, act_out)):
        save(src.at[:, :half_g], dst.at[:, :half_g])

    @pl.loop(half_g // tile, ff // tile)
    def _(j):
        glu(j)

    for src, dst in ((slope_gate, gate_out), (slope_up, up_out), (act, act_out)):
        save(src.at[:, half_g:], dst.at[:, half_g:])
    upto(fourth)
    fourth.from_sib()
    save(w_d, d_full)
    d_hid[...] = jnp.zeros_like(d_hid)
    chips = 4
    deep = 2 * chips * w_d.shape[2]

    @pl.loop(0, 16 // chips)
    def _(j):
        cols = pl.ds(pl.multiple_of(j * deep, deep), deep)
        d_hid[...] += dot(act[:, cols], w_d[pl.ds(j * chips, chips)].reshape(deep, width))

    branch = d_hid[...]
    small[7:8, :] = column_sum(mask * branch * branch)
    norm, inverse = normalized(hid[...] + branch)
    gain = vectors[2:3, :]
    output[...] = (norm * gain + vectors[3:4, :]).astype(low)
    save(output, output_out)
    load.wait()
    grad = grad_v[...].astype(wide)
    small[2:3, :] = column_sum(grad * norm)
    small[3:4, :] = column_sum(grad)
    back = norm_back(grad, gain, norm, inverse)
    d_hid[...] = back
    d_branch[...] = back.astype(low)
    save(d_hid, d_hid_out)
    save(d_branch, d_branch_out)
    for i, (src, dst) in enumerate(saved):
        pltpu.make_async_copy(src, dst, out_sem.at[i]).wait()
    swaps.drain(place.sib)
    copies.drain(place.sib)


def fore(heads, tokens, labels, w_qkv, w_out, w_gu, d_shard, norms, out_grad):
    low, wide = jnp.bfloat16, jnp.float32
    rows, width = tokens.shape
    ff = w_gu.shape[1] // 2
    half_a = 2 * width + lane_width
    keys = labels.shape[1]
    vmem, hbm = pl.BlockSpec(memory_space=pltpu.VMEM), pl.BlockSpec(memory_space=pl.ANY)
    dma = lambda *shape: pltpu.SemaphoreType.DMA(shape)
    shape = jax.ShapeDtypeStruct
    w_a, w_g, w_d = (2, 16, rows_chip, half_a), (2, 16, rows_chip, ff), (16, 2) + d_shard.shape
    stored = [
        (w_a, low), (w_g, low), (w_d, low), ((rows, width), low), ((keys, width), low), ((keys, width), low),
        ((rows, width), low), ((width, rows), low), ((rows, width), wide), ((rows, lane_width), wide),
        ((rows, ff), low), ((rows, ff), low), ((rows, ff), low), ((rows, width), low), ((rows, width), wide),
        ((rows, width), low), ((keys, rows), wide),
    ]
    block = lambda *dims: pltpu.VMEM(dims, low)
    block_wide = lambda *dims: pltpu.VMEM(dims, wide)
    return pl.pallas_call(
        lambda *refs: fore_kernel(heads, *refs),
        out_shape=tuple(shape(dims, kind) for dims, kind in stored)
        + (shape((16, rows), wide), shape((8, width), wide), shape((16, width), wide)),
        in_specs=[vmem] * 7 + [hbm],
        out_specs=(hbm,) * len(stored) + (vmem,) * 3,
        scratch_shapes=[
            block(*w_a), block(*w_g), block(*w_d), block(32, half_a), block(32, ff), block(32, half_a), block(32, ff),
            block_wide(lane_width, lane_width),
            block(rows, width), block(keys, width), block(keys, width), block(rows, width),
            block_wide(keys, rows), block(rows, width), block_wide(rows, width), block(rows, width),
            block(width, rows), block_wide(rows, width), block_wide(rows, lane_width),
            block(rows, ff), block(rows, ff), block(rows, ff), block(rows, width), block_wide(rows, width),
            block(rows, width), dma(2, 4), dma(4 * gather_slots), dma(4 * gather_slots), dma(1), dma(len(stored) + 4),
        ],
        compiler_params=pltpu.CompilerParams(
            collective_id=0, has_side_effects=True, vmem_limit_bytes=62 * 2**20
        ),
        name="gather_and_forward",
    )(tokens, labels, w_qkv, w_out, w_gu, d_shard, norms, out_grad)


def back_kernel(
    heads, tokens, q, k, v, span, att, hid_t, norm, inv, gate, up, act, d_hid, d_branch, a_full, g_full, d_full,
    lse, vectors, small, d_tokens, qkv_out, wout_out, gu_out, down_out, tail, *scratch,
):
    place = Place()
    place.greet()
    c = place.c
    first = c == 0
    low, wide = jnp.bfloat16, jnp.float32
    tok_rows, width = tokens.shape
    ff = gate.shape[1]
    pairs = heads // 2
    bufs, rest = scratch[:33], scratch[33:]
    a_grad, dkv_in, resid, d_att, g_sum, a_sum, g_fin, a_fin, small_buf, send, recv, pair_sem, fin_sem, in_sem, tile_sem = rest
    copies = Copies(send, recv)
    gives, gives_down = Copies(send, recv), Copies(send, recv)
    last = Copies(fin_sem.at[0], fin_sem.at[1])
    half_g, part = ff // 2, width // 2

    def scatter(i, own, *more):
        return Scatter(place, copies, gives if i else gives_down, i * scatter_slots, None, lambda at: own.at[at], *more)

    def projection(i, *more):
        give = lambda four: a_grad.at[i, 1 - c, four]
        own = lambda at: a_grad.at[i, c, at]
        return Scatter(place, copies, copies, (3 + i) * scatter_slots, give, own, *more)

    down, left, right = (scatter(i, *bufs[7 * i : 7 * i + 7]) for i in range(3))
    projs = [projection(i, *bufs[21 + 6 * i : 27 + 6 * i]) for i in range(2)]
    early, late = projs
    planes = (3, 2, 1, 0)
    hops = ((place.sib, 0), (place.xn, 1), (place.yn, 2))

    def exchange(i):
        peer, slot = hops[i]
        last.put(small_buf.at[i], small_buf.at[4 + i], slot, peer, lambda: small_buf.at[4 + i])

    def combine(i):
        peer, slot = hops[i]
        last.got(small_buf.at[4 + i], slot, peer)
        small_buf[i + 1] = small_buf[i] + small_buf[4 + i]

    def spread():
        for z in (1, 2, 3):
            last.put(small_buf.at[3], small_buf.at[6 + z], 2 + z, place.zn[z], lambda z=z: small_buf.at[6 + z])

    tile = 256

    def feed_forward(given, act_v, db, ht, w_gu, w_dn, gate_v, up_v, att_v, norm_v, inv_v, w_out):
        for i, m in enumerate((down, left, right)):
            m.give = lambda four, i=i: given.at[i % 2, four]
        load = lambda i, src, dst: pltpu.make_async_copy(src, dst, in_sem.at[i])
        loads = [
            load(0, d_branch, db), load(1, hid_t, ht), load(2, d_hid, resid), load(3, att, att_v),
            load(4, norm, norm_v), load(5, inv, inv_v), load(6, a_full.at[1, :, :, width : 2 * width], w_out),
        ]

        def act_load(i, z):
            cols = pl.ds(pl.multiple_of(place.plane(z) * width, width), width)
            return load(7 + i % 2, act.at[:, cols], act_v.at[i % 2])

        def fetch(j):
            slot = j % 2
            cols = pl.ds(pl.multiple_of(j * tile, tile), tile)
            return [
                pltpu.make_async_copy(g_full.at[:, :, :, cols], w_gu.at[slot], tile_sem.at[0, slot]),
                pltpu.make_async_copy(d_full.at[cols], w_dn.at[slot], tile_sem.at[1, slot]),
                pltpu.make_async_copy(gate.at[:, cols], gate_v.at[slot], tile_sem.at[2, slot]),
                pltpu.make_async_copy(up.at[:, cols], up_v.at[slot], tile_sem.at[3, slot]),
            ]

        loads[0].start()
        act_load(0, planes[0]).start()
        act_load(1, planes[1]).start()
        for copy in loads[1:] + fetch(0):
            copy.start()
        loads[0].wait()
        own_d = bufs[0]
        for i, z in enumerate(planes):
            act_load(i, z).wait()
            term = dot(act_v[i % 2].T, db[...]).astype(low).reshape(4, 2, 2, rows_chip, width)
            if i < 2:
                act_load(i + 2, planes[i + 2]).start()
            four = pl.ds(place.plane(z) * 4, 4)
            mine = jnp.where(first, term[:, 0], term[:, 1])
            other = jnp.where(first, term[:, 1], term[:, 0])
            for j in range(2):
                cols = slice(j * width, (j + 1) * width)
                bufs[0][four, :, cols] = mine[:, j]
                given[0, four, :, cols] = other[:, j]
            if i == 0:
                place.meet()
            down.begin(z)
        down.first()
        down.rest()
        for copy in loads[1:3]:
            copy.wait()

        def between(i, todo):
            for at, *work in todo:

                @pl.when(i == at)
                def _(work=work):
                    for step in work:
                        step()

        def tiles(begin, own_g, give_g, todo):
            @pl.loop(begin, begin + half_g // tile)
            def _(j):
                slot = j % 2
                for copy in fetch(j):
                    copy.wait()

                @pl.when(j + 1 < ff // tile)
                def _():
                    for copy in fetch(j + 1):
                        copy.start()

                d_act = dot(db[...], w_dn[slot], ((1,), (1,)))
                d_gate = (d_act * gate_v[slot].astype(wide)).astype(low)
                d_up = (d_act * up_v[slot].astype(wide)).astype(low)
                resid[...] += dot(d_gate, w_gu[slot, 0].reshape(width, tile), ((1,), (1,))) + dot(
                    d_up, w_gu[slot, 1].reshape(width, tile), ((1,), (1,))
                )
                cols = pl.ds(pl.multiple_of((j - begin) * tile, tile), tile)
                mine = dot(ht[...], jnp.where(first, d_gate, d_up)).astype(low)
                own_g[:, :, cols] = mine.reshape(16, rows_chip, tile)
                other = dot(ht[...], jnp.where(first, d_up, d_gate)).astype(low)
                give_g[:, :, cols] = other.reshape(16, rows_chip, tile)
                between(j - begin, todo)

        tiles(0, bufs[7], given.at[1], [(5, down.diags)])
        for z in planes:
            left.begin(z)
        gives_down.drain(place.sib)
        tiles(half_g // tile, bufs[14], given.at[0], [(2, down.relays, left.first, left.rest), (5, down.odd)])
        for z in planes:
            right.begin(z)
        for copy in loads[3:]:
            copy.wait()
        grad = resid[...]
        unit = norm_v[...]
        small_buf[0] = small[...]
        small_buf[0, 0:1, :] = column_sum(grad * unit)
        small_buf[0, 1:2, :] = column_sum(grad)
        exchange(0)
        back = norm_back(grad, vectors[0:1, :], unit, inv_v[:, 0:1])
        resid[...] = back
        d_one = back.astype(low)
        d_att[...] = dot(d_one, w_out[...].reshape(width, width), ((1,), (1,))).astype(low)
        grad_out = dot(att_v[...].T, d_one).astype(low).reshape(16, rows_chip, width)
        for i in range(2):
            a_grad[i, 1, :, :, part:] = grad_out[:, :, i * part : (i + 1) * part]
        left.diags()
        right.first()
        right.rest()
        gives.drain(place.sib)

    block = lambda *dims: pltpu.VMEM(dims, low)
    block_wide = lambda *dims: pltpu.VMEM(dims, wide)
    pl.run_scoped(
        feed_forward, block(2, *bufs[0].shape), block(2, tok_rows, width),
        block(tok_rows, width), block(width, tok_rows), block(2, 2, 16, rows_chip, tile), block(2, tile, width),
        block(2, tok_rows, tile), block(2, tok_rows, tile), block(tok_rows, width), block_wide(tok_rows, width),
        block_wide(tok_rows, lane_width), block(16, rows_chip, width),
    )

    half = lambda side: pl.ds(pl.multiple_of(side * tok_rows, tok_rows), tok_rows)

    def attention_part(dq, dkv_own, dkv_out, x_t, d_k, d_v):
        slots = dkv_own.shape[0]

        def send_dkv(pair):
            return pltpu.make_async_remote_copy(
                src_ref=dkv_out.at[pair], dst_ref=dkv_in.at[pair], send_sem=pair_sem.at[0, pair],
                recv_sem=pair_sem.at[1, pair], device_id=place.sib, device_id_type=MESH,
            )

        def project(i):
            for pair in range(i * pairs // 2, (i + 1) * pairs // 2):
                send_dkv(pair).wait_recv()
                at = slice(pair * lane_width, (pair + 1) * lane_width)
                for j, dst in enumerate((d_k, d_v)):
                    dst[:, at] = (dkv_own[pair % slots, j] + dkv_in[pair, j].astype(wide)).astype(low)
            cols = slice(i * part, (i + 1) * part)
            for side, at, src in ((0, 0, dq), (0, part, d_k), (1, 0, d_v)):
                term = dot(x_t[...], src[:, cols]).astype(low)
                a_grad[i, side, :, :, at : at + part] = term.reshape(16, rows_chip, part)
            for z in planes:
                projs[i].begin(z)

        def attention(q_v, k_v, v_v, span_v, att_v, x, dk_sum, dv_sum):
            loads = [
                pltpu.make_async_copy(src, dst, in_sem.at[i])
                for i, (src, dst) in enumerate(((q, q_v), (k, k_v), (v, v_v), (span, span_v), (att, att_v), (tokens, x)))
            ]
            for copy in loads:
                copy.start()
            for copy in loads:
                copy.wait()
            x_t[...] = x[...].T

            def heads_back(begin, end, todo):
                @pl.loop(begin, end)
                def _(pair):
                    attend_back_pair(pair, heads, q_v, k_v, v_v, span_v, lse, att_v, d_att, dq, dk_sum, dv_sum)
                    for i, side in enumerate((dk_sum, dv_sum)):
                        dkv_own[lax.rem(pair, slots), i] = side[half(c), :]
                        dkv_out[pair, i] = side[half(1 - c), :].astype(low)
                    send_dkv(pair).start()
                    for at, *work in todo:

                        @pl.when(pair == at)
                        def _(at=at, work=work):
                            for step in work:
                                step()
                            if at % 2:
                                combine(at // 2)
                                if at < 5:
                                    exchange(at // 2 + 1)
                                else:
                                    spread()

            heads_back(0, 4, [(0, down.even), (1, left.odd), (2, left.relays, right.diags), (3, right.odd)])
            project(0)
            heads_back(4, pairs, [(4, left.even, early.first, early.rest), (5, right.relays)])
            project(1)

        key_rows = k.shape[0]
        pl.run_scoped(
            attention, block(*q.shape), block(*k.shape), block(*v.shape), block_wide(*span.shape), block(*att.shape),
            block(tok_rows, width), block_wide(key_rows, lane_width), block_wide(key_rows, lane_width),
        )

        def finish(w_left, w_right):
            loads = [
                pltpu.make_async_copy(a_full.at[0, :, :, : 2 * width], w_left, in_sem.at[0]),
                pltpu.make_async_copy(a_full.at[1, :, :, :width], w_right, in_sem.at[1]),
            ]
            for copy in loads:
                copy.start()
            for copy in loads:
                copy.wait()
            w_q = w_left[:, :, :width].reshape(width, width)
            total = resid[...] + dot(dq[...], w_q, ((1,), (1,)))
            early.diags()
            late.first()
            late.rest()
            w_k = w_left[:, :, width:].reshape(width, width)
            total += dot(d_k[...], w_k, ((1,), (1,)))
            early.relays()
            late.diags()
            early.odd()
            right.even()
            total += dot(d_v[...], w_right[...].reshape(width, width), ((1,), (1,)))
            d_tokens[...] = total.astype(low)
            late.relays()
            early.even()
            late.odd()

        pl.run_scoped(finish, block(16, rows_chip, 2 * width), block(16, rows_chip, width))

        @pl.loop(0, pairs)
        def _(pair):
            send_dkv(pair).wait_send()

    pl.run_scoped(
        attention_part, block(tok_rows, width), block_wide(4, 2, tok_rows, lane_width),
        block(pairs, 2, tok_rows, lane_width), block(width, tok_rows), block(tok_rows, width), block(tok_rows, width),
    )
    for z in (1, 2, 3):
        last.got(small_buf.at[6 + z], 2 + z, place.zn[z])
    sums = (small_buf[3] + small_buf[7]) + (small_buf[8] + small_buf[9])
    share = width // 32
    mine = (lax.axis_index("rows") * 2 + c) * share
    tail[0:8, :] = pltpu.roll(sums[:8], lax.rem(width - mine, width), 1)[:, :lane_width]
    squares = jnp.sum(sums[:8], 1, keepdims=True) / (sums[8:9, 0:1] * width)
    at = lambda axis: lax.broadcasted_iota(jnp.int32, (8, lane_width), axis)
    stats = jnp.where(at(0) == at(1) + 4, jnp.broadcast_to(jnp.sqrt(squares), (8, lane_width)), 0.0)
    tail[8:16, :] = jnp.broadcast_to(column_sum(stats), (8, lane_width))
    mine, theirs = pl.ds(pl.multiple_of(24 * c, 8), 24), pl.ds(pl.multiple_of(24 - 24 * c, 8), 24)
    total = down.total()
    down_out[:rows_chip] = total[:, :width]
    down_out[rows_chip:] = total[:, width:]

    def swap(i, m, total, other, slot):
        total[i] = m.total()
        last.put(total.at[i, theirs], other.at[i], slot, place.sib, lambda: other.at[i])

    swap(0, left, g_sum, g_fin, 6)
    swap(1, right, g_sum, g_fin, 7)
    swap(0, early, a_sum, a_fin, 8)
    late.even()
    for i in range(2):
        last.got(g_fin.at[i], 6 + i, place.sib)
        own, other = g_sum[i, mine], g_fin[i]
        gu_out[:, i * half_g : (i + 1) * half_g] = jnp.where(first, own, other)
        gu_out[:, (i + 2) * half_g : (i + 3) * half_g] = jnp.where(first, other, own)
    swap(1, late, a_sum, a_fin, 9)
    for i in range(2):
        last.got(a_fin.at[i], 8 + i, place.sib)
        own, other = a_sum[i, mine], a_fin[i]
        qk, vo = jnp.where(first, own, other), jnp.where(first, other, own)
        for j, term in enumerate((qk[:, :part], qk[:, part:], vo[:, :part])):
            at = j * width + i * part
            qkv_out[:, at : at + part] = term
        wout_out[:, i * part : (i + 1) * part] = vo[:, part:]
    copies.drain(place.sib)
    last.drain(place.sib)


def back(
    heads, tokens, q, k, v, span, att, hid_t, norm, inv, gate, up, act, d_hid, d_branch, a_full, g_full, d_full,
    lse, vectors, small,
):
    low, wide = jnp.bfloat16, jnp.float32
    tok_rows, width = tokens.shape
    ff = gate.shape[1]
    half_g = ff // 2
    pairs = heads // 2
    d_rows = ff // 32
    bufs = []
    for i, cols in enumerate((2 * width, half_g, half_g, width, width)):
        bufs += [pltpu.VMEM((count, rows_chip, cols), low) for count in (16, 16, 2, 2, 4, 4, 3)[i >= 3 :]]
    vmem, hbm = pl.BlockSpec(memory_space=pltpu.VMEM), pl.BlockSpec(memory_space=pl.ANY)
    dma = lambda *shape: pltpu.SemaphoreType.DMA(shape)
    shape = jax.ShapeDtypeStruct
    return pl.pallas_call(
        lambda *refs: back_kernel(heads, *refs),
        out_shape=(
            shape((tok_rows, width), low), shape((24, 3 * width), wide), shape((24, width), wide),
            shape((24, 2 * ff), wide), shape((d_rows, width), wide), shape((16, lane_width), wide),
        ),
        in_specs=[hbm] * 17 + [vmem] * 3,
        out_specs=(vmem,) * 6,
        scratch_shapes=bufs
        + [
            pltpu.VMEM((2, 2, 16, rows_chip, width), low),
            pltpu.VMEM((pairs, 2, tok_rows, lane_width), low),
            pltpu.VMEM((tok_rows, width), wide),
            pltpu.VMEM((tok_rows, width), low),
            pltpu.VMEM((2, rows_chip, half_g), wide),
            pltpu.VMEM((2, rows_chip, width), wide),
            pltpu.VMEM((2, 24, half_g), wide),
            pltpu.VMEM((2, 24, width), wide),
            pltpu.VMEM((10,) + small.shape, wide),
            dma(5 * scatter_slots),
            dma(5 * scatter_slots),
            dma(2, pairs),
            dma(2, 10),
            dma(9),
            dma(4, 2),
        ],
        compiler_params=pltpu.CompilerParams(
            collective_id=1, has_side_effects=True, vmem_limit_bytes=63 * 2**20
        ),
        name="backward_and_sums",
    )(tokens, q, k, v, span, att, hid_t, norm, inv, gate, up, act, d_hid, d_branch, a_full, g_full, d_full, lse, vectors, small)


def close_kernel(share, *refs):
    parts, tail, outs = refs[:6], refs[6], refs[7:]
    for part, out in zip(parts, outs):
        out[...] = part[...]
    for i, out in enumerate(outs[6:10]):
        out[...] = tail[i : i + 1, :share]
    outs[10][...] = tail[8:9, :4]


def close(share, *parts):
    vmem = pl.BlockSpec(memory_space=pltpu.VMEM)
    wide = jnp.float32
    return pl.pallas_call(
        lambda *refs: close_kernel(share, *refs),
        out_shape=tuple(jax.ShapeDtypeStruct(part.shape, part.dtype) for part in parts[:6])
        + (jax.ShapeDtypeStruct((1, share), wide),) * 4
        + (jax.ShapeDtypeStruct((1, 4), wide),),
        in_specs=[vmem] * 7,
        out_specs=(vmem,) * 11,
        compiler_params=pltpu.CompilerParams(vmem_limit_bytes=62 * 2**20),
        name="results",
    )(*parts)


def window(cells, width):
    count = lax.axis_size("blk")
    before = lax.ppermute(cells, "blk", [(i, i + 1) for i in range(count - 1)])
    after = lax.ppermute(cells, "blk", [(i + 1, i) for i in range(count - 1)])
    return jnp.concatenate([before, cells, after], 0)


def window_back(terms, width):
    count = lax.axis_size("blk")
    low = jnp.bfloat16
    before = lax.ppermute(terms[2 * width :].astype(low), "blk", [(i, i + 1) for i in range(count - 1)])
    after = lax.ppermute(terms[:width].astype(low), "blk", [(i + 1, i) for i in range(count - 1)])
    return terms[width : 2 * width] + before.astype(terms.dtype) + after.astype(terms.dtype)


def key_spans(labels, first, tok_rows):
    seq_len = labels.shape[0]
    query_pos = first + jnp.arange(tok_rows, dtype=jnp.int32)
    query_labels = lax.dynamic_slice_in_dim(labels, first, tok_rows, 0)
    if seq_len == 2 * tok_rows:
        key_pos, key_labels = jnp.arange(seq_len, dtype=jnp.int32), labels
    else:
        key_pos = first - tok_rows + jnp.arange(3 * tok_rows, dtype=jnp.int32)
        padded = jnp.pad(labels, (tok_rows, tok_rows), constant_values=seq_len)
        key_labels = lax.dynamic_slice_in_dim(padded, first, 3 * tok_rows, 0)
    same = (key_labels[:, None] == query_labels[None, :]) & (key_labels[:, None] != seq_len)
    gap = jnp.abs(key_pos[:, None] - query_pos[None, :])
    return jnp.where(same | (gap == 0), gap.astype(jnp.float32), far)


def on_chip_grid():
    return lax.axis_size("rows") == 16 and lax.axis_size("blk") == 2


def packed_shards(w_qkv, w_out, ln1_gain, ln1_bias, w_gate_up, ln2_gain, ln2_bias):
    width = w_out.shape[1]
    ff = w_gate_up.shape[1] // 2
    table = jnp.stack((ln1_gain, ln1_bias, ln2_gain, ln2_bias), 1)
    table = jnp.pad(table, ((0, 0), (0, lane_width - 4)))
    left = jnp.concatenate([w_qkv[:, : 2 * width], table], 1)
    right = jnp.concatenate([w_qkv[:, 2 * width :], w_out, jnp.zeros_like(table)], 1)
    return jnp.stack([left, right]), jnp.stack([w_gate_up[:, :ff], w_gate_up[:, ff:]])


def on_grid(tokens, labels, w_qkv, w_out, w_gate_up, w_down, norms, out_grad):
    width = tokens.shape[1]
    (
        a_full, g_full, d_full, q, k, v, att, hid_t, norm, inv, gate, up, act, output, d_hid, d_branch, span,
        lse, vectors, small,
    ) = fore(HEADS, tokens, labels, w_qkv, w_out, w_gate_up, w_down, jnp.stack(norms), out_grad)
    parts = back(
        HEADS, tokens, q, k, v, span, att, hid_t, norm, inv, gate, up, act, d_hid, d_branch, a_full, g_full,
        d_full.reshape(-1, width), lse, vectors, small,
    )
    *parts, one, two, three, four, stats = close(norms[0].shape[0], output, *parts)
    rows = [row.reshape(-1) for row in (one, two, three, four)]
    return *parts, rows, stats.reshape(-1)


def on_any(tokens, labels, w_qkv, w_out, w_gate_up, w_down, norms, out_grad):
    both = ("rows", "blk")
    tok_rows, width = tokens.shape
    first = lax.axis_index("blk") * tok_rows
    span = key_spans(labels[0], first, tok_rows)
    here = lax.dynamic_slice_in_dim(labels[0], first, tok_rows, 0)
    valid = (here != labels.shape[1]).astype(jnp.float32)[:, None]
    a_shard, g_shard = packed_shards(w_qkv, w_out, *norms[:2], w_gate_up, *norms[2:])
    low, wide = jnp.bfloat16, jnp.float32
    a_full = lax.all_gather(a_shard, both, axis=1, tiled=True)
    w_gu = lax.all_gather(g_shard, both, axis=1, tiled=True)
    w_dn = lax.all_gather(w_down, both, axis=0, tiled=True)
    vectors = jnp.pad(a_full[0, :, 2 * width : 2 * width + 4].astype(wide).T, ((0, 4), (0, 0)))
    w_qk, w_v = a_full[0, :, : 2 * width], a_full[1, :, :width]
    qk = jnp.dot(tokens, w_qk, preferred_element_type=wide).astype(low)
    v = jnp.dot(tokens, w_v, preferred_element_type=wide).astype(low)
    query = qk[:, :width] * (width // HEADS) ** -0.5
    kv = window(jnp.concatenate([qk[:, width:], v], 1), tok_rows)
    keys, values = kv[:, :width], kv[:, width:]
    attended, lse = attend(query, keys, values, span, HEADS)
    output, d_resid_one, d_att, grad_out, g_grad, d_grad, small = ffn(
        tokens, attended, a_full, vectors, valid, out_grad, w_gu, w_dn
    )
    dq, dk, dv = attend_back(query, keys, values, span, lse, attended, d_att, HEADS)
    dkv = window_back(jnp.concatenate([dk, dv], 1), tok_rows)
    d_qk = jnp.concatenate([dq, dkv[:, :width].astype(low)], 1)
    d_v = dkv[:, width:].astype(low)
    grad_qkv = transposed_times(tokens, jnp.concatenate([d_qk, d_v], 1))
    d_tokens = d_resid_one + times_transposed(d_qk, w_qk) + times_transposed(d_v, w_v)
    share = lambda g, axis: lax.psum_scatter(g.astype(wide), both, scatter_dimension=axis, tiled=True)
    gate, up = share(g_grad, 1)
    small = lax.psum(small, both)
    size = norms[0].shape[0]
    rows = lax.dynamic_slice_in_dim(small[:4], lax.axis_index(both) * size, size, 1)
    stats = jnp.sqrt(jnp.sum(small[4:8], 1) / (small[8, 0] * width))
    return (
        output, d_tokens.astype(low), share(grad_qkv, 0), share(grad_out, 0), jnp.concatenate([gate, up], 1),
        share(d_grad, 0), rows, stats,
    )


def body(
    tokens, segments, w_qkv, w_out, ln1_gain, ln1_bias, w_gate_up, w_down, ln2_gain, ln2_bias, out_grad,
):
    run = on_grid if on_chip_grid() else on_any
    norms = (ln1_gain, ln1_bias, ln2_gain, ln2_bias)
    output, d_tokens, qkv, wout, gate_up, down, rows, stats = run(
        tokens[0], segments, w_qkv, w_out, w_gate_up, w_down, norms, out_grad[0]
    )
    return (
        output[None], d_tokens[None], qkv, wout, rows[0], rows[1], gate_up, down, rows[2], rows[3], stats,
    )


def solution(mesh):
    placed = (
        P("rows", "blk", None),
        P("rows", None),
        P(("rows", "blk"), None),
        P(("rows", "blk"), None),
        P(("rows", "blk")),
        P(("rows", "blk")),
        P(("rows", "blk"), None),
        P(("rows", "blk"), None),
        P(("rows", "blk")),
        P(("rows", "blk")),
        P("rows", "blk", None),
    )
    return jax.shard_map(
        body,
        mesh=mesh,
        in_specs=placed,
        out_specs=(
            P("rows", "blk", None),
            P("rows", "blk", None),
            P(("rows", "blk"), None),
            P(("rows", "blk"), None),
            P(("rows", "blk")),
            P(("rows", "blk")),
            P(("rows", "blk"), None),
            P(("rows", "blk"), None),
            P(("rows", "blk")),
            P(("rows", "blk")),
            P(),
        ),
        check_vma=False,
    )
```

```python
import jax
import jax.numpy as jnp
from jax import lax
from jax.experimental import pallas as pl
from jax.experimental.pallas import tpu as pltpu
from jax.sharding import PartitionSpec as P

HEADS = 12


ln_eps = 1e-12
far = 1e33
lane_width = 128


def times_transposed(left, right):
    return lax.dot_general(
        left, right, (((1,), (1,)), ((), ())), preferred_element_type=jnp.float32
    )


def transposed_times(left, right):
    return lax.dot_general(
        left, right, (((0,), (0,)), ((), ())), preferred_element_type=jnp.float32
    )


MESH = pl.DeviceIdType.MESH


class Place:
    def __init__(self):
        r, self.c = lax.axis_index("rows"), lax.axis_index("blk")
        self.x, self.y, self.z = r % 2, (r // 2) % 2, r // 4
        self.sib = (r, 1 - self.c)
        self.xn = (self.at(0, "x"), self.c)
        self.yn = (self.at(0, "y"), self.c)
        self.zn = {k: (self.at(k, "o"), self.c) for k in (1, 2, 3)}

    def plane(self, k):
        z, low = self.z % 2, self.z // 2
        if k % 2:
            z = 1 - z
        if k // 2:
            low = 1 - low
        return low * 2 + z

    def at(self, k, j):
        x = 1 - self.x if j in "xd" else self.x
        y = 1 - self.y if j in "yd" else self.y
        return self.plane(k) * 4 + y * 2 + x

    def greet(self):
        self.barrier = pltpu.get_barrier_semaphore()
        for peer in (self.sib, self.xn, self.yn, *self.zn.values()):
            pl.semaphore_signal(self.barrier, inc=1, device_id=peer, device_id_type=MESH)

    def meet(self):
        pl.semaphore_wait(self.barrier, 6)


class Copies:
    def __init__(self, send, recv):
        self.send, self.recv = send, recv

    def of(self, src, dst, pool, slot, peer):
        return pltpu.make_async_remote_copy(
            src_ref=src, dst_ref=dst, send_sem=self.send.at[pool], recv_sem=self.recv.at[slot],
            device_id=peer, device_id_type=MESH,
        )

    def put(self, src, dst, pool, slot, peer):
        self.of(src, dst, pool, slot, peer).start()

    def got(self, dst, slot, peer):
        self.of(dst, dst, 0, slot, peer).wait_recv()

    def sent(self, all_of_pool, pool, peer):
        self.of(all_of_pool, all_of_pool, pool, 0, peer).wait_send()


class Gather:
    def __init__(self, place, copies, i, side):
        self.p, self.cp, self.side = place, copies, side
        self.base, self.pool = i * gather_slots, 2 * i

    def slot(self, kind, k=0):
        return self.base + {"z": -1, "x": 3, "y": 7, "d": 11, "s": 15}[kind] + k

    def out(self, half, r):
        return self.side(half).at[r]

    def block(self, k, j):
        return self.out(self.p.c, self.p.at(k, j))

    def send(self, src, dst, slot, peer):
        self.cp.put(src, dst, self.pool, slot, peer)

    def push(self, src, k, j):
        self.cp.put(src, self.block(k, j), self.pool + 1, self.slot("s"), self.p.sib)

    def to_z(self):
        for k in (1, 2):
            self.send(self.block(0, "o"), self.block(0, "o"), self.slot("z", k), self.p.zn[k])

    def to_xy(self):
        self.spread(self.block(0, "o"), 0)

    def spread(self, src, k):
        dst = self.block(k, "o")
        self.send(src, dst, self.slot("x", k), self.p.xn)
        self.send(src, dst, self.slot("y", k), self.p.yn)
        self.push(src, k, "o")

    def from_z(self, k):
        block = self.block(k, "o")
        self.cp.got(block, self.slot("z", k), self.p.zn[k])
        if k == 2:
            self.send(block, block, self.slot("z", 3), self.p.zn[1])
        self.spread(block, k)

    @staticmethod
    def schedule(mats):
        work = [(mats[0].to_z,)] + [(m.to_xy,) for m in mats[:3]]
        for i, m in enumerate(mats):
            before = mats[i - 1] if i else None
            work.append((m.from_z, 1))
            if i + 1 < len(mats):
                work.append((mats[i + 1].to_z,))
            if before:
                work.append((before.from_xy, 3))
            work += [(m.from_xy, 0), (m.from_z, 2)]
            if before:
                work.append((before.from_d, 2))
            if i + 3 < len(mats):
                work.append((mats[i + 3].to_xy,))
            work += [(m.from_xy, 1), (m.from_z, 3)]
            if before:
                work.append((before.from_d, 1))
            work.append((m.from_d, 0))
            if before:
                work.append((before.from_d, 3))
            work.append((m.from_xy, 2))
        last = mats[-1]
        return work + [(last.from_xy, 3), (last.from_d, 2), (last.from_d, 1), (last.from_d, 3)]

    def from_xy(self, k):
        x, y = self.block(k, "x"), self.block(k, "y")
        self.cp.got(x, self.slot("x", k), self.p.xn)
        if k == 2:
            self.send(x, x, self.slot("d", k), self.p.yn)
        self.cp.got(y, self.slot("y", k), self.p.yn)
        if k == 0:
            self.send(y, y, self.slot("d", k), self.p.xn)
        self.push(x, k, "x")
        self.push(y, k, "y")

    def from_d(self, k):
        block = self.block(k, "d")
        self.cp.got(block, self.slot("d", k), self.p.xn)
        if k % 2 == 0:
            self.send(block, block, self.slot("d", k + 1), self.p.zn[1])
        self.push(block, k, "d")

    def from_sib(self):
        self.cp.got(self.side(1 - self.p.c), self.slot("s"), self.p.sib)

    def drain(self):
        side = self.side(self.p.c)
        self.cp.sent(side.at[pl.ds(0, 15)], self.pool, self.p.sib)
        self.cp.sent(side, self.pool + 1, self.p.sib)


class Scatter:
    def __init__(self, place, copies, i, give, own, sib, rly, dia, xin, yin, zin, straight=False, flat=False):
        self.p, self.cp, self.give, self.own = place, copies, give, own
        self.base, self.pool = i * scatter_slots, 2 * i
        self.straight, self.flat = straight, flat
        self.sib, self.rly, self.dia, self.xin, self.yin, self.zin = sib, rly, dia, xin, yin, zin

    def slot(self, kind, k):
        return self.base + {"s": 0, "r": 4, "d": 5, "x": 8, "y": 12, "z": 15}[kind] + k

    def four(self, k):
        return pl.ds(self.p.plane(k) * 4, 4)

    def begin(self, k):
        four = self.four(k)
        self.cp.put(self.give(four), self.sib.at[four], self.pool + 1, self.slot("s", k), self.p.sib)

    def given(self):
        self.cp.sent(self.sib, self.pool + 1, self.p.sib)

    def drain(self):
        self.cp.sent(self.sib.at[pl.ds(0, 15)], self.pool, self.p.sib)

    def to_x(self, own, k):
        self.cp.put(own, self.xin.at[k], self.pool, self.slot("x", k), self.p.xn)

    def to_y(self, own, k):
        self.cp.put(own, self.yin.at[k], self.pool, self.slot("y", k), self.p.yn)

    def both(self, k, j, *more):
        at = self.p.at(k, j)
        own = self.own(at)
        total = own[...] + self.sib[at]
        for ref in more:
            total = total + ref[...]
        own[...] = total
        return own

    def pair(self, k):
        four = self.four(k)
        self.cp.got(self.sib.at[four], self.slot("s", k), self.p.sib)
        if self.flat:
            self.to_relay(self.both(k, "d"), k)
        elif k % 2:
            i = k // 2
            self.cp.put(self.both(k, "d"), self.dia.at[i], self.pool, self.slot("d", 2 * i), self.p.zn[1])
        odd = k % 2 and not self.flat
        if odd or k < 2:
            self.to_x(self.both(k, "x"), k)
        if odd or k >= 2:
            self.to_y(self.both(k, "y"), k)

    def relay_at(self, k):
        return (self.dia if k % 2 else self.rly).at[k // 2]

    def to_relay(self, own, k):
        slot = self.slot("d", k - 1) if k % 2 else self.slot("r", k)
        self.cp.put(own, self.relay_at(k), self.pool, slot, self.p.xn if k < 2 else self.p.yn)

    def diag(self, k):
        i = k // 2
        self.cp.got(self.dia.at[i], self.slot("d", k), self.p.zn[1])
        self.to_relay(self.both(k, "d", self.dia.at[i]), k)

    def relay(self, k):
        rly = self.relay_at(k)
        self.cp.got(rly, self.slot("d", k - 1) if k % 2 else self.slot("r", k), self.p.xn)
        if k < 2:
            self.to_y(self.both(k, "y", rly), k)
        else:
            self.to_x(self.both(k, "x", rly), k)

    def plane(self, k):
        p = self.p
        at = p.at(k, "o")
        self.cp.got(self.xin.at[k], self.slot("x", k), p.xn)
        self.cp.got(self.yin.at[k], self.slot("y", k), p.yn)
        wide = jnp.float32
        own = self.own(at)
        total = (own[...].astype(wide) + self.sib[at].astype(wide)) + (
            self.xin[k].astype(wide) + self.yin[k].astype(wide)
        )
        own[...] = total.astype(jnp.bfloat16)
        if self.straight and k:
            self.to_z(own, k, k)
        elif k % 2:
            self.to_z(own, k, 1)

    def to_z(self, own, k, step):
        self.cp.put(own, self.zin.at[k - 1], self.pool, self.slot("z", k), self.p.zn[step])

    def cross(self):
        self.cp.got(self.zin.at[2], self.slot("z", 3), self.p.zn[1])
        own = self.own(self.p.at(2, "o"))
        own[...] = own[...] + self.zin[2]
        self.to_z(own, 2, 2)

    def all(self, name, *planes):
        for k in planes:
            getattr(self, name)(k)

    def first(self):
        self.all("pair", 3, 1)

    def rest(self):
        self.all("pair", 2, 0)

    def diags(self):
        if not self.flat:
            self.all("diag", 2, 0)

    def relays(self):
        self.all("relay", *((3, 1, 2, 0) if self.flat else (2, 0)))

    def odd(self):
        self.all("plane", 3, 1)

    def even(self):
        self.all("plane", 2, 0)
        if not self.straight:
            self.cross()

    def total(self):
        wide = jnp.float32
        total = self.own(self.p.at(0, "o"))[...].astype(wide)
        for k in (1, 2, 3) if self.straight else (1, 2):
            self.cp.got(self.zin.at[k - 1], self.slot("z", k), self.p.zn[k])
            total = total + self.zin[k - 1].astype(wide)
        return total


rows_chip = 48
gather_slots, scatter_slots = 16, 19


def dot(left, right, dims=((1,), (0,))):
    return lax.dot_general(left, right, (dims, ((), ())), preferred_element_type=jnp.float32)


def row_mean(values):
    return jnp.mean(values, -1, keepdims=True)


def normalized(resid):
    centred = resid - row_mean(resid)
    inverse = lax.rsqrt(row_mean(centred * centred) + ln_eps)
    return centred * inverse, inverse


def norm_back(grad, gain, norm, inverse):
    e = grad * gain
    return inverse * (e - row_mean(e) - norm * row_mean(e * norm))


def column_sum(values):
    return jnp.sum(values, 0, keepdims=True)


def ffn_kernel(
    tokens, attended, w_out, vectors, valid, out_grad, w_gu, w_down,
    output, d_resid_one, d_att, grad_out, grad_gu, grad_down, small,
    hid, hid_low, hid_t, norm_one, inv_one, slope_gate, slope_up, act, total, d_hid, d_branch,
):
    i = pl.program_id(0)
    tiles = pl.num_programs(0) // 2
    low = jnp.bfloat16
    wide = jnp.float32

    @pl.when(i == 0)
    def _():
        branch = dot(attended[...], w_out[0])
        toks = tokens[...].astype(wide)
        norm, inverse = normalized(toks + branch)
        norm_one[...] = norm
        inv_one[...] = inverse
        hidden = norm * vectors[0:1, :] + vectors[1:2, :]
        hid[...] = hidden
        hid_low[...] = hidden.astype(low)
        hid_t[...] = hidden.T.astype(low)
        mask = valid[...]
        small[4:5, :] = column_sum(mask * toks * toks)
        small[5:6, :] = column_sum(mask * branch * branch)
        small[6:7, :] = column_sum(mask * hidden * hidden)
        small[8:16, :] = jnp.zeros((8, small.shape[1]), wide)
        small[8:9, :] = jnp.broadcast_to(jnp.sum(mask, 0, keepdims=True), (1, small.shape[1]))
        total[...] = jnp.zeros_like(total)

    @pl.when(i < tiles)
    def _():
        h = hid_low[...]
        gate = dot(h, w_gu[0])
        up = dot(h, w_gu[1])
        cdf = 0.5 + 0.5 * lax.erf(gate * 0.7071067811865476)
        glu = gate * cdf
        density = 0.3989422804014327 * jnp.exp(-0.5 * gate * gate)
        slope_up[i] = glu
        slope_gate[i] = up * (cdf + gate * density)
        a = (glu * up).astype(low)
        act[i] = a
        total[...] += dot(a, w_down[...])

    @pl.when(i == tiles - 1)
    def _():
        branch = total[...]
        mask = valid[...]
        small[7:8, :] = column_sum(mask * branch * branch)
        norm, inverse = normalized(hid[...] + branch)
        gain = vectors[2:3, :]
        output[...] = (norm * gain + vectors[3:4, :]).astype(low)
        grad = out_grad[...].astype(wide)
        small[2:3, :] = column_sum(grad * norm)
        small[3:4, :] = column_sum(grad)
        back = norm_back(grad, gain, norm, inverse)
        d_hid[...] = back
        d_branch[...] = back.astype(low)

    @pl.when(i >= tiles)
    def _():
        j = i - tiles
        db = d_branch[...]
        grad_down[...] = dot(act[j].T, db).astype(low)
        d_act = dot(db, w_down[...], ((1,), (1,)))
        d_gate = (d_act * slope_gate[j]).astype(low)
        d_up = (d_act * slope_up[j]).astype(low)
        h_t = hid_t[...]
        grad_gu[0] = dot(h_t, d_gate).astype(low)
        grad_gu[1] = dot(h_t, d_up).astype(low)
        d_hid[...] += dot(d_gate, w_gu[0], ((1,), (1,))) + dot(d_up, w_gu[1], ((1,), (1,)))

    @pl.when(i == 2 * tiles - 1)
    def _():
        grad = d_hid[...]
        norm = norm_one[...]
        small[0:1, :] = column_sum(grad * norm)
        small[1:2, :] = column_sum(grad)
        back = norm_back(grad, vectors[0:1, :], norm, inv_one[...])
        d_resid_one[...] = back
        db = back.astype(low)
        grad_out[...] = dot(attended[...].T, db).astype(low)
        d_att[...] = dot(db, w_out[0], ((1,), (1,))).astype(low)


def ffn(tokens, attended, a_full, vectors, valid, out_grad, w_gu, w_down):
    rows, width = tokens.shape
    ff = w_down.shape[0]
    tile = 512
    tiles = ff // tile
    low, wide = jnp.bfloat16, jnp.float32
    whole = lambda *shape: pl.BlockSpec(shape, lambda i: (0,) * len(shape))
    at = lambda i: jnp.where(i < tiles, i, i - tiles)
    late = lambda i: jnp.maximum(i - tiles, 0)
    return pl.pallas_call(
        ffn_kernel,
        grid=(2 * tiles,),
        out_shape=(
            jax.ShapeDtypeStruct((rows, width), low),
            jax.ShapeDtypeStruct((rows, width), wide),
            jax.ShapeDtypeStruct((rows, width), low),
            jax.ShapeDtypeStruct((width, width), low),
            jax.ShapeDtypeStruct((2, width, ff), low),
            jax.ShapeDtypeStruct((ff, width), low),
            jax.ShapeDtypeStruct((16, width), wide),
        ),
        in_specs=[
            whole(rows, width),
            whole(rows, width),
            pl.BlockSpec((1, width, width), lambda i: (1, 0, 1)),
            whole(8, width),
            whole(rows, 1),
            whole(rows, width),
            pl.BlockSpec((2, width, tile), lambda i: (0, 0, at(i))),
            pl.BlockSpec((tile, width), lambda i: (at(i), 0)),
        ],
        out_specs=(
            whole(rows, width),
            whole(rows, width),
            whole(rows, width),
            whole(width, width),
            pl.BlockSpec((2, width, tile), lambda i: (0, 0, late(i))),
            pl.BlockSpec((tile, width), lambda i: (late(i), 0)),
            whole(16, width),
        ),
        scratch_shapes=[
            pltpu.VMEM((rows, width), wide),
            pltpu.VMEM((rows, width), low),
            pltpu.VMEM((width, rows), low),
            pltpu.VMEM((rows, width), wide),
            pltpu.VMEM((rows, 1), wide),
            pltpu.VMEM((tiles, rows, tile), wide),
            pltpu.VMEM((tiles, rows, tile), wide),
            pltpu.VMEM((tiles, rows, tile), low),
            pltpu.VMEM((rows, width), wide),
            pltpu.VMEM((rows, width), wide),
            pltpu.VMEM((rows, width), low),
        ],
        compiler_params=pltpu.CompilerParams(vmem_limit_bytes=60 * 2**20),
        cost_estimate=pl.CostEstimate(
            flops=2 * rows * width * (9 * ff + 3 * width), bytes_accessed=18 * ff * width, transcendentals=2 * rows * ff
        ),
        name="feed_forward",
    )(tokens, attended, a_full, vectors, valid, out_grad, w_gu, w_down)


def half_of(block, axis, second):
    place = lax.broadcasted_iota(jnp.int32, block.shape, axis)
    depth = block.shape[axis] // 2
    keep = place >= depth if second else place < depth
    return jnp.where(keep, block, jnp.zeros_like(block))


def attend_kernel(heads, q, k, v, span, attended, lse):
    @pl.loop(0, heads // 2)
    def _(pair):
        attend_pair(pair, heads, q, k, v, span, lse, attended)


def attend(q, k, v, span, heads):
    rows, width = q.shape
    keys = k.shape[0]
    low, wide = jnp.bfloat16, jnp.float32
    return pl.pallas_call(
        lambda *refs: attend_kernel(heads, *refs),
        out_shape=(
            jax.ShapeDtypeStruct((rows, width), low),
            jax.ShapeDtypeStruct((16, rows), wide),
        ),
        in_specs=[pl.BlockSpec(memory_space=pltpu.VMEM)] * 4,
        out_specs=(pl.BlockSpec(memory_space=pltpu.VMEM),) * 2,
        compiler_params=pltpu.CompilerParams(vmem_limit_bytes=60 * 2**20),
        cost_estimate=pl.CostEstimate(flops=4 * rows * keys * width, bytes_accessed=8 * keys * width, transcendentals=heads * rows * keys),
        name="attend",
    )(q, k, v, span)


def attend_back_pair(pair, heads, q, k, v, span, lse, att, d_att, dq, dk_sum, dv_sum):
    low, wide = jnp.bfloat16, jnp.float32
    rows, width = q.shape
    lanes = lane_width
    depth = width // heads
    chunk = 256
    scale = depth**-0.5
    at = pl.ds(pl.multiple_of(pair * lanes, lanes), lanes)
    keys, values = k[:, at], v[:, at]
    keys_t = keys.astype(wide).T.astype(low)
    for c in range(rows // chunk):
        here = pl.ds(c * chunk, chunk)
        q_wide = q[here, at].astype(wide)
        do_here = d_att[here, at]
        do_wide = do_here.astype(wide)
        q_here = q_wide.astype(low)
        q_t, do_t = q_wide.T.astype(low), do_wide.T.astype(low)
        both_t = (do_wide * att[here, at].astype(wide)).T
        dk_part, dv_part, dq_parts = None, None, []
        for h in (0, 1):
            head = 2 * pair + h
            own = slice(h * depth, (h + 1) * depth)
            slope = jnp.exp2(jnp.full((1, 1), -8.0 / heads, wide) * (head + 1).astype(wide))
            delta = jnp.sum(both_t[own], 0, keepdims=True)
            logits = dot(keys, half_of(q_t, 0, h)) - slope * span[:, here]
            probs = jnp.exp(logits - lse[pl.ds(head, 1), here])
            d_probs = dot(values, half_of(do_t, 0, h))
            d_logits = (probs * (d_probs - delta)).astype(low)
            dv_term = dot(probs.astype(low), half_of(do_here, 1, h))
            dk_term = dot(d_logits, half_of(q_here, 1, h))
            dv_part = dv_term if dv_part is None else dv_part + dv_term
            dk_part = dk_term if dk_part is None else dk_part + dk_term
            dq_parts.append(dot(keys_t[own], d_logits) * scale)
        if c == 0:
            dk_sum[...] = dk_part
            dv_sum[...] = dv_part
        else:
            dk_sum[...] += dk_part
            dv_sum[...] += dv_part
        dq[here, at] = jnp.concatenate(dq_parts, 0).T.astype(low)


def attend_back_kernel(heads, q, k, v, span, lse, att, d_att, dq, dk, dv, dk_sum, dv_sum):
    @pl.loop(0, heads // 2)
    def _(pair):
        attend_back_pair(pair, heads, q, k, v, span, lse, att, d_att, dq, dk_sum, dv_sum)
        at = pl.ds(pl.multiple_of(pair * lane_width, lane_width), lane_width)
        dk[:, at] = dk_sum[...]
        dv[:, at] = dv_sum[...]


def attend_back(q, k, v, span, lse, att, d_att, heads):
    rows, width = q.shape
    keys = k.shape[0]
    low, wide = jnp.bfloat16, jnp.float32
    return pl.pallas_call(
        lambda *refs: attend_back_kernel(heads, *refs),
        out_shape=(
            jax.ShapeDtypeStruct((rows, width), low),
            jax.ShapeDtypeStruct((keys, width), wide),
            jax.ShapeDtypeStruct((keys, width), wide),
        ),
        in_specs=[pl.BlockSpec(memory_space=pltpu.VMEM)] * 7,
        out_specs=(pl.BlockSpec(memory_space=pltpu.VMEM),) * 3,
        scratch_shapes=[
            pltpu.VMEM((keys, lane_width), wide),
            pltpu.VMEM((keys, lane_width), wide),
        ],
        compiler_params=pltpu.CompilerParams(vmem_limit_bytes=60 * 2**20),
        cost_estimate=pl.CostEstimate(flops=10 * rows * keys * width, bytes_accessed=16 * keys * width, transcendentals=heads * rows * keys),
        name="attend_back",
    )(q, k, v, span, lse, att, d_att)


def attend_pair(pair, heads, q, k, v, span, lse, attended):
    low, wide = jnp.bfloat16, jnp.float32
    rows, width = q.shape
    lanes = lane_width
    depth = width // heads
    chunk = 256
    at = pl.ds(pl.multiple_of(pair * lanes, lanes), lanes)
    keys = k[:, at]
    values_t = v[:, at].astype(wide).T.astype(low)
    for c in range(rows // chunk):
        here = pl.ds(c * chunk, chunk)
        q_t = q[here, at].astype(wide).T.astype(low)
        parts = []
        for h in (0, 1):
            head = 2 * pair + h
            slope = jnp.exp2(jnp.full((1, 1), -8.0 / heads, wide) * (head + 1).astype(wide))
            logits = dot(keys, half_of(q_t, 0, h)) - slope * span[:, here]
            top = jnp.max(logits, 0, keepdims=True)
            weights = jnp.exp(logits - top)
            norm = jnp.sum(weights, 0, keepdims=True)
            lse[pl.ds(head, 1), here] = top + jnp.log(norm)
            parts.append(dot(values_t[h * depth : (h + 1) * depth], weights.astype(low)) / norm)
        attended[here, at] = jnp.concatenate(parts, 0).T.astype(low)


def fore_kernel(
    heads, tokens, labels, w_qkv, w_out, w_gu, d_shard, norms, out_grad,
    a_full, g_full, d_full, q_out, k_out, v_out, att_out, hid_t_out, norm_out, inv_out, gate_out, up_out, act_out,
    output_out, d_hid_out, d_branch_out, span_out, lse, vectors, small,
    w_a, w_g, w_d, a_give, g_give, a_pair, g_pair, turned, q, k, v, att, span_v, grad_v, hid, hid_low, hid_t, norm_one, inv_one,
    slope_gate, slope_up, act, output, d_hid, d_branch, pair_sem, send, recv, in_sem, out_sem,
):
    place = Place()
    place.greet()
    c = place.c
    low, wide = jnp.bfloat16, jnp.float32
    tok_rows, width = tokens.shape
    ff = w_g.shape[3]
    half_g = ff // 2
    pairs = heads // 2
    load = pltpu.make_async_copy(out_grad, grad_v, in_sem.at[0])
    load.start()
    core_one = c == 1
    turned[...] = jnp.zeros_like(turned)
    turned[0:4, 0 : norms.shape[1]] = norms[...].astype(wide)
    table = turned[...].T[: norms.shape[1]].astype(low)
    left = jnp.concatenate([w_qkv[:, : 2 * width], table], 1)
    right = jnp.concatenate([w_qkv[:, 2 * width :], w_out[...], jnp.zeros_like(table)], 1)
    gate, up = w_gu[:, :ff], w_gu[:, ff:]
    rows = w_qkv.shape[0]
    a_give[:rows, :] = jnp.where(core_one, left, right)
    g_give[:rows, :] = jnp.where(core_one, gate, up)
    swaps = Copies(pair_sem.at[0], pair_sem.at[1])
    place.meet()
    for i, (give, other) in enumerate(((a_give, a_pair), (g_give, g_pair))):
        swaps.put(give, other, i, i, place.sib)
    copies = Copies(send, recv)
    sides = [
        lambda half: w_a.at[half],
        lambda half: w_g.at[half, :, :, :half_g],
        lambda half: w_g.at[half, :, :, half_g:],
        lambda half: w_d.at[:, half],
    ]
    mats = [Gather(place, copies, i, side) for i, side in enumerate(sides)]
    first, second, third, fourth = mats
    me = place.at(0, "o")

    def assemble(mine, other, full, i):
        swaps.got(other, i, place.sib)
        mine = mine.astype(wide)
        theirs = other[:rows, :].astype(wide)
        top = jnp.where(core_one, theirs, mine)
        rest = jnp.where(core_one, mine, theirs)
        full[c, me] = jnp.concatenate([top, rest], 0).astype(low)

    work = Gather.schedule(mats)

    def go(count):
        for step, *plane in work[:count]:
            step(*plane)
        del work[:count]

    def upto(matrix):
        done = [i for i, (step, *_) in enumerate(work) if step == matrix.from_d]
        go(done[-1] + 1 if done else 0)

    assemble(jnp.where(core_one, right, left), a_pair, w_a, 0)
    go(2)
    assemble(jnp.where(core_one, up, gate), g_pair, w_g, 1)
    w_d[me, c] = d_shard[...]
    seq_len = labels.shape[1]
    label_row = labels[...].astype(wide)
    label_column = jnp.broadcast_to(label_row, (lane_width, seq_len)).T[:, 0:1]
    half = pl.ds(pl.multiple_of(c * tok_rows, tok_rows), tok_rows)
    same = (label_column == labels[:, half].astype(wide)) & (label_column != seq_len)
    key_at = lax.broadcasted_iota(jnp.int32, span_v.shape, 0)
    gap = jnp.abs(key_at - lax.broadcasted_iota(jnp.int32, span_v.shape, 1) - c * tok_rows)
    span_v[...] = jnp.where(same | (gap == 0), gap.astype(wide), far)
    mask = jnp.broadcast_to(labels[:, half].astype(wide), (lane_width, tok_rows)).T[:, 0:1]
    mask = (mask != seq_len).astype(wide)
    upto(first)
    first.from_sib()
    saved = []

    def save(src, dst):
        copy = pltpu.make_async_copy(src, dst, out_sem.at[len(saved)])
        copy.start()
        saved.append((src, dst))

    save(w_a, a_full)
    save(span_v, span_out)
    part = lambda half, at, size: w_a[half, :, :, at : at + size].reshape(width, size)
    vectors[...] = part(0, 2 * width, lane_width).astype(wide).T[:8]
    x = tokens[...]
    k[half, :] = dot(x, part(0, width, width)).astype(low)
    swaps.put(k.at[half], k.at[half], 2, 2, place.sib)
    v[half, :] = dot(x, part(1, 0, width)).astype(low)
    swaps.put(v.at[half], v.at[half], 3, 3, place.sib)
    depth = width // heads
    q[...] = dot(x, part(0, 0, width)).astype(low) * depth**-0.5
    go(3)
    other = pl.ds(pl.multiple_of((1 - c) * tok_rows, tok_rows), tok_rows)
    swaps.got(k.at[other], 2, place.sib)
    swaps.got(v.at[other], 3, place.sib)
    save(q, q_out)
    save(k, k_out)
    save(v, v_out)

    shares = (4, 4, 4, 4, 3, 3)
    todo = []
    for count in shares:
        todo.append(work[:count])
        del work[:count]

    @pl.loop(0, pairs)
    def _(pair):
        attend_pair(pair, heads, q, k, v, span_v, lse, att)
        for at, steps in enumerate(todo):

            @pl.when(pair == at)
            def _(steps=steps):
                for step, *plane in steps:
                    step(*plane)

    save(att, att_out)
    branch = dot(att[...], part(1, width, width))
    toks = x.astype(wide)
    norm, inverse = normalized(toks + branch)
    norm_one[...] = norm
    inv_one[...] = jnp.broadcast_to(inverse, inv_one.shape)
    hidden = norm * vectors[0:1, :] + vectors[1:2, :]
    hid[...] = hidden
    hid_low[...] = hidden.astype(low)
    hid_t[...] = hidden.T.astype(low)
    save(hid_t, hid_t_out)
    save(norm_one, norm_out)
    save(inv_one, inv_out)
    small[0:4, :] = jnp.zeros((4, width), wide)
    small[4:5, :] = column_sum(mask * toks * toks)
    small[5:6, :] = column_sum(mask * branch * branch)
    small[6:7, :] = column_sum(mask * hidden * hidden)
    small[8:16, :] = jnp.zeros((8, width), wide)
    small[8:9, :] = jnp.broadcast_to(jnp.sum(mask, 0, keepdims=True), (1, width))
    tile = 512

    def glu(j):
        cols = pl.ds(pl.multiple_of(j * tile, tile), tile)
        h = hid_low[...]
        gate = dot(h, w_g[0, :, :, cols].reshape(width, tile))
        up = dot(h, w_g[1, :, :, cols].reshape(width, tile))
        cdf = 0.5 + 0.5 * lax.erf(gate * 0.7071067811865476)
        mixed = gate * cdf
        density = 0.3989422804014327 * jnp.exp(-0.5 * gate * gate)
        slope_up[:, cols] = mixed.astype(low)
        slope_gate[:, cols] = (up * (cdf + gate * density)).astype(low)
        act[:, cols] = (mixed * up).astype(low)

    upto(second)
    second.from_sib()
    go(1)
    save(w_g.at[:, :, :, :half_g], g_full.at[:, :, :, :half_g])

    @pl.loop(0, half_g // tile)
    def _(j):
        glu(j)

    third.from_sib()
    save(w_g.at[:, :, :, half_g:], g_full.at[:, :, :, half_g:])
    for src, dst in ((slope_gate, gate_out), (slope_up, up_out), (act, act_out)):
        save(src.at[:, :half_g], dst.at[:, :half_g])

    @pl.loop(half_g // tile, ff // tile)
    def _(j):
        glu(j)

    for src, dst in ((slope_gate, gate_out), (slope_up, up_out), (act, act_out)):
        save(src.at[:, half_g:], dst.at[:, half_g:])
    upto(fourth)
    fourth.from_sib()
    save(w_d, d_full)
    d_hid[...] = jnp.zeros_like(d_hid)
    chips = 4
    deep = 2 * chips * w_d.shape[2]

    @pl.loop(0, 16 // chips)
    def _(j):
        cols = pl.ds(pl.multiple_of(j * deep, deep), deep)
        d_hid[...] += dot(act[:, cols], w_d[pl.ds(j * chips, chips)].reshape(deep, width))

    branch = d_hid[...]
    small[7:8, :] = column_sum(mask * branch * branch)
    norm, inverse = normalized(hid[...] + branch)
    gain = vectors[2:3, :]
    output[...] = (norm * gain + vectors[3:4, :]).astype(low)
    save(output, output_out)
    load.wait()
    grad = grad_v[...].astype(wide)
    small[2:3, :] = column_sum(grad * norm)
    small[3:4, :] = column_sum(grad)
    back = norm_back(grad, gain, norm, inverse)
    d_hid[...] = back
    d_branch[...] = back.astype(low)
    save(d_hid, d_hid_out)
    save(d_branch, d_branch_out)
    for i, (src, dst) in enumerate(saved):
        pltpu.make_async_copy(src, dst, out_sem.at[i]).wait()
    for i, ref in enumerate((a_give, g_give, k.at[half], v.at[half])):
        swaps.sent(ref, i, place.sib)
    for m in mats:
        m.drain()


def fore(heads, tokens, labels, w_qkv, w_out, w_gu, d_shard, norms, out_grad):
    low, wide = jnp.bfloat16, jnp.float32
    rows, width = tokens.shape
    ff = w_gu.shape[1] // 2
    half_a = 2 * width + lane_width
    keys = labels.shape[1]
    vmem, hbm = pl.BlockSpec(memory_space=pltpu.VMEM), pl.BlockSpec(memory_space=pl.ANY)
    dma = lambda *shape: pltpu.SemaphoreType.DMA(shape)
    shape = jax.ShapeDtypeStruct
    w_a, w_g, w_d = (2, 16, rows_chip, half_a), (2, 16, rows_chip, ff), (16, 2) + d_shard.shape
    stored = [
        (w_a, low), (w_g, low), (w_d, low), ((rows, width), low), ((keys, width), low), ((keys, width), low),
        ((rows, width), low), ((width, rows), low), ((rows, width), wide), ((rows, lane_width), wide),
        ((rows, ff), low), ((rows, ff), low), ((rows, ff), low), ((rows, width), low), ((rows, width), wide),
        ((rows, width), low), ((keys, rows), wide),
    ]
    block = lambda *dims: pltpu.VMEM(dims, low)
    block_wide = lambda *dims: pltpu.VMEM(dims, wide)
    return pl.pallas_call(
        lambda *refs: fore_kernel(heads, *refs),
        out_shape=tuple(shape(dims, kind) for dims, kind in stored)
        + (shape((16, rows), wide), shape((8, width), wide), shape((16, width), wide)),
        in_specs=[vmem] * 7 + [hbm],
        out_specs=(hbm,) * len(stored) + (vmem,) * 3,
        scratch_shapes=[
            block(*w_a), block(*w_g), block(*w_d), block(32, half_a), block(32, ff), block(32, half_a), block(32, ff),
            block_wide(lane_width, lane_width),
            block(rows, width), block(keys, width), block(keys, width), block(rows, width),
            block_wide(keys, rows), block(rows, width), block_wide(rows, width), block(rows, width),
            block(width, rows), block_wide(rows, width), block_wide(rows, lane_width),
            block(rows, ff), block(rows, ff), block(rows, ff), block(rows, width), block_wide(rows, width),
            block(rows, width), dma(2, 4), dma(8), dma(4 * gather_slots), dma(1), dma(len(stored) + 4),
        ],
        compiler_params=pltpu.CompilerParams(
            collective_id=0, has_side_effects=True, vmem_limit_bytes=62 * 2**20
        ),
        name="gather_and_forward",
    )(tokens, labels, w_qkv, w_out, w_gu, d_shard, norms, out_grad)


def back_kernel(
    heads, tokens, q, k, v, span, att, hid_t, norm, inv, gate, up, act, d_hid, d_branch, a_full, g_full, d_full,
    lse, vectors, small, d_tokens, qkv_out, wout_out, gu_out, down_out, tail, *scratch,
):
    place = Place()
    place.greet()
    c = place.c
    first = c == 0
    low, wide = jnp.bfloat16, jnp.float32
    tok_rows, width = tokens.shape
    ff = gate.shape[1]
    pairs = heads // 2
    bufs, rest = scratch[:33], scratch[33:]
    a_grad, dkv_in, resid, d_att, g_sum, a_sum, g_fin, a_fin, small_buf, send, recv, pair_sem, fin_sem, in_sem, tile_sem = rest
    copies = Copies(send, recv)
    last = Copies(fin_sem.at[0], fin_sem.at[1])
    half_g, part = ff // 2, width // 2

    def scatter(i, own, *more):
        return Scatter(place, copies, i, None, lambda at: own.at[at], *more)

    def projection(i, *more):
        give = lambda four: a_grad.at[i, 1 - c, four]
        own = lambda at: a_grad.at[i, c, at]
        return Scatter(place, copies, 3 + i, give, own, *more, straight=i == 1)

    down, left, right = (scatter(i, *bufs[7 * i : 7 * i + 7]) for i in range(3))
    projs = [projection(i, *bufs[21 + 6 * i : 27 + 6 * i]) for i in range(2)]
    early, late = projs
    planes = (3, 2, 1, 0)
    hops = ((place.sib, 0), (place.xn, 1), (place.yn, 2))

    def exchange(i):
        peer, slot = hops[i]
        last.put(small_buf.at[i], small_buf.at[4 + i], slot, slot, peer)

    def combine(i):
        peer, slot = hops[i]
        last.got(small_buf.at[4 + i], slot, peer)
        small_buf[i + 1] = small_buf[i] + small_buf[4 + i]

    def spread():
        for z in (1, 2, 3):
            last.put(small_buf.at[3], small_buf.at[6 + z], 2 + z, 2 + z, place.zn[z])

    tile = 256

    def feed_forward(given, act_v, db, ht, w_gu, w_dn, gate_v, up_v, att_v, norm_v, inv_v, w_out):
        for i, m in enumerate((down, left, right)):
            m.give = lambda four, i=i: given.at[i % 2, four]
        load = lambda i, src, dst: pltpu.make_async_copy(src, dst, in_sem.at[i])
        loads = [
            load(0, d_branch, db), load(1, hid_t, ht), load(2, d_hid, resid), load(3, att, att_v),
            load(4, norm, norm_v), load(5, inv, inv_v), load(6, a_full.at[1, :, :, width : 2 * width], w_out),
        ]

        def act_load(i, z):
            cols = pl.ds(pl.multiple_of(place.plane(z) * width, width), width)
            return load(7 + i % 2, act.at[:, cols], act_v.at[i % 2])

        def fetch(j):
            slot = j % 2
            cols = pl.ds(pl.multiple_of(j * tile, tile), tile)
            return [
                pltpu.make_async_copy(g_full.at[:, :, :, cols], w_gu.at[slot], tile_sem.at[0, slot]),
                pltpu.make_async_copy(d_full.at[cols], w_dn.at[slot], tile_sem.at[1, slot]),
                pltpu.make_async_copy(gate.at[:, cols], gate_v.at[slot], tile_sem.at[2, slot]),
                pltpu.make_async_copy(up.at[:, cols], up_v.at[slot], tile_sem.at[3, slot]),
            ]

        loads[0].start()
        act_load(0, planes[0]).start()
        act_load(1, planes[1]).start()
        for copy in loads[1:] + fetch(0):
            copy.start()
        loads[0].wait()
        own_d = bufs[0]
        for i, z in enumerate(planes):
            act_load(i, z).wait()
            term = dot(act_v[i % 2].T, db[...]).astype(low).reshape(4, 2, 2, rows_chip, width)
            if i < 2:
                act_load(i + 2, planes[i + 2]).start()
            four = pl.ds(place.plane(z) * 4, 4)
            mine = jnp.where(first, term[:, 0], term[:, 1])
            other = jnp.where(first, term[:, 1], term[:, 0])
            for j in range(2):
                cols = slice(j * width, (j + 1) * width)
                bufs[0][four, :, cols] = mine[:, j]
                given[0, four, :, cols] = other[:, j]
            if i == 0:
                place.meet()
            down.begin(z)
            if i > 1:
                down.pair(planes[i - 2])
        down.all("pair", 1, 0)
        for copy in loads[1:3]:
            copy.wait()

        def between(i, todo):
            for at, *work in todo:

                @pl.when(i == at)
                def _(work=work):
                    for step in work:
                        step()

        def tiles(begin, own_g, give_g, todo):
            @pl.loop(begin, begin + half_g // tile)
            def _(j):
                slot = j % 2
                for copy in fetch(j):
                    copy.wait()

                @pl.when(j + 1 < ff // tile)
                def _():
                    for copy in fetch(j + 1):
                        copy.start()

                d_act = dot(db[...], w_dn[slot], ((1,), (1,)))
                d_gate = (d_act * gate_v[slot].astype(wide)).astype(low)
                d_up = (d_act * up_v[slot].astype(wide)).astype(low)
                resid[...] += dot(d_gate, w_gu[slot, 0].reshape(width, tile), ((1,), (1,))) + dot(
                    d_up, w_gu[slot, 1].reshape(width, tile), ((1,), (1,))
                )
                cols = pl.ds(pl.multiple_of((j - begin) * tile, tile), tile)
                mine = dot(ht[...], jnp.where(first, d_gate, d_up)).astype(low)
                own_g[:, :, cols] = mine.reshape(16, rows_chip, tile)
                other = dot(ht[...], jnp.where(first, d_up, d_gate)).astype(low)
                give_g[:, :, cols] = other.reshape(16, rows_chip, tile)
                between(j - begin, todo)

        tiles(0, bufs[7], given.at[1], [(5, down.diags)])
        for z in planes:
            left.begin(z)
        down.given()
        tiles(half_g // tile, bufs[14], given.at[0], [(2, down.relays, left.first, left.rest), (5, down.odd)])
        for z in planes:
            right.begin(z)
        for copy in loads[3:]:
            copy.wait()
        grad = resid[...]
        unit = norm_v[...]
        small_buf[0] = small[...]
        small_buf[0, 0:1, :] = column_sum(grad * unit)
        small_buf[0, 1:2, :] = column_sum(grad)
        exchange(0)
        back = norm_back(grad, vectors[0:1, :], unit, inv_v[:, 0:1])
        resid[...] = back
        d_one = back.astype(low)
        d_att[...] = dot(d_one, w_out[...].reshape(width, width), ((1,), (1,))).astype(low)
        grad_out = dot(att_v[...].T, d_one).astype(low).reshape(16, rows_chip, width)
        for i in range(2):
            a_grad[i, 1, :, :, part:] = grad_out[:, :, i * part : (i + 1) * part]
        left.diags()
        right.first()
        right.rest()
        left.given()
        right.given()

    block = lambda *dims: pltpu.VMEM(dims, low)
    block_wide = lambda *dims: pltpu.VMEM(dims, wide)
    pl.run_scoped(
        feed_forward, block(2, *bufs[0].shape), block(2, tok_rows, width),
        block(tok_rows, width), block(width, tok_rows), block(2, 2, 16, rows_chip, tile), block(2, tile, width),
        block(2, tok_rows, tile), block(2, tok_rows, tile), block(tok_rows, width), block_wide(tok_rows, width),
        block_wide(tok_rows, lane_width), block(16, rows_chip, width),
    )

    half = lambda side: pl.ds(pl.multiple_of(side * tok_rows, tok_rows), tok_rows)

    def attention_part(dq, dkv_own, dkv_out, x_t, d_k, d_v):
        slots = dkv_own.shape[0]

        def send_dkv(pair):
            return pltpu.make_async_remote_copy(
                src_ref=dkv_out.at[pair], dst_ref=dkv_in.at[pair], send_sem=pair_sem.at[0, pair],
                recv_sem=pair_sem.at[1, pair], device_id=place.sib, device_id_type=MESH,
            )

        def project(i):
            for pair in range(i * pairs // 2, (i + 1) * pairs // 2):
                send_dkv(pair).wait_recv()
                at = slice(pair * lane_width, (pair + 1) * lane_width)
                for j, dst in enumerate((d_k, d_v)):
                    dst[:, at] = (dkv_own[pair % slots, j] + dkv_in[pair, j].astype(wide)).astype(low)
            cols = slice(i * part, (i + 1) * part)
            for side, at, src in ((0, 0, dq), (0, part, d_k), (1, 0, d_v)):
                term = dot(x_t[...], src[:, cols]).astype(low)
                a_grad[i, side, :, :, at : at + part] = term.reshape(16, rows_chip, part)
            for z in planes:
                projs[i].begin(z)

        def attention(q_v, k_v, v_v, span_v, att_v, x, dk_sum, dv_sum):
            load = lambda i, src, dst: pltpu.make_async_copy(src, dst, in_sem.at[i])
            sources = ((q, q_v), (k, k_v), (v, v_v), (att, att_v))
            head, rest = slice(0, lane_width), slice(lane_width, width)
            loads = [load(0, span, span_v)]
            loads += [load(1 + i, src.at[:, head], dst.at[:, head]) for i, (src, dst) in enumerate(sources)]
            later = [load(5 + i, src.at[:, rest], dst.at[:, rest]) for i, (src, dst) in enumerate(sources)]
            later.append(load(9, tokens, x))
            for copy in loads + later:
                copy.start()
            for copy in loads:
                copy.wait()

            def arrive():
                for i, (src, dst) in enumerate(sources):
                    load(5 + i, src.at[:, rest], dst.at[:, rest]).wait()
                load(9, tokens, x).wait()
                x_t[...] = x[...].T

            def meet_small(i):
                combine(i)
                exchange(i + 1)

            def heads_back(begin, end, todo):
                @pl.loop(begin, end)
                def _(pair):
                    attend_back_pair(pair, heads, q_v, k_v, v_v, span_v, lse, att_v, d_att, dq, dk_sum, dv_sum)
                    for i, side in enumerate((dk_sum, dv_sum)):
                        dkv_own[lax.rem(pair, slots), i] = side[half(c), :]
                        dkv_out[pair, i] = side[half(1 - c), :].astype(low)
                    send_dkv(pair).start()
                    for at, *work in todo:

                        @pl.when(pair == at)
                        def _(at=at, work=work):
                            for step in work:
                                step()

            small_step = lambda i: lambda: meet_small(i)
            heads_back(0, 4, [
                (0, arrive, down.even, small_step(0)), (1, left.odd), (2, left.relays, right.diags), (3, right.odd),
            ])
            project(0)
            heads_back(4, pairs, [(4, left.even, early.first, early.rest, small_step(1)), (5, right.relays)])
            project(1)

        key_rows = k.shape[0]
        pl.run_scoped(
            attention, block(*q.shape), block(*k.shape), block(*v.shape), block_wide(*span.shape), block(*att.shape),
            block(tok_rows, width), block_wide(key_rows, lane_width), block_wide(key_rows, lane_width),
        )

        def meet_last():
            combine(2)
            spread()

        def finish(w_left, w_right):
            loads = [
                pltpu.make_async_copy(a_full.at[0, :, :, : 2 * width], w_left, in_sem.at[0]),
                pltpu.make_async_copy(a_full.at[1, :, :, :width], w_right, in_sem.at[1]),
            ]
            for copy in loads:
                copy.start()
            for copy in loads:
                copy.wait()
            w_q = w_left[:, :, :width].reshape(width, width)
            total = resid[...] + dot(dq[...], w_q, ((1,), (1,)))
            early.diags()
            late.first()
            late.rest()
            right.even()
            meet_last()
            w_k = w_left[:, :, width:].reshape(width, width)
            total += dot(d_k[...], w_k, ((1,), (1,)))
            early.relays()
            late.diags()
            early.odd()
            total += dot(d_v[...], w_right[...].reshape(width, width), ((1,), (1,)))
            d_tokens[...] = total.astype(low)
            late.relays()
            early.even()
            late.odd()

        pl.run_scoped(finish, block(16, rows_chip, 2 * width), block(16, rows_chip, width))

        @pl.loop(0, pairs)
        def _(pair):
            send_dkv(pair).wait_send()

    pl.run_scoped(
        attention_part, block(tok_rows, width), block_wide(4, 2, tok_rows, lane_width),
        block(pairs, 2, tok_rows, lane_width), block(width, tok_rows), block(tok_rows, width), block(tok_rows, width),
    )
    mine, theirs = pl.ds(pl.multiple_of(24 * c, 8), 24), pl.ds(pl.multiple_of(24 - 24 * c, 8), 24)
    total = down.total()
    down_out[:rows_chip] = total[:, :width]
    down_out[rows_chip:] = total[:, width:]

    def swap(i, m, total, other, slot):
        total[i] = m.total()
        last.put(total.at[i, theirs], other.at[i], slot, slot, place.sib)

    swap(0, left, g_sum, g_fin, 6)
    swap(1, right, g_sum, g_fin, 7)
    late.even()
    swap(0, early, a_sum, a_fin, 8)
    for z in (1, 2, 3):
        last.got(small_buf.at[6 + z], 2 + z, place.zn[z])
    sums = (small_buf[3] + small_buf[7]) + (small_buf[8] + small_buf[9])
    share = width // 32
    at_row = (lax.axis_index("rows") * 2 + c) * share
    tail[0:8, :] = pltpu.roll(sums[:8], lax.rem(width - at_row, width), 1)[:, :lane_width]
    squares = jnp.sum(sums[:8], 1, keepdims=True) / (sums[8:9, 0:1] * width)
    at = lambda axis: lax.broadcasted_iota(jnp.int32, (8, lane_width), axis)
    stats = jnp.where(at(0) == at(1) + 4, jnp.broadcast_to(jnp.sqrt(squares), (8, lane_width)), 0.0)
    tail[8:16, :] = jnp.broadcast_to(column_sum(stats), (8, lane_width))
    for i in range(2):
        last.got(g_fin.at[i], 6 + i, place.sib)
        own, other = g_sum[i, mine], g_fin[i]
        gu_out[:, i * half_g : (i + 1) * half_g] = jnp.where(first, own, other)
        gu_out[:, (i + 2) * half_g : (i + 3) * half_g] = jnp.where(first, other, own)
    swap(1, late, a_sum, a_fin, 9)
    for i in range(2):
        last.got(a_fin.at[i], 8 + i, place.sib)
        own, other = a_sum[i, mine], a_fin[i]
        qk, vo = jnp.where(first, own, other), jnp.where(first, other, own)
        for j, term in enumerate((qk[:, :part], qk[:, part:], vo[:, :part])):
            at = j * width + i * part
            qkv_out[:, at : at + part] = term
        wout_out[:, i * part : (i + 1) * part] = vo[:, part:]
    for m in (down, left, right, early, late):
        m.drain()
    for m in (early, late):
        m.given()
    sent = [small_buf.at[0]] * 6 + [g_fin.at[0]] * 2 + [a_fin.at[0]] * 2
    for slot, ref in enumerate(sent):
        last.sent(ref, slot, place.sib)


def back(
    heads, tokens, q, k, v, span, att, hid_t, norm, inv, gate, up, act, d_hid, d_branch, a_full, g_full, d_full,
    lse, vectors, small,
):
    low, wide = jnp.bfloat16, jnp.float32
    tok_rows, width = tokens.shape
    ff = gate.shape[1]
    half_g = ff // 2
    pairs = heads // 2
    d_rows = ff // 32
    bufs = []
    for i, cols in enumerate((2 * width, half_g, half_g, width, width)):
        bufs += [pltpu.VMEM((count, rows_chip, cols), low) for count in (16, 16, 2, 2, 4, 4, 3)[i >= 3 :]]
    vmem, hbm = pl.BlockSpec(memory_space=pltpu.VMEM), pl.BlockSpec(memory_space=pl.ANY)
    dma = lambda *shape: pltpu.SemaphoreType.DMA(shape)
    shape = jax.ShapeDtypeStruct
    return pl.pallas_call(
        lambda *refs: back_kernel(heads, *refs),
        out_shape=(
            shape((tok_rows, width), low), shape((24, 3 * width), wide), shape((24, width), wide),
            shape((24, 2 * ff), wide), shape((d_rows, width), wide), shape((16, lane_width), wide),
        ),
        in_specs=[hbm] * 17 + [vmem] * 3,
        out_specs=(vmem,) * 6,
        scratch_shapes=bufs
        + [
            pltpu.VMEM((2, 2, 16, rows_chip, width), low),
            pltpu.VMEM((pairs, 2, tok_rows, lane_width), low),
            pltpu.VMEM((tok_rows, width), wide),
            pltpu.VMEM((tok_rows, width), low),
            pltpu.VMEM((2, rows_chip, half_g), wide),
            pltpu.VMEM((2, rows_chip, width), wide),
            pltpu.VMEM((2, 24, half_g), wide),
            pltpu.VMEM((2, 24, width), wide),
            pltpu.VMEM((10,) + small.shape, wide),
            dma(10),
            dma(5 * scatter_slots),
            dma(2, pairs),
            dma(2, 10),
            dma(10),
            dma(4, 2),
        ],
        compiler_params=pltpu.CompilerParams(
            collective_id=1, has_side_effects=True, vmem_limit_bytes=63 * 2**20
        ),
        name="backward_and_sums",
    )(tokens, q, k, v, span, att, hid_t, norm, inv, gate, up, act, d_hid, d_branch, a_full, g_full, d_full, lse, vectors, small)


def close_kernel(share, *refs):
    parts, tail, outs = refs[:6], refs[6], refs[7:]
    for part, out in zip(parts, outs):
        out[...] = part[...]
    for i, out in enumerate(outs[6:10]):
        out[...] = tail[i : i + 1, :share]
    outs[10][...] = tail[8:9, :4]


def close(share, *parts):
    vmem = pl.BlockSpec(memory_space=pltpu.VMEM)
    wide = jnp.float32
    return pl.pallas_call(
        lambda *refs: close_kernel(share, *refs),
        out_shape=tuple(jax.ShapeDtypeStruct(part.shape, part.dtype) for part in parts[:6])
        + (jax.ShapeDtypeStruct((1, share), wide),) * 4
        + (jax.ShapeDtypeStruct((1, 4), wide),),
        in_specs=[vmem] * 7,
        out_specs=(vmem,) * 11,
        compiler_params=pltpu.CompilerParams(vmem_limit_bytes=62 * 2**20),
        name="results",
    )(*parts)


def window(cells, width):
    count = lax.axis_size("blk")
    before = lax.ppermute(cells, "blk", [(i, i + 1) for i in range(count - 1)])
    after = lax.ppermute(cells, "blk", [(i + 1, i) for i in range(count - 1)])
    return jnp.concatenate([before, cells, after], 0)


def window_back(terms, width):
    count = lax.axis_size("blk")
    low = jnp.bfloat16
    before = lax.ppermute(terms[2 * width :].astype(low), "blk", [(i, i + 1) for i in range(count - 1)])
    after = lax.ppermute(terms[:width].astype(low), "blk", [(i + 1, i) for i in range(count - 1)])
    return terms[width : 2 * width] + before.astype(terms.dtype) + after.astype(terms.dtype)


def key_spans(labels, first, tok_rows):
    seq_len = labels.shape[0]
    query_pos = first + jnp.arange(tok_rows, dtype=jnp.int32)
    query_labels = lax.dynamic_slice_in_dim(labels, first, tok_rows, 0)
    if seq_len == 2 * tok_rows:
        key_pos, key_labels = jnp.arange(seq_len, dtype=jnp.int32), labels
    else:
        key_pos = first - tok_rows + jnp.arange(3 * tok_rows, dtype=jnp.int32)
        padded = jnp.pad(labels, (tok_rows, tok_rows), constant_values=seq_len)
        key_labels = lax.dynamic_slice_in_dim(padded, first, 3 * tok_rows, 0)
    same = (key_labels[:, None] == query_labels[None, :]) & (key_labels[:, None] != seq_len)
    gap = jnp.abs(key_pos[:, None] - query_pos[None, :])
    return jnp.where(same | (gap == 0), gap.astype(jnp.float32), far)


def on_chip_grid():
    return lax.axis_size("rows") == 16 and lax.axis_size("blk") == 2


def packed_shards(w_qkv, w_out, ln1_gain, ln1_bias, w_gate_up, ln2_gain, ln2_bias):
    width = w_out.shape[1]
    ff = w_gate_up.shape[1] // 2
    table = jnp.stack((ln1_gain, ln1_bias, ln2_gain, ln2_bias), 1)
    table = jnp.pad(table, ((0, 0), (0, lane_width - 4)))
    left = jnp.concatenate([w_qkv[:, : 2 * width], table], 1)
    right = jnp.concatenate([w_qkv[:, 2 * width :], w_out, jnp.zeros_like(table)], 1)
    return jnp.stack([left, right]), jnp.stack([w_gate_up[:, :ff], w_gate_up[:, ff:]])


def on_grid(tokens, labels, w_qkv, w_out, w_gate_up, w_down, norms, out_grad):
    width = tokens.shape[1]
    (
        a_full, g_full, d_full, q, k, v, att, hid_t, norm, inv, gate, up, act, output, d_hid, d_branch, span,
        lse, vectors, small,
    ) = fore(HEADS, tokens, labels, w_qkv, w_out, w_gate_up, w_down, jnp.stack(norms), out_grad)
    parts = back(
        HEADS, tokens, q, k, v, span, att, hid_t, norm, inv, gate, up, act, d_hid, d_branch, a_full, g_full,
        d_full.reshape(-1, width), lse, vectors, small,
    )
    *parts, one, two, three, four, stats = close(norms[0].shape[0], output, *parts)
    rows = [row.reshape(-1) for row in (one, two, three, four)]
    return *parts, rows, stats.reshape(-1)


def on_any(tokens, labels, w_qkv, w_out, w_gate_up, w_down, norms, out_grad):
    both = ("rows", "blk")
    tok_rows, width = tokens.shape
    first = lax.axis_index("blk") * tok_rows
    span = key_spans(labels[0], first, tok_rows)
    here = lax.dynamic_slice_in_dim(labels[0], first, tok_rows, 0)
    valid = (here != labels.shape[1]).astype(jnp.float32)[:, None]
    a_shard, g_shard = packed_shards(w_qkv, w_out, *norms[:2], w_gate_up, *norms[2:])
    low, wide = jnp.bfloat16, jnp.float32
    a_full = lax.all_gather(a_shard, both, axis=1, tiled=True)
    w_gu = lax.all_gather(g_shard, both, axis=1, tiled=True)
    w_dn = lax.all_gather(w_down, both, axis=0, tiled=True)
    vectors = jnp.pad(a_full[0, :, 2 * width : 2 * width + 4].astype(wide).T, ((0, 4), (0, 0)))
    w_qk, w_v = a_full[0, :, : 2 * width], a_full[1, :, :width]
    qk = jnp.dot(tokens, w_qk, preferred_element_type=wide).astype(low)
    v = jnp.dot(tokens, w_v, preferred_element_type=wide).astype(low)
    query = qk[:, :width] * (width // HEADS) ** -0.5
    kv = window(jnp.concatenate([qk[:, width:], v], 1), tok_rows)
    keys, values = kv[:, :width], kv[:, width:]
    attended, lse = attend(query, keys, values, span, HEADS)
    output, d_resid_one, d_att, grad_out, g_grad, d_grad, small = ffn(
        tokens, attended, a_full, vectors, valid, out_grad, w_gu, w_dn
    )
    dq, dk, dv = attend_back(query, keys, values, span, lse, attended, d_att, HEADS)
    dkv = window_back(jnp.concatenate([dk, dv], 1), tok_rows)
    d_qk = jnp.concatenate([dq, dkv[:, :width].astype(low)], 1)
    d_v = dkv[:, width:].astype(low)
    grad_qkv = transposed_times(tokens, jnp.concatenate([d_qk, d_v], 1))
    d_tokens = d_resid_one + times_transposed(d_qk, w_qk) + times_transposed(d_v, w_v)
    share = lambda g, axis: lax.psum_scatter(g.astype(wide), both, scatter_dimension=axis, tiled=True)
    gate, up = share(g_grad, 1)
    small = lax.psum(small, both)
    size = norms[0].shape[0]
    rows = lax.dynamic_slice_in_dim(small[:4], lax.axis_index(both) * size, size, 1)
    stats = jnp.sqrt(jnp.sum(small[4:8], 1) / (small[8, 0] * width))
    return (
        output, d_tokens.astype(low), share(grad_qkv, 0), share(grad_out, 0), jnp.concatenate([gate, up], 1),
        share(d_grad, 0), rows, stats,
    )


def body(
    tokens, segments, w_qkv, w_out, ln1_gain, ln1_bias, w_gate_up, w_down, ln2_gain, ln2_bias, out_grad,
):
    run = on_grid if on_chip_grid() else on_any
    norms = (ln1_gain, ln1_bias, ln2_gain, ln2_bias)
    output, d_tokens, qkv, wout, gate_up, down, rows, stats = run(
        tokens[0], segments, w_qkv, w_out, w_gate_up, w_down, norms, out_grad[0]
    )
    return (
        output[None], d_tokens[None], qkv, wout, rows[0], rows[1], gate_up, down, rows[2], rows[3], stats,
    )


def solution(mesh):
    placed = (
        P("rows", "blk", None),
        P("rows", None),
        P(("rows", "blk"), None),
        P(("rows", "blk"), None),
        P(("rows", "blk")),
        P(("rows", "blk")),
        P(("rows", "blk"), None),
        P(("rows", "blk"), None),
        P(("rows", "blk")),
        P(("rows", "blk")),
        P("rows", "blk", None),
    )
    return jax.shard_map(
        body,
        mesh=mesh,
        in_specs=placed,
        out_specs=(
            P("rows", "blk", None),
            P("rows", "blk", None),
            P(("rows", "blk"), None),
            P(("rows", "blk"), None),
            P(("rows", "blk")),
            P(("rows", "blk")),
            P(("rows", "blk"), None),
            P(("rows", "blk"), None),
            P(("rows", "blk")),
            P(("rows", "blk")),
            P(),
        ),
        check_vma=False,
    )
```

```python
import jax
import jax.numpy as jnp
from jax import lax
from jax.experimental import pallas as pl
from jax.experimental.pallas import tpu as pltpu
from jax.sharding import PartitionSpec as P

HEADS = 12


ln_eps = 1e-12
far = 1e33
lane_width = 128


def times_transposed(left, right):
    return lax.dot_general(
        left, right, (((1,), (1,)), ((), ())), preferred_element_type=jnp.float32
    )


def transposed_times(left, right):
    return lax.dot_general(
        left, right, (((0,), (0,)), ((), ())), preferred_element_type=jnp.float32
    )


MESH = pl.DeviceIdType.MESH


class Place:
    def __init__(self):
        r, self.c = lax.axis_index("rows"), lax.axis_index("blk")
        self.x, self.y, self.z = r % 2, (r // 2) % 2, r // 4
        self.sib = (r, 1 - self.c)
        self.xn = (self.at(0, "x"), self.c)
        self.yn = (self.at(0, "y"), self.c)
        self.zn = {k: (self.at(k, "o"), self.c) for k in (1, 2, 3)}

    def plane(self, k):
        z, low = self.z % 2, self.z // 2
        if k % 2:
            z = 1 - z
        if k // 2:
            low = 1 - low
        return low * 2 + z

    def at(self, k, j):
        x = 1 - self.x if j in "xd" else self.x
        y = 1 - self.y if j in "yd" else self.y
        return self.plane(k) * 4 + y * 2 + x

    def greet(self):
        self.barrier = pltpu.get_barrier_semaphore()
        for peer in (self.sib, self.xn, self.yn, *self.zn.values()):
            pl.semaphore_signal(self.barrier, inc=1, device_id=peer, device_id_type=MESH)

    def meet(self):
        pl.semaphore_wait(self.barrier, 6)


class Copies:
    def __init__(self, send, recv):
        self.send, self.recv = send, recv

    def of(self, src, dst, pool, slot, peer):
        return pltpu.make_async_remote_copy(
            src_ref=src, dst_ref=dst, send_sem=self.send.at[pool], recv_sem=self.recv.at[slot],
            device_id=peer, device_id_type=MESH,
        )

    def put(self, src, dst, pool, slot, peer):
        self.of(src, dst, pool, slot, peer).start()

    def got(self, dst, slot, peer):
        self.of(dst, dst, 0, slot, peer).wait_recv()

    def sent(self, all_of_pool, pool, peer):
        self.of(all_of_pool, all_of_pool, pool, 0, peer).wait_send()


class Gather:
    def __init__(self, place, copies, i, side):
        self.p, self.cp, self.side = place, copies, side
        self.base, self.pool = i * gather_slots, 2 * i

    def slot(self, kind, k=0):
        return self.base + {"z": -1, "x": 3, "y": 7, "d": 11, "s": 15}[kind] + k

    def out(self, half, r):
        return self.side(half).at[r]

    def block(self, k, j):
        return self.out(self.p.c, self.p.at(k, j))

    def send(self, src, dst, slot, peer):
        self.cp.put(src, dst, self.pool, slot, peer)

    def push(self, src, k, j):
        self.cp.put(src, self.block(k, j), self.pool + 1, self.slot("s", k), self.p.sib)

    def to_z(self):
        for k in (1, 2):
            self.send(self.block(0, "o"), self.block(0, "o"), self.slot("z", k), self.p.zn[k])

    def to_xy(self):
        self.spread(self.block(0, "o"), 0)

    def spread(self, src, k):
        dst = self.block(k, "o")
        self.send(src, dst, self.slot("x", k), self.p.xn)
        self.send(src, dst, self.slot("y", k), self.p.yn)
        self.push(src, k, "o")

    def from_z(self, k):
        block = self.block(k, "o")
        self.cp.got(block, self.slot("z", k), self.p.zn[k])
        if k == 2:
            self.send(block, block, self.slot("z", 3), self.p.zn[1])
        self.spread(block, k)

    @staticmethod
    def schedule(mats):
        work = [(mats[0].to_z,)] + [(m.to_xy,) for m in mats[:3]]
        for i, m in enumerate(mats):
            before = mats[i - 1] if i else None
            work.append((m.from_z, 1))
            if i + 1 < len(mats):
                work.append((mats[i + 1].to_z,))
            if before:
                work.append((before.from_xy, 3))
            work += [(m.from_xy, 0), (m.from_z, 2)]
            if before:
                work.append((before.from_d, 2))
            if i + 3 < len(mats):
                work.append((mats[i + 3].to_xy,))
            work += [(m.from_xy, 1), (m.from_z, 3)]
            if before:
                work.append((before.from_d, 1))
            work.append((m.from_d, 0))
            if before:
                work.append((before.from_d, 3))
            work.append((m.from_xy, 2))
        last = mats[-1]
        return work + [(last.from_xy, 3), (last.from_d, 2), (last.from_d, 1), (last.from_d, 3)]

    def from_xy(self, k):
        x, y = self.block(k, "x"), self.block(k, "y")
        self.cp.got(x, self.slot("x", k), self.p.xn)
        if k == 2:
            self.send(x, x, self.slot("d", k), self.p.yn)
        self.cp.got(y, self.slot("y", k), self.p.yn)
        if k == 0:
            self.send(y, y, self.slot("d", k), self.p.xn)
        self.push(x, k, "x")
        self.push(y, k, "y")

    def from_d(self, k):
        block = self.block(k, "d")
        self.cp.got(block, self.slot("d", k), self.p.xn)
        if k % 2 == 0:
            self.send(block, block, self.slot("d", k + 1), self.p.zn[1])
        self.push(block, k, "d")

    def from_sib(self, *planes):
        for k in planes or range(4):
            four = pl.ds(self.p.plane(k) * 4, 4)
            self.cp.got(self.side(1 - self.p.c).at[four], self.slot("s", k), self.p.sib)

    def drain(self):
        side = self.side(self.p.c)
        self.cp.sent(side.at[pl.ds(0, 15)], self.pool, self.p.sib)
        self.cp.sent(side, self.pool + 1, self.p.sib)


class Scatter:
    def __init__(self, place, copies, i, give, own, sib, rly, dia, xin, yin, zin, straight=False, flat=False):
        self.p, self.cp, self.give, self.own = place, copies, give, own
        self.base, self.pool = i * scatter_slots, 2 * i
        self.straight, self.flat = straight, flat
        self.sib, self.rly, self.dia, self.xin, self.yin, self.zin = sib, rly, dia, xin, yin, zin

    def slot(self, kind, k):
        return self.base + {"s": 0, "r": 4, "d": 5, "x": 8, "y": 12, "z": 15}[kind] + k

    def four(self, k):
        return pl.ds(self.p.plane(k) * 4, 4)

    def begin(self, k):
        four = self.four(k)
        self.cp.put(self.give(four), self.sib.at[four], self.pool + 1, self.slot("s", k), self.p.sib)

    def given(self):
        self.cp.sent(self.sib, self.pool + 1, self.p.sib)

    def drain(self):
        self.cp.sent(self.sib.at[pl.ds(0, 15)], self.pool, self.p.sib)

    def to_x(self, own, k):
        self.cp.put(own, self.xin.at[k], self.pool, self.slot("x", k), self.p.xn)

    def to_y(self, own, k):
        self.cp.put(own, self.yin.at[k], self.pool, self.slot("y", k), self.p.yn)

    def both(self, k, j, *more):
        at = self.p.at(k, j)
        own = self.own(at)
        total = own[...] + self.sib[at]
        for ref in more:
            total = total + ref[...]
        own[...] = total
        return own

    def pair(self, k):
        four = self.four(k)
        self.cp.got(self.sib.at[four], self.slot("s", k), self.p.sib)
        if self.flat:
            self.to_relay(self.both(k, "d"), k)
        elif k % 2:
            i = k // 2
            self.cp.put(self.both(k, "d"), self.dia.at[i], self.pool, self.slot("d", 2 * i), self.p.zn[1])
        odd = k % 2 and not self.flat
        if odd or k < 2:
            self.to_x(self.both(k, "x"), k)
        if odd or k >= 2:
            self.to_y(self.both(k, "y"), k)

    def relay_at(self, k):
        return (self.dia if k % 2 else self.rly).at[k // 2]

    def to_relay(self, own, k):
        slot = self.slot("d", k - 1) if k % 2 else self.slot("r", k)
        self.cp.put(own, self.relay_at(k), self.pool, slot, self.p.xn if k < 2 else self.p.yn)

    def diag(self, k):
        i = k // 2
        self.cp.got(self.dia.at[i], self.slot("d", k), self.p.zn[1])
        self.to_relay(self.both(k, "d", self.dia.at[i]), k)

    def relay(self, k):
        rly = self.relay_at(k)
        self.cp.got(rly, self.slot("d", k - 1) if k % 2 else self.slot("r", k), self.p.xn)
        if k < 2:
            self.to_y(self.both(k, "y", rly), k)
        else:
            self.to_x(self.both(k, "x", rly), k)

    def plane(self, k):
        p = self.p
        at = p.at(k, "o")
        self.cp.got(self.xin.at[k], self.slot("x", k), p.xn)
        self.cp.got(self.yin.at[k], self.slot("y", k), p.yn)
        wide = jnp.float32
        own = self.own(at)
        total = (own[...].astype(wide) + self.sib[at].astype(wide)) + (
            self.xin[k].astype(wide) + self.yin[k].astype(wide)
        )
        own[...] = total.astype(jnp.bfloat16)
        if self.straight and k:
            self.to_z(own, k, k)
        elif k % 2:
            self.to_z(own, k, 1)

    def to_z(self, own, k, step):
        self.cp.put(own, self.zin.at[k - 1], self.pool, self.slot("z", k), self.p.zn[step])

    def cross(self):
        self.cp.got(self.zin.at[2], self.slot("z", 3), self.p.zn[1])
        own = self.own(self.p.at(2, "o"))
        own[...] = own[...] + self.zin[2]
        self.to_z(own, 2, 2)

    def all(self, name, *planes):
        for k in planes:
            getattr(self, name)(k)

    def first(self):
        self.all("pair", 3, 1)

    def rest(self):
        self.all("pair", 2, 0)

    def diags(self):
        if not self.flat:
            self.all("diag", 2, 0)

    def relays(self):
        self.all("relay", *((3, 1, 2, 0) if self.flat else (2, 0)))

    def odd(self):
        self.all("plane", 3, 1)

    def even(self):
        self.all("plane", 2, 0)
        if not self.straight:
            self.cross()

    def total(self):
        wide = jnp.float32
        total = self.own(self.p.at(0, "o"))[...].astype(wide)
        for k in (1, 2, 3) if self.straight else (1, 2):
            self.cp.got(self.zin.at[k - 1], self.slot("z", k), self.p.zn[k])
            total = total + self.zin[k - 1].astype(wide)
        return total


rows_chip = 48
gather_slots, scatter_slots = 19, 19


def dot(left, right, dims=((1,), (0,))):
    return lax.dot_general(left, right, (dims, ((), ())), preferred_element_type=jnp.float32)


def row_mean(values):
    return jnp.mean(values, -1, keepdims=True)


def normalized(resid):
    centred = resid - row_mean(resid)
    inverse = lax.rsqrt(row_mean(centred * centred) + ln_eps)
    return centred * inverse, inverse


def norm_back(grad, gain, norm, inverse):
    e = grad * gain
    return inverse * (e - row_mean(e) - norm * row_mean(e * norm))


def column_sum(values):
    return jnp.sum(values, 0, keepdims=True)


def ffn_kernel(
    tokens, attended, w_out, vectors, valid, out_grad, w_gu, w_down,
    output, d_resid_one, d_att, grad_out, grad_gu, grad_down, small,
    hid, hid_low, hid_t, norm_one, inv_one, slope_gate, slope_up, act, total, d_hid, d_branch,
):
    i = pl.program_id(0)
    tiles = pl.num_programs(0) // 2
    low = jnp.bfloat16
    wide = jnp.float32

    @pl.when(i == 0)
    def _():
        branch = dot(attended[...], w_out[0])
        toks = tokens[...].astype(wide)
        norm, inverse = normalized(toks + branch)
        norm_one[...] = norm
        inv_one[...] = inverse
        hidden = norm * vectors[0:1, :] + vectors[1:2, :]
        hid[...] = hidden
        hid_low[...] = hidden.astype(low)
        hid_t[...] = hidden.T.astype(low)
        mask = valid[...]
        small[4:5, :] = column_sum(mask * toks * toks)
        small[5:6, :] = column_sum(mask * branch * branch)
        small[6:7, :] = column_sum(mask * hidden * hidden)
        small[8:16, :] = jnp.zeros((8, small.shape[1]), wide)
        small[8:9, :] = jnp.broadcast_to(jnp.sum(mask, 0, keepdims=True), (1, small.shape[1]))
        total[...] = jnp.zeros_like(total)

    @pl.when(i < tiles)
    def _():
        h = hid_low[...]
        gate = dot(h, w_gu[0])
        up = dot(h, w_gu[1])
        cdf = 0.5 + 0.5 * lax.erf(gate * 0.7071067811865476)
        glu = gate * cdf
        density = 0.3989422804014327 * jnp.exp(-0.5 * gate * gate)
        slope_up[i] = glu
        slope_gate[i] = up * (cdf + gate * density)
        a = (glu * up).astype(low)
        act[i] = a
        total[...] += dot(a, w_down[...])

    @pl.when(i == tiles - 1)
    def _():
        branch = total[...]
        mask = valid[...]
        small[7:8, :] = column_sum(mask * branch * branch)
        norm, inverse = normalized(hid[...] + branch)
        gain = vectors[2:3, :]
        output[...] = (norm * gain + vectors[3:4, :]).astype(low)
        grad = out_grad[...].astype(wide)
        small[2:3, :] = column_sum(grad * norm)
        small[3:4, :] = column_sum(grad)
        back = norm_back(grad, gain, norm, inverse)
        d_hid[...] = back
        d_branch[...] = back.astype(low)

    @pl.when(i >= tiles)
    def _():
        j = i - tiles
        db = d_branch[...]
        grad_down[...] = dot(act[j].T, db).astype(low)
        d_act = dot(db, w_down[...], ((1,), (1,)))
        d_gate = (d_act * slope_gate[j]).astype(low)
        d_up = (d_act * slope_up[j]).astype(low)
        h_t = hid_t[...]
        grad_gu[0] = dot(h_t, d_gate).astype(low)
        grad_gu[1] = dot(h_t, d_up).astype(low)
        d_hid[...] += dot(d_gate, w_gu[0], ((1,), (1,))) + dot(d_up, w_gu[1], ((1,), (1,)))

    @pl.when(i == 2 * tiles - 1)
    def _():
        grad = d_hid[...]
        norm = norm_one[...]
        small[0:1, :] = column_sum(grad * norm)
        small[1:2, :] = column_sum(grad)
        back = norm_back(grad, vectors[0:1, :], norm, inv_one[...])
        d_resid_one[...] = back
        db = back.astype(low)
        grad_out[...] = dot(attended[...].T, db).astype(low)
        d_att[...] = dot(db, w_out[0], ((1,), (1,))).astype(low)


def ffn(tokens, attended, a_full, vectors, valid, out_grad, w_gu, w_down):
    rows, width = tokens.shape
    ff = w_down.shape[0]
    tile = 512
    tiles = ff // tile
    low, wide = jnp.bfloat16, jnp.float32
    whole = lambda *shape: pl.BlockSpec(shape, lambda i: (0,) * len(shape))
    at = lambda i: jnp.where(i < tiles, i, i - tiles)
    late = lambda i: jnp.maximum(i - tiles, 0)
    return pl.pallas_call(
        ffn_kernel,
        grid=(2 * tiles,),
        out_shape=(
            jax.ShapeDtypeStruct((rows, width), low),
            jax.ShapeDtypeStruct((rows, width), wide),
            jax.ShapeDtypeStruct((rows, width), low),
            jax.ShapeDtypeStruct((width, width), low),
            jax.ShapeDtypeStruct((2, width, ff), low),
            jax.ShapeDtypeStruct((ff, width), low),
            jax.ShapeDtypeStruct((16, width), wide),
        ),
        in_specs=[
            whole(rows, width),
            whole(rows, width),
            pl.BlockSpec((1, width, width), lambda i: (1, 0, 1)),
            whole(8, width),
            whole(rows, 1),
            whole(rows, width),
            pl.BlockSpec((2, width, tile), lambda i: (0, 0, at(i))),
            pl.BlockSpec((tile, width), lambda i: (at(i), 0)),
        ],
        out_specs=(
            whole(rows, width),
            whole(rows, width),
            whole(rows, width),
            whole(width, width),
            pl.BlockSpec((2, width, tile), lambda i: (0, 0, late(i))),
            pl.BlockSpec((tile, width), lambda i: (late(i), 0)),
            whole(16, width),
        ),
        scratch_shapes=[
            pltpu.VMEM((rows, width), wide),
            pltpu.VMEM((rows, width), low),
            pltpu.VMEM((width, rows), low),
            pltpu.VMEM((rows, width), wide),
            pltpu.VMEM((rows, 1), wide),
            pltpu.VMEM((tiles, rows, tile), wide),
            pltpu.VMEM((tiles, rows, tile), wide),
            pltpu.VMEM((tiles, rows, tile), low),
            pltpu.VMEM((rows, width), wide),
            pltpu.VMEM((rows, width), wide),
            pltpu.VMEM((rows, width), low),
        ],
        compiler_params=pltpu.CompilerParams(vmem_limit_bytes=60 * 2**20),
        cost_estimate=pl.CostEstimate(
            flops=2 * rows * width * (9 * ff + 3 * width), bytes_accessed=18 * ff * width, transcendentals=2 * rows * ff
        ),
        name="feed_forward",
    )(tokens, attended, a_full, vectors, valid, out_grad, w_gu, w_down)


def half_of(block, axis, second):
    place = lax.broadcasted_iota(jnp.int32, block.shape, axis)
    depth = block.shape[axis] // 2
    keep = place >= depth if second else place < depth
    return jnp.where(keep, block, jnp.zeros_like(block))


def attend_kernel(heads, q, k, v, span, attended, lse):
    @pl.loop(0, heads // 2)
    def _(pair):
        attend_pair(pair, heads, q, k, v, span, lse, attended)


def attend(q, k, v, span, heads):
    rows, width = q.shape
    keys = k.shape[0]
    low, wide = jnp.bfloat16, jnp.float32
    return pl.pallas_call(
        lambda *refs: attend_kernel(heads, *refs),
        out_shape=(
            jax.ShapeDtypeStruct((rows, width), low),
            jax.ShapeDtypeStruct((16, rows), wide),
        ),
        in_specs=[pl.BlockSpec(memory_space=pltpu.VMEM)] * 4,
        out_specs=(pl.BlockSpec(memory_space=pltpu.VMEM),) * 2,
        compiler_params=pltpu.CompilerParams(vmem_limit_bytes=60 * 2**20),
        cost_estimate=pl.CostEstimate(flops=4 * rows * keys * width, bytes_accessed=8 * keys * width, transcendentals=heads * rows * keys),
        name="attend",
    )(q, k, v, span)


def attend_back_pair(pair, heads, q, k, v, span, lse, att, d_att, dq, dk_sum, dv_sum):
    low, wide = jnp.bfloat16, jnp.float32
    rows, width = q.shape
    lanes = lane_width
    depth = width // heads
    chunk = 256
    scale = depth**-0.5
    at = pl.ds(pl.multiple_of(pair * lanes, lanes), lanes)
    keys, values = k[:, at], v[:, at]
    keys_t = keys.astype(wide).T.astype(low)
    for c in range(rows // chunk):
        here = pl.ds(c * chunk, chunk)
        q_wide = q[here, at].astype(wide)
        do_here = d_att[here, at]
        do_wide = do_here.astype(wide)
        q_here = q_wide.astype(low)
        q_t, do_t = q_wide.T.astype(low), do_wide.T.astype(low)
        both_t = (do_wide * att[here, at].astype(wide)).T
        dk_part, dv_part, dq_parts = None, None, []
        for h in (0, 1):
            head = 2 * pair + h
            own = slice(h * depth, (h + 1) * depth)
            slope = jnp.exp2(jnp.full((1, 1), -8.0 / heads, wide) * (head + 1).astype(wide))
            delta = jnp.sum(both_t[own], 0, keepdims=True)
            logits = dot(keys, half_of(q_t, 0, h)) - slope * span[:, here]
            probs = jnp.exp(logits - lse[pl.ds(head, 1), here])
            d_probs = dot(values, half_of(do_t, 0, h))
            d_logits = (probs * (d_probs - delta)).astype(low)
            dv_term = dot(probs.astype(low), half_of(do_here, 1, h))
            dk_term = dot(d_logits, half_of(q_here, 1, h))
            dv_part = dv_term if dv_part is None else dv_part + dv_term
            dk_part = dk_term if dk_part is None else dk_part + dk_term
            dq_parts.append(dot(keys_t[own], d_logits) * scale)
        if c == 0:
            dk_sum[...] = dk_part
            dv_sum[...] = dv_part
        else:
            dk_sum[...] += dk_part
            dv_sum[...] += dv_part
        dq[here, at] = jnp.concatenate(dq_parts, 0).T.astype(low)


def attend_back_kernel(heads, q, k, v, span, lse, att, d_att, dq, dk, dv, dk_sum, dv_sum):
    @pl.loop(0, heads // 2)
    def _(pair):
        attend_back_pair(pair, heads, q, k, v, span, lse, att, d_att, dq, dk_sum, dv_sum)
        at = pl.ds(pl.multiple_of(pair * lane_width, lane_width), lane_width)
        dk[:, at] = dk_sum[...]
        dv[:, at] = dv_sum[...]


def attend_back(q, k, v, span, lse, att, d_att, heads):
    rows, width = q.shape
    keys = k.shape[0]
    low, wide = jnp.bfloat16, jnp.float32
    return pl.pallas_call(
        lambda *refs: attend_back_kernel(heads, *refs),
        out_shape=(
            jax.ShapeDtypeStruct((rows, width), low),
            jax.ShapeDtypeStruct((keys, width), wide),
            jax.ShapeDtypeStruct((keys, width), wide),
        ),
        in_specs=[pl.BlockSpec(memory_space=pltpu.VMEM)] * 7,
        out_specs=(pl.BlockSpec(memory_space=pltpu.VMEM),) * 3,
        scratch_shapes=[
            pltpu.VMEM((keys, lane_width), wide),
            pltpu.VMEM((keys, lane_width), wide),
        ],
        compiler_params=pltpu.CompilerParams(vmem_limit_bytes=60 * 2**20),
        cost_estimate=pl.CostEstimate(flops=10 * rows * keys * width, bytes_accessed=16 * keys * width, transcendentals=heads * rows * keys),
        name="attend_back",
    )(q, k, v, span, lse, att, d_att)


def attend_pair(pair, heads, q, k, v, span, lse, attended):
    low, wide = jnp.bfloat16, jnp.float32
    rows, width = q.shape
    lanes = lane_width
    depth = width // heads
    chunk = 256
    at = pl.ds(pl.multiple_of(pair * lanes, lanes), lanes)
    keys = k[:, at]
    values_t = v[:, at].astype(wide).T.astype(low)
    for c in range(rows // chunk):
        here = pl.ds(c * chunk, chunk)
        q_t = q[here, at].astype(wide).T.astype(low)
        parts = []
        for h in (0, 1):
            head = 2 * pair + h
            slope = jnp.exp2(jnp.full((1, 1), -8.0 / heads, wide) * (head + 1).astype(wide))
            logits = dot(keys, half_of(q_t, 0, h)) - slope * span[:, here]
            top = jnp.max(logits, 0, keepdims=True)
            weights = jnp.exp(logits - top)
            norm = jnp.sum(weights, 0, keepdims=True)
            lse[pl.ds(head, 1), here] = top + jnp.log(norm)
            parts.append(dot(values_t[h * depth : (h + 1) * depth], weights.astype(low)) / norm)
        attended[here, at] = jnp.concatenate(parts, 0).T.astype(low)


def fore_kernel(
    heads, tokens, labels, w_qkv, w_out, w_gu, d_shard, norms, out_grad,
    a_full, g_full, d_full, q_out, k_out, v_out, att_out, hid_t_out, norm_out, inv_out, gate_out, up_out, act_out,
    output_out, d_hid_out, d_branch_out, span_out, lse, vectors, small,
    w_a, w_g, w_d, a_give, g_give, a_pair, g_pair, turned, q, k, v, att, span_v, grad_v, hid, hid_low, hid_t, norm_one, inv_one,
    slope_gate, slope_up, act, output, d_hid, d_branch, pair_sem, send, recv, in_sem, out_sem,
):
    place = Place()
    place.greet()
    c = place.c
    low, wide = jnp.bfloat16, jnp.float32
    tok_rows, width = tokens.shape
    ff = w_g.shape[3]
    half_g = ff // 2
    pairs = heads // 2
    load = pltpu.make_async_copy(out_grad, grad_v, in_sem.at[0])
    load.start()
    core_one = c == 1
    turned[...] = jnp.zeros_like(turned)
    turned[0:4, 0 : norms.shape[1]] = norms[...].astype(wide)
    table = turned[...].T[: norms.shape[1]].astype(low)
    left = jnp.concatenate([w_qkv[:, : 2 * width], table], 1)
    right = jnp.concatenate([w_qkv[:, 2 * width :], w_out[...], jnp.zeros_like(table)], 1)
    gate, up = w_gu[:, :ff], w_gu[:, ff:]
    rows = w_qkv.shape[0]
    a_give[:rows, :] = jnp.where(core_one, left, right)
    g_give[:rows, :] = jnp.where(core_one, gate, up)
    swaps = Copies(pair_sem.at[0], pair_sem.at[1])
    place.meet()
    for i, (give, other) in enumerate(((a_give, a_pair), (g_give, g_pair))):
        swaps.put(give, other, i, i, place.sib)
    copies = Copies(send, recv)
    sides = [
        lambda half: w_a.at[half],
        lambda half: w_g.at[half, :, :, :half_g],
        lambda half: w_g.at[half, :, :, half_g:],
        lambda half: w_d.at[:, half],
    ]
    mats = [Gather(place, copies, i, side) for i, side in enumerate(sides)]
    first, second, third, fourth = mats
    me = place.at(0, "o")

    def assemble(mine, other, full, i):
        swaps.got(other, i, place.sib)
        mine = mine.astype(wide)
        theirs = other[:rows, :].astype(wide)
        top = jnp.where(core_one, theirs, mine)
        rest = jnp.where(core_one, mine, theirs)
        full[c, me] = jnp.concatenate([top, rest], 0).astype(low)

    work = Gather.schedule(mats)

    def go(count):
        for step, *plane in work[:count]:
            step(*plane)
        del work[:count]

    def upto(matrix):
        done = [i for i, (step, *_) in enumerate(work) if step == matrix.from_d]
        go(done[-1] + 1 if done else 0)

    assemble(jnp.where(core_one, right, left), a_pair, w_a, 0)
    go(2)
    assemble(jnp.where(core_one, up, gate), g_pair, w_g, 1)
    w_d[me, c] = d_shard[...]
    seq_len = labels.shape[1]
    label_row = labels[...].astype(wide)
    label_column = jnp.broadcast_to(label_row, (lane_width, seq_len)).T[:, 0:1]
    half = pl.ds(pl.multiple_of(c * tok_rows, tok_rows), tok_rows)
    same = (label_column == labels[:, half].astype(wide)) & (label_column != seq_len)
    key_at = lax.broadcasted_iota(jnp.int32, span_v.shape, 0)
    gap = jnp.abs(key_at - lax.broadcasted_iota(jnp.int32, span_v.shape, 1) - c * tok_rows)
    span_v[...] = jnp.where(same | (gap == 0), gap.astype(wide), far)
    mask = jnp.broadcast_to(labels[:, half].astype(wide), (lane_width, tok_rows)).T[:, 0:1]
    mask = (mask != seq_len).astype(wide)
    upto(first)
    first.from_sib()
    saved = []

    def save(src, dst):
        copy = pltpu.make_async_copy(src, dst, out_sem.at[len(saved)])
        copy.start()
        saved.append((src, dst))

    save(w_a, a_full)
    save(span_v, span_out)
    part = lambda half, at, size: w_a[half, :, :, at : at + size].reshape(width, size)
    vectors[...] = part(0, 2 * width, lane_width).astype(wide).T[:8]
    x = tokens[...]
    k[half, :] = dot(x, part(0, width, width)).astype(low)
    swaps.put(k.at[half], k.at[half], 2, 2, place.sib)
    v[half, :] = dot(x, part(1, 0, width)).astype(low)
    swaps.put(v.at[half], v.at[half], 3, 3, place.sib)
    depth = width // heads
    q[...] = dot(x, part(0, 0, width)).astype(low) * depth**-0.5
    go(3)
    other = pl.ds(pl.multiple_of((1 - c) * tok_rows, tok_rows), tok_rows)
    swaps.got(k.at[other], 2, place.sib)
    swaps.got(v.at[other], 3, place.sib)
    save(q, q_out)
    save(k, k_out)
    save(v, v_out)

    shares = (4, 4, 4, 4, 3, 2)
    todo = []
    for count in shares:
        todo.append(work[:count])
        del work[:count]

    @pl.loop(0, pairs)
    def _(pair):
        attend_pair(pair, heads, q, k, v, span_v, lse, att)
        for at, steps in enumerate(todo):

            @pl.when(pair == at)
            def _(steps=steps):
                for step, *plane in steps:
                    step(*plane)

    save(att, att_out)
    branch = dot(att[...], part(1, width, width))
    toks = x.astype(wide)
    norm, inverse = normalized(toks + branch)
    norm_one[...] = norm
    inv_one[...] = jnp.broadcast_to(inverse, inv_one.shape)
    hidden = norm * vectors[0:1, :] + vectors[1:2, :]
    hid[...] = hidden
    hid_low[...] = hidden.astype(low)
    hid_t[...] = hidden.T.astype(low)
    save(hid_t, hid_t_out)
    save(norm_one, norm_out)
    save(inv_one, inv_out)
    small[0:4, :] = jnp.zeros((4, width), wide)
    small[4:5, :] = column_sum(mask * toks * toks)
    small[5:6, :] = column_sum(mask * branch * branch)
    small[6:7, :] = column_sum(mask * hidden * hidden)
    small[8:16, :] = jnp.zeros((8, width), wide)
    small[8:9, :] = jnp.broadcast_to(jnp.sum(mask, 0, keepdims=True), (1, width))
    tile = 512

    def glu(j):
        cols = pl.ds(pl.multiple_of(j * tile, tile), tile)
        h = hid_low[...]
        gate = dot(h, w_g[0, :, :, cols].reshape(width, tile))
        up = dot(h, w_g[1, :, :, cols].reshape(width, tile))
        cdf = 0.5 + 0.5 * lax.erf(gate * 0.7071067811865476)
        mixed = gate * cdf
        density = 0.3989422804014327 * jnp.exp(-0.5 * gate * gate)
        slope_up[:, cols] = mixed.astype(low)
        slope_gate[:, cols] = (up * (cdf + gate * density)).astype(low)
        act[:, cols] = (mixed * up).astype(low)

    upto(second)
    go(1)
    second.from_sib()
    save(w_g.at[:, :, :, :half_g], g_full.at[:, :, :, :half_g])

    @pl.loop(0, half_g // tile)
    def _(j):
        glu(j)

    go(1)
    third.from_sib()
    save(w_g.at[:, :, :, half_g:], g_full.at[:, :, :, half_g:])
    for src, dst in ((slope_gate, gate_out), (slope_up, up_out), (act, act_out)):
        save(src.at[:, :half_g], dst.at[:, :half_g])

    @pl.loop(half_g // tile, ff // tile)
    def _(j):
        glu(j)

    for src, dst in ((slope_gate, gate_out), (slope_up, up_out), (act, act_out)):
        save(src.at[:, half_g:], dst.at[:, half_g:])

    def down(plane):
        at = place.plane(plane)
        cols = pl.ds(pl.multiple_of(at * width, width), width)
        return dot(act[:, cols], w_d[pl.ds(at * 4, 4)].reshape(width, width))

    go(1)
    fourth.from_sib(0, 2, 1)
    d_hid[...] = down(0)
    for plane in (2, 1):
        d_hid[...] += down(plane)
    upto(fourth)
    fourth.from_sib(3)
    save(w_d, d_full)
    d_hid[...] += down(3)
    branch = d_hid[...]
    small[7:8, :] = column_sum(mask * branch * branch)
    norm, inverse = normalized(hid[...] + branch)
    gain = vectors[2:3, :]
    output[...] = (norm * gain + vectors[3:4, :]).astype(low)
    save(output, output_out)
    load.wait()
    grad = grad_v[...].astype(wide)
    small[2:3, :] = column_sum(grad * norm)
    small[3:4, :] = column_sum(grad)
    back = norm_back(grad, gain, norm, inverse)
    d_hid[...] = back
    d_branch[...] = back.astype(low)
    save(d_hid, d_hid_out)
    save(d_branch, d_branch_out)
    for i, (src, dst) in enumerate(saved):
        pltpu.make_async_copy(src, dst, out_sem.at[i]).wait()
    for i, ref in enumerate((a_give, g_give, k.at[half], v.at[half])):
        swaps.sent(ref, i, place.sib)
    for m in mats:
        m.drain()


def fore(heads, tokens, labels, w_qkv, w_out, w_gu, d_shard, norms, out_grad):
    low, wide = jnp.bfloat16, jnp.float32
    rows, width = tokens.shape
    ff = w_gu.shape[1] // 2
    half_a = 2 * width + lane_width
    keys = labels.shape[1]
    vmem, hbm = pl.BlockSpec(memory_space=pltpu.VMEM), pl.BlockSpec(memory_space=pl.ANY)
    dma = lambda *shape: pltpu.SemaphoreType.DMA(shape)
    shape = jax.ShapeDtypeStruct
    w_a, w_g, w_d = (2, 16, rows_chip, half_a), (2, 16, rows_chip, ff), (16, 2) + d_shard.shape
    stored = [
        (w_a, low), (w_g, low), (w_d, low), ((rows, width), low), ((keys, width), low), ((keys, width), low),
        ((rows, width), low), ((width, rows), low), ((rows, width), wide), ((rows, lane_width), wide),
        ((rows, ff), low), ((rows, ff), low), ((rows, ff), low), ((rows, width), low), ((rows, width), wide),
        ((rows, width), low), ((keys, rows), wide),
    ]
    block = lambda *dims: pltpu.VMEM(dims, low)
    block_wide = lambda *dims: pltpu.VMEM(dims, wide)
    return pl.pallas_call(
        lambda *refs: fore_kernel(heads, *refs),
        out_shape=tuple(shape(dims, kind) for dims, kind in stored)
        + (shape((16, rows), wide), shape((8, width), wide), shape((16, width), wide)),
        in_specs=[vmem] * 7 + [hbm],
        out_specs=(hbm,) * len(stored) + (vmem,) * 3,
        scratch_shapes=[
            block(*w_a), block(*w_g), block(*w_d), block(32, half_a), block(32, ff), block(32, half_a), block(32, ff),
            block_wide(lane_width, lane_width),
            block(rows, width), block(keys, width), block(keys, width), block(rows, width),
            block_wide(keys, rows), block(rows, width), block_wide(rows, width), block(rows, width),
            block(width, rows), block_wide(rows, width), block_wide(rows, lane_width),
            block(rows, ff), block(rows, ff), block(rows, ff), block(rows, width), block_wide(rows, width),
            block(rows, width), dma(2, 4), dma(8), dma(4 * gather_slots), dma(1), dma(len(stored) + 4),
        ],
        compiler_params=pltpu.CompilerParams(
            collective_id=0, has_side_effects=True, vmem_limit_bytes=62 * 2**20
        ),
        name="gather_and_forward",
    )(tokens, labels, w_qkv, w_out, w_gu, d_shard, norms, out_grad)


def back_kernel(
    heads, tokens, q, k, v, span, att, hid_t, norm, inv, gate, up, act, d_hid, d_branch, a_full, g_full, d_full,
    lse, vectors, small, d_tokens, qkv_out, wout_out, gu_out, down_out, tail, *scratch,
):
    place = Place()
    place.greet()
    c = place.c
    first = c == 0
    low, wide = jnp.bfloat16, jnp.float32
    tok_rows, width = tokens.shape
    ff = gate.shape[1]
    pairs = heads // 2
    bufs, rest = scratch[:33], scratch[33:]
    a_grad, dkv_in, resid, d_att, g_sum, a_sum, g_fin, a_fin, small_buf, send, recv, tokens_v, down_v, gu_v, pair_sem, fin_sem, in_sem, tile_sem = rest
    copies = Copies(send, recv)
    last = Copies(fin_sem.at[0], fin_sem.at[1])
    half_g, part = ff // 2, width // 2

    def scatter(i, own, *more):
        return Scatter(place, copies, i, None, lambda at: own.at[at], *more)

    def projection(i, *more):
        give = lambda four: a_grad.at[i, 1 - c, four]
        own = lambda at: a_grad.at[i, c, at]
        return Scatter(place, copies, 3 + i, give, own, *more)

    down, left, right = (scatter(i, *bufs[7 * i : 7 * i + 7]) for i in range(3))
    projs = [projection(i, *bufs[21 + 6 * i : 27 + 6 * i]) for i in range(2)]
    early, late = projs
    planes = (3, 2, 1, 0)
    hand_over = lambda i, src, dst: pltpu.make_async_copy(src, dst, in_sem.at[i])
    hops = ((place.sib, 0), (place.xn, 1), (place.yn, 2))

    def exchange(i):
        peer, slot = hops[i]
        last.put(small_buf.at[i], small_buf.at[4 + i], slot, slot, peer)

    def combine(i):
        peer, slot = hops[i]
        last.got(small_buf.at[4 + i], slot, peer)
        small_buf[i + 1] = small_buf[i] + small_buf[4 + i]

    def spread():
        for z in (1, 2, 3):
            last.put(small_buf.at[3], small_buf.at[6 + z], 2 + z, 2 + z, place.zn[z])

    tile = 256

    def feed_forward(given, act_v, db, ht, w_gu, w_dn, gate_v, up_v, att_v, norm_v, inv_v, w_out):
        for i, m in enumerate((down, left, right)):
            m.give = lambda four, i=i: given.at[i % 2, four]
        load = lambda i, src, dst: pltpu.make_async_copy(src, dst, in_sem.at[i])
        loads = [
            load(0, d_branch, db), load(1, hid_t, ht), load(2, d_hid, resid), load(3, att, att_v),
            load(4, norm, norm_v), load(5, inv, inv_v), load(6, a_full.at[1, :, :, width : 2 * width], w_out),
        ]

        def act_load(i, z):
            cols = pl.ds(pl.multiple_of(place.plane(z) * width, width), width)
            return load(7 + i % 2, act.at[:, cols], act_v.at[i % 2])

        def fetch(j):
            slot = j % 2
            cols = pl.ds(pl.multiple_of(j * tile, tile), tile)
            return [
                pltpu.make_async_copy(g_full.at[:, :, :, cols], w_gu.at[slot], tile_sem.at[0, slot]),
                pltpu.make_async_copy(d_full.at[cols], w_dn.at[slot], tile_sem.at[1, slot]),
                pltpu.make_async_copy(gate.at[:, cols], gate_v.at[slot], tile_sem.at[2, slot]),
                pltpu.make_async_copy(up.at[:, cols], up_v.at[slot], tile_sem.at[3, slot]),
            ]

        loads[0].start()
        act_load(0, planes[0]).start()
        act_load(1, planes[1]).start()
        for copy in loads[1:] + fetch(0):
            copy.start()
        loads[0].wait()
        own_d = bufs[0]
        for i, z in enumerate(planes):
            act_load(i, z).wait()
            term = dot(act_v[i % 2].T, db[...]).astype(low).reshape(4, 2, 2, rows_chip, width)
            if i < 2:
                act_load(i + 2, planes[i + 2]).start()
            four = pl.ds(place.plane(z) * 4, 4)
            mine = jnp.where(first, term[:, 0], term[:, 1])
            other = jnp.where(first, term[:, 1], term[:, 0])
            for j in range(2):
                cols = slice(j * width, (j + 1) * width)
                bufs[0][four, :, cols] = mine[:, j]
                given[0, four, :, cols] = other[:, j]
            if i == 0:
                place.meet()
            down.begin(z)
            if i > 1:
                down.pair(planes[i - 2])
        for copy in loads[1:3]:
            copy.wait()

        def between(i, todo):
            for at, *work in todo:

                @pl.when(i == at)
                def _(work=work):
                    for step in work:
                        step()

        def tiles(begin, own_g, give_g, todo):
            @pl.loop(begin, begin + half_g // tile)
            def _(j):
                slot = j % 2
                for copy in fetch(j):
                    copy.wait()

                @pl.when(j + 1 < ff // tile)
                def _():
                    for copy in fetch(j + 1):
                        copy.start()

                d_act = dot(db[...], w_dn[slot], ((1,), (1,)))
                d_gate = (d_act * gate_v[slot].astype(wide)).astype(low)
                d_up = (d_act * up_v[slot].astype(wide)).astype(low)
                resid[...] += dot(d_gate, w_gu[slot, 0].reshape(width, tile), ((1,), (1,))) + dot(
                    d_up, w_gu[slot, 1].reshape(width, tile), ((1,), (1,))
                )
                cols = pl.ds(pl.multiple_of((j - begin) * tile, tile), tile)
                mine = dot(ht[...], jnp.where(first, d_gate, d_up)).astype(low)
                own_g[:, :, cols] = mine.reshape(16, rows_chip, tile)
                other = dot(ht[...], jnp.where(first, d_up, d_gate)).astype(low)
                give_g[:, :, cols] = other.reshape(16, rows_chip, tile)
                between(j - begin, todo)

        tiles(0, bufs[7], given.at[1], [(0, lambda: down.pair(1)), (1, lambda: down.pair(0)), (5, down.diags)])
        for z in planes:
            left.begin(z)
        down.given()
        tiles(half_g // tile, bufs[14], given.at[0], [(2, down.relays, left.first, left.rest), (5, down.odd)])
        for z in planes:
            right.begin(z)
        for copy in loads[3:]:
            copy.wait()
        grad = resid[...]
        unit = norm_v[...]
        small_buf[0] = small[...]
        small_buf[0, 0:1, :] = column_sum(grad * unit)
        small_buf[0, 1:2, :] = column_sum(grad)
        exchange(0)
        back = norm_back(grad, vectors[0:1, :], unit, inv_v[:, 0:1])
        resid[...] = back
        d_one = back.astype(low)
        d_att[...] = dot(d_one, w_out[...].reshape(width, width), ((1,), (1,))).astype(low)
        grad_out = dot(att_v[...].T, d_one).astype(low).reshape(16, rows_chip, width)
        for i in range(2):
            a_grad[i, 1, :, :, part:] = grad_out[:, :, i * part : (i + 1) * part]
        left.diags()
        right.first()
        right.rest()
        left.given()
        right.given()

    block = lambda *dims: pltpu.VMEM(dims, low)
    block_wide = lambda *dims: pltpu.VMEM(dims, wide)
    pl.run_scoped(
        feed_forward, block(2, *bufs[0].shape), block(2, tok_rows, width),
        block(tok_rows, width), block(width, tok_rows), block(2, 2, 16, rows_chip, tile), block(2, tile, width),
        block(2, tok_rows, tile), block(2, tok_rows, tile), block(tok_rows, width), block_wide(tok_rows, width),
        block_wide(tok_rows, lane_width), block(16, rows_chip, width),
    )

    half = lambda side: pl.ds(pl.multiple_of(side * tok_rows, tok_rows), tok_rows)

    def attention_part(dq, dkv_own, dkv_out, x_t, d_k, d_v):
        slots = dkv_own.shape[0]

        def send_dkv(pair):
            return pltpu.make_async_remote_copy(
                src_ref=dkv_out.at[pair], dst_ref=dkv_in.at[pair], send_sem=pair_sem.at[0, pair],
                recv_sem=pair_sem.at[1, pair], device_id=place.sib, device_id_type=MESH,
            )

        def project(i):
            for pair in range(i * pairs // 2, (i + 1) * pairs // 2):
                send_dkv(pair).wait_recv()
                at = slice(pair * lane_width, (pair + 1) * lane_width)
                for j, dst in enumerate((d_k, d_v)):
                    dst[:, at] = (dkv_own[pair % slots, j] + dkv_in[pair, j].astype(wide)).astype(low)
            cols = slice(i * part, (i + 1) * part)
            for side, at, src in ((0, 0, dq), (0, part, d_k), (1, 0, d_v)):
                term = dot(x_t[...], src[:, cols]).astype(low)
                a_grad[i, side, :, :, at : at + part] = term.reshape(16, rows_chip, part)
            for z in planes:
                projs[i].begin(z)

        def attention(q_v, k_v, v_v, span_v, att_v, x, dk_sum, dv_sum):
            load = lambda i, src, dst: pltpu.make_async_copy(src, dst, in_sem.at[i])
            sources = ((q, q_v), (k, k_v), (v, v_v), (att, att_v))
            head, rest = slice(0, lane_width), slice(lane_width, width)
            loads = [load(0, span, span_v)]
            loads += [load(1 + i, src.at[:, head], dst.at[:, head]) for i, (src, dst) in enumerate(sources)]
            later = [load(5 + i, src.at[:, rest], dst.at[:, rest]) for i, (src, dst) in enumerate(sources)]
            later.append(load(9, tokens, x))
            for copy in loads + later:
                copy.start()
            for copy in loads:
                copy.wait()

            def arrive():
                for i, (src, dst) in enumerate(sources):
                    load(5 + i, src.at[:, rest], dst.at[:, rest]).wait()
                load(9, tokens, x).wait()
                x_t[...] = x[...].T

            def meet_small(i):
                combine(i)
                exchange(i + 1)

            def heads_back(begin, end, todo):
                @pl.loop(begin, end)
                def _(pair):
                    attend_back_pair(pair, heads, q_v, k_v, v_v, span_v, lse, att_v, d_att, dq, dk_sum, dv_sum)
                    for i, side in enumerate((dk_sum, dv_sum)):
                        dkv_own[lax.rem(pair, slots), i] = side[half(c), :]
                        dkv_out[pair, i] = side[half(1 - c), :].astype(low)
                    send_dkv(pair).start()
                    for at, *work in todo:

                        @pl.when(pair == at)
                        def _(at=at, work=work):
                            for step in work:
                                step()

            small_step = lambda i: lambda: meet_small(i)
            heads_back(0, 4, [
                (0, arrive, down.even, small_step(0)), (1, left.odd), (2, left.relays, right.diags), (3, right.odd),
            ])
            project(0)
            heads_back(4, pairs, [(4, left.even, early.first, early.rest, small_step(1)), (5, right.relays)])
            project(1)

        key_rows = k.shape[0]
        pl.run_scoped(
            attention, block(*q.shape), block(*k.shape), block(*v.shape), block_wide(*span.shape), block(*att.shape),
            block(tok_rows, width), block_wide(key_rows, lane_width), block_wide(key_rows, lane_width),
        )

        def meet_last():
            combine(2)
            spread()

        def finish(w_left, w_right):
            loads = [
                pltpu.make_async_copy(a_full.at[0, :, :, : 2 * width], w_left, in_sem.at[0]),
                pltpu.make_async_copy(a_full.at[1, :, :, :width], w_right, in_sem.at[1]),
            ]
            for copy in loads:
                copy.start()
            for copy in loads:
                copy.wait()
            w_q = w_left[:, :, :width].reshape(width, width)
            total = resid[...] + dot(dq[...], w_q, ((1,), (1,)))
            early.diags()
            late.first()
            late.rest()
            right.even()
            meet_last()
            w_k = w_left[:, :, width:].reshape(width, width)
            total += dot(d_k[...], w_k, ((1,), (1,)))
            early.relays()
            late.diags()
            early.odd()
            early.even()
            total += dot(d_v[...], w_right[...].reshape(width, width), ((1,), (1,)))
            tokens_v[...] = total.astype(low)
            hand_over(0, tokens_v, d_tokens).start()
            late.relays()
            late.odd()

        pl.run_scoped(finish, block(16, rows_chip, 2 * width), block(16, rows_chip, width))

        @pl.loop(0, pairs)
        def _(pair):
            send_dkv(pair).wait_send()

    pl.run_scoped(
        attention_part, block(tok_rows, width), block_wide(4, 2, tok_rows, lane_width),
        block(pairs, 2, tok_rows, lane_width), block(width, tok_rows), block(tok_rows, width), block(tok_rows, width),
    )
    mine, theirs = pl.ds(pl.multiple_of(24 * c, 8), 24), pl.ds(pl.multiple_of(24 - 24 * c, 8), 24)
    total = down.total()
    down_v[:rows_chip] = total[:, :width]
    down_v[rows_chip:] = total[:, width:]
    hand_over(1, down_v, down_out).start()

    def swap(i, m, total, other, slot):
        total[i] = m.total()
        last.put(total.at[i, theirs], other.at[i], slot, slot, place.sib)

    swap(0, left, g_sum, g_fin, 6)
    swap(1, right, g_sum, g_fin, 7)
    late.even()
    swap(0, early, a_sum, a_fin, 8)
    for z in (1, 2, 3):
        last.got(small_buf.at[6 + z], 2 + z, place.zn[z])
    sums = (small_buf[3] + small_buf[7]) + (small_buf[8] + small_buf[9])
    share = width // 32
    at_row = (lax.axis_index("rows") * 2 + c) * share
    tail[0:8, :] = pltpu.roll(sums[:8], lax.rem(width - at_row, width), 1)[:, :lane_width]
    squares = jnp.sum(sums[:8], 1, keepdims=True) / (sums[8:9, 0:1] * width)
    at = lambda axis: lax.broadcasted_iota(jnp.int32, (8, lane_width), axis)
    stats = jnp.where(at(0) == at(1) + 4, jnp.broadcast_to(jnp.sqrt(squares), (8, lane_width)), 0.0)
    tail[8:16, :] = jnp.broadcast_to(column_sum(stats), (8, lane_width))
    for i in range(2):
        last.got(g_fin.at[i], 6 + i, place.sib)
        own, other = g_sum[i, mine], g_fin[i]
        gu_v[:, i * half_g : (i + 1) * half_g] = jnp.where(first, own, other)
        gu_v[:, (i + 2) * half_g : (i + 3) * half_g] = jnp.where(first, other, own)
    hand_over(2, gu_v, gu_out).start()
    swap(1, late, a_sum, a_fin, 9)
    for i in range(2):
        last.got(a_fin.at[i], 8 + i, place.sib)
        own, other = a_sum[i, mine], a_fin[i]
        qk, vo = jnp.where(first, own, other), jnp.where(first, other, own)
        for j, term in enumerate((qk[:, :part], qk[:, part:], vo[:, :part])):
            at = j * width + i * part
            qkv_out[:, at : at + part] = term
        wout_out[:, i * part : (i + 1) * part] = vo[:, part:]
    for m in (down, left, right, early, late):
        m.drain()
    for m in (early, late):
        m.given()
    sent = [small_buf.at[0]] * 6 + [g_fin.at[0]] * 2 + [a_fin.at[0]] * 2
    for slot, ref in enumerate(sent):
        last.sent(ref, slot, place.sib)
    for i, pair in enumerate(((tokens_v, d_tokens), (down_v, down_out), (gu_v, gu_out))):
        hand_over(i, *pair).wait()


def back(
    heads, tokens, q, k, v, span, att, hid_t, norm, inv, gate, up, act, d_hid, d_branch, a_full, g_full, d_full,
    lse, vectors, small,
):
    low, wide = jnp.bfloat16, jnp.float32
    tok_rows, width = tokens.shape
    ff = gate.shape[1]
    half_g = ff // 2
    pairs = heads // 2
    d_rows = ff // 32
    bufs = []
    for i, cols in enumerate((2 * width, half_g, half_g, width, width)):
        bufs += [pltpu.VMEM((count, rows_chip, cols), low) for count in (16, 16, 2, 2, 4, 4, 3)[i >= 3 :]]
    vmem, hbm = pl.BlockSpec(memory_space=pltpu.VMEM), pl.BlockSpec(memory_space=pl.ANY)
    dma = lambda *shape: pltpu.SemaphoreType.DMA(shape)
    shape = jax.ShapeDtypeStruct
    return pl.pallas_call(
        lambda *refs: back_kernel(heads, *refs),
        out_shape=(
            shape((tok_rows, width), low), shape((24, 3 * width), wide), shape((24, width), wide),
            shape((24, 2 * ff), wide), shape((d_rows, width), wide), shape((16, lane_width), wide),
        ),
        in_specs=[hbm] * 17 + [vmem] * 3,
        out_specs=(hbm, vmem, vmem, hbm, hbm, vmem),
        scratch_shapes=bufs
        + [
            pltpu.VMEM((2, 2, 16, rows_chip, width), low),
            pltpu.VMEM((pairs, 2, tok_rows, lane_width), low),
            pltpu.VMEM((tok_rows, width), wide),
            pltpu.VMEM((tok_rows, width), low),
            pltpu.VMEM((2, rows_chip, half_g), wide),
            pltpu.VMEM((2, rows_chip, width), wide),
            pltpu.VMEM((2, 24, half_g), wide),
            pltpu.VMEM((2, 24, width), wide),
            pltpu.VMEM((10,) + small.shape, wide),
            dma(10),
            dma(5 * scatter_slots),
            pltpu.VMEM((tok_rows, width), low),
            pltpu.VMEM((d_rows, width), wide),
            pltpu.VMEM((24, 2 * ff), wide),
            dma(2, pairs),
            dma(2, 10),
            dma(10),
            dma(4, 2),
        ],
        compiler_params=pltpu.CompilerParams(
            collective_id=1, has_side_effects=True, vmem_limit_bytes=63 * 2**20
        ),
        name="backward_and_sums",
    )(tokens, q, k, v, span, att, hid_t, norm, inv, gate, up, act, d_hid, d_branch, a_full, g_full, d_full, lse, vectors, small)


def close_kernel(share, *refs):
    parts, tail, outs = refs[:6], refs[6], refs[7:]
    for part, out in zip(parts, outs):
        out[...] = part[...]
    for i, out in enumerate(outs[6:10]):
        out[...] = tail[i : i + 1, :share]
    outs[10][...] = tail[8:9, :4]


def close(share, *parts):
    vmem = pl.BlockSpec(memory_space=pltpu.VMEM)
    wide = jnp.float32
    return pl.pallas_call(
        lambda *refs: close_kernel(share, *refs),
        out_shape=tuple(jax.ShapeDtypeStruct(part.shape, part.dtype) for part in parts[:6])
        + (jax.ShapeDtypeStruct((1, share), wide),) * 4
        + (jax.ShapeDtypeStruct((1, 4), wide),),
        in_specs=[vmem] * 7,
        out_specs=(vmem,) * 11,
        compiler_params=pltpu.CompilerParams(vmem_limit_bytes=62 * 2**20),
        name="results",
    )(*parts)


def window(cells, width):
    count = lax.axis_size("blk")
    before = lax.ppermute(cells, "blk", [(i, i + 1) for i in range(count - 1)])
    after = lax.ppermute(cells, "blk", [(i + 1, i) for i in range(count - 1)])
    return jnp.concatenate([before, cells, after], 0)


def window_back(terms, width):
    count = lax.axis_size("blk")
    low = jnp.bfloat16
    before = lax.ppermute(terms[2 * width :].astype(low), "blk", [(i, i + 1) for i in range(count - 1)])
    after = lax.ppermute(terms[:width].astype(low), "blk", [(i + 1, i) for i in range(count - 1)])
    return terms[width : 2 * width] + before.astype(terms.dtype) + after.astype(terms.dtype)


def key_spans(labels, first, tok_rows):
    seq_len = labels.shape[0]
    query_pos = first + jnp.arange(tok_rows, dtype=jnp.int32)
    query_labels = lax.dynamic_slice_in_dim(labels, first, tok_rows, 0)
    if seq_len == 2 * tok_rows:
        key_pos, key_labels = jnp.arange(seq_len, dtype=jnp.int32), labels
    else:
        key_pos = first - tok_rows + jnp.arange(3 * tok_rows, dtype=jnp.int32)
        padded = jnp.pad(labels, (tok_rows, tok_rows), constant_values=seq_len)
        key_labels = lax.dynamic_slice_in_dim(padded, first, 3 * tok_rows, 0)
    same = (key_labels[:, None] == query_labels[None, :]) & (key_labels[:, None] != seq_len)
    gap = jnp.abs(key_pos[:, None] - query_pos[None, :])
    return jnp.where(same | (gap == 0), gap.astype(jnp.float32), far)


def on_chip_grid():
    return lax.axis_size("rows") == 16 and lax.axis_size("blk") == 2


def packed_shards(w_qkv, w_out, ln1_gain, ln1_bias, w_gate_up, ln2_gain, ln2_bias):
    width = w_out.shape[1]
    ff = w_gate_up.shape[1] // 2
    table = jnp.stack((ln1_gain, ln1_bias, ln2_gain, ln2_bias), 1)
    table = jnp.pad(table, ((0, 0), (0, lane_width - 4)))
    left = jnp.concatenate([w_qkv[:, : 2 * width], table], 1)
    right = jnp.concatenate([w_qkv[:, 2 * width :], w_out, jnp.zeros_like(table)], 1)
    return jnp.stack([left, right]), jnp.stack([w_gate_up[:, :ff], w_gate_up[:, ff:]])


def on_grid(tokens, labels, w_qkv, w_out, w_gate_up, w_down, norms, out_grad):
    width = tokens.shape[1]
    (
        a_full, g_full, d_full, q, k, v, att, hid_t, norm, inv, gate, up, act, output, d_hid, d_branch, span,
        lse, vectors, small,
    ) = fore(HEADS, tokens, labels, w_qkv, w_out, w_gate_up, w_down, jnp.stack(norms), out_grad)
    parts = back(
        HEADS, tokens, q, k, v, span, att, hid_t, norm, inv, gate, up, act, d_hid, d_branch, a_full, g_full,
        d_full.reshape(-1, width), lse, vectors, small,
    )
    *parts, one, two, three, four, stats = close(norms[0].shape[0], output, *parts)
    rows = [row.reshape(-1) for row in (one, two, three, four)]
    return *parts, rows, stats.reshape(-1)


def on_any(tokens, labels, w_qkv, w_out, w_gate_up, w_down, norms, out_grad):
    both = ("rows", "blk")
    tok_rows, width = tokens.shape
    first = lax.axis_index("blk") * tok_rows
    span = key_spans(labels[0], first, tok_rows)
    here = lax.dynamic_slice_in_dim(labels[0], first, tok_rows, 0)
    valid = (here != labels.shape[1]).astype(jnp.float32)[:, None]
    a_shard, g_shard = packed_shards(w_qkv, w_out, *norms[:2], w_gate_up, *norms[2:])
    low, wide = jnp.bfloat16, jnp.float32
    a_full = lax.all_gather(a_shard, both, axis=1, tiled=True)
    w_gu = lax.all_gather(g_shard, both, axis=1, tiled=True)
    w_dn = lax.all_gather(w_down, both, axis=0, tiled=True)
    vectors = jnp.pad(a_full[0, :, 2 * width : 2 * width + 4].astype(wide).T, ((0, 4), (0, 0)))
    w_qk, w_v = a_full[0, :, : 2 * width], a_full[1, :, :width]
    qk = jnp.dot(tokens, w_qk, preferred_element_type=wide).astype(low)
    v = jnp.dot(tokens, w_v, preferred_element_type=wide).astype(low)
    query = qk[:, :width] * (width // HEADS) ** -0.5
    kv = window(jnp.concatenate([qk[:, width:], v], 1), tok_rows)
    keys, values = kv[:, :width], kv[:, width:]
    attended, lse = attend(query, keys, values, span, HEADS)
    output, d_resid_one, d_att, grad_out, g_grad, d_grad, small = ffn(
        tokens, attended, a_full, vectors, valid, out_grad, w_gu, w_dn
    )
    dq, dk, dv = attend_back(query, keys, values, span, lse, attended, d_att, HEADS)
    dkv = window_back(jnp.concatenate([dk, dv], 1), tok_rows)
    d_qk = jnp.concatenate([dq, dkv[:, :width].astype(low)], 1)
    d_v = dkv[:, width:].astype(low)
    grad_qkv = transposed_times(tokens, jnp.concatenate([d_qk, d_v], 1))
    d_tokens = d_resid_one + times_transposed(d_qk, w_qk) + times_transposed(d_v, w_v)
    share = lambda g, axis: lax.psum_scatter(g.astype(wide), both, scatter_dimension=axis, tiled=True)
    gate, up = share(g_grad, 1)
    small = lax.psum(small, both)
    size = norms[0].shape[0]
    rows = lax.dynamic_slice_in_dim(small[:4], lax.axis_index(both) * size, size, 1)
    stats = jnp.sqrt(jnp.sum(small[4:8], 1) / (small[8, 0] * width))
    return (
        output, d_tokens.astype(low), share(grad_qkv, 0), share(grad_out, 0), jnp.concatenate([gate, up], 1),
        share(d_grad, 0), rows, stats,
    )


def body(
    tokens, segments, w_qkv, w_out, ln1_gain, ln1_bias, w_gate_up, w_down, ln2_gain, ln2_bias, out_grad,
):
    run = on_grid if on_chip_grid() else on_any
    norms = (ln1_gain, ln1_bias, ln2_gain, ln2_bias)
    output, d_tokens, qkv, wout, gate_up, down, rows, stats = run(
        tokens[0], segments, w_qkv, w_out, w_gate_up, w_down, norms, out_grad[0]
    )
    return (
        output[None], d_tokens[None], qkv, wout, rows[0], rows[1], gate_up, down, rows[2], rows[3], stats,
    )


def solution(mesh):
    placed = (
        P("rows", "blk", None),
        P("rows", None),
        P(("rows", "blk"), None),
        P(("rows", "blk"), None),
        P(("rows", "blk")),
        P(("rows", "blk")),
        P(("rows", "blk"), None),
        P(("rows", "blk"), None),
        P(("rows", "blk")),
        P(("rows", "blk")),
        P("rows", "blk", None),
    )
    return jax.shard_map(
        body,
        mesh=mesh,
        in_specs=placed,
        out_specs=(
            P("rows", "blk", None),
            P("rows", "blk", None),
            P(("rows", "blk"), None),
            P(("rows", "blk"), None),
            P(("rows", "blk")),
            P(("rows", "blk")),
            P(("rows", "blk"), None),
            P(("rows", "blk"), None),
            P(("rows", "blk")),
            P(("rows", "blk")),
            P(),
        ),
        check_vma=False,
    )
```

```python
import jax
import jax.numpy as jnp
from jax import lax
from jax.experimental import pallas as pl
from jax.experimental.pallas import tpu as pltpu
from jax.sharding import PartitionSpec as P

HEADS = 12


ln_eps = 1e-12
far = 1e33
lane_width = 128


def times_transposed(left, right):
    return lax.dot_general(
        left, right, (((1,), (1,)), ((), ())), preferred_element_type=jnp.float32
    )


def transposed_times(left, right):
    return lax.dot_general(
        left, right, (((0,), (0,)), ((), ())), preferred_element_type=jnp.float32
    )


MESH = pl.DeviceIdType.MESH


class Place:
    def __init__(self):
        r, self.c = lax.axis_index("rows"), lax.axis_index("blk")
        self.x, self.y, self.z = r % 2, (r // 2) % 2, r // 4
        self.sib = (r, 1 - self.c)
        self.xn = (self.at(0, "x"), self.c)
        self.yn = (self.at(0, "y"), self.c)
        self.zn = {k: (self.at(k, "o"), self.c) for k in (1, 2, 3)}

    def plane(self, k):
        z, low = self.z % 2, self.z // 2
        if k % 2:
            z = 1 - z
        if k // 2:
            low = 1 - low
        return low * 2 + z

    def at(self, k, j):
        x = 1 - self.x if j in "xd" else self.x
        y = 1 - self.y if j in "yd" else self.y
        return self.plane(k) * 4 + y * 2 + x

    def greet(self):
        self.barrier = pltpu.get_barrier_semaphore()
        for peer in (self.sib, self.xn, self.yn, *self.zn.values()):
            pl.semaphore_signal(self.barrier, inc=1, device_id=peer, device_id_type=MESH)

    def meet(self):
        pl.semaphore_wait(self.barrier, 6)


class Copies:
    def __init__(self, send, recv):
        self.send, self.recv = send, recv

    def of(self, src, dst, pool, slot, peer):
        return pltpu.make_async_remote_copy(
            src_ref=src, dst_ref=dst, send_sem=self.send.at[pool], recv_sem=self.recv.at[slot],
            device_id=peer, device_id_type=MESH,
        )

    def put(self, src, dst, pool, slot, peer):
        self.of(src, dst, pool, slot, peer).start()

    def got(self, dst, slot, peer):
        self.of(dst, dst, 0, slot, peer).wait_recv()

    def sent(self, all_of_pool, pool, peer):
        self.of(all_of_pool, all_of_pool, pool, 0, peer).wait_send()


class Gather:
    def __init__(self, place, copies, i, side):
        self.p, self.cp, self.side = place, copies, side
        self.base, self.pool = i * gather_slots, 2 * i

    def slot(self, kind, k=0):
        return self.base + {"z": -1, "x": 3, "y": 7, "d": 11, "s": 15}[kind] + k

    def out(self, half, r):
        return self.side(half).at[r]

    def block(self, k, j):
        return self.out(self.p.c, self.p.at(k, j))

    def send(self, src, dst, slot, peer):
        self.cp.put(src, dst, self.pool, slot, peer)

    def push(self, src, k, j):
        self.cp.put(src, self.block(k, j), self.pool + 1, self.slot("s", k), self.p.sib)

    def to_z(self):
        for k in (1, 2):
            self.send(self.block(0, "o"), self.block(0, "o"), self.slot("z", k), self.p.zn[k])

    def to_xy(self):
        self.spread(self.block(0, "o"), 0)

    def spread(self, src, k):
        dst = self.block(k, "o")
        self.send(src, dst, self.slot("x", k), self.p.xn)
        self.send(src, dst, self.slot("y", k), self.p.yn)
        self.push(src, k, "o")

    def from_z(self, k):
        block = self.block(k, "o")
        self.cp.got(block, self.slot("z", k), self.p.zn[k])
        if k == 2:
            self.send(block, block, self.slot("z", 3), self.p.zn[1])
        self.spread(block, k)

    @staticmethod
    def schedule(mats):
        work = [(mats[0].to_z,)] + [(m.to_xy,) for m in mats[:3]]
        for i, m in enumerate(mats):
            before = mats[i - 1] if i else None
            work.append((m.from_z, 1))
            if i + 1 < len(mats):
                work.append((mats[i + 1].to_z,))
            if before:
                work.append((before.from_xy, 3))
            work += [(m.from_xy, 0), (m.from_z, 2)]
            if before:
                work.append((before.from_d, 2))
            if i + 3 < len(mats):
                work.append((mats[i + 3].to_xy,))
            work += [(m.from_xy, 1), (m.from_z, 3)]
            if before:
                work.append((before.from_d, 1))
            work.append((m.from_d, 0))
            if before:
                work.append((before.from_d, 3))
            work.append((m.from_xy, 2))
        last = mats[-1]
        return work + [(last.from_xy, 3), (last.from_d, 2), (last.from_d, 1), (last.from_d, 3)]

    def from_xy(self, k):
        x, y = self.block(k, "x"), self.block(k, "y")
        self.cp.got(x, self.slot("x", k), self.p.xn)
        if k == 2:
            self.send(x, x, self.slot("d", k), self.p.yn)
        self.cp.got(y, self.slot("y", k), self.p.yn)
        if k == 0:
            self.send(y, y, self.slot("d", k), self.p.xn)
        self.push(x, k, "x")
        self.push(y, k, "y")

    def from_d(self, k):
        block = self.block(k, "d")
        self.cp.got(block, self.slot("d", k), self.p.xn)
        if k % 2 == 0:
            self.send(block, block, self.slot("d", k + 1), self.p.zn[1])
        self.push(block, k, "d")

    def from_sib(self, *planes):
        for k in planes or range(4):
            four = pl.ds(self.p.plane(k) * 4, 4)
            self.cp.got(self.side(1 - self.p.c).at[four], self.slot("s", k), self.p.sib)

    def drain(self):
        side = self.side(self.p.c)
        self.cp.sent(side.at[pl.ds(0, 15)], self.pool, self.p.sib)
        self.cp.sent(side, self.pool + 1, self.p.sib)


class Scatter:
    def __init__(self, place, copies, i, give, own, sib, rly, dia, xin, yin, zin, straight=False, flat=False):
        self.p, self.cp, self.give, self.own = place, copies, give, own
        self.base, self.pool = i * scatter_slots, 2 * i
        self.straight, self.flat = straight, flat
        self.sib, self.rly, self.dia, self.xin, self.yin, self.zin = sib, rly, dia, xin, yin, zin

    def slot(self, kind, k):
        return self.base + {"s": 0, "r": 4, "d": 5, "x": 8, "y": 12, "z": 15}[kind] + k

    def four(self, k):
        return pl.ds(self.p.plane(k) * 4, 4)

    def begin(self, k):
        four = self.four(k)
        self.cp.put(self.give(four), self.sib.at[four], self.pool + 1, self.slot("s", k), self.p.sib)

    def given(self):
        self.cp.sent(self.sib, self.pool + 1, self.p.sib)

    def drain(self):
        self.cp.sent(self.sib.at[pl.ds(0, 15)], self.pool, self.p.sib)

    def to_x(self, own, k):
        self.cp.put(own, self.xin.at[k], self.pool, self.slot("x", k), self.p.xn)

    def to_y(self, own, k):
        self.cp.put(own, self.yin.at[k], self.pool, self.slot("y", k), self.p.yn)

    def both(self, k, j, *more):
        at = self.p.at(k, j)
        own = self.own(at)
        total = own[...] + self.sib[at]
        for ref in more:
            total = total + ref[...]
        own[...] = total
        return own

    def pair(self, k):
        four = self.four(k)
        self.cp.got(self.sib.at[four], self.slot("s", k), self.p.sib)
        if self.flat:
            self.to_relay(self.both(k, "d"), k)
        elif k % 2:
            i = k // 2
            self.cp.put(self.both(k, "d"), self.dia.at[i], self.pool, self.slot("d", 2 * i), self.p.zn[1])
        odd = k % 2 and not self.flat
        if odd or k < 2:
            self.to_x(self.both(k, "x"), k)
        if odd or k >= 2:
            self.to_y(self.both(k, "y"), k)

    def relay_at(self, k):
        return (self.dia if k % 2 else self.rly).at[k // 2]

    def to_relay(self, own, k):
        slot = self.slot("d", k - 1) if k % 2 else self.slot("r", k)
        self.cp.put(own, self.relay_at(k), self.pool, slot, self.p.xn if k < 2 else self.p.yn)

    def diag(self, k):
        i = k // 2
        self.cp.got(self.dia.at[i], self.slot("d", k), self.p.zn[1])
        self.to_relay(self.both(k, "d", self.dia.at[i]), k)

    def relay(self, k):
        rly = self.relay_at(k)
        self.cp.got(rly, self.slot("d", k - 1) if k % 2 else self.slot("r", k), self.p.xn)
        if k < 2:
            self.to_y(self.both(k, "y", rly), k)
        else:
            self.to_x(self.both(k, "x", rly), k)

    def plane(self, k):
        p = self.p
        at = p.at(k, "o")
        self.cp.got(self.xin.at[k], self.slot("x", k), p.xn)
        self.cp.got(self.yin.at[k], self.slot("y", k), p.yn)
        wide = jnp.float32
        own = self.own(at)
        total = (own[...].astype(wide) + self.sib[at].astype(wide)) + (
            self.xin[k].astype(wide) + self.yin[k].astype(wide)
        )
        own[...] = total.astype(jnp.bfloat16)
        if self.straight and k:
            self.to_z(own, k, k)
        elif k % 2:
            self.to_z(own, k, 1)

    def to_z(self, own, k, step):
        self.cp.put(own, self.zin.at[k - 1], self.pool, self.slot("z", k), self.p.zn[step])

    def cross(self):
        self.cp.got(self.zin.at[2], self.slot("z", 3), self.p.zn[1])
        own = self.own(self.p.at(2, "o"))
        own[...] = own[...] + self.zin[2]
        self.to_z(own, 2, 2)

    def all(self, name, *planes):
        for k in planes:
            getattr(self, name)(k)

    def first(self):
        self.all("pair", 3, 1)

    def rest(self):
        self.all("pair", 2, 0)

    def diags(self):
        if not self.flat:
            self.all("diag", 2, 0)

    def relays(self):
        self.all("relay", *((3, 1, 2, 0) if self.flat else (2, 0)))

    def odd(self):
        self.all("plane", 3, 1)

    def even(self):
        self.all("plane", 2, 0)
        if not self.straight:
            self.cross()

    def total(self):
        wide = jnp.float32
        total = self.own(self.p.at(0, "o"))[...].astype(wide)
        for k in (1, 2, 3) if self.straight else (1, 2):
            self.cp.got(self.zin.at[k - 1], self.slot("z", k), self.p.zn[k])
            total = total + self.zin[k - 1].astype(wide)
        return total


rows_chip = 48
gather_slots, scatter_slots = 19, 19


def dot(left, right, dims=((1,), (0,))):
    return lax.dot_general(left, right, (dims, ((), ())), preferred_element_type=jnp.float32)


def row_mean(values):
    return jnp.mean(values, -1, keepdims=True)


def normalized(resid):
    centred = resid - row_mean(resid)
    inverse = lax.rsqrt(row_mean(centred * centred) + ln_eps)
    return centred * inverse, inverse


def norm_back(grad, gain, norm, inverse):
    e = grad * gain
    return inverse * (e - row_mean(e) - norm * row_mean(e * norm))


def column_sum(values):
    return jnp.sum(values, 0, keepdims=True)


def ffn_kernel(
    tokens, attended, w_out, vectors, valid, out_grad, w_gu, w_down,
    output, d_resid_one, d_att, grad_out, grad_gu, grad_down, small,
    hid, hid_low, hid_t, norm_one, inv_one, slope_gate, slope_up, act, total, d_hid, d_branch,
):
    i = pl.program_id(0)
    tiles = pl.num_programs(0) // 2
    low = jnp.bfloat16
    wide = jnp.float32

    @pl.when(i == 0)
    def _():
        branch = dot(attended[...], w_out[0])
        toks = tokens[...].astype(wide)
        norm, inverse = normalized(toks + branch)
        norm_one[...] = norm
        inv_one[...] = inverse
        hidden = norm * vectors[0:1, :] + vectors[1:2, :]
        hid[...] = hidden
        hid_low[...] = hidden.astype(low)
        hid_t[...] = hidden.T.astype(low)
        mask = valid[...]
        small[4:5, :] = column_sum(mask * toks * toks)
        small[5:6, :] = column_sum(mask * branch * branch)
        small[6:7, :] = column_sum(mask * hidden * hidden)
        small[8:16, :] = jnp.zeros((8, small.shape[1]), wide)
        small[8:9, :] = jnp.broadcast_to(jnp.sum(mask, 0, keepdims=True), (1, small.shape[1]))
        total[...] = jnp.zeros_like(total)

    @pl.when(i < tiles)
    def _():
        h = hid_low[...]
        gate = dot(h, w_gu[0])
        up = dot(h, w_gu[1])
        cdf = 0.5 + 0.5 * lax.erf(gate * 0.7071067811865476)
        glu = gate * cdf
        density = 0.3989422804014327 * jnp.exp(-0.5 * gate * gate)
        slope_up[i] = glu
        slope_gate[i] = up * (cdf + gate * density)
        a = (glu * up).astype(low)
        act[i] = a
        total[...] += dot(a, w_down[...])

    @pl.when(i == tiles - 1)
    def _():
        branch = total[...]
        mask = valid[...]
        small[7:8, :] = column_sum(mask * branch * branch)
        norm, inverse = normalized(hid[...] + branch)
        gain = vectors[2:3, :]
        output[...] = (norm * gain + vectors[3:4, :]).astype(low)
        grad = out_grad[...].astype(wide)
        small[2:3, :] = column_sum(grad * norm)
        small[3:4, :] = column_sum(grad)
        back = norm_back(grad, gain, norm, inverse)
        d_hid[...] = back
        d_branch[...] = back.astype(low)

    @pl.when(i >= tiles)
    def _():
        j = i - tiles
        db = d_branch[...]
        grad_down[...] = dot(act[j].T, db).astype(low)
        d_act = dot(db, w_down[...], ((1,), (1,)))
        d_gate = (d_act * slope_gate[j]).astype(low)
        d_up = (d_act * slope_up[j]).astype(low)
        h_t = hid_t[...]
        grad_gu[0] = dot(h_t, d_gate).astype(low)
        grad_gu[1] = dot(h_t, d_up).astype(low)
        d_hid[...] += dot(d_gate, w_gu[0], ((1,), (1,))) + dot(d_up, w_gu[1], ((1,), (1,)))

    @pl.when(i == 2 * tiles - 1)
    def _():
        grad = d_hid[...]
        norm = norm_one[...]
        small[0:1, :] = column_sum(grad * norm)
        small[1:2, :] = column_sum(grad)
        back = norm_back(grad, vectors[0:1, :], norm, inv_one[...])
        d_resid_one[...] = back
        db = back.astype(low)
        grad_out[...] = dot(attended[...].T, db).astype(low)
        d_att[...] = dot(db, w_out[0], ((1,), (1,))).astype(low)


def ffn(tokens, attended, a_full, vectors, valid, out_grad, w_gu, w_down):
    rows, width = tokens.shape
    ff = w_down.shape[0]
    tile = 512
    tiles = ff // tile
    low, wide = jnp.bfloat16, jnp.float32
    whole = lambda *shape: pl.BlockSpec(shape, lambda i: (0,) * len(shape))
    at = lambda i: jnp.where(i < tiles, i, i - tiles)
    late = lambda i: jnp.maximum(i - tiles, 0)
    return pl.pallas_call(
        ffn_kernel,
        grid=(2 * tiles,),
        out_shape=(
            jax.ShapeDtypeStruct((rows, width), low),
            jax.ShapeDtypeStruct((rows, width), wide),
            jax.ShapeDtypeStruct((rows, width), low),
            jax.ShapeDtypeStruct((width, width), low),
            jax.ShapeDtypeStruct((2, width, ff), low),
            jax.ShapeDtypeStruct((ff, width), low),
            jax.ShapeDtypeStruct((16, width), wide),
        ),
        in_specs=[
            whole(rows, width),
            whole(rows, width),
            pl.BlockSpec((1, width, width), lambda i: (1, 0, 1)),
            whole(8, width),
            whole(rows, 1),
            whole(rows, width),
            pl.BlockSpec((2, width, tile), lambda i: (0, 0, at(i))),
            pl.BlockSpec((tile, width), lambda i: (at(i), 0)),
        ],
        out_specs=(
            whole(rows, width),
            whole(rows, width),
            whole(rows, width),
            whole(width, width),
            pl.BlockSpec((2, width, tile), lambda i: (0, 0, late(i))),
            pl.BlockSpec((tile, width), lambda i: (late(i), 0)),
            whole(16, width),
        ),
        scratch_shapes=[
            pltpu.VMEM((rows, width), wide),
            pltpu.VMEM((rows, width), low),
            pltpu.VMEM((width, rows), low),
            pltpu.VMEM((rows, width), wide),
            pltpu.VMEM((rows, 1), wide),
            pltpu.VMEM((tiles, rows, tile), wide),
            pltpu.VMEM((tiles, rows, tile), wide),
            pltpu.VMEM((tiles, rows, tile), low),
            pltpu.VMEM((rows, width), wide),
            pltpu.VMEM((rows, width), wide),
            pltpu.VMEM((rows, width), low),
        ],
        compiler_params=pltpu.CompilerParams(vmem_limit_bytes=60 * 2**20),
        cost_estimate=pl.CostEstimate(
            flops=2 * rows * width * (9 * ff + 3 * width), bytes_accessed=18 * ff * width, transcendentals=2 * rows * ff
        ),
        name="feed_forward",
    )(tokens, attended, a_full, vectors, valid, out_grad, w_gu, w_down)


def half_of(block, axis, second):
    place = lax.broadcasted_iota(jnp.int32, block.shape, axis)
    depth = block.shape[axis] // 2
    keep = place >= depth if second else place < depth
    return jnp.where(keep, block, jnp.zeros_like(block))


def attend_kernel(heads, q, k, v, span, attended, lse):
    @pl.loop(0, heads // 2)
    def _(pair):
        attend_pair(pair, heads, q, k, v, span, lse, attended)


def attend(q, k, v, span, heads):
    rows, width = q.shape
    keys = k.shape[0]
    low, wide = jnp.bfloat16, jnp.float32
    return pl.pallas_call(
        lambda *refs: attend_kernel(heads, *refs),
        out_shape=(
            jax.ShapeDtypeStruct((rows, width), low),
            jax.ShapeDtypeStruct((16, rows), wide),
        ),
        in_specs=[pl.BlockSpec(memory_space=pltpu.VMEM)] * 4,
        out_specs=(pl.BlockSpec(memory_space=pltpu.VMEM),) * 2,
        compiler_params=pltpu.CompilerParams(vmem_limit_bytes=60 * 2**20),
        cost_estimate=pl.CostEstimate(flops=4 * rows * keys * width, bytes_accessed=8 * keys * width, transcendentals=heads * rows * keys),
        name="attend",
    )(q, k, v, span)


def attend_back_pair(pair, heads, q, k, v, span, lse, att, d_att, dq, dk_sum, dv_sum):
    low, wide = jnp.bfloat16, jnp.float32
    rows, width = q.shape
    lanes = lane_width
    depth = width // heads
    chunk = 256
    scale = depth**-0.5
    at = pl.ds(pl.multiple_of(pair * lanes, lanes), lanes)
    keys, values = k[:, at], v[:, at]
    keys_t = keys.astype(wide).T.astype(low)
    for c in range(rows // chunk):
        here = pl.ds(c * chunk, chunk)
        q_wide = q[here, at].astype(wide)
        do_here = d_att[here, at]
        do_wide = do_here.astype(wide)
        q_here = q_wide.astype(low)
        q_t, do_t = q_wide.T.astype(low), do_wide.T.astype(low)
        both_t = (do_wide * att[here, at].astype(wide)).T
        dk_part, dv_part, dq_parts = None, None, []
        for h in (0, 1):
            head = 2 * pair + h
            own = slice(h * depth, (h + 1) * depth)
            slope = jnp.exp2(jnp.full((1, 1), -8.0 / heads, wide) * (head + 1).astype(wide))
            delta = jnp.sum(both_t[own], 0, keepdims=True)
            logits = dot(keys, half_of(q_t, 0, h)) - slope * span[:, here]
            probs = jnp.exp(logits - lse[pl.ds(head, 1), here])
            d_probs = dot(values, half_of(do_t, 0, h))
            d_logits = (probs * (d_probs - delta)).astype(low)
            dv_term = dot(probs.astype(low), half_of(do_here, 1, h))
            dk_term = dot(d_logits, half_of(q_here, 1, h))
            dv_part = dv_term if dv_part is None else dv_part + dv_term
            dk_part = dk_term if dk_part is None else dk_part + dk_term
            dq_parts.append(dot(keys_t[own], d_logits) * scale)
        if c == 0:
            dk_sum[...] = dk_part
            dv_sum[...] = dv_part
        else:
            dk_sum[...] += dk_part
            dv_sum[...] += dv_part
        dq[here, at] = jnp.concatenate(dq_parts, 0).T.astype(low)


def attend_back_kernel(heads, q, k, v, span, lse, att, d_att, dq, dk, dv, dk_sum, dv_sum):
    @pl.loop(0, heads // 2)
    def _(pair):
        attend_back_pair(pair, heads, q, k, v, span, lse, att, d_att, dq, dk_sum, dv_sum)
        at = pl.ds(pl.multiple_of(pair * lane_width, lane_width), lane_width)
        dk[:, at] = dk_sum[...]
        dv[:, at] = dv_sum[...]


def attend_back(q, k, v, span, lse, att, d_att, heads):
    rows, width = q.shape
    keys = k.shape[0]
    low, wide = jnp.bfloat16, jnp.float32
    return pl.pallas_call(
        lambda *refs: attend_back_kernel(heads, *refs),
        out_shape=(
            jax.ShapeDtypeStruct((rows, width), low),
            jax.ShapeDtypeStruct((keys, width), wide),
            jax.ShapeDtypeStruct((keys, width), wide),
        ),
        in_specs=[pl.BlockSpec(memory_space=pltpu.VMEM)] * 7,
        out_specs=(pl.BlockSpec(memory_space=pltpu.VMEM),) * 3,
        scratch_shapes=[
            pltpu.VMEM((keys, lane_width), wide),
            pltpu.VMEM((keys, lane_width), wide),
        ],
        compiler_params=pltpu.CompilerParams(vmem_limit_bytes=60 * 2**20),
        cost_estimate=pl.CostEstimate(flops=10 * rows * keys * width, bytes_accessed=16 * keys * width, transcendentals=heads * rows * keys),
        name="attend_back",
    )(q, k, v, span, lse, att, d_att)


def attend_pair(pair, heads, q, k, v, span, lse, attended):
    low, wide = jnp.bfloat16, jnp.float32
    rows, width = q.shape
    lanes = lane_width
    depth = width // heads
    chunk = 256
    at = pl.ds(pl.multiple_of(pair * lanes, lanes), lanes)
    keys = k[:, at]
    values_t = v[:, at].astype(wide).T.astype(low)
    for c in range(rows // chunk):
        here = pl.ds(c * chunk, chunk)
        q_t = q[here, at].astype(wide).T.astype(low)
        parts = []
        for h in (0, 1):
            head = 2 * pair + h
            slope = jnp.exp2(jnp.full((1, 1), -8.0 / heads, wide) * (head + 1).astype(wide))
            logits = dot(keys, half_of(q_t, 0, h)) - slope * span[:, here]
            top = jnp.max(logits, 0, keepdims=True)
            weights = jnp.exp(logits - top)
            norm = jnp.sum(weights, 0, keepdims=True)
            lse[pl.ds(head, 1), here] = top + jnp.log(norm)
            parts.append(dot(values_t[h * depth : (h + 1) * depth], weights.astype(low)) / norm)
        attended[here, at] = jnp.concatenate(parts, 0).T.astype(low)


def fore_kernel(
    heads, tokens, labels, w_qkv, w_out, w_gu, d_shard, gain_one, bias_one, gain_two, bias_two, out_grad,
    a_full, g_full, d_full, q_out, k_out, v_out, att_out, hid_t_out, norm_out, inv_out, gate_out, up_out, act_out,
    output_out, d_hid_out, d_branch_out, span_out, lse, vectors, small,
    w_a, w_g, w_d, a_give, g_give, a_pair, g_pair, turned, q, k, v, att, span_v, grad_v, hid, hid_low, hid_t, norm_one, inv_one,
    slope_gate, slope_up, act, output, d_hid, d_branch, pair_sem, send, recv, in_sem, out_sem,
):
    place = Place()
    place.greet()
    c = place.c
    low, wide = jnp.bfloat16, jnp.float32
    tok_rows, width = tokens.shape
    ff = w_g.shape[3]
    half_g = ff // 2
    pairs = heads // 2
    load = pltpu.make_async_copy(out_grad, grad_v, in_sem.at[0])
    load.start()
    core_one = c == 1
    turned[...] = jnp.zeros_like(turned)
    share = w_out.shape[0]
    for i, norm in enumerate((gain_one, bias_one, gain_two, bias_two)):
        turned[i : i + 1, 0:share] = norm[...].astype(wide).reshape(1, share)
    table = turned[...].T[:share].astype(low)
    left = jnp.concatenate([w_qkv[:, : 2 * width], table], 1)
    right = jnp.concatenate([w_qkv[:, 2 * width :], w_out[...], jnp.zeros_like(table)], 1)
    gate, up = w_gu[:, :ff], w_gu[:, ff:]
    rows = w_qkv.shape[0]
    a_give[:rows, :] = jnp.where(core_one, left, right)
    g_give[:rows, :] = jnp.where(core_one, gate, up)
    swaps = Copies(pair_sem.at[0], pair_sem.at[1])
    place.meet()
    for i, (give, other) in enumerate(((a_give, a_pair), (g_give, g_pair))):
        swaps.put(give, other, i, i, place.sib)
    copies = Copies(send, recv)
    sides = [
        lambda half: w_a.at[half],
        lambda half: w_g.at[half, :, :, :half_g],
        lambda half: w_g.at[half, :, :, half_g:],
        lambda half: w_d.at[:, half],
    ]
    mats = [Gather(place, copies, i, side) for i, side in enumerate(sides)]
    first, second, third, fourth = mats
    me = place.at(0, "o")

    def assemble(mine, other, full, i):
        swaps.got(other, i, place.sib)
        mine = mine.astype(wide)
        theirs = other[:rows, :].astype(wide)
        top = jnp.where(core_one, theirs, mine)
        rest = jnp.where(core_one, mine, theirs)
        full[c, me] = jnp.concatenate([top, rest], 0).astype(low)

    work = Gather.schedule(mats)

    def go(count):
        for step, *plane in work[:count]:
            step(*plane)
        del work[:count]

    def upto(matrix):
        done = [i for i, (step, *_) in enumerate(work) if step == matrix.from_d]
        go(done[-1] + 1 if done else 0)

    assemble(jnp.where(core_one, right, left), a_pair, w_a, 0)
    go(2)
    assemble(jnp.where(core_one, up, gate), g_pair, w_g, 1)
    w_d[me, c] = d_shard[...]
    seq_len = labels.shape[1]
    label_row = labels[...].astype(wide)
    label_column = jnp.broadcast_to(label_row, (lane_width, seq_len)).T[:, 0:1]
    half = pl.ds(pl.multiple_of(c * tok_rows, tok_rows), tok_rows)
    same = (label_column == labels[:, half].astype(wide)) & (label_column != seq_len)
    key_at = lax.broadcasted_iota(jnp.int32, span_v.shape, 0)
    gap = jnp.abs(key_at - lax.broadcasted_iota(jnp.int32, span_v.shape, 1) - c * tok_rows)
    span_v[...] = jnp.where(same | (gap == 0), gap.astype(wide), far)
    mask = jnp.broadcast_to(labels[:, half].astype(wide), (lane_width, tok_rows)).T[:, 0:1]
    mask = (mask != seq_len).astype(wide)
    upto(first)
    first.from_sib()
    saved = []

    def save(src, dst):
        copy = pltpu.make_async_copy(src, dst, out_sem.at[len(saved)])
        copy.start()
        saved.append((src, dst))

    save(w_a, a_full)
    save(span_v, span_out)
    part = lambda half, at, size: w_a[half, :, :, at : at + size].reshape(width, size)
    vectors[...] = part(0, 2 * width, lane_width).astype(wide).T[:8]
    x = tokens[...]
    k[half, :] = dot(x, part(0, width, width)).astype(low)
    swaps.put(k.at[half], k.at[half], 2, 2, place.sib)
    v[half, :] = dot(x, part(1, 0, width)).astype(low)
    swaps.put(v.at[half], v.at[half], 3, 3, place.sib)
    depth = width // heads
    q[...] = dot(x, part(0, 0, width)).astype(low) * depth**-0.5
    go(3)
    other = pl.ds(pl.multiple_of((1 - c) * tok_rows, tok_rows), tok_rows)
    swaps.got(k.at[other], 2, place.sib)
    swaps.got(v.at[other], 3, place.sib)
    save(q, q_out)
    save(k, k_out)
    save(v, v_out)

    shares = (3, 4, 4, 4, 4, 2)
    todo = []
    for count in shares:
        todo.append(work[:count])
        del work[:count]

    @pl.loop(0, pairs)
    def _(pair):
        attend_pair(pair, heads, q, k, v, span_v, lse, att)
        for at, steps in enumerate(todo):

            @pl.when(pair == at)
            def _(steps=steps):
                for step, *plane in steps:
                    step(*plane)

    save(att, att_out)
    branch = dot(att[...], part(1, width, width))
    toks = x.astype(wide)
    norm, inverse = normalized(toks + branch)
    norm_one[...] = norm
    inv_one[...] = jnp.broadcast_to(inverse, inv_one.shape)
    hidden = norm * vectors[0:1, :] + vectors[1:2, :]
    hid[...] = hidden
    hid_low[...] = hidden.astype(low)
    hid_t[...] = hidden.T.astype(low)
    save(hid_t, hid_t_out)
    save(norm_one, norm_out)
    save(inv_one, inv_out)
    small[0:4, :] = jnp.zeros((4, width), wide)
    small[4:5, :] = column_sum(mask * toks * toks)
    small[5:6, :] = column_sum(mask * branch * branch)
    small[6:7, :] = column_sum(mask * hidden * hidden)
    small[8:16, :] = jnp.zeros((8, width), wide)
    small[8:9, :] = jnp.broadcast_to(jnp.sum(mask, 0, keepdims=True), (1, width))
    tile = 512

    def glu(j):
        cols = pl.ds(pl.multiple_of(j * tile, tile), tile)
        h = hid_low[...]
        gate = dot(h, w_g[0, :, :, cols].reshape(width, tile))
        up = dot(h, w_g[1, :, :, cols].reshape(width, tile))
        cdf = 0.5 + 0.5 * lax.erf(gate * 0.7071067811865476)
        mixed = gate * cdf
        density = 0.3989422804014327 * jnp.exp(-0.5 * gate * gate)
        slope_up[:, cols] = mixed.astype(low)
        slope_gate[:, cols] = (up * (cdf + gate * density)).astype(low)
        act[:, cols] = (mixed * up).astype(low)

    upto(second)
    go(1)
    second.from_sib()
    save(w_g.at[:, :, :, :half_g], g_full.at[:, :, :, :half_g])

    @pl.loop(0, half_g // tile)
    def _(j):
        glu(j)

    go(1)
    third.from_sib()
    save(w_g.at[:, :, :, half_g:], g_full.at[:, :, :, half_g:])
    for src, dst in ((slope_gate, gate_out), (slope_up, up_out), (act, act_out)):
        save(src.at[:, :half_g], dst.at[:, :half_g])

    @pl.loop(half_g // tile, ff // tile)
    def _(j):
        glu(j)

    for src, dst in ((slope_gate, gate_out), (slope_up, up_out), (act, act_out)):
        save(src.at[:, half_g:], dst.at[:, half_g:])

    def down(plane):
        at = place.plane(plane)
        cols = pl.ds(pl.multiple_of(at * width, width), width)
        return dot(act[:, cols], w_d[pl.ds(at * 4, 4)].reshape(width, width))

    go(1)
    fourth.from_sib(0, 2, 1)
    d_hid[...] = down(0)
    for plane in (2, 1):
        d_hid[...] += down(plane)
    upto(fourth)
    fourth.from_sib(3)
    save(w_d, d_full)
    d_hid[...] += down(3)
    branch = d_hid[...]
    small[7:8, :] = column_sum(mask * branch * branch)
    norm, inverse = normalized(hid[...] + branch)
    gain = vectors[2:3, :]
    output[...] = (norm * gain + vectors[3:4, :]).astype(low)
    save(output, output_out)
    load.wait()
    grad = grad_v[...].astype(wide)
    small[2:3, :] = column_sum(grad * norm)
    small[3:4, :] = column_sum(grad)
    back = norm_back(grad, gain, norm, inverse)
    d_hid[...] = back
    d_branch[...] = back.astype(low)
    save(d_hid, d_hid_out)
    save(d_branch, d_branch_out)
    for i, (src, dst) in enumerate(saved):
        pltpu.make_async_copy(src, dst, out_sem.at[i]).wait()
    for i, ref in enumerate((a_give, g_give, k.at[half], v.at[half])):
        swaps.sent(ref, i, place.sib)
    for m in mats:
        m.drain()


def fore(heads, tokens, labels, w_qkv, w_out, w_gu, d_shard, norms, out_grad):
    low, wide = jnp.bfloat16, jnp.float32
    rows, width = tokens.shape
    ff = w_gu.shape[1] // 2
    half_a = 2 * width + lane_width
    keys = labels.shape[1]
    vmem, hbm = pl.BlockSpec(memory_space=pltpu.VMEM), pl.BlockSpec(memory_space=pl.ANY)
    dma = lambda *shape: pltpu.SemaphoreType.DMA(shape)
    shape = jax.ShapeDtypeStruct
    w_a, w_g, w_d = (2, 16, rows_chip, half_a), (2, 16, rows_chip, ff), (16, 2) + d_shard.shape
    stored = [
        (w_a, low), (w_g, low), (w_d, low), ((rows, width), low), ((keys, width), low), ((keys, width), low),
        ((rows, width), low), ((width, rows), low), ((rows, width), wide), ((rows, lane_width), wide),
        ((rows, ff), low), ((rows, ff), low), ((rows, ff), low), ((rows, width), low), ((rows, width), wide),
        ((rows, width), low), ((keys, rows), wide),
    ]
    block = lambda *dims: pltpu.VMEM(dims, low)
    block_wide = lambda *dims: pltpu.VMEM(dims, wide)
    return pl.pallas_call(
        lambda *refs: fore_kernel(heads, *refs),
        out_shape=tuple(shape(dims, kind) for dims, kind in stored)
        + (shape((16, rows), wide), shape((8, width), wide), shape((16, width), wide)),
        in_specs=[vmem] * 10 + [hbm],
        out_specs=(hbm,) * len(stored) + (vmem,) * 3,
        scratch_shapes=[
            block(*w_a), block(*w_g), block(*w_d), block(32, half_a), block(32, ff), block(32, half_a), block(32, ff),
            block_wide(lane_width, lane_width),
            block(rows, width), block(keys, width), block(keys, width), block(rows, width),
            block_wide(keys, rows), block(rows, width), block_wide(rows, width), block(rows, width),
            block(width, rows), block_wide(rows, width), block_wide(rows, lane_width),
            block(rows, ff), block(rows, ff), block(rows, ff), block(rows, width), block_wide(rows, width),
            block(rows, width), dma(2, 4), dma(8), dma(4 * gather_slots), dma(1), dma(len(stored) + 4),
        ],
        compiler_params=pltpu.CompilerParams(
            collective_id=0, has_side_effects=True, vmem_limit_bytes=62 * 2**20
        ),
        name="gather_and_forward",
    )(tokens, labels, w_qkv, w_out, w_gu, d_shard, *norms, out_grad)


def back_kernel(
    heads, tokens, q, k, v, span, att, hid_t, norm, inv, gate, up, act, d_hid, d_branch, a_full, g_full, d_full,
    lse, vectors, small, d_tokens, qkv_out, wout_out, gu_out, down_out, tail, *scratch,
):
    place = Place()
    place.greet()
    c = place.c
    first = c == 0
    low, wide = jnp.bfloat16, jnp.float32
    tok_rows, width = tokens.shape
    ff = gate.shape[1]
    pairs = heads // 2
    bufs, rest = scratch[:33], scratch[33:]
    a_grad, dkv_in, resid, d_att, g_sum, a_sum, g_fin, a_fin, small_buf, send, recv, tokens_v, down_v, gu_v, pair_sem, fin_sem, in_sem, tile_sem = rest
    copies = Copies(send, recv)
    last = Copies(fin_sem.at[0], fin_sem.at[1])
    half_g, part = ff // 2, width // 2

    def scatter(i, own, *more):
        return Scatter(place, copies, i, None, lambda at: own.at[at], *more)

    def projection(i, *more):
        give = lambda four: a_grad.at[i, 1 - c, four]
        own = lambda at: a_grad.at[i, c, at]
        return Scatter(place, copies, 3 + i, give, own, *more)

    down, left, right = (scatter(i, *bufs[7 * i : 7 * i + 7]) for i in range(3))
    projs = [projection(i, *bufs[21 + 6 * i : 27 + 6 * i]) for i in range(2)]
    early, late = projs
    planes = (3, 2, 1, 0)
    hand_over = lambda i, src, dst: pltpu.make_async_copy(src, dst, in_sem.at[i])
    hops = ((place.sib, 0), (place.xn, 1), (place.yn, 2))

    def exchange(i):
        peer, slot = hops[i]
        last.put(small_buf.at[i], small_buf.at[4 + i], slot, slot, peer)

    def combine(i):
        peer, slot = hops[i]
        last.got(small_buf.at[4 + i], slot, peer)
        small_buf[i + 1] = small_buf[i] + small_buf[4 + i]

    def spread():
        for z in (1, 2, 3):
            last.put(small_buf.at[3], small_buf.at[6 + z], 2 + z, 2 + z, place.zn[z])

    tile = 256

    def feed_forward(given, act_v, db, ht, w_gu, w_dn, gate_v, up_v, att_v, norm_v, inv_v, w_out):
        for i, m in enumerate((down, left, right)):
            m.give = lambda four, i=i: given.at[i % 2, four]
        load = lambda i, src, dst: pltpu.make_async_copy(src, dst, in_sem.at[i])
        loads = [
            load(0, d_branch, db), load(1, hid_t, ht), load(2, d_hid, resid), load(3, att, att_v),
            load(4, norm, norm_v), load(5, inv, inv_v), load(6, a_full.at[1, :, :, width : 2 * width], w_out),
        ]

        def act_load(i, z):
            cols = pl.ds(pl.multiple_of(place.plane(z) * width, width), width)
            return load(7 + i % 2, act.at[:, cols], act_v.at[i % 2])

        def fetch(j):
            slot = j % 2
            cols = pl.ds(pl.multiple_of(j * tile, tile), tile)
            return [
                pltpu.make_async_copy(g_full.at[:, :, :, cols], w_gu.at[slot], tile_sem.at[0, slot]),
                pltpu.make_async_copy(d_full.at[cols], w_dn.at[slot], tile_sem.at[1, slot]),
                pltpu.make_async_copy(gate.at[:, cols], gate_v.at[slot], tile_sem.at[2, slot]),
                pltpu.make_async_copy(up.at[:, cols], up_v.at[slot], tile_sem.at[3, slot]),
            ]

        loads[0].start()
        act_load(0, planes[0]).start()
        act_load(1, planes[1]).start()
        for copy in loads[1:] + fetch(0):
            copy.start()
        loads[0].wait()
        own_d = bufs[0]
        for i, z in enumerate(planes):
            act_load(i, z).wait()
            term = dot(act_v[i % 2].T, db[...]).astype(low).reshape(4, 2, 2, rows_chip, width)
            if i < 2:
                act_load(i + 2, planes[i + 2]).start()
            four = pl.ds(place.plane(z) * 4, 4)
            mine = jnp.where(first, term[:, 0], term[:, 1])
            other = jnp.where(first, term[:, 1], term[:, 0])
            for j in range(2):
                cols = slice(j * width, (j + 1) * width)
                bufs[0][four, :, cols] = mine[:, j]
                given[0, four, :, cols] = other[:, j]
            if i == 0:
                place.meet()
            down.begin(z)
            if i > 1:
                down.pair(planes[i - 2])
        for copy in loads[1:3]:
            copy.wait()

        def between(i, todo):
            for at, *work in todo:

                @pl.when(i == at)
                def _(work=work):
                    for step in work:
                        step()

        def tiles(begin, own_g, give_g, todo):
            @pl.loop(begin, begin + half_g // tile)
            def _(j):
                slot = j % 2
                for copy in fetch(j):
                    copy.wait()

                @pl.when(j + 1 < ff // tile)
                def _():
                    for copy in fetch(j + 1):
                        copy.start()

                d_act = dot(db[...], w_dn[slot], ((1,), (1,)))
                d_gate = (d_act * gate_v[slot].astype(wide)).astype(low)
                d_up = (d_act * up_v[slot].astype(wide)).astype(low)
                resid[...] += dot(d_gate, w_gu[slot, 0].reshape(width, tile), ((1,), (1,))) + dot(
                    d_up, w_gu[slot, 1].reshape(width, tile), ((1,), (1,))
                )
                cols = pl.ds(pl.multiple_of((j - begin) * tile, tile), tile)
                mine = dot(ht[...], jnp.where(first, d_gate, d_up)).astype(low)
                own_g[:, :, cols] = mine.reshape(16, rows_chip, tile)
                other = dot(ht[...], jnp.where(first, d_up, d_gate)).astype(low)
                give_g[:, :, cols] = other.reshape(16, rows_chip, tile)
                between(j - begin, todo)

        tiles(0, bufs[7], given.at[1], [(0, lambda: down.pair(1)), (1, lambda: down.pair(0)), (5, down.diags)])
        for z in planes:
            left.begin(z)
        down.given()
        tiles(half_g // tile, bufs[14], given.at[0], [(2, down.relays, left.first, left.rest), (5, down.odd)])
        for z in planes:
            right.begin(z)
        for copy in loads[3:]:
            copy.wait()
        grad = resid[...]
        unit = norm_v[...]
        small_buf[0] = small[...]
        small_buf[0, 0:1, :] = column_sum(grad * unit)
        small_buf[0, 1:2, :] = column_sum(grad)
        exchange(0)
        back = norm_back(grad, vectors[0:1, :], unit, inv_v[:, 0:1])
        resid[...] = back
        d_one = back.astype(low)
        d_att[...] = dot(d_one, w_out[...].reshape(width, width), ((1,), (1,))).astype(low)
        grad_out = dot(att_v[...].T, d_one).astype(low).reshape(16, rows_chip, width)
        for i in range(2):
            a_grad[i, 1, :, :, part:] = grad_out[:, :, i * part : (i + 1) * part]
        left.diags()
        right.first()
        right.rest()
        left.given()
        right.given()

    block = lambda *dims: pltpu.VMEM(dims, low)
    block_wide = lambda *dims: pltpu.VMEM(dims, wide)
    pl.run_scoped(
        feed_forward, block(2, *bufs[0].shape), block(2, tok_rows, width),
        block(tok_rows, width), block(width, tok_rows), block(2, 2, 16, rows_chip, tile), block(2, tile, width),
        block(2, tok_rows, tile), block(2, tok_rows, tile), block(tok_rows, width), block_wide(tok_rows, width),
        block_wide(tok_rows, lane_width), block(16, rows_chip, width),
    )

    half = lambda side: pl.ds(pl.multiple_of(side * tok_rows, tok_rows), tok_rows)

    def attention_part(dq, dkv_own, dkv_out, x_t, d_k, d_v):
        slots = dkv_own.shape[0]

        def send_dkv(pair):
            return pltpu.make_async_remote_copy(
                src_ref=dkv_out.at[pair], dst_ref=dkv_in.at[pair], send_sem=pair_sem.at[0, pair],
                recv_sem=pair_sem.at[1, pair], device_id=place.sib, device_id_type=MESH,
            )

        def project(i):
            for pair in range(i * pairs // 2, (i + 1) * pairs // 2):
                send_dkv(pair).wait_recv()
                at = slice(pair * lane_width, (pair + 1) * lane_width)
                for j, dst in enumerate((d_k, d_v)):
                    dst[:, at] = (dkv_own[pair % slots, j] + dkv_in[pair, j].astype(wide)).astype(low)
            cols = slice(i * part, (i + 1) * part)
            for side, at, src in ((0, 0, dq), (0, part, d_k), (1, 0, d_v)):
                term = dot(x_t[...], src[:, cols]).astype(low)
                a_grad[i, side, :, :, at : at + part] = term.reshape(16, rows_chip, part)
            for z in planes:
                projs[i].begin(z)

        def attention(q_v, k_v, v_v, span_v, att_v, x, dk_sum, dv_sum):
            load = lambda i, src, dst: pltpu.make_async_copy(src, dst, in_sem.at[i])
            sources = ((q, q_v), (k, k_v), (v, v_v), (att, att_v))
            head, rest = slice(0, lane_width), slice(lane_width, width)
            loads = [load(0, span, span_v)]
            loads += [load(1 + i, src.at[:, head], dst.at[:, head]) for i, (src, dst) in enumerate(sources)]
            later = [load(5 + i, src.at[:, rest], dst.at[:, rest]) for i, (src, dst) in enumerate(sources)]
            later.append(load(9, tokens, x))
            for copy in loads + later:
                copy.start()
            for copy in loads:
                copy.wait()

            def arrive():
                for i, (src, dst) in enumerate(sources):
                    load(5 + i, src.at[:, rest], dst.at[:, rest]).wait()
                load(9, tokens, x).wait()
                x_t[...] = x[...].T

            def meet_small(i):
                combine(i)
                exchange(i + 1)

            def heads_back(begin, end, todo):
                @pl.loop(begin, end)
                def _(pair):
                    attend_back_pair(pair, heads, q_v, k_v, v_v, span_v, lse, att_v, d_att, dq, dk_sum, dv_sum)
                    for i, side in enumerate((dk_sum, dv_sum)):
                        dkv_own[lax.rem(pair, slots), i] = side[half(c), :]
                        dkv_out[pair, i] = side[half(1 - c), :].astype(low)
                    send_dkv(pair).start()
                    for at, *work in todo:

                        @pl.when(pair == at)
                        def _(at=at, work=work):
                            for step in work:
                                step()

            small_step = lambda i: lambda: meet_small(i)
            heads_back(0, 4, [
                (0, arrive, down.even, small_step(0)), (1, left.odd), (2, left.relays, right.diags), (3, right.odd),
            ])
            project(0)
            heads_back(4, pairs, [(4, left.even, early.first, early.rest, small_step(1)), (5, right.relays)])
            project(1)

        key_rows = k.shape[0]
        pl.run_scoped(
            attention, block(*q.shape), block(*k.shape), block(*v.shape), block_wide(*span.shape), block(*att.shape),
            block(tok_rows, width), block_wide(key_rows, lane_width), block_wide(key_rows, lane_width),
        )

        def meet_last():
            combine(2)
            spread()

        def finish(w_left, w_right):
            loads = [
                pltpu.make_async_copy(a_full.at[0, :, :, : 2 * width], w_left, in_sem.at[0]),
                pltpu.make_async_copy(a_full.at[1, :, :, :width], w_right, in_sem.at[1]),
            ]
            for copy in loads:
                copy.start()
            for copy in loads:
                copy.wait()
            w_q = w_left[:, :, :width].reshape(width, width)
            total = resid[...] + dot(dq[...], w_q, ((1,), (1,)))
            early.diags()
            late.first()
            late.rest()
            right.even()
            meet_last()
            w_k = w_left[:, :, width:].reshape(width, width)
            total += dot(d_k[...], w_k, ((1,), (1,)))
            early.relays()
            late.diags()
            early.odd()
            early.even()
            total += dot(d_v[...], w_right[...].reshape(width, width), ((1,), (1,)))
            tokens_v[...] = total.astype(low)
            hand_over(0, tokens_v, d_tokens).start()
            late.relays()
            late.odd()

        pl.run_scoped(finish, block(16, rows_chip, 2 * width), block(16, rows_chip, width))

        @pl.loop(0, pairs)
        def _(pair):
            send_dkv(pair).wait_send()

    pl.run_scoped(
        attention_part, block(tok_rows, width), block_wide(4, 2, tok_rows, lane_width),
        block(pairs, 2, tok_rows, lane_width), block(width, tok_rows), block(tok_rows, width), block(tok_rows, width),
    )
    mine, theirs = pl.ds(pl.multiple_of(24 * c, 8), 24), pl.ds(pl.multiple_of(24 - 24 * c, 8), 24)
    total = down.total()
    down_v[:rows_chip] = total[:, :width]
    down_v[rows_chip:] = total[:, width:]
    hand_over(1, down_v, down_out).start()

    def swap(i, m, total, other, slot):
        total[i] = m.total()
        last.put(total.at[i, theirs], other.at[i], slot, slot, place.sib)

    swap(0, left, g_sum, g_fin, 6)
    swap(1, right, g_sum, g_fin, 7)
    late.even()
    swap(0, early, a_sum, a_fin, 8)
    for z in (1, 2, 3):
        last.got(small_buf.at[6 + z], 2 + z, place.zn[z])
    sums = (small_buf[3] + small_buf[7]) + (small_buf[8] + small_buf[9])
    share = width // 32
    at_row = (lax.axis_index("rows") * 2 + c) * share
    tail[0:8, :] = pltpu.roll(sums[:8], lax.rem(width - at_row, width), 1)[:, :lane_width]
    squares = jnp.sum(sums[:8], 1, keepdims=True) / (sums[8:9, 0:1] * width)
    at = lambda axis: lax.broadcasted_iota(jnp.int32, (8, lane_width), axis)
    stats = jnp.where(at(0) == at(1) + 4, jnp.broadcast_to(jnp.sqrt(squares), (8, lane_width)), 0.0)
    tail[8:16, :] = jnp.broadcast_to(column_sum(stats), (8, lane_width))
    for i in range(2):
        last.got(g_fin.at[i], 6 + i, place.sib)
        own, other = g_sum[i, mine], g_fin[i]
        gu_v[:, i * half_g : (i + 1) * half_g] = jnp.where(first, own, other)
        gu_v[:, (i + 2) * half_g : (i + 3) * half_g] = jnp.where(first, other, own)
    hand_over(2, gu_v, gu_out).start()
    swap(1, late, a_sum, a_fin, 9)
    for i in range(2):
        last.got(a_fin.at[i], 8 + i, place.sib)
        own, other = a_sum[i, mine], a_fin[i]
        qk, vo = jnp.where(first, own, other), jnp.where(first, other, own)
        for j, term in enumerate((qk[:, :part], qk[:, part:], vo[:, :part])):
            at = j * width + i * part
            qkv_out[:, at : at + part] = term
        wout_out[:, i * part : (i + 1) * part] = vo[:, part:]
    for m in (down, left, right, early, late):
        m.drain()
    for m in (early, late):
        m.given()
    sent = [small_buf.at[0]] * 6 + [g_fin.at[0]] * 2 + [a_fin.at[0]] * 2
    for slot, ref in enumerate(sent):
        last.sent(ref, slot, place.sib)
    for i, pair in enumerate(((tokens_v, d_tokens), (down_v, down_out), (gu_v, gu_out))):
        hand_over(i, *pair).wait()


def back(
    heads, tokens, q, k, v, span, att, hid_t, norm, inv, gate, up, act, d_hid, d_branch, a_full, g_full, d_full,
    lse, vectors, small,
):
    low, wide = jnp.bfloat16, jnp.float32
    tok_rows, width = tokens.shape
    ff = gate.shape[1]
    half_g = ff // 2
    pairs = heads // 2
    d_rows = ff // 32
    bufs = []
    for i, cols in enumerate((2 * width, half_g, half_g, width, width)):
        bufs += [pltpu.VMEM((count, rows_chip, cols), low) for count in (16, 16, 2, 2, 4, 4, 3)[i >= 3 :]]
    vmem, hbm = pl.BlockSpec(memory_space=pltpu.VMEM), pl.BlockSpec(memory_space=pl.ANY)
    dma = lambda *shape: pltpu.SemaphoreType.DMA(shape)
    shape = jax.ShapeDtypeStruct
    return pl.pallas_call(
        lambda *refs: back_kernel(heads, *refs),
        out_shape=(
            shape((tok_rows, width), low), shape((24, 3 * width), wide), shape((24, width), wide),
            shape((24, 2 * ff), wide), shape((d_rows, width), wide), shape((16, lane_width), wide),
        ),
        in_specs=[hbm] * 17 + [vmem] * 3,
        out_specs=(hbm, vmem, vmem, hbm, hbm, vmem),
        scratch_shapes=bufs
        + [
            pltpu.VMEM((2, 2, 16, rows_chip, width), low),
            pltpu.VMEM((pairs, 2, tok_rows, lane_width), low),
            pltpu.VMEM((tok_rows, width), wide),
            pltpu.VMEM((tok_rows, width), low),
            pltpu.VMEM((2, rows_chip, half_g), wide),
            pltpu.VMEM((2, rows_chip, width), wide),
            pltpu.VMEM((2, 24, half_g), wide),
            pltpu.VMEM((2, 24, width), wide),
            pltpu.VMEM((10,) + small.shape, wide),
            dma(10),
            dma(5 * scatter_slots),
            pltpu.VMEM((tok_rows, width), low),
            pltpu.VMEM((d_rows, width), wide),
            pltpu.VMEM((24, 2 * ff), wide),
            dma(2, pairs),
            dma(2, 10),
            dma(10),
            dma(4, 2),
        ],
        compiler_params=pltpu.CompilerParams(
            collective_id=1, has_side_effects=True, vmem_limit_bytes=63 * 2**20
        ),
        name="backward_and_sums",
    )(tokens, q, k, v, span, att, hid_t, norm, inv, gate, up, act, d_hid, d_branch, a_full, g_full, d_full, lse, vectors, small)


def close_kernel(share, *refs):
    parts, tail, outs = refs[:6], refs[6], refs[7:]
    for part, out in zip(parts, outs):
        out[...] = part[...]
    for i, out in enumerate(outs[6:10]):
        out[...] = tail[i : i + 1, :share]
    outs[10][...] = tail[8:9, :4]


def close(share, *parts):
    vmem = pl.BlockSpec(memory_space=pltpu.VMEM)
    wide = jnp.float32
    return pl.pallas_call(
        lambda *refs: close_kernel(share, *refs),
        out_shape=tuple(jax.ShapeDtypeStruct(part.shape, part.dtype) for part in parts[:6])
        + (jax.ShapeDtypeStruct((1, share), wide),) * 4
        + (jax.ShapeDtypeStruct((1, 4), wide),),
        in_specs=[vmem] * 7,
        out_specs=(vmem,) * 11,
        compiler_params=pltpu.CompilerParams(vmem_limit_bytes=62 * 2**20),
        name="results",
    )(*parts)


def window(cells, width):
    count = lax.axis_size("blk")
    before = lax.ppermute(cells, "blk", [(i, i + 1) for i in range(count - 1)])
    after = lax.ppermute(cells, "blk", [(i + 1, i) for i in range(count - 1)])
    return jnp.concatenate([before, cells, after], 0)


def window_back(terms, width):
    count = lax.axis_size("blk")
    low = jnp.bfloat16
    before = lax.ppermute(terms[2 * width :].astype(low), "blk", [(i, i + 1) for i in range(count - 1)])
    after = lax.ppermute(terms[:width].astype(low), "blk", [(i + 1, i) for i in range(count - 1)])
    return terms[width : 2 * width] + before.astype(terms.dtype) + after.astype(terms.dtype)


def key_spans(labels, first, tok_rows):
    seq_len = labels.shape[0]
    query_pos = first + jnp.arange(tok_rows, dtype=jnp.int32)
    query_labels = lax.dynamic_slice_in_dim(labels, first, tok_rows, 0)
    if seq_len == 2 * tok_rows:
        key_pos, key_labels = jnp.arange(seq_len, dtype=jnp.int32), labels
    else:
        key_pos = first - tok_rows + jnp.arange(3 * tok_rows, dtype=jnp.int32)
        padded = jnp.pad(labels, (tok_rows, tok_rows), constant_values=seq_len)
        key_labels = lax.dynamic_slice_in_dim(padded, first, 3 * tok_rows, 0)
    same = (key_labels[:, None] == query_labels[None, :]) & (key_labels[:, None] != seq_len)
    gap = jnp.abs(key_pos[:, None] - query_pos[None, :])
    return jnp.where(same | (gap == 0), gap.astype(jnp.float32), far)


def on_chip_grid():
    return lax.axis_size("rows") == 16 and lax.axis_size("blk") == 2


def packed_shards(w_qkv, w_out, ln1_gain, ln1_bias, w_gate_up, ln2_gain, ln2_bias):
    width = w_out.shape[1]
    ff = w_gate_up.shape[1] // 2
    table = jnp.stack((ln1_gain, ln1_bias, ln2_gain, ln2_bias), 1)
    table = jnp.pad(table, ((0, 0), (0, lane_width - 4)))
    left = jnp.concatenate([w_qkv[:, : 2 * width], table], 1)
    right = jnp.concatenate([w_qkv[:, 2 * width :], w_out, jnp.zeros_like(table)], 1)
    return jnp.stack([left, right]), jnp.stack([w_gate_up[:, :ff], w_gate_up[:, ff:]])


def on_grid(tokens, labels, w_qkv, w_out, w_gate_up, w_down, norms, out_grad):
    width = tokens.shape[1]
    (
        a_full, g_full, d_full, q, k, v, att, hid_t, norm, inv, gate, up, act, output, d_hid, d_branch, span,
        lse, vectors, small,
    ) = fore(HEADS, tokens, labels, w_qkv, w_out, w_gate_up, w_down, norms, out_grad)
    parts = back(
        HEADS, tokens, q, k, v, span, att, hid_t, norm, inv, gate, up, act, d_hid, d_branch, a_full, g_full,
        d_full.reshape(-1, width), lse, vectors, small,
    )
    *parts, one, two, three, four, stats = close(norms[0].shape[0], output, *parts)
    rows = [row.reshape(-1) for row in (one, two, three, four)]
    return *parts, rows, stats.reshape(-1)


def on_any(tokens, labels, w_qkv, w_out, w_gate_up, w_down, norms, out_grad):
    both = ("rows", "blk")
    tok_rows, width = tokens.shape
    first = lax.axis_index("blk") * tok_rows
    span = key_spans(labels[0], first, tok_rows)
    here = lax.dynamic_slice_in_dim(labels[0], first, tok_rows, 0)
    valid = (here != labels.shape[1]).astype(jnp.float32)[:, None]
    a_shard, g_shard = packed_shards(w_qkv, w_out, *norms[:2], w_gate_up, *norms[2:])
    low, wide = jnp.bfloat16, jnp.float32
    a_full = lax.all_gather(a_shard, both, axis=1, tiled=True)
    w_gu = lax.all_gather(g_shard, both, axis=1, tiled=True)
    w_dn = lax.all_gather(w_down, both, axis=0, tiled=True)
    vectors = jnp.pad(a_full[0, :, 2 * width : 2 * width + 4].astype(wide).T, ((0, 4), (0, 0)))
    w_qk, w_v = a_full[0, :, : 2 * width], a_full[1, :, :width]
    qk = jnp.dot(tokens, w_qk, preferred_element_type=wide).astype(low)
    v = jnp.dot(tokens, w_v, preferred_element_type=wide).astype(low)
    query = qk[:, :width] * (width // HEADS) ** -0.5
    kv = window(jnp.concatenate([qk[:, width:], v], 1), tok_rows)
    keys, values = kv[:, :width], kv[:, width:]
    attended, lse = attend(query, keys, values, span, HEADS)
    output, d_resid_one, d_att, grad_out, g_grad, d_grad, small = ffn(
        tokens, attended, a_full, vectors, valid, out_grad, w_gu, w_dn
    )
    dq, dk, dv = attend_back(query, keys, values, span, lse, attended, d_att, HEADS)
    dkv = window_back(jnp.concatenate([dk, dv], 1), tok_rows)
    d_qk = jnp.concatenate([dq, dkv[:, :width].astype(low)], 1)
    d_v = dkv[:, width:].astype(low)
    grad_qkv = transposed_times(tokens, jnp.concatenate([d_qk, d_v], 1))
    d_tokens = d_resid_one + times_transposed(d_qk, w_qk) + times_transposed(d_v, w_v)
    share = lambda g, axis: lax.psum_scatter(g.astype(wide), both, scatter_dimension=axis, tiled=True)
    gate, up = share(g_grad, 1)
    small = lax.psum(small, both)
    size = norms[0].shape[0]
    rows = lax.dynamic_slice_in_dim(small[:4], lax.axis_index(both) * size, size, 1)
    stats = jnp.sqrt(jnp.sum(small[4:8], 1) / (small[8, 0] * width))
    return (
        output, d_tokens.astype(low), share(grad_qkv, 0), share(grad_out, 0), jnp.concatenate([gate, up], 1),
        share(d_grad, 0), rows, stats,
    )


def body(
    tokens, segments, w_qkv, w_out, ln1_gain, ln1_bias, w_gate_up, w_down, ln2_gain, ln2_bias, out_grad,
):
    run = on_grid if on_chip_grid() else on_any
    norms = (ln1_gain, ln1_bias, ln2_gain, ln2_bias)
    output, d_tokens, qkv, wout, gate_up, down, rows, stats = run(
        tokens[0], segments, w_qkv, w_out, w_gate_up, w_down, norms, out_grad[0]
    )
    return (
        output[None], d_tokens[None], qkv, wout, rows[0], rows[1], gate_up, down, rows[2], rows[3], stats,
    )


def solution(mesh):
    placed = (
        P("rows", "blk", None),
        P("rows", None),
        P(("rows", "blk"), None),
        P(("rows", "blk"), None),
        P(("rows", "blk")),
        P(("rows", "blk")),
        P(("rows", "blk"), None),
        P(("rows", "blk"), None),
        P(("rows", "blk")),
        P(("rows", "blk")),
        P("rows", "blk", None),
    )
    return jax.shard_map(
        body,
        mesh=mesh,
        in_specs=placed,
        out_specs=(
            P("rows", "blk", None),
            P("rows", "blk", None),
            P(("rows", "blk"), None),
            P(("rows", "blk"), None),
            P(("rows", "blk")),
            P(("rows", "blk")),
            P(("rows", "blk"), None),
            P(("rows", "blk"), None),
            P(("rows", "blk")),
            P(("rows", "blk")),
            P(),
        ),
        check_vma=False,
    )
```

```python
import jax
import jax.numpy as jnp
from jax import lax
from jax.experimental import pallas as pl
from jax.experimental.pallas import tpu as pltpu
from jax.sharding import PartitionSpec as P

HEADS = 12


ln_eps = 1e-12
far = 1e33
lane_width = 128


def times_transposed(left, right):
    return lax.dot_general(
        left, right, (((1,), (1,)), ((), ())), preferred_element_type=jnp.float32
    )


def transposed_times(left, right):
    return lax.dot_general(
        left, right, (((0,), (0,)), ((), ())), preferred_element_type=jnp.float32
    )


MESH = pl.DeviceIdType.MESH


class Place:
    def __init__(self):
        r, self.c = lax.axis_index("rows"), lax.axis_index("blk")
        self.x, self.y, self.z = r % 2, (r // 2) % 2, r // 4
        self.sib = (r, 1 - self.c)
        self.xn = (self.at(0, "x"), self.c)
        self.yn = (self.at(0, "y"), self.c)
        self.zn = {k: (self.at(k, "o"), self.c) for k in (1, 2, 3)}

    def plane(self, k):
        z, low = self.z % 2, self.z // 2
        if k % 2:
            z = 1 - z
        if k // 2:
            low = 1 - low
        return low * 2 + z

    def at(self, k, j):
        x = 1 - self.x if j in "xd" else self.x
        y = 1 - self.y if j in "yd" else self.y
        return self.plane(k) * 4 + y * 2 + x

    def greet(self):
        self.barrier = pltpu.get_barrier_semaphore()
        for peer in (self.sib, self.xn, self.yn, *self.zn.values()):
            pl.semaphore_signal(self.barrier, inc=1, device_id=peer, device_id_type=MESH)

    def meet(self):
        pl.semaphore_wait(self.barrier, 6)


class Copies:
    def __init__(self, send, recv):
        self.send, self.recv = send, recv

    def of(self, src, dst, pool, slot, peer):
        return pltpu.make_async_remote_copy(
            src_ref=src, dst_ref=dst, send_sem=self.send.at[pool], recv_sem=self.recv.at[slot],
            device_id=peer, device_id_type=MESH,
        )

    def put(self, src, dst, pool, slot, peer):
        self.of(src, dst, pool, slot, peer).start()

    def got(self, dst, slot, peer):
        self.of(dst, dst, 0, slot, peer).wait_recv()

    def sent(self, all_of_pool, pool, peer):
        self.of(all_of_pool, all_of_pool, pool, 0, peer).wait_send()


class Gather:
    def __init__(self, place, copies, i, side):
        self.p, self.cp, self.side = place, copies, side
        self.base, self.pool = i * gather_slots, 2 * i

    def slot(self, kind, k=0):
        return self.base + {"z": -1, "x": 3, "y": 7, "d": 11, "s": 15}[kind] + k

    def out(self, half, r):
        return self.side(half).at[r]

    def block(self, k, j):
        return self.out(self.p.c, self.p.at(k, j))

    def send(self, src, dst, slot, peer):
        self.cp.put(src, dst, self.pool, slot, peer)

    def push(self, src, k, j):
        self.cp.put(src, self.block(k, j), self.pool + 1, self.slot("s", k), self.p.sib)

    def to_z(self):
        for k in (1, 2):
            self.send(self.block(0, "o"), self.block(0, "o"), self.slot("z", k), self.p.zn[k])

    def to_xy(self):
        self.spread(self.block(0, "o"), 0)

    def spread(self, src, k):
        dst = self.block(k, "o")
        self.send(src, dst, self.slot("x", k), self.p.xn)
        self.send(src, dst, self.slot("y", k), self.p.yn)
        self.push(src, k, "o")

    def from_z(self, k):
        block = self.block(k, "o")
        self.cp.got(block, self.slot("z", k), self.p.zn[k])
        if k == 2:
            self.send(block, block, self.slot("z", 3), self.p.zn[1])
        self.spread(block, k)

    @staticmethod
    def schedule(mats):
        work = [(mats[0].to_z,)] + [(m.to_xy,) for m in mats[:3]]
        for i, m in enumerate(mats):
            before = mats[i - 1] if i else None
            work.append((m.from_z, 1))
            if i + 1 < len(mats):
                work.append((mats[i + 1].to_z,))
            if before:
                work.append((before.from_xy, 3))
            work += [(m.from_xy, 0), (m.from_z, 2)]
            if before:
                work.append((before.from_d, 2))
            if i + 3 < len(mats):
                work.append((mats[i + 3].to_xy,))
            work += [(m.from_xy, 1), (m.from_z, 3)]
            if before:
                work.append((before.from_d, 1))
            work.append((m.from_d, 0))
            if before:
                work.append((before.from_d, 3))
            work.append((m.from_xy, 2))
        last = mats[-1]
        return work + [(last.from_xy, 3), (last.from_d, 2), (last.from_d, 1), (last.from_d, 3)]

    def from_xy(self, k):
        x, y = self.block(k, "x"), self.block(k, "y")
        self.cp.got(x, self.slot("x", k), self.p.xn)
        if k == 2:
            self.send(x, x, self.slot("d", k), self.p.yn)
        self.cp.got(y, self.slot("y", k), self.p.yn)
        if k == 0:
            self.send(y, y, self.slot("d", k), self.p.xn)
        self.push(x, k, "x")
        self.push(y, k, "y")

    def from_d(self, k):
        block = self.block(k, "d")
        self.cp.got(block, self.slot("d", k), self.p.xn)
        if k % 2 == 0:
            self.send(block, block, self.slot("d", k + 1), self.p.zn[1])
        self.push(block, k, "d")

    def from_sib(self, *planes):
        for k in planes or range(4):
            four = pl.ds(self.p.plane(k) * 4, 4)
            self.cp.got(self.side(1 - self.p.c).at[four], self.slot("s", k), self.p.sib)

    def drain(self):
        side = self.side(self.p.c)
        self.cp.sent(side.at[pl.ds(0, 15)], self.pool, self.p.sib)
        self.cp.sent(side, self.pool + 1, self.p.sib)


class Scatter:
    def __init__(self, place, copies, i, give, own, sib, rly, dia, xin, yin, zin, straight=False, flat=False):
        self.p, self.cp, self.give, self.own = place, copies, give, own
        self.base, self.pool = i * scatter_slots, 2 * i
        self.straight, self.flat = straight, flat
        self.sib, self.rly, self.dia, self.xin, self.yin, self.zin = sib, rly, dia, xin, yin, zin

    def slot(self, kind, k):
        return self.base + {"s": 0, "r": 4, "d": 5, "x": 8, "y": 12, "z": 15}[kind] + k

    def four(self, k):
        return pl.ds(self.p.plane(k) * 4, 4)

    def begin(self, k):
        four = self.four(k)
        self.cp.put(self.give(four), self.sib.at[four], self.pool + 1, self.slot("s", k), self.p.sib)

    def given(self):
        self.cp.sent(self.sib, self.pool + 1, self.p.sib)

    def drain(self):
        self.cp.sent(self.sib.at[pl.ds(0, 15)], self.pool, self.p.sib)

    def to_x(self, own, k):
        self.cp.put(own, self.xin.at[k], self.pool, self.slot("x", k), self.p.xn)

    def to_y(self, own, k):
        self.cp.put(own, self.yin.at[k], self.pool, self.slot("y", k), self.p.yn)

    def both(self, k, j, *more):
        at = self.p.at(k, j)
        own = self.own(at)
        total = own[...] + self.sib[at]
        for ref in more:
            total = total + ref[...]
        own[...] = total
        return own

    def pair(self, k):
        four = self.four(k)
        self.cp.got(self.sib.at[four], self.slot("s", k), self.p.sib)
        if self.flat:
            self.to_relay(self.both(k, "d"), k)
        elif k % 2:
            i = k // 2
            self.cp.put(self.both(k, "d"), self.dia.at[i], self.pool, self.slot("d", 2 * i), self.p.zn[1])
        odd = k % 2 and not self.flat
        if odd or k < 2:
            self.to_x(self.both(k, "x"), k)
        if odd or k >= 2:
            self.to_y(self.both(k, "y"), k)

    def relay_at(self, k):
        return (self.dia if k % 2 else self.rly).at[k // 2]

    def to_relay(self, own, k):
        slot = self.slot("d", k - 1) if k % 2 else self.slot("r", k)
        self.cp.put(own, self.relay_at(k), self.pool, slot, self.p.xn if k < 2 else self.p.yn)

    def diag(self, k):
        i = k // 2
        self.cp.got(self.dia.at[i], self.slot("d", k), self.p.zn[1])
        self.to_relay(self.both(k, "d", self.dia.at[i]), k)

    def relay(self, k):
        rly = self.relay_at(k)
        self.cp.got(rly, self.slot("d", k - 1) if k % 2 else self.slot("r", k), self.p.xn)
        if k < 2:
            self.to_y(self.both(k, "y", rly), k)
        else:
            self.to_x(self.both(k, "x", rly), k)

    def plane(self, k):
        p = self.p
        at = p.at(k, "o")
        self.cp.got(self.xin.at[k], self.slot("x", k), p.xn)
        self.cp.got(self.yin.at[k], self.slot("y", k), p.yn)
        wide = jnp.float32
        own = self.own(at)
        total = (own[...].astype(wide) + self.sib[at].astype(wide)) + (
            self.xin[k].astype(wide) + self.yin[k].astype(wide)
        )
        own[...] = total.astype(jnp.bfloat16)
        if self.straight and k:
            self.to_z(own, k, k)
        elif k % 2:
            self.to_z(own, k, 1)

    def to_z(self, own, k, step):
        self.cp.put(own, self.zin.at[k - 1], self.pool, self.slot("z", k), self.p.zn[step])

    def cross(self):
        self.cp.got(self.zin.at[2], self.slot("z", 3), self.p.zn[1])
        own = self.own(self.p.at(2, "o"))
        own[...] = own[...] + self.zin[2]
        self.to_z(own, 2, 2)

    def all(self, name, *planes):
        for k in planes:
            getattr(self, name)(k)

    def first(self):
        self.all("pair", 3, 1)

    def rest(self):
        self.all("pair", 2, 0)

    def diags(self):
        if not self.flat:
            self.all("diag", 2, 0)

    def relays(self):
        self.all("relay", *((3, 1, 2, 0) if self.flat else (2, 0)))

    def odd(self):
        self.all("plane", 3, 1)

    def even(self):
        self.all("plane", 2, 0)
        if not self.straight:
            self.cross()

    def total(self):
        wide = jnp.float32
        total = self.own(self.p.at(0, "o"))[...].astype(wide)
        for k in (1, 2, 3) if self.straight else (1, 2):
            self.cp.got(self.zin.at[k - 1], self.slot("z", k), self.p.zn[k])
            total = total + self.zin[k - 1].astype(wide)
        return total


rows_chip = 48
gather_slots, scatter_slots = 19, 19


def dot(left, right, dims=((1,), (0,))):
    return lax.dot_general(left, right, (dims, ((), ())), preferred_element_type=jnp.float32)


def row_mean(values):
    return jnp.mean(values, -1, keepdims=True)


def normalized(resid):
    centred = resid - row_mean(resid)
    inverse = lax.rsqrt(row_mean(centred * centred) + ln_eps)
    return centred * inverse, inverse


def norm_back(grad, gain, norm, inverse):
    e = grad * gain
    return inverse * (e - row_mean(e) - norm * row_mean(e * norm))


def column_sum(values):
    return jnp.sum(values, 0, keepdims=True)


def ffn_kernel(
    tokens, attended, w_out, vectors, valid, out_grad, w_gu, w_down,
    output, d_resid_one, d_att, grad_out, grad_gu, grad_down, small,
    hid, hid_low, hid_t, norm_one, inv_one, slope_gate, slope_up, act, total, d_hid, d_branch,
):
    i = pl.program_id(0)
    tiles = pl.num_programs(0) // 2
    low = jnp.bfloat16
    wide = jnp.float32

    @pl.when(i == 0)
    def _():
        branch = dot(attended[...], w_out[0])
        toks = tokens[...].astype(wide)
        norm, inverse = normalized(toks + branch)
        norm_one[...] = norm
        inv_one[...] = inverse
        hidden = norm * vectors[0:1, :] + vectors[1:2, :]
        hid[...] = hidden
        hid_low[...] = hidden.astype(low)
        hid_t[...] = hidden.T.astype(low)
        mask = valid[...]
        small[4:5, :] = column_sum(mask * toks * toks)
        small[5:6, :] = column_sum(mask * branch * branch)
        small[6:7, :] = column_sum(mask * hidden * hidden)
        small[8:16, :] = jnp.zeros((8, small.shape[1]), wide)
        small[8:9, :] = jnp.broadcast_to(jnp.sum(mask, 0, keepdims=True), (1, small.shape[1]))
        total[...] = jnp.zeros_like(total)

    @pl.when(i < tiles)
    def _():
        h = hid_low[...]
        gate = dot(h, w_gu[0])
        up = dot(h, w_gu[1])
        cdf = 0.5 + 0.5 * lax.erf(gate * 0.7071067811865476)
        glu = gate * cdf
        density = 0.3989422804014327 * jnp.exp(-0.5 * gate * gate)
        slope_up[i] = glu
        slope_gate[i] = up * (cdf + gate * density)
        a = (glu * up).astype(low)
        act[i] = a
        total[...] += dot(a, w_down[...])

    @pl.when(i == tiles - 1)
    def _():
        branch = total[...]
        mask = valid[...]
        small[7:8, :] = column_sum(mask * branch * branch)
        norm, inverse = normalized(hid[...] + branch)
        gain = vectors[2:3, :]
        output[...] = (norm * gain + vectors[3:4, :]).astype(low)
        grad = out_grad[...].astype(wide)
        small[2:3, :] = column_sum(grad * norm)
        small[3:4, :] = column_sum(grad)
        back = norm_back(grad, gain, norm, inverse)
        d_hid[...] = back
        d_branch[...] = back.astype(low)

    @pl.when(i >= tiles)
    def _():
        j = i - tiles
        db = d_branch[...]
        grad_down[...] = dot(act[j].T, db).astype(low)
        d_act = dot(db, w_down[...], ((1,), (1,)))
        d_gate = (d_act * slope_gate[j]).astype(low)
        d_up = (d_act * slope_up[j]).astype(low)
        h_t = hid_t[...]
        grad_gu[0] = dot(h_t, d_gate).astype(low)
        grad_gu[1] = dot(h_t, d_up).astype(low)
        d_hid[...] += dot(d_gate, w_gu[0], ((1,), (1,))) + dot(d_up, w_gu[1], ((1,), (1,)))

    @pl.when(i == 2 * tiles - 1)
    def _():
        grad = d_hid[...]
        norm = norm_one[...]
        small[0:1, :] = column_sum(grad * norm)
        small[1:2, :] = column_sum(grad)
        back = norm_back(grad, vectors[0:1, :], norm, inv_one[...])
        d_resid_one[...] = back
        db = back.astype(low)
        grad_out[...] = dot(attended[...].T, db).astype(low)
        d_att[...] = dot(db, w_out[0], ((1,), (1,))).astype(low)


def ffn(tokens, attended, a_full, vectors, valid, out_grad, w_gu, w_down):
    rows, width = tokens.shape
    ff = w_down.shape[0]
    tile = 512
    tiles = ff // tile
    low, wide = jnp.bfloat16, jnp.float32
    whole = lambda *shape: pl.BlockSpec(shape, lambda i: (0,) * len(shape))
    at = lambda i: jnp.where(i < tiles, i, i - tiles)
    late = lambda i: jnp.maximum(i - tiles, 0)
    return pl.pallas_call(
        ffn_kernel,
        grid=(2 * tiles,),
        out_shape=(
            jax.ShapeDtypeStruct((rows, width), low),
            jax.ShapeDtypeStruct((rows, width), wide),
            jax.ShapeDtypeStruct((rows, width), low),
            jax.ShapeDtypeStruct((width, width), low),
            jax.ShapeDtypeStruct((2, width, ff), low),
            jax.ShapeDtypeStruct((ff, width), low),
            jax.ShapeDtypeStruct((16, width), wide),
        ),
        in_specs=[
            whole(rows, width),
            whole(rows, width),
            pl.BlockSpec((1, width, width), lambda i: (1, 0, 1)),
            whole(8, width),
            whole(rows, 1),
            whole(rows, width),
            pl.BlockSpec((2, width, tile), lambda i: (0, 0, at(i))),
            pl.BlockSpec((tile, width), lambda i: (at(i), 0)),
        ],
        out_specs=(
            whole(rows, width),
            whole(rows, width),
            whole(rows, width),
            whole(width, width),
            pl.BlockSpec((2, width, tile), lambda i: (0, 0, late(i))),
            pl.BlockSpec((tile, width), lambda i: (late(i), 0)),
            whole(16, width),
        ),
        scratch_shapes=[
            pltpu.VMEM((rows, width), wide),
            pltpu.VMEM((rows, width), low),
            pltpu.VMEM((width, rows), low),
            pltpu.VMEM((rows, width), wide),
            pltpu.VMEM((rows, 1), wide),
            pltpu.VMEM((tiles, rows, tile), wide),
            pltpu.VMEM((tiles, rows, tile), wide),
            pltpu.VMEM((tiles, rows, tile), low),
            pltpu.VMEM((rows, width), wide),
            pltpu.VMEM((rows, width), wide),
            pltpu.VMEM((rows, width), low),
        ],
        compiler_params=pltpu.CompilerParams(vmem_limit_bytes=60 * 2**20),
        cost_estimate=pl.CostEstimate(
            flops=2 * rows * width * (9 * ff + 3 * width), bytes_accessed=18 * ff * width, transcendentals=2 * rows * ff
        ),
        name="feed_forward",
    )(tokens, attended, a_full, vectors, valid, out_grad, w_gu, w_down)


def half_of(block, axis, second):
    place = lax.broadcasted_iota(jnp.int32, block.shape, axis)
    depth = block.shape[axis] // 2
    keep = place >= depth if second else place < depth
    return jnp.where(keep, block, jnp.zeros_like(block))


def attend_kernel(heads, q, k, v, span, attended, lse):
    @pl.loop(0, heads // 2)
    def _(pair):
        attend_pair(pair, heads, q, k, v, span, lse, attended)


def attend(q, k, v, span, heads):
    rows, width = q.shape
    keys = k.shape[0]
    low, wide = jnp.bfloat16, jnp.float32
    return pl.pallas_call(
        lambda *refs: attend_kernel(heads, *refs),
        out_shape=(
            jax.ShapeDtypeStruct((rows, width), low),
            jax.ShapeDtypeStruct((16, rows), wide),
        ),
        in_specs=[pl.BlockSpec(memory_space=pltpu.VMEM)] * 4,
        out_specs=(pl.BlockSpec(memory_space=pltpu.VMEM),) * 2,
        compiler_params=pltpu.CompilerParams(vmem_limit_bytes=60 * 2**20),
        cost_estimate=pl.CostEstimate(flops=4 * rows * keys * width, bytes_accessed=8 * keys * width, transcendentals=heads * rows * keys),
        name="attend",
    )(q, k, v, span)


def attend_back_pair(pair, heads, q, k, v, span, lse, att, d_att, dq, dk_sum, dv_sum):
    low, wide = jnp.bfloat16, jnp.float32
    rows, width = q.shape
    lanes = lane_width
    depth = width // heads
    chunk = 256
    scale = depth**-0.5
    at = pl.ds(pl.multiple_of(pair * lanes, lanes), lanes)
    keys, values = k[:, at], v[:, at]
    keys_t = keys.astype(wide).T.astype(low)
    for c in range(rows // chunk):
        here = pl.ds(c * chunk, chunk)
        q_wide = q[here, at].astype(wide)
        do_here = d_att[here, at]
        do_wide = do_here.astype(wide)
        q_here = q_wide.astype(low)
        q_t, do_t = q_wide.T.astype(low), do_wide.T.astype(low)
        both_t = (do_wide * att[here, at].astype(wide)).T
        dk_part, dv_part, dq_parts = None, None, []
        for h in (0, 1):
            head = 2 * pair + h
            own = slice(h * depth, (h + 1) * depth)
            slope = jnp.exp2(jnp.full((1, 1), -8.0 / heads, wide) * (head + 1).astype(wide))
            delta = jnp.sum(both_t[own], 0, keepdims=True)
            logits = dot(keys, half_of(q_t, 0, h)) - slope * span[:, here]
            probs = jnp.exp(logits - lse[pl.ds(head, 1), here])
            d_probs = dot(values, half_of(do_t, 0, h))
            d_logits = (probs * (d_probs - delta)).astype(low)
            dv_term = dot(probs.astype(low), half_of(do_here, 1, h))
            dk_term = dot(d_logits, half_of(q_here, 1, h))
            dv_part = dv_term if dv_part is None else dv_part + dv_term
            dk_part = dk_term if dk_part is None else dk_part + dk_term
            dq_parts.append(dot(keys_t[own], d_logits) * scale)
        if c == 0:
            dk_sum[...] = dk_part
            dv_sum[...] = dv_part
        else:
            dk_sum[...] += dk_part
            dv_sum[...] += dv_part
        dq[here, at] = jnp.concatenate(dq_parts, 0).T.astype(low)


def attend_back_kernel(heads, q, k, v, span, lse, att, d_att, dq, dk, dv, dk_sum, dv_sum):
    @pl.loop(0, heads // 2)
    def _(pair):
        attend_back_pair(pair, heads, q, k, v, span, lse, att, d_att, dq, dk_sum, dv_sum)
        at = pl.ds(pl.multiple_of(pair * lane_width, lane_width), lane_width)
        dk[:, at] = dk_sum[...]
        dv[:, at] = dv_sum[...]


def attend_back(q, k, v, span, lse, att, d_att, heads):
    rows, width = q.shape
    keys = k.shape[0]
    low, wide = jnp.bfloat16, jnp.float32
    return pl.pallas_call(
        lambda *refs: attend_back_kernel(heads, *refs),
        out_shape=(
            jax.ShapeDtypeStruct((rows, width), low),
            jax.ShapeDtypeStruct((keys, width), wide),
            jax.ShapeDtypeStruct((keys, width), wide),
        ),
        in_specs=[pl.BlockSpec(memory_space=pltpu.VMEM)] * 7,
        out_specs=(pl.BlockSpec(memory_space=pltpu.VMEM),) * 3,
        scratch_shapes=[
            pltpu.VMEM((keys, lane_width), wide),
            pltpu.VMEM((keys, lane_width), wide),
        ],
        compiler_params=pltpu.CompilerParams(vmem_limit_bytes=60 * 2**20),
        cost_estimate=pl.CostEstimate(flops=10 * rows * keys * width, bytes_accessed=16 * keys * width, transcendentals=heads * rows * keys),
        name="attend_back",
    )(q, k, v, span, lse, att, d_att)


def attend_pair(pair, heads, q, k, v, span, lse, attended):
    low, wide = jnp.bfloat16, jnp.float32
    rows, width = q.shape
    lanes = lane_width
    depth = width // heads
    chunk = 256
    at = pl.ds(pl.multiple_of(pair * lanes, lanes), lanes)
    keys = k[:, at]
    values_t = v[:, at].astype(wide).T.astype(low)
    for c in range(rows // chunk):
        here = pl.ds(c * chunk, chunk)
        q_t = q[here, at].astype(wide).T.astype(low)
        parts = []
        for h in (0, 1):
            head = 2 * pair + h
            slope = jnp.exp2(jnp.full((1, 1), -8.0 / heads, wide) * (head + 1).astype(wide))
            logits = dot(keys, half_of(q_t, 0, h)) - slope * span[:, here]
            top = jnp.max(logits, 0, keepdims=True)
            weights = jnp.exp(logits - top)
            norm = jnp.sum(weights, 0, keepdims=True)
            lse[pl.ds(head, 1), here] = top + jnp.log(norm)
            parts.append(dot(values_t[h * depth : (h + 1) * depth], weights.astype(low)) / norm)
        attended[here, at] = jnp.concatenate(parts, 0).T.astype(low)


def fore_kernel(
    heads, tokens_at, labels_at, w_qkv_at, w_out_at, w_gu_at, d_shard_at, gain_one_at, bias_one_at, gain_two_at, bias_two_at,
    out_grad, a_full, g_full, d_full, q_out, k_out, v_out, att_out, hid_t_out, norm_out, inv_out, gate_out, up_out, act_out,
    output_out, d_hid_out, d_branch_out, span_out, lse, vectors, small,
    w_a, w_g, w_d, a_give, g_give, a_pair, g_pair, turned, q, k, v, att, span_v, grad_v, hid, hid_low, hid_t, norm_one, inv_one,
    slope_gate, slope_up, act, output, d_hid, d_branch,
    tokens, labels, w_qkv, w_out, w_gu, d_shard, gain_one, bias_one, gain_two, bias_two, pair_sem, send, recv, in_sem, out_sem,
):
    place = Place()
    sources = (
        w_gu_at, w_qkv_at, w_out_at, gain_one_at, bias_one_at, gain_two_at, bias_two_at, d_shard_at, labels_at, tokens_at,
    )
    held = (w_gu, w_qkv, w_out, gain_one, bias_one, gain_two, bias_two, d_shard, labels, tokens)
    inward = [pltpu.make_async_copy(src, dst, in_sem.at[1 + i]) for i, (src, dst) in enumerate(zip(sources, held))]
    for copy in inward:
        copy.start()
    place.greet()
    c = place.c
    low, wide = jnp.bfloat16, jnp.float32
    tok_rows, width = tokens.shape
    ff = w_g.shape[3]
    half_g = ff // 2
    pairs = heads // 2
    load = pltpu.make_async_copy(out_grad, grad_v, in_sem.at[0])
    load.start()
    core_one = c == 1
    for copy in inward:
        copy.wait()
    turned[...] = jnp.zeros_like(turned)
    share = w_out.shape[0]
    for i, norm in enumerate((gain_one, bias_one, gain_two, bias_two)):
        turned[i : i + 1, 0:share] = norm[...].astype(wide).reshape(1, share)
    table = turned[...].T[:share].astype(low)
    left = jnp.concatenate([w_qkv[:, : 2 * width], table], 1)
    right = jnp.concatenate([w_qkv[:, 2 * width :], w_out[...], jnp.zeros_like(table)], 1)
    gate, up = w_gu[:, :ff], w_gu[:, ff:]
    rows = w_qkv.shape[0]
    a_give[:rows, :] = jnp.where(core_one, left, right)
    g_give[:rows, :] = jnp.where(core_one, gate, up)
    swaps = Copies(pair_sem.at[0], pair_sem.at[1])
    place.meet()
    for i, (give, other) in enumerate(((a_give, a_pair), (g_give, g_pair))):
        swaps.put(give, other, i, i, place.sib)
    copies = Copies(send, recv)
    sides = [
        lambda half: w_a.at[half],
        lambda half: w_g.at[half, :, :, :half_g],
        lambda half: w_g.at[half, :, :, half_g:],
        lambda half: w_d.at[:, half],
    ]
    mats = [Gather(place, copies, i, side) for i, side in enumerate(sides)]
    first, second, third, fourth = mats
    me = place.at(0, "o")

    def assemble(mine, other, full, i):
        swaps.got(other, i, place.sib)
        mine = mine.astype(wide)
        theirs = other[:rows, :].astype(wide)
        top = jnp.where(core_one, theirs, mine)
        rest = jnp.where(core_one, mine, theirs)
        full[c, me] = jnp.concatenate([top, rest], 0).astype(low)

    work = Gather.schedule(mats)

    def go(count):
        for step, *plane in work[:count]:
            step(*plane)
        del work[:count]

    def upto(matrix):
        done = [i for i, (step, *_) in enumerate(work) if step == matrix.from_d]
        go(done[-1] + 1 if done else 0)

    assemble(jnp.where(core_one, right, left), a_pair, w_a, 0)
    go(2)
    assemble(jnp.where(core_one, up, gate), g_pair, w_g, 1)
    w_d[me, c] = d_shard[...]
    seq_len = labels.shape[1]
    label_row = labels[...].astype(wide)
    label_column = jnp.broadcast_to(label_row, (lane_width, seq_len)).T[:, 0:1]
    half = pl.ds(pl.multiple_of(c * tok_rows, tok_rows), tok_rows)
    same = (label_column == labels[:, half].astype(wide)) & (label_column != seq_len)
    key_at = lax.broadcasted_iota(jnp.int32, span_v.shape, 0)
    gap = jnp.abs(key_at - lax.broadcasted_iota(jnp.int32, span_v.shape, 1) - c * tok_rows)
    span_v[...] = jnp.where(same | (gap == 0), gap.astype(wide), far)
    mask = jnp.broadcast_to(labels[:, half].astype(wide), (lane_width, tok_rows)).T[:, 0:1]
    mask = (mask != seq_len).astype(wide)
    upto(first)
    first.from_sib()
    saved = []

    def save(src, dst):
        copy = pltpu.make_async_copy(src, dst, out_sem.at[len(saved)])
        copy.start()
        saved.append((src, dst))

    save(w_a, a_full)
    save(span_v, span_out)
    part = lambda half, at, size: w_a[half, :, :, at : at + size].reshape(width, size)
    vectors[...] = part(0, 2 * width, lane_width).astype(wide).T[:8]
    x = tokens[...]
    k[half, :] = dot(x, part(0, width, width)).astype(low)
    swaps.put(k.at[half], k.at[half], 2, 2, place.sib)
    v[half, :] = dot(x, part(1, 0, width)).astype(low)
    swaps.put(v.at[half], v.at[half], 3, 3, place.sib)
    depth = width // heads
    q[...] = dot(x, part(0, 0, width)).astype(low) * depth**-0.5
    go(3)
    other = pl.ds(pl.multiple_of((1 - c) * tok_rows, tok_rows), tok_rows)
    swaps.got(k.at[other], 2, place.sib)
    swaps.got(v.at[other], 3, place.sib)
    save(q, q_out)
    save(k, k_out)
    save(v, v_out)

    shares = (3, 4, 4, 4, 4, 2)
    todo = []
    for count in shares:
        todo.append(work[:count])
        del work[:count]

    @pl.loop(0, pairs)
    def _(pair):
        attend_pair(pair, heads, q, k, v, span_v, lse, att)
        for at, steps in enumerate(todo):

            @pl.when(pair == at)
            def _(steps=steps):
                for step, *plane in steps:
                    step(*plane)

    save(att, att_out)
    branch = dot(att[...], part(1, width, width))
    toks = x.astype(wide)
    norm, inverse = normalized(toks + branch)
    norm_one[...] = norm
    inv_one[...] = jnp.broadcast_to(inverse, inv_one.shape)
    hidden = norm * vectors[0:1, :] + vectors[1:2, :]
    hid[...] = hidden
    hid_low[...] = hidden.astype(low)
    hid_t[...] = hidden.T.astype(low)
    save(hid_t, hid_t_out)
    save(norm_one, norm_out)
    save(inv_one, inv_out)
    small[0:4, :] = jnp.zeros((4, width), wide)
    small[4:5, :] = column_sum(mask * toks * toks)
    small[5:6, :] = column_sum(mask * branch * branch)
    small[6:7, :] = column_sum(mask * hidden * hidden)
    small[8:16, :] = jnp.zeros((8, width), wide)
    small[8:9, :] = jnp.broadcast_to(jnp.sum(mask, 0, keepdims=True), (1, width))
    tile = 512

    def glu(j):
        cols = pl.ds(pl.multiple_of(j * tile, tile), tile)
        h = hid_low[...]
        gate = dot(h, w_g[0, :, :, cols].reshape(width, tile))
        up = dot(h, w_g[1, :, :, cols].reshape(width, tile))
        cdf = 0.5 + 0.5 * lax.erf(gate * 0.7071067811865476)
        mixed = gate * cdf
        density = 0.3989422804014327 * jnp.exp(-0.5 * gate * gate)
        slope_up[:, cols] = mixed.astype(low)
        slope_gate[:, cols] = (up * (cdf + gate * density)).astype(low)
        act[:, cols] = (mixed * up).astype(low)

    upto(second)
    go(1)
    second.from_sib()
    save(w_g.at[:, :, :, :half_g], g_full.at[:, :, :, :half_g])

    @pl.loop(0, half_g // tile)
    def _(j):
        glu(j)

    go(1)
    third.from_sib()
    save(w_g.at[:, :, :, half_g:], g_full.at[:, :, :, half_g:])
    for src, dst in ((slope_gate, gate_out), (slope_up, up_out), (act, act_out)):
        save(src.at[:, :half_g], dst.at[:, :half_g])

    @pl.loop(half_g // tile, ff // tile)
    def _(j):
        glu(j)

    for src, dst in ((slope_gate, gate_out), (slope_up, up_out), (act, act_out)):
        save(src.at[:, half_g:], dst.at[:, half_g:])

    def down(plane):
        at = place.plane(plane)
        cols = pl.ds(pl.multiple_of(at * width, width), width)
        return dot(act[:, cols], w_d[pl.ds(at * 4, 4)].reshape(width, width))

    go(1)
    fourth.from_sib(0, 2, 1)
    d_hid[...] = down(0)
    for plane in (2, 1):
        d_hid[...] += down(plane)
    upto(fourth)
    fourth.from_sib(3)
    save(w_d, d_full)
    d_hid[...] += down(3)
    branch = d_hid[...]
    small[7:8, :] = column_sum(mask * branch * branch)
    norm, inverse = normalized(hid[...] + branch)
    gain = vectors[2:3, :]
    output[...] = (norm * gain + vectors[3:4, :]).astype(low)
    save(output, output_out)
    load.wait()
    grad = grad_v[...].astype(wide)
    small[2:3, :] = column_sum(grad * norm)
    small[3:4, :] = column_sum(grad)
    back = norm_back(grad, gain, norm, inverse)
    d_hid[...] = back
    d_branch[...] = back.astype(low)
    save(d_hid, d_hid_out)
    save(d_branch, d_branch_out)
    for i, (src, dst) in enumerate(saved):
        pltpu.make_async_copy(src, dst, out_sem.at[i]).wait()
    for i, ref in enumerate((a_give, g_give, k.at[half], v.at[half])):
        swaps.sent(ref, i, place.sib)
    for m in mats:
        m.drain()


def fore(heads, tokens, labels, w_qkv, w_out, w_gu, d_shard, norms, out_grad):
    low, wide = jnp.bfloat16, jnp.float32
    rows, width = tokens.shape
    ff = w_gu.shape[1] // 2
    half_a = 2 * width + lane_width
    keys = labels.shape[1]
    vmem, hbm = pl.BlockSpec(memory_space=pltpu.VMEM), pl.BlockSpec(memory_space=pl.ANY)
    dma = lambda *shape: pltpu.SemaphoreType.DMA(shape)
    shape = jax.ShapeDtypeStruct
    w_a, w_g, w_d = (2, 16, rows_chip, half_a), (2, 16, rows_chip, ff), (16, 2) + d_shard.shape
    stored = [
        (w_a, low), (w_g, low), (w_d, low), ((rows, width), low), ((keys, width), low), ((keys, width), low),
        ((rows, width), low), ((width, rows), low), ((rows, width), wide), ((rows, lane_width), wide),
        ((rows, ff), low), ((rows, ff), low), ((rows, ff), low), ((rows, width), low), ((rows, width), wide),
        ((rows, width), low), ((keys, rows), wide),
    ]
    block = lambda *dims: pltpu.VMEM(dims, low)
    block_wide = lambda *dims: pltpu.VMEM(dims, wide)
    return pl.pallas_call(
        lambda *refs: fore_kernel(heads, *refs),
        out_shape=tuple(shape(dims, kind) for dims, kind in stored)
        + (shape((16, rows), wide), shape((8, width), wide), shape((16, width), wide)),
        in_specs=[hbm] * 11,
        out_specs=(hbm,) * len(stored) + (vmem,) * 3,
        scratch_shapes=[
            block(*w_a), block(*w_g), block(*w_d), block(32, half_a), block(32, ff), block(32, half_a), block(32, ff),
            block_wide(lane_width, lane_width),
            block(rows, width), block(keys, width), block(keys, width), block(rows, width),
            block_wide(keys, rows), block(rows, width), block_wide(rows, width), block(rows, width),
            block(width, rows), block_wide(rows, width), block_wide(rows, lane_width),
            block(rows, ff), block(rows, ff), block(rows, ff), block(rows, width), block_wide(rows, width),
            block(rows, width),
            *(pltpu.VMEM(part.shape, part.dtype) for part in (tokens, labels, w_qkv, w_out, w_gu, d_shard, *norms)),
            dma(2, 4), dma(8), dma(4 * gather_slots), dma(11), dma(len(stored) + 4),
        ],
        compiler_params=pltpu.CompilerParams(
            collective_id=0, has_side_effects=True, vmem_limit_bytes=62 * 2**20
        ),
        name="gather_and_forward",
    )(tokens, labels, w_qkv, w_out, w_gu, d_shard, *norms, out_grad)


def back_kernel(
    heads, tokens, q, k, v, span, att, hid_t, norm, inv, gate, up, act, d_hid, d_branch, a_full, g_full, d_full,
    lse_at, vectors_at, small_at, d_tokens, qkv_out, wout_out, gu_out, down_out, tail, *scratch,
):
    place = Place()
    place.greet()
    c = place.c
    first = c == 0
    low, wide = jnp.bfloat16, jnp.float32
    tok_rows, width = tokens.shape
    ff = gate.shape[1]
    pairs = heads // 2
    bufs, rest = scratch[:33], scratch[33:]
    a_grad, dkv_in, resid, d_att, g_sum, a_sum, g_fin, a_fin, small_buf, send, recv, tokens_v, down_v, gu_v, lse, vectors, small, pair_sem, fin_sem, in_sem, tile_sem = rest
    copies = Copies(send, recv)
    last = Copies(fin_sem.at[0], fin_sem.at[1])
    half_g, part = ff // 2, width // 2

    def scatter(i, own, *more):
        return Scatter(place, copies, i, None, lambda at: own.at[at], *more)

    def projection(i, *more):
        give = lambda four: a_grad.at[i, 1 - c, four]
        own = lambda at: a_grad.at[i, c, at]
        return Scatter(place, copies, 3 + i, give, own, *more)

    down, left, right = (scatter(i, *bufs[7 * i : 7 * i + 7]) for i in range(3))
    projs = [projection(i, *bufs[21 + 6 * i : 27 + 6 * i]) for i in range(2)]
    early, late = projs
    planes = (3, 2, 1, 0)
    hand_over = lambda i, src, dst: pltpu.make_async_copy(src, dst, in_sem.at[i])
    hops = ((place.sib, 0), (place.xn, 1), (place.yn, 2))

    def exchange(i):
        peer, slot = hops[i]
        last.put(small_buf.at[i], small_buf.at[4 + i], slot, slot, peer)

    def combine(i):
        peer, slot = hops[i]
        last.got(small_buf.at[4 + i], slot, peer)
        small_buf[i + 1] = small_buf[i] + small_buf[4 + i]

    def spread():
        for z in (1, 2, 3):
            last.put(small_buf.at[3], small_buf.at[6 + z], 2 + z, 2 + z, place.zn[z])

    tile = 256

    def feed_forward(given, act_v, db, ht, w_gu, w_dn, gate_v, up_v, att_v, norm_v, inv_v, w_out):
        for i, m in enumerate((down, left, right)):
            m.give = lambda four, i=i: given.at[i % 2, four]
        load = lambda i, src, dst: pltpu.make_async_copy(src, dst, in_sem.at[i])
        loads = [
            load(0, d_branch, db), load(1, hid_t, ht), load(2, d_hid, resid), load(3, att, att_v),
            load(4, norm, norm_v), load(5, inv, inv_v), load(6, a_full.at[1, :, :, width : 2 * width], w_out),
        ]

        def act_load(i, z):
            cols = pl.ds(pl.multiple_of(place.plane(z) * width, width), width)
            return load(7 + i % 2, act.at[:, cols], act_v.at[i % 2])

        def fetch(j):
            slot = j % 2
            cols = pl.ds(pl.multiple_of(j * tile, tile), tile)
            return [
                pltpu.make_async_copy(g_full.at[:, :, :, cols], w_gu.at[slot], tile_sem.at[0, slot]),
                pltpu.make_async_copy(d_full.at[cols], w_dn.at[slot], tile_sem.at[1, slot]),
                pltpu.make_async_copy(gate.at[:, cols], gate_v.at[slot], tile_sem.at[2, slot]),
                pltpu.make_async_copy(up.at[:, cols], up_v.at[slot], tile_sem.at[3, slot]),
            ]

        loads[0].start()
        tables = [load(9 + i, src, dst) for i, (src, dst) in enumerate(((lse_at, lse), (vectors_at, vectors), (small_at, small)))]
        act_load(0, planes[0]).start()
        act_load(1, planes[1]).start()
        for copy in loads[1:] + fetch(0) + tables:
            copy.start()
        loads[0].wait()
        own_d = bufs[0]
        for i, z in enumerate(planes):
            act_load(i, z).wait()
            term = dot(act_v[i % 2].T, db[...]).astype(low).reshape(4, 2, 2, rows_chip, width)
            if i < 2:
                act_load(i + 2, planes[i + 2]).start()
            four = pl.ds(place.plane(z) * 4, 4)
            mine = jnp.where(first, term[:, 0], term[:, 1])
            other = jnp.where(first, term[:, 1], term[:, 0])
            for j in range(2):
                cols = slice(j * width, (j + 1) * width)
                bufs[0][four, :, cols] = mine[:, j]
                given[0, four, :, cols] = other[:, j]
            if i == 0:
                place.meet()
            down.begin(z)
            if i > 1:
                down.pair(planes[i - 2])
        for copy in loads[1:3]:
            copy.wait()

        def between(i, todo):
            for at, *work in todo:

                @pl.when(i == at)
                def _(work=work):
                    for step in work:
                        step()

        def tiles(begin, own_g, give_g, todo):
            @pl.loop(begin, begin + half_g // tile)
            def _(j):
                slot = j % 2
                for copy in fetch(j):
                    copy.wait()

                @pl.when(j + 1 < ff // tile)
                def _():
                    for copy in fetch(j + 1):
                        copy.start()

                d_act = dot(db[...], w_dn[slot], ((1,), (1,)))
                d_gate = (d_act * gate_v[slot].astype(wide)).astype(low)
                d_up = (d_act * up_v[slot].astype(wide)).astype(low)
                resid[...] += dot(d_gate, w_gu[slot, 0].reshape(width, tile), ((1,), (1,))) + dot(
                    d_up, w_gu[slot, 1].reshape(width, tile), ((1,), (1,))
                )
                cols = pl.ds(pl.multiple_of((j - begin) * tile, tile), tile)
                mine = dot(ht[...], jnp.where(first, d_gate, d_up)).astype(low)
                own_g[:, :, cols] = mine.reshape(16, rows_chip, tile)
                other = dot(ht[...], jnp.where(first, d_up, d_gate)).astype(low)
                give_g[:, :, cols] = other.reshape(16, rows_chip, tile)
                between(j - begin, todo)

        tiles(0, bufs[7], given.at[1], [(0, lambda: down.pair(1)), (1, lambda: down.pair(0)), (5, down.diags)])
        for z in planes:
            left.begin(z)
        down.given()
        tiles(half_g // tile, bufs[14], given.at[0], [(2, down.relays, left.first, left.rest), (5, down.odd)])
        for z in planes:
            right.begin(z)
        for copy in loads[3:] + tables:
            copy.wait()
        grad = resid[...]
        unit = norm_v[...]
        small_buf[0] = small[...]
        small_buf[0, 0:1, :] = column_sum(grad * unit)
        small_buf[0, 1:2, :] = column_sum(grad)
        exchange(0)
        back = norm_back(grad, vectors[0:1, :], unit, inv_v[:, 0:1])
        resid[...] = back
        d_one = back.astype(low)
        d_att[...] = dot(d_one, w_out[...].reshape(width, width), ((1,), (1,))).astype(low)
        grad_out = dot(att_v[...].T, d_one).astype(low).reshape(16, rows_chip, width)
        for i in range(2):
            a_grad[i, 1, :, :, part:] = grad_out[:, :, i * part : (i + 1) * part]
        left.diags()
        right.first()
        right.rest()
        left.given()
        right.given()

    block = lambda *dims: pltpu.VMEM(dims, low)
    block_wide = lambda *dims: pltpu.VMEM(dims, wide)
    pl.run_scoped(
        feed_forward, block(2, *bufs[0].shape), block(2, tok_rows, width),
        block(tok_rows, width), block(width, tok_rows), block(2, 2, 16, rows_chip, tile), block(2, tile, width),
        block(2, tok_rows, tile), block(2, tok_rows, tile), block(tok_rows, width), block_wide(tok_rows, width),
        block_wide(tok_rows, lane_width), block(16, rows_chip, width),
    )

    half = lambda side: pl.ds(pl.multiple_of(side * tok_rows, tok_rows), tok_rows)

    def attention_part(dq, dkv_own, dkv_out, x_t, d_k, d_v):
        slots = dkv_own.shape[0]

        def send_dkv(pair):
            return pltpu.make_async_remote_copy(
                src_ref=dkv_out.at[pair], dst_ref=dkv_in.at[pair], send_sem=pair_sem.at[0, pair],
                recv_sem=pair_sem.at[1, pair], device_id=place.sib, device_id_type=MESH,
            )

        def project(i):
            for pair in range(i * pairs // 2, (i + 1) * pairs // 2):
                send_dkv(pair).wait_recv()
                at = slice(pair * lane_width, (pair + 1) * lane_width)
                for j, dst in enumerate((d_k, d_v)):
                    dst[:, at] = (dkv_own[pair % slots, j] + dkv_in[pair, j].astype(wide)).astype(low)
            cols = slice(i * part, (i + 1) * part)
            for side, at, src in ((0, 0, dq), (0, part, d_k), (1, 0, d_v)):
                term = dot(x_t[...], src[:, cols]).astype(low)
                a_grad[i, side, :, :, at : at + part] = term.reshape(16, rows_chip, part)
            for z in planes:
                projs[i].begin(z)

        def attention(q_v, k_v, v_v, span_v, att_v, x, dk_sum, dv_sum):
            load = lambda i, src, dst: pltpu.make_async_copy(src, dst, in_sem.at[i])
            sources = ((q, q_v), (k, k_v), (v, v_v), (att, att_v))
            head, rest = slice(0, lane_width), slice(lane_width, width)
            loads = [load(0, span, span_v)]
            loads += [load(1 + i, src.at[:, head], dst.at[:, head]) for i, (src, dst) in enumerate(sources)]
            later = [load(5 + i, src.at[:, rest], dst.at[:, rest]) for i, (src, dst) in enumerate(sources)]
            later.append(load(9, tokens, x))
            for copy in loads + later:
                copy.start()
            for copy in loads:
                copy.wait()

            def arrive():
                for i, (src, dst) in enumerate(sources):
                    load(5 + i, src.at[:, rest], dst.at[:, rest]).wait()
                load(9, tokens, x).wait()
                x_t[...] = x[...].T

            def meet_small(i):
                combine(i)
                exchange(i + 1)

            def heads_back(begin, end, todo):
                @pl.loop(begin, end)
                def _(pair):
                    attend_back_pair(pair, heads, q_v, k_v, v_v, span_v, lse, att_v, d_att, dq, dk_sum, dv_sum)
                    for i, side in enumerate((dk_sum, dv_sum)):
                        dkv_own[lax.rem(pair, slots), i] = side[half(c), :]
                        dkv_out[pair, i] = side[half(1 - c), :].astype(low)
                    send_dkv(pair).start()
                    for at, *work in todo:

                        @pl.when(pair == at)
                        def _(at=at, work=work):
                            for step in work:
                                step()

            small_step = lambda i: lambda: meet_small(i)
            heads_back(0, 4, [
                (0, arrive, down.even, small_step(0)), (1, left.odd), (2, left.relays, right.diags), (3, right.odd),
            ])
            project(0)
            heads_back(4, pairs, [(4, left.even, early.first, early.rest, small_step(1)), (5, right.relays)])
            project(1)

        key_rows = k.shape[0]
        pl.run_scoped(
            attention, block(*q.shape), block(*k.shape), block(*v.shape), block_wide(*span.shape), block(*att.shape),
            block(tok_rows, width), block_wide(key_rows, lane_width), block_wide(key_rows, lane_width),
        )

        def meet_last():
            combine(2)
            spread()

        def finish(w_left, w_right):
            loads = [
                pltpu.make_async_copy(a_full.at[0, :, :, : 2 * width], w_left, in_sem.at[0]),
                pltpu.make_async_copy(a_full.at[1, :, :, :width], w_right, in_sem.at[1]),
            ]
            for copy in loads:
                copy.start()
            for copy in loads:
                copy.wait()
            w_q = w_left[:, :, :width].reshape(width, width)
            total = resid[...] + dot(dq[...], w_q, ((1,), (1,)))
            early.diags()
            late.first()
            late.rest()
            right.even()
            meet_last()
            w_k = w_left[:, :, width:].reshape(width, width)
            total += dot(d_k[...], w_k, ((1,), (1,)))
            early.relays()
            late.diags()
            early.odd()
            early.even()
            total += dot(d_v[...], w_right[...].reshape(width, width), ((1,), (1,)))
            tokens_v[...] = total.astype(low)
            hand_over(0, tokens_v, d_tokens).start()
            late.relays()
            late.odd()

        pl.run_scoped(finish, block(16, rows_chip, 2 * width), block(16, rows_chip, width))

        @pl.loop(0, pairs)
        def _(pair):
            send_dkv(pair).wait_send()

    pl.run_scoped(
        attention_part, block(tok_rows, width), block_wide(4, 2, tok_rows, lane_width),
        block(pairs, 2, tok_rows, lane_width), block(width, tok_rows), block(tok_rows, width), block(tok_rows, width),
    )
    mine, theirs = pl.ds(pl.multiple_of(24 * c, 8), 24), pl.ds(pl.multiple_of(24 - 24 * c, 8), 24)
    total = down.total()
    down_v[:rows_chip] = total[:, :width]
    down_v[rows_chip:] = total[:, width:]
    hand_over(1, down_v, down_out).start()

    def swap(i, m, total, other, slot):
        total[i] = m.total()
        last.put(total.at[i, theirs], other.at[i], slot, slot, place.sib)

    swap(0, left, g_sum, g_fin, 6)
    swap(1, right, g_sum, g_fin, 7)
    late.even()
    swap(0, early, a_sum, a_fin, 8)
    for z in (1, 2, 3):
        last.got(small_buf.at[6 + z], 2 + z, place.zn[z])
    sums = (small_buf[3] + small_buf[7]) + (small_buf[8] + small_buf[9])
    share = width // 32
    at_row = (lax.axis_index("rows") * 2 + c) * share
    tail[0:8, :] = pltpu.roll(sums[:8], lax.rem(width - at_row, width), 1)[:, :lane_width]
    squares = jnp.sum(sums[:8], 1, keepdims=True) / (sums[8:9, 0:1] * width)
    at = lambda axis: lax.broadcasted_iota(jnp.int32, (8, lane_width), axis)
    stats = jnp.where(at(0) == at(1) + 4, jnp.broadcast_to(jnp.sqrt(squares), (8, lane_width)), 0.0)
    tail[8:16, :] = jnp.broadcast_to(column_sum(stats), (8, lane_width))
    for i in range(2):
        last.got(g_fin.at[i], 6 + i, place.sib)
        own, other = g_sum[i, mine], g_fin[i]
        gu_v[:, i * half_g : (i + 1) * half_g] = jnp.where(first, own, other)
        gu_v[:, (i + 2) * half_g : (i + 3) * half_g] = jnp.where(first, other, own)
    hand_over(2, gu_v, gu_out).start()
    swap(1, late, a_sum, a_fin, 9)
    for i in range(2):
        last.got(a_fin.at[i], 8 + i, place.sib)
        own, other = a_sum[i, mine], a_fin[i]
        qk, vo = jnp.where(first, own, other), jnp.where(first, other, own)
        for j, term in enumerate((qk[:, :part], qk[:, part:], vo[:, :part])):
            at = j * width + i * part
            qkv_out[:, at : at + part] = term
        wout_out[:, i * part : (i + 1) * part] = vo[:, part:]
    for m in (down, left, right, early, late):
        m.drain()
    for m in (early, late):
        m.given()
    sent = [small_buf.at[0]] * 6 + [g_fin.at[0]] * 2 + [a_fin.at[0]] * 2
    for slot, ref in enumerate(sent):
        last.sent(ref, slot, place.sib)
    for i, pair in enumerate(((tokens_v, d_tokens), (down_v, down_out), (gu_v, gu_out))):
        hand_over(i, *pair).wait()


def back(
    heads, tokens, q, k, v, span, att, hid_t, norm, inv, gate, up, act, d_hid, d_branch, a_full, g_full, d_full,
    lse, vectors, small,
):
    low, wide = jnp.bfloat16, jnp.float32
    tok_rows, width = tokens.shape
    ff = gate.shape[1]
    half_g = ff // 2
    pairs = heads // 2
    d_rows = ff // 32
    bufs = []
    for i, cols in enumerate((2 * width, half_g, half_g, width, width)):
        bufs += [pltpu.VMEM((count, rows_chip, cols), low) for count in (16, 16, 2, 2, 4, 4, 3)[i >= 3 :]]
    vmem, hbm = pl.BlockSpec(memory_space=pltpu.VMEM), pl.BlockSpec(memory_space=pl.ANY)
    dma = lambda *shape: pltpu.SemaphoreType.DMA(shape)
    shape = jax.ShapeDtypeStruct
    return pl.pallas_call(
        lambda *refs: back_kernel(heads, *refs),
        out_shape=(
            shape((tok_rows, width), low), shape((24, 3 * width), wide), shape((24, width), wide),
            shape((24, 2 * ff), wide), shape((d_rows, width), wide), shape((16, lane_width), wide),
        ),
        in_specs=[hbm] * 20,
        out_specs=(hbm, vmem, vmem, hbm, hbm, vmem),
        scratch_shapes=bufs
        + [
            pltpu.VMEM((2, 2, 16, rows_chip, width), low),
            pltpu.VMEM((pairs, 2, tok_rows, lane_width), low),
            pltpu.VMEM((tok_rows, width), wide),
            pltpu.VMEM((tok_rows, width), low),
            pltpu.VMEM((2, rows_chip, half_g), wide),
            pltpu.VMEM((2, rows_chip, width), wide),
            pltpu.VMEM((2, 24, half_g), wide),
            pltpu.VMEM((2, 24, width), wide),
            pltpu.VMEM((10,) + small.shape, wide),
            dma(10),
            dma(5 * scatter_slots),
            pltpu.VMEM((tok_rows, width), low),
            pltpu.VMEM((d_rows, width), wide),
            pltpu.VMEM((24, 2 * ff), wide),
            *(pltpu.VMEM(part.shape, wide) for part in (lse, vectors, small)),
            dma(2, pairs),
            dma(2, 10),
            dma(12),
            dma(4, 2),
        ],
        compiler_params=pltpu.CompilerParams(
            collective_id=1, has_side_effects=True, vmem_limit_bytes=63 * 2**20
        ),
        name="backward_and_sums",
    )(tokens, q, k, v, span, att, hid_t, norm, inv, gate, up, act, d_hid, d_branch, a_full, g_full, d_full, lse, vectors, small)


def close_kernel(share, *refs):
    parts, tail, outs = refs[:6], refs[6], refs[7:]
    for part, out in zip(parts, outs):
        out[...] = part[...]
    for i, out in enumerate(outs[6:10]):
        out[...] = tail[i : i + 1, :share]
    outs[10][...] = tail[8:9, :4]


def close(share, *parts):
    vmem = pl.BlockSpec(memory_space=pltpu.VMEM)
    wide = jnp.float32
    return pl.pallas_call(
        lambda *refs: close_kernel(share, *refs),
        out_shape=tuple(jax.ShapeDtypeStruct(part.shape, part.dtype) for part in parts[:6])
        + (jax.ShapeDtypeStruct((1, share), wide),) * 4
        + (jax.ShapeDtypeStruct((1, 4), wide),),
        in_specs=[vmem] * 7,
        out_specs=(vmem,) * 11,
        compiler_params=pltpu.CompilerParams(vmem_limit_bytes=62 * 2**20),
        name="results",
    )(*parts)


def window(cells, width):
    count = lax.axis_size("blk")
    before = lax.ppermute(cells, "blk", [(i, i + 1) for i in range(count - 1)])
    after = lax.ppermute(cells, "blk", [(i + 1, i) for i in range(count - 1)])
    return jnp.concatenate([before, cells, after], 0)


def window_back(terms, width):
    count = lax.axis_size("blk")
    low = jnp.bfloat16
    before = lax.ppermute(terms[2 * width :].astype(low), "blk", [(i, i + 1) for i in range(count - 1)])
    after = lax.ppermute(terms[:width].astype(low), "blk", [(i + 1, i) for i in range(count - 1)])
    return terms[width : 2 * width] + before.astype(terms.dtype) + after.astype(terms.dtype)


def key_spans(labels, first, tok_rows):
    seq_len = labels.shape[0]
    query_pos = first + jnp.arange(tok_rows, dtype=jnp.int32)
    query_labels = lax.dynamic_slice_in_dim(labels, first, tok_rows, 0)
    if seq_len == 2 * tok_rows:
        key_pos, key_labels = jnp.arange(seq_len, dtype=jnp.int32), labels
    else:
        key_pos = first - tok_rows + jnp.arange(3 * tok_rows, dtype=jnp.int32)
        padded = jnp.pad(labels, (tok_rows, tok_rows), constant_values=seq_len)
        key_labels = lax.dynamic_slice_in_dim(padded, first, 3 * tok_rows, 0)
    same = (key_labels[:, None] == query_labels[None, :]) & (key_labels[:, None] != seq_len)
    gap = jnp.abs(key_pos[:, None] - query_pos[None, :])
    return jnp.where(same | (gap == 0), gap.astype(jnp.float32), far)


def on_chip_grid():
    return lax.axis_size("rows") == 16 and lax.axis_size("blk") == 2


def packed_shards(w_qkv, w_out, ln1_gain, ln1_bias, w_gate_up, ln2_gain, ln2_bias):
    width = w_out.shape[1]
    ff = w_gate_up.shape[1] // 2
    table = jnp.stack((ln1_gain, ln1_bias, ln2_gain, ln2_bias), 1)
    table = jnp.pad(table, ((0, 0), (0, lane_width - 4)))
    left = jnp.concatenate([w_qkv[:, : 2 * width], table], 1)
    right = jnp.concatenate([w_qkv[:, 2 * width :], w_out, jnp.zeros_like(table)], 1)
    return jnp.stack([left, right]), jnp.stack([w_gate_up[:, :ff], w_gate_up[:, ff:]])


def on_grid(tokens, labels, w_qkv, w_out, w_gate_up, w_down, norms, out_grad):
    width = tokens.shape[1]
    (
        a_full, g_full, d_full, q, k, v, att, hid_t, norm, inv, gate, up, act, output, d_hid, d_branch, span,
        lse, vectors, small,
    ) = fore(HEADS, tokens, labels, w_qkv, w_out, w_gate_up, w_down, norms, out_grad)
    parts = back(
        HEADS, tokens, q, k, v, span, att, hid_t, norm, inv, gate, up, act, d_hid, d_branch, a_full, g_full,
        d_full.reshape(-1, width), lse, vectors, small,
    )
    *parts, one, two, three, four, stats = close(norms[0].shape[0], output, *parts)
    rows = [row.reshape(-1) for row in (one, two, three, four)]
    return *parts, rows, stats.reshape(-1)


def on_any(tokens, labels, w_qkv, w_out, w_gate_up, w_down, norms, out_grad):
    both = ("rows", "blk")
    tok_rows, width = tokens.shape
    first = lax.axis_index("blk") * tok_rows
    span = key_spans(labels[0], first, tok_rows)
    here = lax.dynamic_slice_in_dim(labels[0], first, tok_rows, 0)
    valid = (here != labels.shape[1]).astype(jnp.float32)[:, None]
    a_shard, g_shard = packed_shards(w_qkv, w_out, *norms[:2], w_gate_up, *norms[2:])
    low, wide = jnp.bfloat16, jnp.float32
    a_full = lax.all_gather(a_shard, both, axis=1, tiled=True)
    w_gu = lax.all_gather(g_shard, both, axis=1, tiled=True)
    w_dn = lax.all_gather(w_down, both, axis=0, tiled=True)
    vectors = jnp.pad(a_full[0, :, 2 * width : 2 * width + 4].astype(wide).T, ((0, 4), (0, 0)))
    w_qk, w_v = a_full[0, :, : 2 * width], a_full[1, :, :width]
    qk = jnp.dot(tokens, w_qk, preferred_element_type=wide).astype(low)
    v = jnp.dot(tokens, w_v, preferred_element_type=wide).astype(low)
    query = qk[:, :width] * (width // HEADS) ** -0.5
    kv = window(jnp.concatenate([qk[:, width:], v], 1), tok_rows)
    keys, values = kv[:, :width], kv[:, width:]
    attended, lse = attend(query, keys, values, span, HEADS)
    output, d_resid_one, d_att, grad_out, g_grad, d_grad, small = ffn(
        tokens, attended, a_full, vectors, valid, out_grad, w_gu, w_dn
    )
    dq, dk, dv = attend_back(query, keys, values, span, lse, attended, d_att, HEADS)
    dkv = window_back(jnp.concatenate([dk, dv], 1), tok_rows)
    d_qk = jnp.concatenate([dq, dkv[:, :width].astype(low)], 1)
    d_v = dkv[:, width:].astype(low)
    grad_qkv = transposed_times(tokens, jnp.concatenate([d_qk, d_v], 1))
    d_tokens = d_resid_one + times_transposed(d_qk, w_qk) + times_transposed(d_v, w_v)
    share = lambda g, axis: lax.psum_scatter(g.astype(wide), both, scatter_dimension=axis, tiled=True)
    gate, up = share(g_grad, 1)
    small = lax.psum(small, both)
    size = norms[0].shape[0]
    rows = lax.dynamic_slice_in_dim(small[:4], lax.axis_index(both) * size, size, 1)
    stats = jnp.sqrt(jnp.sum(small[4:8], 1) / (small[8, 0] * width))
    return (
        output, d_tokens.astype(low), share(grad_qkv, 0), share(grad_out, 0), jnp.concatenate([gate, up], 1),
        share(d_grad, 0), rows, stats,
    )


def body(
    tokens, segments, w_qkv, w_out, ln1_gain, ln1_bias, w_gate_up, w_down, ln2_gain, ln2_bias, out_grad,
):
    run = on_grid if on_chip_grid() else on_any
    norms = (ln1_gain, ln1_bias, ln2_gain, ln2_bias)
    output, d_tokens, qkv, wout, gate_up, down, rows, stats = run(
        tokens[0], segments, w_qkv, w_out, w_gate_up, w_down, norms, out_grad[0]
    )
    return (
        output[None], d_tokens[None], qkv, wout, rows[0], rows[1], gate_up, down, rows[2], rows[3], stats,
    )


def solution(mesh):
    placed = (
        P("rows", "blk", None),
        P("rows", None),
        P(("rows", "blk"), None),
        P(("rows", "blk"), None),
        P(("rows", "blk")),
        P(("rows", "blk")),
        P(("rows", "blk"), None),
        P(("rows", "blk"), None),
        P(("rows", "blk")),
        P(("rows", "blk")),
        P("rows", "blk", None),
    )
    return jax.shard_map(
        body,
        mesh=mesh,
        in_specs=placed,
        out_specs=(
            P("rows", "blk", None),
            P("rows", "blk", None),
            P(("rows", "blk"), None),
            P(("rows", "blk"), None),
            P(("rows", "blk")),
            P(("rows", "blk")),
            P(("rows", "blk"), None),
            P(("rows", "blk"), None),
            P(("rows", "blk")),
            P(("rows", "blk")),
            P(),
        ),
        check_vma=False,
    )
```

```python
import jax
import jax.numpy as jnp
from jax import lax
from jax.experimental import pallas as pl
from jax.experimental.pallas import tpu as pltpu
from jax.sharding import PartitionSpec as P

HEADS = 12


ln_eps = 1e-12
far = 1e33
lane_width = 128


def times_transposed(left, right):
    return lax.dot_general(
        left, right, (((1,), (1,)), ((), ())), preferred_element_type=jnp.float32
    )


def transposed_times(left, right):
    return lax.dot_general(
        left, right, (((0,), (0,)), ((), ())), preferred_element_type=jnp.float32
    )


MESH = pl.DeviceIdType.MESH


class Place:
    def __init__(self):
        r, self.c = lax.axis_index("rows"), lax.axis_index("blk")
        self.x, self.y, self.z = r % 2, (r // 2) % 2, r // 4
        self.sib = (r, 1 - self.c)
        self.xn = (self.at(0, "x"), self.c)
        self.yn = (self.at(0, "y"), self.c)
        self.zn = {k: (self.at(k, "o"), self.c) for k in (1, 2, 3)}

    def plane(self, k):
        z, low = self.z % 2, self.z // 2
        if k % 2:
            z = 1 - z
        if k // 2:
            low = 1 - low
        return low * 2 + z

    def at(self, k, j):
        x = 1 - self.x if j in "xd" else self.x
        y = 1 - self.y if j in "yd" else self.y
        return self.plane(k) * 4 + y * 2 + x

    def greet(self):
        self.barrier = pltpu.get_barrier_semaphore()
        for peer in (self.sib, self.xn, self.yn, *self.zn.values()):
            pl.semaphore_signal(self.barrier, inc=1, device_id=peer, device_id_type=MESH)

    def meet(self):
        pl.semaphore_wait(self.barrier, 6)


class Copies:
    def __init__(self, send, recv):
        self.send, self.recv = send, recv

    def of(self, src, dst, pool, slot, peer):
        return pltpu.make_async_remote_copy(
            src_ref=src, dst_ref=dst, send_sem=self.send.at[pool], recv_sem=self.recv.at[slot],
            device_id=peer, device_id_type=MESH,
        )

    def put(self, src, dst, pool, slot, peer):
        self.of(src, dst, pool, slot, peer).start()

    def got(self, dst, slot, peer):
        self.of(dst, dst, 0, slot, peer).wait_recv()

    def sent(self, all_of_pool, pool, peer):
        self.of(all_of_pool, all_of_pool, pool, 0, peer).wait_send()


class Gather:
    def __init__(self, place, copies, i, side):
        self.p, self.cp, self.side = place, copies, side
        self.base, self.pool = i * gather_slots, 2 * i

    def slot(self, kind, k=0):
        return self.base + {"z": -1, "x": 3, "y": 7, "d": 11, "s": 15}[kind] + k

    def out(self, half, r):
        return self.side(half).at[r]

    def block(self, k, j):
        return self.out(self.p.c, self.p.at(k, j))

    def send(self, src, dst, slot, peer):
        self.cp.put(src, dst, self.pool, slot, peer)

    def push(self, src, k, j):
        self.cp.put(src, self.block(k, j), self.pool + 1, self.slot("s", k), self.p.sib)

    def to_z(self):
        for k in (1, 2):
            self.send(self.block(0, "o"), self.block(0, "o"), self.slot("z", k), self.p.zn[k])

    def to_xy(self):
        self.spread(self.block(0, "o"), 0)

    def spread(self, src, k):
        dst = self.block(k, "o")
        self.send(src, dst, self.slot("x", k), self.p.xn)
        self.send(src, dst, self.slot("y", k), self.p.yn)
        self.push(src, k, "o")

    def from_z(self, k):
        block = self.block(k, "o")
        self.cp.got(block, self.slot("z", k), self.p.zn[k])
        if k == 2:
            self.send(block, block, self.slot("z", 3), self.p.zn[1])
        self.spread(block, k)

    @staticmethod
    def schedule(mats):
        work = [(mats[0].to_z,)] + [(m.to_xy,) for m in mats[:3]]
        for i, m in enumerate(mats):
            before = mats[i - 1] if i else None
            work.append((m.from_z, 1))
            if i + 1 < len(mats):
                work.append((mats[i + 1].to_z,))
            if before:
                work.append((before.from_xy, 3))
            work += [(m.from_xy, 0), (m.from_z, 2)]
            if before:
                work.append((before.from_d, 2))
            if i + 3 < len(mats):
                work.append((mats[i + 3].to_xy,))
            work += [(m.from_xy, 1), (m.from_z, 3)]
            if before:
                work.append((before.from_d, 1))
            work.append((m.from_d, 0))
            if before:
                work.append((before.from_d, 3))
            work.append((m.from_xy, 2))
        last = mats[-1]
        return work + [(last.from_xy, 3), (last.from_d, 2), (last.from_d, 1), (last.from_d, 3)]

    def from_xy(self, k):
        x, y = self.block(k, "x"), self.block(k, "y")
        self.cp.got(x, self.slot("x", k), self.p.xn)
        if k == 2:
            self.send(x, x, self.slot("d", k), self.p.yn)
        self.cp.got(y, self.slot("y", k), self.p.yn)
        if k == 0:
            self.send(y, y, self.slot("d", k), self.p.xn)
        self.push(x, k, "x")
        self.push(y, k, "y")

    def from_d(self, k):
        block = self.block(k, "d")
        self.cp.got(block, self.slot("d", k), self.p.xn)
        if k % 2 == 0:
            self.send(block, block, self.slot("d", k + 1), self.p.zn[1])
        self.push(block, k, "d")

    def from_sib(self, *planes):
        for k in planes or range(4):
            four = pl.ds(self.p.plane(k) * 4, 4)
            self.cp.got(self.side(1 - self.p.c).at[four], self.slot("s", k), self.p.sib)

    def drain(self):
        side = self.side(self.p.c)
        self.cp.sent(side.at[pl.ds(0, 15)], self.pool, self.p.sib)
        self.cp.sent(side, self.pool + 1, self.p.sib)


class Scatter:
    def __init__(self, place, copies, i, give, own, sib, rly, dia, xin, yin, zin, straight=False, flat=False):
        self.p, self.cp, self.give, self.own = place, copies, give, own
        self.base, self.pool = i * scatter_slots, 2 * i
        self.straight, self.flat = straight, flat
        self.sib, self.rly, self.dia, self.xin, self.yin, self.zin = sib, rly, dia, xin, yin, zin

    def slot(self, kind, k):
        return self.base + {"s": 0, "r": 4, "d": 5, "x": 8, "y": 12, "z": 15}[kind] + k

    def four(self, k):
        return pl.ds(self.p.plane(k) * 4, 4)

    def begin(self, k):
        four = self.four(k)
        self.cp.put(self.give(four), self.sib.at[four], self.pool + 1, self.slot("s", k), self.p.sib)

    def given(self):
        self.cp.sent(self.sib, self.pool + 1, self.p.sib)

    def drain(self):
        self.cp.sent(self.sib.at[pl.ds(0, 15)], self.pool, self.p.sib)

    def to_x(self, own, k):
        self.cp.put(own, self.xin.at[k], self.pool, self.slot("x", k), self.p.xn)

    def to_y(self, own, k):
        self.cp.put(own, self.yin.at[k], self.pool, self.slot("y", k), self.p.yn)

    def both(self, k, j, *more):
        at = self.p.at(k, j)
        own = self.own(at)
        total = own[...] + self.sib[at]
        for ref in more:
            total = total + ref[...]
        own[...] = total
        return own

    def pair(self, k):
        four = self.four(k)
        self.cp.got(self.sib.at[four], self.slot("s", k), self.p.sib)
        if self.flat:
            self.to_relay(self.both(k, "d"), k)
        elif k % 2:
            i = k // 2
            self.cp.put(self.both(k, "d"), self.dia.at[i], self.pool, self.slot("d", 2 * i), self.p.zn[1])
        odd = k % 2 and not self.flat
        if odd or k < 2:
            self.to_x(self.both(k, "x"), k)
        if odd or k >= 2:
            self.to_y(self.both(k, "y"), k)

    def relay_at(self, k):
        return (self.dia if k % 2 else self.rly).at[k // 2]

    def to_relay(self, own, k):
        slot = self.slot("d", k - 1) if k % 2 else self.slot("r", k)
        self.cp.put(own, self.relay_at(k), self.pool, slot, self.p.xn if k < 2 else self.p.yn)

    def diag(self, k):
        i = k // 2
        self.cp.got(self.dia.at[i], self.slot("d", k), self.p.zn[1])
        self.to_relay(self.both(k, "d", self.dia.at[i]), k)

    def relay(self, k):
        rly = self.relay_at(k)
        self.cp.got(rly, self.slot("d", k - 1) if k % 2 else self.slot("r", k), self.p.xn)
        if k < 2:
            self.to_y(self.both(k, "y", rly), k)
        else:
            self.to_x(self.both(k, "x", rly), k)

    def plane(self, k):
        p = self.p
        at = p.at(k, "o")
        self.cp.got(self.xin.at[k], self.slot("x", k), p.xn)
        self.cp.got(self.yin.at[k], self.slot("y", k), p.yn)
        wide = jnp.float32
        own = self.own(at)
        total = (own[...].astype(wide) + self.sib[at].astype(wide)) + (
            self.xin[k].astype(wide) + self.yin[k].astype(wide)
        )
        own[...] = total.astype(jnp.bfloat16)
        if self.straight and k:
            self.to_z(own, k, k)
        elif k % 2:
            self.to_z(own, k, 1)

    def to_z(self, own, k, step):
        self.cp.put(own, self.zin.at[k - 1], self.pool, self.slot("z", k), self.p.zn[step])

    def cross(self):
        self.cp.got(self.zin.at[2], self.slot("z", 3), self.p.zn[1])
        own = self.own(self.p.at(2, "o"))
        own[...] = own[...] + self.zin[2]
        self.to_z(own, 2, 2)

    def all(self, name, *planes):
        for k in planes:
            getattr(self, name)(k)

    def first(self):
        self.all("pair", 3, 1)

    def rest(self):
        self.all("pair", 2, 0)

    def diags(self):
        if not self.flat:
            self.all("diag", 2, 0)

    def relays(self):
        self.all("relay", *((3, 1, 2, 0) if self.flat else (2, 0)))

    def odd(self):
        self.all("plane", 3, 1)

    def even(self):
        self.all("plane", 2, 0)
        if not self.straight:
            self.cross()

    def total(self):
        wide = jnp.float32
        total = self.own(self.p.at(0, "o"))[...].astype(wide)
        for k in (1, 2, 3) if self.straight else (1, 2):
            self.cp.got(self.zin.at[k - 1], self.slot("z", k), self.p.zn[k])
            total = total + self.zin[k - 1].astype(wide)
        return total


rows_chip = 48
gather_slots, scatter_slots = 19, 19


def dot(left, right, dims=((1,), (0,))):
    return lax.dot_general(left, right, (dims, ((), ())), preferred_element_type=jnp.float32)


def row_mean(values):
    return jnp.mean(values, -1, keepdims=True)


def normalized(resid):
    centred = resid - row_mean(resid)
    inverse = lax.rsqrt(row_mean(centred * centred) + ln_eps)
    return centred * inverse, inverse


def norm_back(grad, gain, norm, inverse):
    e = grad * gain
    return inverse * (e - row_mean(e) - norm * row_mean(e * norm))


def column_sum(values):
    return jnp.sum(values, 0, keepdims=True)


def ffn_kernel(
    tokens, attended, w_out, vectors, valid, out_grad, w_gu, w_down,
    output, d_resid_one, d_att, grad_out, grad_gu, grad_down, small,
    hid, hid_low, hid_t, norm_one, inv_one, slope_gate, slope_up, act, total, d_hid, d_branch,
):
    i = pl.program_id(0)
    tiles = pl.num_programs(0) // 2
    low = jnp.bfloat16
    wide = jnp.float32

    @pl.when(i == 0)
    def _():
        branch = dot(attended[...], w_out[0])
        toks = tokens[...].astype(wide)
        norm, inverse = normalized(toks + branch)
        norm_one[...] = norm
        inv_one[...] = inverse
        hidden = norm * vectors[0:1, :] + vectors[1:2, :]
        hid[...] = hidden
        hid_low[...] = hidden.astype(low)
        hid_t[...] = hidden.T.astype(low)
        mask = valid[...]
        small[4:5, :] = column_sum(mask * toks * toks)
        small[5:6, :] = column_sum(mask * branch * branch)
        small[6:7, :] = column_sum(mask * hidden * hidden)
        small[8:16, :] = jnp.zeros((8, small.shape[1]), wide)
        small[8:9, :] = jnp.broadcast_to(jnp.sum(mask, 0, keepdims=True), (1, small.shape[1]))
        total[...] = jnp.zeros_like(total)

    @pl.when(i < tiles)
    def _():
        h = hid_low[...]
        gate = dot(h, w_gu[0])
        up = dot(h, w_gu[1])
        cdf = 0.5 + 0.5 * lax.erf(gate * 0.7071067811865476)
        glu = gate * cdf
        density = 0.3989422804014327 * jnp.exp(-0.5 * gate * gate)
        slope_up[i] = glu
        slope_gate[i] = up * (cdf + gate * density)
        a = (glu * up).astype(low)
        act[i] = a
        total[...] += dot(a, w_down[...])

    @pl.when(i == tiles - 1)
    def _():
        branch = total[...]
        mask = valid[...]
        small[7:8, :] = column_sum(mask * branch * branch)
        norm, inverse = normalized(hid[...] + branch)
        gain = vectors[2:3, :]
        output[...] = (norm * gain + vectors[3:4, :]).astype(low)
        grad = out_grad[...].astype(wide)
        small[2:3, :] = column_sum(grad * norm)
        small[3:4, :] = column_sum(grad)
        back = norm_back(grad, gain, norm, inverse)
        d_hid[...] = back
        d_branch[...] = back.astype(low)

    @pl.when(i >= tiles)
    def _():
        j = i - tiles
        db = d_branch[...]
        grad_down[...] = dot(act[j].T, db).astype(low)
        d_act = dot(db, w_down[...], ((1,), (1,)))
        d_gate = (d_act * slope_gate[j]).astype(low)
        d_up = (d_act * slope_up[j]).astype(low)
        h_t = hid_t[...]
        grad_gu[0] = dot(h_t, d_gate).astype(low)
        grad_gu[1] = dot(h_t, d_up).astype(low)
        d_hid[...] += dot(d_gate, w_gu[0], ((1,), (1,))) + dot(d_up, w_gu[1], ((1,), (1,)))

    @pl.when(i == 2 * tiles - 1)
    def _():
        grad = d_hid[...]
        norm = norm_one[...]
        small[0:1, :] = column_sum(grad * norm)
        small[1:2, :] = column_sum(grad)
        back = norm_back(grad, vectors[0:1, :], norm, inv_one[...])
        d_resid_one[...] = back
        db = back.astype(low)
        grad_out[...] = dot(attended[...].T, db).astype(low)
        d_att[...] = dot(db, w_out[0], ((1,), (1,))).astype(low)


def ffn(tokens, attended, a_full, vectors, valid, out_grad, w_gu, w_down):
    rows, width = tokens.shape
    ff = w_down.shape[0]
    tile = 512
    tiles = ff // tile
    low, wide = jnp.bfloat16, jnp.float32
    whole = lambda *shape: pl.BlockSpec(shape, lambda i: (0,) * len(shape))
    at = lambda i: jnp.where(i < tiles, i, i - tiles)
    late = lambda i: jnp.maximum(i - tiles, 0)
    return pl.pallas_call(
        ffn_kernel,
        grid=(2 * tiles,),
        out_shape=(
            jax.ShapeDtypeStruct((rows, width), low),
            jax.ShapeDtypeStruct((rows, width), wide),
            jax.ShapeDtypeStruct((rows, width), low),
            jax.ShapeDtypeStruct((width, width), low),
            jax.ShapeDtypeStruct((2, width, ff), low),
            jax.ShapeDtypeStruct((ff, width), low),
            jax.ShapeDtypeStruct((16, width), wide),
        ),
        in_specs=[
            whole(rows, width),
            whole(rows, width),
            pl.BlockSpec((1, width, width), lambda i: (1, 0, 1)),
            whole(8, width),
            whole(rows, 1),
            whole(rows, width),
            pl.BlockSpec((2, width, tile), lambda i: (0, 0, at(i))),
            pl.BlockSpec((tile, width), lambda i: (at(i), 0)),
        ],
        out_specs=(
            whole(rows, width),
            whole(rows, width),
            whole(rows, width),
            whole(width, width),
            pl.BlockSpec((2, width, tile), lambda i: (0, 0, late(i))),
            pl.BlockSpec((tile, width), lambda i: (late(i), 0)),
            whole(16, width),
        ),
        scratch_shapes=[
            pltpu.VMEM((rows, width), wide),
            pltpu.VMEM((rows, width), low),
            pltpu.VMEM((width, rows), low),
            pltpu.VMEM((rows, width), wide),
            pltpu.VMEM((rows, 1), wide),
            pltpu.VMEM((tiles, rows, tile), wide),
            pltpu.VMEM((tiles, rows, tile), wide),
            pltpu.VMEM((tiles, rows, tile), low),
            pltpu.VMEM((rows, width), wide),
            pltpu.VMEM((rows, width), wide),
            pltpu.VMEM((rows, width), low),
        ],
        compiler_params=pltpu.CompilerParams(vmem_limit_bytes=60 * 2**20),
        cost_estimate=pl.CostEstimate(
            flops=2 * rows * width * (9 * ff + 3 * width), bytes_accessed=18 * ff * width, transcendentals=2 * rows * ff
        ),
        name="feed_forward",
    )(tokens, attended, a_full, vectors, valid, out_grad, w_gu, w_down)


def half_of(block, axis, second):
    place = lax.broadcasted_iota(jnp.int32, block.shape, axis)
    depth = block.shape[axis] // 2
    keep = place >= depth if second else place < depth
    return jnp.where(keep, block, jnp.zeros_like(block))


def attend_kernel(heads, q, k, v, span, attended, lse):
    @pl.loop(0, heads // 2)
    def _(pair):
        attend_pair(pair, heads, q, k, v, span, lse, attended)


def attend(q, k, v, span, heads):
    rows, width = q.shape
    keys = k.shape[0]
    low, wide = jnp.bfloat16, jnp.float32
    return pl.pallas_call(
        lambda *refs: attend_kernel(heads, *refs),
        out_shape=(
            jax.ShapeDtypeStruct((rows, width), low),
            jax.ShapeDtypeStruct((16, rows), wide),
        ),
        in_specs=[pl.BlockSpec(memory_space=pltpu.VMEM)] * 4,
        out_specs=(pl.BlockSpec(memory_space=pltpu.VMEM),) * 2,
        compiler_params=pltpu.CompilerParams(vmem_limit_bytes=60 * 2**20),
        cost_estimate=pl.CostEstimate(flops=4 * rows * keys * width, bytes_accessed=8 * keys * width, transcendentals=heads * rows * keys),
        name="attend",
    )(q, k, v, span)


def attend_back_pair(pair, heads, q, k, v, span, lse, att, d_att, dq, dk_sum, dv_sum):
    low, wide = jnp.bfloat16, jnp.float32
    rows, width = q.shape
    lanes = lane_width
    depth = width // heads
    chunk = 256
    scale = depth**-0.5
    at = pl.ds(pl.multiple_of(pair * lanes, lanes), lanes)
    keys, values = k[:, at], v[:, at]
    keys_t = keys.astype(wide).T.astype(low)
    for c in range(rows // chunk):
        here = pl.ds(c * chunk, chunk)
        q_wide = q[here, at].astype(wide)
        do_here = d_att[here, at]
        do_wide = do_here.astype(wide)
        q_here = q_wide.astype(low)
        q_t, do_t = q_wide.T.astype(low), do_wide.T.astype(low)
        both_t = (do_wide * att[here, at].astype(wide)).T
        dk_part, dv_part, dq_parts = None, None, []
        for h in (0, 1):
            head = 2 * pair + h
            own = slice(h * depth, (h + 1) * depth)
            slope = jnp.exp2(jnp.full((1, 1), -8.0 / heads, wide) * (head + 1).astype(wide))
            delta = jnp.sum(both_t[own], 0, keepdims=True)
            logits = dot(keys, half_of(q_t, 0, h)) - slope * span[:, here]
            probs = jnp.exp(logits - lse[pl.ds(head, 1), here])
            d_probs = dot(values, half_of(do_t, 0, h))
            d_logits = (probs * (d_probs - delta)).astype(low)
            dv_term = dot(probs.astype(low), half_of(do_here, 1, h))
            dk_term = dot(d_logits, half_of(q_here, 1, h))
            dv_part = dv_term if dv_part is None else dv_part + dv_term
            dk_part = dk_term if dk_part is None else dk_part + dk_term
            dq_parts.append(dot(keys_t[own], d_logits) * scale)
        if c == 0:
            dk_sum[...] = dk_part
            dv_sum[...] = dv_part
        else:
            dk_sum[...] += dk_part
            dv_sum[...] += dv_part
        dq[here, at] = jnp.concatenate(dq_parts, 0).T.astype(low)


def attend_back_kernel(heads, q, k, v, span, lse, att, d_att, dq, dk, dv, dk_sum, dv_sum):
    @pl.loop(0, heads // 2)
    def _(pair):
        attend_back_pair(pair, heads, q, k, v, span, lse, att, d_att, dq, dk_sum, dv_sum)
        at = pl.ds(pl.multiple_of(pair * lane_width, lane_width), lane_width)
        dk[:, at] = dk_sum[...]
        dv[:, at] = dv_sum[...]


def attend_back(q, k, v, span, lse, att, d_att, heads):
    rows, width = q.shape
    keys = k.shape[0]
    low, wide = jnp.bfloat16, jnp.float32
    return pl.pallas_call(
        lambda *refs: attend_back_kernel(heads, *refs),
        out_shape=(
            jax.ShapeDtypeStruct((rows, width), low),
            jax.ShapeDtypeStruct((keys, width), wide),
            jax.ShapeDtypeStruct((keys, width), wide),
        ),
        in_specs=[pl.BlockSpec(memory_space=pltpu.VMEM)] * 7,
        out_specs=(pl.BlockSpec(memory_space=pltpu.VMEM),) * 3,
        scratch_shapes=[
            pltpu.VMEM((keys, lane_width), wide),
            pltpu.VMEM((keys, lane_width), wide),
        ],
        compiler_params=pltpu.CompilerParams(vmem_limit_bytes=60 * 2**20),
        cost_estimate=pl.CostEstimate(flops=10 * rows * keys * width, bytes_accessed=16 * keys * width, transcendentals=heads * rows * keys),
        name="attend_back",
    )(q, k, v, span, lse, att, d_att)


def attend_pair(pair, heads, q, k, v, span, lse, attended):
    low, wide = jnp.bfloat16, jnp.float32
    rows, width = q.shape
    lanes = lane_width
    depth = width // heads
    chunk = 256
    at = pl.ds(pl.multiple_of(pair * lanes, lanes), lanes)
    keys = k[:, at]
    values_t = v[:, at].astype(wide).T.astype(low)
    for c in range(rows // chunk):
        here = pl.ds(c * chunk, chunk)
        q_t = q[here, at].astype(wide).T.astype(low)
        parts = []
        for h in (0, 1):
            head = 2 * pair + h
            slope = jnp.exp2(jnp.full((1, 1), -8.0 / heads, wide) * (head + 1).astype(wide))
            logits = dot(keys, half_of(q_t, 0, h)) - slope * span[:, here]
            top = jnp.max(logits, 0, keepdims=True)
            weights = jnp.exp(logits - top)
            norm = jnp.sum(weights, 0, keepdims=True)
            lse[pl.ds(head, 1), here] = top + jnp.log(norm)
            parts.append(dot(values_t[h * depth : (h + 1) * depth], weights.astype(low)) / norm)
        attended[here, at] = jnp.concatenate(parts, 0).T.astype(low)


def fore_kernel(
    heads, tokens_at, labels_at, w_qkv_at, w_out_at, w_gu_at, d_shard_at, gain_one_at, bias_one_at, gain_two_at, bias_two_at,
    out_grad, a_full, g_full, d_full, q_out, k_out, v_out, att_out, hid_t_out, norm_out, inv_out, gate_out, up_out, act_out,
    output_out, d_branch_out, span_out, lse, vectors, small,
    w_a, w_g, w_d, a_give, g_give, a_pair, g_pair, turned, q, k, v, att, span_v, grad_v, hid, hid_low, hid_t, norm_one, inv_one,
    slope_gate, slope_up, act, output, d_hid, d_branch,
    tokens, labels, w_qkv, w_out, w_gu, d_shard, gain_one, bias_one, gain_two, bias_two, pair_sem, send, recv, in_sem, out_sem,
):
    place = Place()
    sources = (
        w_gu_at, w_qkv_at, w_out_at, gain_one_at, bias_one_at, gain_two_at, bias_two_at, d_shard_at, labels_at, tokens_at,
    )
    held = (w_gu, w_qkv, w_out, gain_one, bias_one, gain_two, bias_two, d_shard, labels, tokens)
    inward = [pltpu.make_async_copy(src, dst, in_sem.at[1 + i]) for i, (src, dst) in enumerate(zip(sources, held))]
    for copy in inward:
        copy.start()
    place.greet()
    c = place.c
    low, wide = jnp.bfloat16, jnp.float32
    tok_rows, width = tokens.shape
    ff = w_g.shape[3]
    half_g = ff // 2
    pairs = heads // 2
    load = pltpu.make_async_copy(out_grad, grad_v, in_sem.at[0])
    load.start()
    core_one = c == 1
    for copy in inward:
        copy.wait()
    turned[...] = jnp.zeros_like(turned)
    share = w_out.shape[0]
    for i, norm in enumerate((gain_one, bias_one, gain_two, bias_two)):
        turned[i : i + 1, 0:share] = norm[...].astype(wide).reshape(1, share)
    table = turned[...].T[:share].astype(low)
    left = jnp.concatenate([w_qkv[:, : 2 * width], table], 1)
    right = jnp.concatenate([w_qkv[:, 2 * width :], w_out[...], jnp.zeros_like(table)], 1)
    gate, up = w_gu[:, :ff], w_gu[:, ff:]
    rows = w_qkv.shape[0]
    a_give[:rows, :] = jnp.where(core_one, left, right)
    g_give[:rows, :] = jnp.where(core_one, gate, up)
    swaps = Copies(pair_sem.at[0], pair_sem.at[1])
    place.meet()
    for i, (give, other) in enumerate(((a_give, a_pair), (g_give, g_pair))):
        swaps.put(give, other, i, i, place.sib)
    copies = Copies(send, recv)
    sides = [
        lambda half: w_a.at[half],
        lambda half: w_g.at[half, :, :, :half_g],
        lambda half: w_g.at[half, :, :, half_g:],
        lambda half: w_d.at[:, half],
    ]
    mats = [Gather(place, copies, i, side) for i, side in enumerate(sides)]
    first, second, third, fourth = mats
    me = place.at(0, "o")

    def assemble(mine, other, full, i):
        swaps.got(other, i, place.sib)
        mine = mine.astype(wide)
        theirs = other[:rows, :].astype(wide)
        top = jnp.where(core_one, theirs, mine)
        rest = jnp.where(core_one, mine, theirs)
        full[c, me] = jnp.concatenate([top, rest], 0).astype(low)

    work = Gather.schedule(mats)

    def go(count):
        for step, *plane in work[:count]:
            step(*plane)
        del work[:count]

    def upto(matrix):
        done = [i for i, (step, *_) in enumerate(work) if step == matrix.from_d]
        go(done[-1] + 1 if done else 0)

    assemble(jnp.where(core_one, right, left), a_pair, w_a, 0)
    go(2)
    assemble(jnp.where(core_one, up, gate), g_pair, w_g, 1)
    w_d[me, c] = d_shard[...]
    seq_len = labels.shape[1]
    label_row = labels[...].astype(wide)
    label_column = jnp.broadcast_to(label_row, (lane_width, seq_len)).T[:, 0:1]
    half = pl.ds(pl.multiple_of(c * tok_rows, tok_rows), tok_rows)
    same = (label_column == labels[:, half].astype(wide)) & (label_column != seq_len)
    key_at = lax.broadcasted_iota(jnp.int32, span_v.shape, 0)
    gap = jnp.abs(key_at - lax.broadcasted_iota(jnp.int32, span_v.shape, 1) - c * tok_rows)
    span_v[...] = jnp.where(same | (gap == 0), gap.astype(wide), far)
    mask = jnp.broadcast_to(labels[:, half].astype(wide), (lane_width, tok_rows)).T[:, 0:1]
    mask = (mask != seq_len).astype(wide)
    upto(first)
    first.from_sib()
    saved = []

    def save(src, dst):
        copy = pltpu.make_async_copy(src, dst, out_sem.at[len(saved)])
        copy.start()
        saved.append((src, dst))

    save(w_a, a_full)
    save(span_v, span_out)
    part = lambda half, at, size: w_a[half, :, :, at : at + size].reshape(width, size)
    vectors[...] = part(0, 2 * width, lane_width).astype(wide).T[:8]
    x = tokens[...]
    k[half, :] = dot(x, part(0, width, width)).astype(low)
    swaps.put(k.at[half], k.at[half], 2, 2, place.sib)
    v[half, :] = dot(x, part(1, 0, width)).astype(low)
    swaps.put(v.at[half], v.at[half], 3, 3, place.sib)
    depth = width // heads
    q[...] = dot(x, part(0, 0, width)).astype(low) * depth**-0.5
    go(3)
    other = pl.ds(pl.multiple_of((1 - c) * tok_rows, tok_rows), tok_rows)
    swaps.got(k.at[other], 2, place.sib)
    swaps.got(v.at[other], 3, place.sib)
    save(q, q_out)
    save(k, k_out)
    save(v, v_out)

    shares = (3, 4, 4, 4, 4, 2)
    todo = []
    for count in shares:
        todo.append(work[:count])
        del work[:count]

    @pl.loop(0, pairs)
    def _(pair):
        attend_pair(pair, heads, q, k, v, span_v, lse, att)
        for at, steps in enumerate(todo):

            @pl.when(pair == at)
            def _(steps=steps):
                for step, *plane in steps:
                    step(*plane)

    save(att, att_out)
    branch = dot(att[...], part(1, width, width))
    toks = x.astype(wide)
    norm, inverse = normalized(toks + branch)
    norm_one[...] = norm
    inv_one[...] = jnp.broadcast_to(inverse, inv_one.shape)
    hidden = norm * vectors[0:1, :] + vectors[1:2, :]
    hid[...] = hidden
    hid_low[...] = hidden.astype(low)
    hid_t[...] = hidden.T.astype(low)
    save(hid_t, hid_t_out)
    save(norm_one, norm_out)
    save(inv_one, inv_out)
    small[0:4, :] = jnp.zeros((4, width), wide)
    small[4:5, :] = column_sum(mask * toks * toks)
    small[5:6, :] = column_sum(mask * branch * branch)
    small[6:7, :] = column_sum(mask * hidden * hidden)
    small[8:16, :] = jnp.zeros((8, width), wide)
    small[8:9, :] = jnp.broadcast_to(jnp.sum(mask, 0, keepdims=True), (1, width))
    tile = 512

    def glu(j):
        cols = pl.ds(pl.multiple_of(j * tile, tile), tile)
        h = hid_low[...]
        gate = dot(h, w_g[0, :, :, cols].reshape(width, tile))
        up = dot(h, w_g[1, :, :, cols].reshape(width, tile))
        cdf = 0.5 + 0.5 * lax.erf(gate * 0.7071067811865476)
        mixed = gate * cdf
        density = 0.3989422804014327 * jnp.exp(-0.5 * gate * gate)
        slope_up[:, cols] = mixed.astype(low)
        slope_gate[:, cols] = (up * (cdf + gate * density)).astype(low)
        act[:, cols] = (mixed * up).astype(low)

    upto(second)
    go(1)
    second.from_sib()
    save(w_g.at[:, :, :, :half_g], g_full.at[:, :, :, :half_g])

    @pl.loop(0, half_g // tile)
    def _(j):
        glu(j)

    go(1)
    third.from_sib()
    save(w_g.at[:, :, :, half_g:], g_full.at[:, :, :, half_g:])
    for src, dst in ((slope_gate, gate_out), (slope_up, up_out), (act, act_out)):
        save(src.at[:, :half_g], dst.at[:, :half_g])

    @pl.loop(half_g // tile, ff // tile)
    def _(j):
        glu(j)

    for src, dst in ((slope_gate, gate_out), (slope_up, up_out), (act, act_out)):
        save(src.at[:, half_g:], dst.at[:, half_g:])

    def down(plane):
        at = place.plane(plane)
        cols = pl.ds(pl.multiple_of(at * width, width), width)
        return dot(act[:, cols], w_d[pl.ds(at * 4, 4)].reshape(width, width))

    go(1)
    fourth.from_sib(0, 2, 1)
    d_hid[...] = down(0)
    for plane in (2, 1):
        d_hid[...] += down(plane)
    upto(fourth)
    fourth.from_sib(3)
    save(w_d, d_full)
    d_hid[...] += down(3)
    branch = d_hid[...]
    small[7:8, :] = column_sum(mask * branch * branch)
    norm, inverse = normalized(hid[...] + branch)
    gain = vectors[2:3, :]
    output[...] = (norm * gain + vectors[3:4, :]).astype(low)
    save(output, output_out)
    load.wait()
    grad = grad_v[...].astype(wide)
    small[2:3, :] = column_sum(grad * norm)
    small[3:4, :] = column_sum(grad)
    back = norm_back(grad, gain, norm, inverse)
    d_branch[...] = back.astype(low)
    save(d_branch, d_branch_out)
    for i, (src, dst) in enumerate(saved):
        pltpu.make_async_copy(src, dst, out_sem.at[i]).wait()
    for i, ref in enumerate((a_give, g_give, k.at[half], v.at[half])):
        swaps.sent(ref, i, place.sib)
    for m in mats:
        m.drain()


def fore(heads, tokens, labels, w_qkv, w_out, w_gu, d_shard, norms, out_grad):
    low, wide = jnp.bfloat16, jnp.float32
    rows, width = tokens.shape
    ff = w_gu.shape[1] // 2
    half_a = 2 * width + lane_width
    keys = labels.shape[1]
    vmem, hbm = pl.BlockSpec(memory_space=pltpu.VMEM), pl.BlockSpec(memory_space=pl.ANY)
    dma = lambda *shape: pltpu.SemaphoreType.DMA(shape)
    shape = jax.ShapeDtypeStruct
    w_a, w_g, w_d = (2, 16, rows_chip, half_a), (2, 16, rows_chip, ff), (16, 2) + d_shard.shape
    stored = [
        (w_a, low), (w_g, low), (w_d, low), ((rows, width), low), ((keys, width), low), ((keys, width), low),
        ((rows, width), low), ((width, rows), low), ((rows, width), wide), ((rows, lane_width), wide),
        ((rows, ff), low), ((rows, ff), low), ((rows, ff), low), ((rows, width), low),
        ((rows, width), low), ((keys, rows), wide),
    ]
    block = lambda *dims: pltpu.VMEM(dims, low)
    block_wide = lambda *dims: pltpu.VMEM(dims, wide)
    return pl.pallas_call(
        lambda *refs: fore_kernel(heads, *refs),
        out_shape=tuple(shape(dims, kind) for dims, kind in stored)
        + (shape((16, rows), wide), shape((8, width), wide), shape((16, width), wide)),
        in_specs=[hbm] * 11,
        out_specs=(hbm,) * len(stored) + (vmem,) * 3,
        scratch_shapes=[
            block(*w_a), block(*w_g), block(*w_d), block(32, half_a), block(32, ff), block(32, half_a), block(32, ff),
            block_wide(lane_width, lane_width),
            block(rows, width), block(keys, width), block(keys, width), block(rows, width),
            block_wide(keys, rows), block(rows, width), block_wide(rows, width), block(rows, width),
            block(width, rows), block_wide(rows, width), block_wide(rows, lane_width),
            block(rows, ff), block(rows, ff), block(rows, ff), block(rows, width), block_wide(rows, width),
            block(rows, width),
            *(pltpu.VMEM(part.shape, part.dtype) for part in (tokens, labels, w_qkv, w_out, w_gu, d_shard, *norms)),
            dma(2, 4), dma(8), dma(4 * gather_slots), dma(11), dma(len(stored) + 4),
        ],
        compiler_params=pltpu.CompilerParams(
            collective_id=0, has_side_effects=True, vmem_limit_bytes=62 * 2**20
        ),
        name="gather_and_forward",
    )(tokens, labels, w_qkv, w_out, w_gu, d_shard, *norms, out_grad)


def back_kernel(
    heads, tokens, q, k, v, span, att, hid_t, norm, inv, gate, up, act, d_branch, a_full, g_full, d_full,
    lse_at, vectors_at, small_at, d_tokens, qkv_out, wout_out, gu_out, down_out, tail, *scratch,
):
    place = Place()
    place.greet()
    c = place.c
    first = c == 0
    low, wide = jnp.bfloat16, jnp.float32
    tok_rows, width = tokens.shape
    ff = gate.shape[1]
    pairs = heads // 2
    bufs, rest = scratch[:33], scratch[33:]
    a_grad, dkv_in, resid, d_att, g_sum, a_sum, g_fin, a_fin, small_buf, send, recv, tokens_v, down_v, gu_v, lse, vectors, small, pair_sem, fin_sem, in_sem, tile_sem = rest
    copies = Copies(send, recv)
    last = Copies(fin_sem.at[0], fin_sem.at[1])
    half_g, part = ff // 2, width // 2

    def scatter(i, own, *more):
        return Scatter(place, copies, i, None, lambda at: own.at[at], *more)

    def projection(i, *more):
        give = lambda four: a_grad.at[i, 1 - c, four]
        own = lambda at: a_grad.at[i, c, at]
        return Scatter(place, copies, 3 + i, give, own, *more)

    down, left, right = (scatter(i, *bufs[7 * i : 7 * i + 7]) for i in range(3))
    projs = [projection(i, *bufs[21 + 6 * i : 27 + 6 * i]) for i in range(2)]
    early, late = projs
    planes = (3, 2, 1, 0)
    hand_over = lambda i, src, dst: pltpu.make_async_copy(src, dst, in_sem.at[i])
    hops = ((place.sib, 0), (place.xn, 1), (place.yn, 2))

    def exchange(i):
        peer, slot = hops[i]
        last.put(small_buf.at[i], small_buf.at[4 + i], slot, slot, peer)

    def combine(i):
        peer, slot = hops[i]
        last.got(small_buf.at[4 + i], slot, peer)
        small_buf[i + 1] = small_buf[i] + small_buf[4 + i]

    def spread():
        for z in (1, 2, 3):
            last.put(small_buf.at[3], small_buf.at[6 + z], 2 + z, 2 + z, place.zn[z])

    tile = 256

    def feed_forward(given, act_v, db, ht, w_gu, w_dn, gate_v, up_v, att_v, norm_v, inv_v, w_out):
        for i, m in enumerate((down, left, right)):
            m.give = lambda four, i=i: given.at[i % 2, four]
        load = lambda i, src, dst: pltpu.make_async_copy(src, dst, in_sem.at[i])
        loads = [
            load(0, d_branch, db), load(1, hid_t, ht), load(3, att, att_v),
            load(4, norm, norm_v), load(5, inv, inv_v), load(6, a_full.at[1, :, :, width : 2 * width], w_out),
        ]

        def act_load(i, z):
            cols = pl.ds(pl.multiple_of(place.plane(z) * width, width), width)
            return load(7 + i % 2, act.at[:, cols], act_v.at[i % 2])

        def fetch(j):
            slot = j % 2
            cols = pl.ds(pl.multiple_of(j * tile, tile), tile)
            return [
                pltpu.make_async_copy(g_full.at[:, :, :, cols], w_gu.at[slot], tile_sem.at[0, slot]),
                pltpu.make_async_copy(d_full.at[cols], w_dn.at[slot], tile_sem.at[1, slot]),
                pltpu.make_async_copy(gate.at[:, cols], gate_v.at[slot], tile_sem.at[2, slot]),
                pltpu.make_async_copy(up.at[:, cols], up_v.at[slot], tile_sem.at[3, slot]),
            ]

        loads[0].start()
        tables = [load(9 + i, src, dst) for i, (src, dst) in enumerate(((lse_at, lse), (vectors_at, vectors), (small_at, small)))]
        act_load(0, planes[0]).start()
        act_load(1, planes[1]).start()
        for copy in loads[1:] + fetch(0) + tables:
            copy.start()
        loads[0].wait()
        own_d = bufs[0]
        for i, z in enumerate(planes):
            act_load(i, z).wait()
            term = dot(act_v[i % 2].T, db[...]).astype(low).reshape(4, 2, 2, rows_chip, width)
            if i < 2:
                act_load(i + 2, planes[i + 2]).start()
            four = pl.ds(place.plane(z) * 4, 4)
            mine = jnp.where(first, term[:, 0], term[:, 1])
            other = jnp.where(first, term[:, 1], term[:, 0])
            for j in range(2):
                cols = slice(j * width, (j + 1) * width)
                bufs[0][four, :, cols] = mine[:, j]
                given[0, four, :, cols] = other[:, j]
            if i == 0:
                place.meet()
            down.begin(z)
            if i > 1:
                down.pair(planes[i - 2])
        loads[1].wait()
        resid[...] = db[...].astype(wide)

        def between(i, todo):
            for at, *work in todo:

                @pl.when(i == at)
                def _(work=work):
                    for step in work:
                        step()

        def tiles(begin, own_g, give_g, todo):
            @pl.loop(begin, begin + half_g // tile)
            def _(j):
                slot = j % 2
                for copy in fetch(j):
                    copy.wait()

                @pl.when(j + 1 < ff // tile)
                def _():
                    for copy in fetch(j + 1):
                        copy.start()

                d_act = dot(db[...], w_dn[slot], ((1,), (1,)))
                d_gate = (d_act * gate_v[slot].astype(wide)).astype(low)
                d_up = (d_act * up_v[slot].astype(wide)).astype(low)
                resid[...] += dot(d_gate, w_gu[slot, 0].reshape(width, tile), ((1,), (1,))) + dot(
                    d_up, w_gu[slot, 1].reshape(width, tile), ((1,), (1,))
                )
                cols = pl.ds(pl.multiple_of((j - begin) * tile, tile), tile)
                mine = dot(ht[...], jnp.where(first, d_gate, d_up)).astype(low)
                own_g[:, :, cols] = mine.reshape(16, rows_chip, tile)
                other = dot(ht[...], jnp.where(first, d_up, d_gate)).astype(low)
                give_g[:, :, cols] = other.reshape(16, rows_chip, tile)
                between(j - begin, todo)

        tiles(0, bufs[7], given.at[1], [(0, lambda: down.pair(1)), (1, lambda: down.pair(0)), (5, down.diags)])
        for z in planes:
            left.begin(z)
        down.given()
        tiles(half_g // tile, bufs[14], given.at[0], [(2, down.relays, left.first, left.rest), (5, down.odd)])
        for z in planes:
            right.begin(z)
        for copy in loads[2:] + tables:
            copy.wait()
        grad = resid[...]
        unit = norm_v[...]
        small_buf[0] = small[...]
        small_buf[0, 0:1, :] = column_sum(grad * unit)
        small_buf[0, 1:2, :] = column_sum(grad)
        exchange(0)
        back = norm_back(grad, vectors[0:1, :], unit, inv_v[:, 0:1])
        resid[...] = back
        d_one = back.astype(low)
        d_att[...] = dot(d_one, w_out[...].reshape(width, width), ((1,), (1,))).astype(low)
        grad_out = dot(att_v[...].T, d_one).astype(low).reshape(16, rows_chip, width)
        for i in range(2):
            a_grad[i, 1, :, :, part:] = grad_out[:, :, i * part : (i + 1) * part]
        left.diags()
        right.first()
        right.rest()
        left.given()
        right.given()

    block = lambda *dims: pltpu.VMEM(dims, low)
    block_wide = lambda *dims: pltpu.VMEM(dims, wide)
    pl.run_scoped(
        feed_forward, block(2, *bufs[0].shape), block(2, tok_rows, width),
        block(tok_rows, width), block(width, tok_rows), block(2, 2, 16, rows_chip, tile), block(2, tile, width),
        block(2, tok_rows, tile), block(2, tok_rows, tile), block(tok_rows, width), block_wide(tok_rows, width),
        block_wide(tok_rows, lane_width), block(16, rows_chip, width),
    )

    half = lambda side: pl.ds(pl.multiple_of(side * tok_rows, tok_rows), tok_rows)

    def attention_part(dq, dkv_own, dkv_out, x_t, d_k, d_v):
        slots = dkv_own.shape[0]

        def send_dkv(pair):
            return pltpu.make_async_remote_copy(
                src_ref=dkv_out.at[pair], dst_ref=dkv_in.at[pair], send_sem=pair_sem.at[0, pair],
                recv_sem=pair_sem.at[1, pair], device_id=place.sib, device_id_type=MESH,
            )

        def project(i):
            for pair in range(i * pairs // 2, (i + 1) * pairs // 2):
                send_dkv(pair).wait_recv()
                at = slice(pair * lane_width, (pair + 1) * lane_width)
                for j, dst in enumerate((d_k, d_v)):
                    dst[:, at] = (dkv_own[pair % slots, j] + dkv_in[pair, j].astype(wide)).astype(low)
            cols = slice(i * part, (i + 1) * part)
            for side, at, src in ((0, 0, dq), (0, part, d_k), (1, 0, d_v)):
                term = dot(x_t[...], src[:, cols]).astype(low)
                a_grad[i, side, :, :, at : at + part] = term.reshape(16, rows_chip, part)
            for z in planes:
                projs[i].begin(z)

        def attention(q_v, k_v, v_v, span_v, att_v, x, dk_sum, dv_sum):
            load = lambda i, src, dst: pltpu.make_async_copy(src, dst, in_sem.at[i])
            sources = ((q, q_v), (k, k_v), (v, v_v), (att, att_v))
            head, rest = slice(0, lane_width), slice(lane_width, width)
            loads = [load(0, span, span_v)]
            loads += [load(1 + i, src.at[:, head], dst.at[:, head]) for i, (src, dst) in enumerate(sources)]
            later = [load(5 + i, src.at[:, rest], dst.at[:, rest]) for i, (src, dst) in enumerate(sources)]
            later.append(load(9, tokens, x))
            for copy in loads + later:
                copy.start()
            for copy in loads:
                copy.wait()

            def arrive():
                for i, (src, dst) in enumerate(sources):
                    load(5 + i, src.at[:, rest], dst.at[:, rest]).wait()
                load(9, tokens, x).wait()
                x_t[...] = x[...].T

            def meet_small(i):
                combine(i)
                exchange(i + 1)

            def heads_back(begin, end, todo):
                @pl.loop(begin, end)
                def _(pair):
                    attend_back_pair(pair, heads, q_v, k_v, v_v, span_v, lse, att_v, d_att, dq, dk_sum, dv_sum)
                    for i, side in enumerate((dk_sum, dv_sum)):
                        dkv_own[lax.rem(pair, slots), i] = side[half(c), :]
                        dkv_out[pair, i] = side[half(1 - c), :].astype(low)
                    send_dkv(pair).start()
                    for at, *work in todo:

                        @pl.when(pair == at)
                        def _(at=at, work=work):
                            for step in work:
                                step()

            small_step = lambda i: lambda: meet_small(i)
            heads_back(0, 4, [
                (0, arrive, down.even, small_step(0)), (1, left.odd), (2, left.relays, right.diags), (3, right.odd),
            ])
            project(0)
            heads_back(4, pairs, [(4, left.even, early.first, early.rest, small_step(1)), (5, right.relays)])
            project(1)

        key_rows = k.shape[0]
        pl.run_scoped(
            attention, block(*q.shape), block(*k.shape), block(*v.shape), block_wide(*span.shape), block(*att.shape),
            block(tok_rows, width), block_wide(key_rows, lane_width), block_wide(key_rows, lane_width),
        )

        def meet_last():
            combine(2)
            spread()

        def finish(w_left, w_right):
            loads = [
                pltpu.make_async_copy(a_full.at[0, :, :, : 2 * width], w_left, in_sem.at[0]),
                pltpu.make_async_copy(a_full.at[1, :, :, :width], w_right, in_sem.at[1]),
            ]
            for copy in loads:
                copy.start()
            for copy in loads:
                copy.wait()
            w_q = w_left[:, :, :width].reshape(width, width)
            total = resid[...] + dot(dq[...], w_q, ((1,), (1,)))
            early.diags()
            late.first()
            late.rest()
            right.even()
            meet_last()
            w_k = w_left[:, :, width:].reshape(width, width)
            total += dot(d_k[...], w_k, ((1,), (1,)))
            early.relays()
            late.diags()
            early.odd()
            early.even()
            total += dot(d_v[...], w_right[...].reshape(width, width), ((1,), (1,)))
            tokens_v[...] = total.astype(low)
            hand_over(0, tokens_v, d_tokens).start()
            late.relays()
            late.odd()

        pl.run_scoped(finish, block(16, rows_chip, 2 * width), block(16, rows_chip, width))

        @pl.loop(0, pairs)
        def _(pair):
            send_dkv(pair).wait_send()

    pl.run_scoped(
        attention_part, block(tok_rows, width), block_wide(4, 2, tok_rows, lane_width),
        block(pairs, 2, tok_rows, lane_width), block(width, tok_rows), block(tok_rows, width), block(tok_rows, width),
    )
    mine, theirs = pl.ds(pl.multiple_of(24 * c, 8), 24), pl.ds(pl.multiple_of(24 - 24 * c, 8), 24)
    total = down.total()
    down_v[:rows_chip] = total[:, :width]
    down_v[rows_chip:] = total[:, width:]
    hand_over(1, down_v, down_out).start()

    def swap(i, m, total, other, slot):
        total[i] = m.total()
        last.put(total.at[i, theirs], other.at[i], slot, slot, place.sib)

    swap(0, left, g_sum, g_fin, 6)
    swap(1, right, g_sum, g_fin, 7)
    late.even()
    swap(0, early, a_sum, a_fin, 8)
    for z in (1, 2, 3):
        last.got(small_buf.at[6 + z], 2 + z, place.zn[z])
    sums = (small_buf[3] + small_buf[7]) + (small_buf[8] + small_buf[9])
    share = width // 32
    at_row = (lax.axis_index("rows") * 2 + c) * share
    tail[0:8, :] = pltpu.roll(sums[:8], lax.rem(width - at_row, width), 1)[:, :lane_width]
    squares = jnp.sum(sums[:8], 1, keepdims=True) / (sums[8:9, 0:1] * width)
    at = lambda axis: lax.broadcasted_iota(jnp.int32, (8, lane_width), axis)
    stats = jnp.where(at(0) == at(1) + 4, jnp.broadcast_to(jnp.sqrt(squares), (8, lane_width)), 0.0)
    tail[8:16, :] = jnp.broadcast_to(column_sum(stats), (8, lane_width))
    for i in range(2):
        last.got(g_fin.at[i], 6 + i, place.sib)
        own, other = g_sum[i, mine], g_fin[i]
        gu_v[:, i * half_g : (i + 1) * half_g] = jnp.where(first, own, other)
        gu_v[:, (i + 2) * half_g : (i + 3) * half_g] = jnp.where(first, other, own)
    hand_over(2, gu_v, gu_out).start()
    swap(1, late, a_sum, a_fin, 9)
    for i in range(2):
        last.got(a_fin.at[i], 8 + i, place.sib)
        own, other = a_sum[i, mine], a_fin[i]
        qk, vo = jnp.where(first, own, other), jnp.where(first, other, own)
        for j, term in enumerate((qk[:, :part], qk[:, part:], vo[:, :part])):
            at = j * width + i * part
            qkv_out[:, at : at + part] = term
        wout_out[:, i * part : (i + 1) * part] = vo[:, part:]
    for m in (down, left, right, early, late):
        m.drain()
    for m in (early, late):
        m.given()
    sent = [small_buf.at[0]] * 6 + [g_fin.at[0]] * 2 + [a_fin.at[0]] * 2
    for slot, ref in enumerate(sent):
        last.sent(ref, slot, place.sib)
    for i, pair in enumerate(((tokens_v, d_tokens), (down_v, down_out), (gu_v, gu_out))):
        hand_over(i, *pair).wait()


def back(
    heads, tokens, q, k, v, span, att, hid_t, norm, inv, gate, up, act, d_branch, a_full, g_full, d_full,
    lse, vectors, small,
):
    low, wide = jnp.bfloat16, jnp.float32
    tok_rows, width = tokens.shape
    ff = gate.shape[1]
    half_g = ff // 2
    pairs = heads // 2
    d_rows = ff // 32
    bufs = []
    for i, cols in enumerate((2 * width, half_g, half_g, width, width)):
        bufs += [pltpu.VMEM((count, rows_chip, cols), low) for count in (16, 16, 2, 2, 4, 4, 3)[i >= 3 :]]
    vmem, hbm = pl.BlockSpec(memory_space=pltpu.VMEM), pl.BlockSpec(memory_space=pl.ANY)
    dma = lambda *shape: pltpu.SemaphoreType.DMA(shape)
    shape = jax.ShapeDtypeStruct
    return pl.pallas_call(
        lambda *refs: back_kernel(heads, *refs),
        out_shape=(
            shape((tok_rows, width), low), shape((24, 3 * width), wide), shape((24, width), wide),
            shape((24, 2 * ff), wide), shape((d_rows, width), wide), shape((16, lane_width), wide),
        ),
        in_specs=[hbm] * 19,
        out_specs=(hbm, vmem, vmem, hbm, hbm, vmem),
        scratch_shapes=bufs
        + [
            pltpu.VMEM((2, 2, 16, rows_chip, width), low),
            pltpu.VMEM((pairs, 2, tok_rows, lane_width), low),
            pltpu.VMEM((tok_rows, width), wide),
            pltpu.VMEM((tok_rows, width), low),
            pltpu.VMEM((2, rows_chip, half_g), wide),
            pltpu.VMEM((2, rows_chip, width), wide),
            pltpu.VMEM((2, 24, half_g), wide),
            pltpu.VMEM((2, 24, width), wide),
            pltpu.VMEM((10,) + small.shape, wide),
            dma(10),
            dma(5 * scatter_slots),
            pltpu.VMEM((tok_rows, width), low),
            pltpu.VMEM((d_rows, width), wide),
            pltpu.VMEM((24, 2 * ff), wide),
            *(pltpu.VMEM(part.shape, wide) for part in (lse, vectors, small)),
            dma(2, pairs),
            dma(2, 10),
            dma(12),
            dma(4, 2),
        ],
        compiler_params=pltpu.CompilerParams(
            collective_id=1, has_side_effects=True, vmem_limit_bytes=63 * 2**20
        ),
        name="backward_and_sums",
    )(tokens, q, k, v, span, att, hid_t, norm, inv, gate, up, act, d_branch, a_full, g_full, d_full, lse, vectors, small)


def close_kernel(share, *refs):
    parts, tail, outs = refs[:6], refs[6], refs[7:]
    for part, out in zip(parts, outs):
        out[...] = part[...]
    for i, out in enumerate(outs[6:10]):
        out[...] = tail[i : i + 1, :share]
    outs[10][...] = tail[8:9, :4]


def close(share, *parts):
    vmem = pl.BlockSpec(memory_space=pltpu.VMEM)
    wide = jnp.float32
    return pl.pallas_call(
        lambda *refs: close_kernel(share, *refs),
        out_shape=tuple(jax.ShapeDtypeStruct(part.shape, part.dtype) for part in parts[:6])
        + (jax.ShapeDtypeStruct((1, share), wide),) * 4
        + (jax.ShapeDtypeStruct((1, 4), wide),),
        in_specs=[vmem] * 7,
        out_specs=(vmem,) * 11,
        compiler_params=pltpu.CompilerParams(vmem_limit_bytes=62 * 2**20),
        name="results",
    )(*parts)


def window(cells, width):
    count = lax.axis_size("blk")
    before = lax.ppermute(cells, "blk", [(i, i + 1) for i in range(count - 1)])
    after = lax.ppermute(cells, "blk", [(i + 1, i) for i in range(count - 1)])
    return jnp.concatenate([before, cells, after], 0)


def window_back(terms, width):
    count = lax.axis_size("blk")
    low = jnp.bfloat16
    before = lax.ppermute(terms[2 * width :].astype(low), "blk", [(i, i + 1) for i in range(count - 1)])
    after = lax.ppermute(terms[:width].astype(low), "blk", [(i + 1, i) for i in range(count - 1)])
    return terms[width : 2 * width] + before.astype(terms.dtype) + after.astype(terms.dtype)


def key_spans(labels, first, tok_rows):
    seq_len = labels.shape[0]
    query_pos = first + jnp.arange(tok_rows, dtype=jnp.int32)
    query_labels = lax.dynamic_slice_in_dim(labels, first, tok_rows, 0)
    if seq_len == 2 * tok_rows:
        key_pos, key_labels = jnp.arange(seq_len, dtype=jnp.int32), labels
    else:
        key_pos = first - tok_rows + jnp.arange(3 * tok_rows, dtype=jnp.int32)
        padded = jnp.pad(labels, (tok_rows, tok_rows), constant_values=seq_len)
        key_labels = lax.dynamic_slice_in_dim(padded, first, 3 * tok_rows, 0)
    same = (key_labels[:, None] == query_labels[None, :]) & (key_labels[:, None] != seq_len)
    gap = jnp.abs(key_pos[:, None] - query_pos[None, :])
    return jnp.where(same | (gap == 0), gap.astype(jnp.float32), far)


def on_chip_grid():
    return lax.axis_size("rows") == 16 and lax.axis_size("blk") == 2


def packed_shards(w_qkv, w_out, ln1_gain, ln1_bias, w_gate_up, ln2_gain, ln2_bias):
    width = w_out.shape[1]
    ff = w_gate_up.shape[1] // 2
    table = jnp.stack((ln1_gain, ln1_bias, ln2_gain, ln2_bias), 1)
    table = jnp.pad(table, ((0, 0), (0, lane_width - 4)))
    left = jnp.concatenate([w_qkv[:, : 2 * width], table], 1)
    right = jnp.concatenate([w_qkv[:, 2 * width :], w_out, jnp.zeros_like(table)], 1)
    return jnp.stack([left, right]), jnp.stack([w_gate_up[:, :ff], w_gate_up[:, ff:]])


def on_grid(tokens, labels, w_qkv, w_out, w_gate_up, w_down, norms, out_grad):
    width = tokens.shape[1]
    (
        a_full, g_full, d_full, q, k, v, att, hid_t, norm, inv, gate, up, act, output, d_branch, span,
        lse, vectors, small,
    ) = fore(HEADS, tokens, labels, w_qkv, w_out, w_gate_up, w_down, norms, out_grad)
    parts = back(
        HEADS, tokens, q, k, v, span, att, hid_t, norm, inv, gate, up, act, d_branch, a_full, g_full,
        d_full.reshape(-1, width), lse, vectors, small,
    )
    *parts, one, two, three, four, stats = close(norms[0].shape[0], output, *parts)
    rows = [row.reshape(-1) for row in (one, two, three, four)]
    return *parts, rows, stats.reshape(-1)


def on_any(tokens, labels, w_qkv, w_out, w_gate_up, w_down, norms, out_grad):
    both = ("rows", "blk")
    tok_rows, width = tokens.shape
    first = lax.axis_index("blk") * tok_rows
    span = key_spans(labels[0], first, tok_rows)
    here = lax.dynamic_slice_in_dim(labels[0], first, tok_rows, 0)
    valid = (here != labels.shape[1]).astype(jnp.float32)[:, None]
    a_shard, g_shard = packed_shards(w_qkv, w_out, *norms[:2], w_gate_up, *norms[2:])
    low, wide = jnp.bfloat16, jnp.float32
    a_full = lax.all_gather(a_shard, both, axis=1, tiled=True)
    w_gu = lax.all_gather(g_shard, both, axis=1, tiled=True)
    w_dn = lax.all_gather(w_down, both, axis=0, tiled=True)
    vectors = jnp.pad(a_full[0, :, 2 * width : 2 * width + 4].astype(wide).T, ((0, 4), (0, 0)))
    w_qk, w_v = a_full[0, :, : 2 * width], a_full[1, :, :width]
    qk = jnp.dot(tokens, w_qk, preferred_element_type=wide).astype(low)
    v = jnp.dot(tokens, w_v, preferred_element_type=wide).astype(low)
    query = qk[:, :width] * (width // HEADS) ** -0.5
    kv = window(jnp.concatenate([qk[:, width:], v], 1), tok_rows)
    keys, values = kv[:, :width], kv[:, width:]
    attended, lse = attend(query, keys, values, span, HEADS)
    output, d_resid_one, d_att, grad_out, g_grad, d_grad, small = ffn(
        tokens, attended, a_full, vectors, valid, out_grad, w_gu, w_dn
    )
    dq, dk, dv = attend_back(query, keys, values, span, lse, attended, d_att, HEADS)
    dkv = window_back(jnp.concatenate([dk, dv], 1), tok_rows)
    d_qk = jnp.concatenate([dq, dkv[:, :width].astype(low)], 1)
    d_v = dkv[:, width:].astype(low)
    grad_qkv = transposed_times(tokens, jnp.concatenate([d_qk, d_v], 1))
    d_tokens = d_resid_one + times_transposed(d_qk, w_qk) + times_transposed(d_v, w_v)
    share = lambda g, axis: lax.psum_scatter(g.astype(wide), both, scatter_dimension=axis, tiled=True)
    gate, up = share(g_grad, 1)
    small = lax.psum(small, both)
    size = norms[0].shape[0]
    rows = lax.dynamic_slice_in_dim(small[:4], lax.axis_index(both) * size, size, 1)
    stats = jnp.sqrt(jnp.sum(small[4:8], 1) / (small[8, 0] * width))
    return (
        output, d_tokens.astype(low), share(grad_qkv, 0), share(grad_out, 0), jnp.concatenate([gate, up], 1),
        share(d_grad, 0), rows, stats,
    )


def body(
    tokens, segments, w_qkv, w_out, ln1_gain, ln1_bias, w_gate_up, w_down, ln2_gain, ln2_bias, out_grad,
):
    run = on_grid if on_chip_grid() else on_any
    norms = (ln1_gain, ln1_bias, ln2_gain, ln2_bias)
    output, d_tokens, qkv, wout, gate_up, down, rows, stats = run(
        tokens[0], segments, w_qkv, w_out, w_gate_up, w_down, norms, out_grad[0]
    )
    return (
        output[None], d_tokens[None], qkv, wout, rows[0], rows[1], gate_up, down, rows[2], rows[3], stats,
    )


def solution(mesh):
    placed = (
        P("rows", "blk", None),
        P("rows", None),
        P(("rows", "blk"), None),
        P(("rows", "blk"), None),
        P(("rows", "blk")),
        P(("rows", "blk")),
        P(("rows", "blk"), None),
        P(("rows", "blk"), None),
        P(("rows", "blk")),
        P(("rows", "blk")),
        P("rows", "blk", None),
    )
    return jax.shard_map(
        body,
        mesh=mesh,
        in_specs=placed,
        out_specs=(
            P("rows", "blk", None),
            P("rows", "blk", None),
            P(("rows", "blk"), None),
            P(("rows", "blk"), None),
            P(("rows", "blk")),
            P(("rows", "blk")),
            P(("rows", "blk"), None),
            P(("rows", "blk"), None),
            P(("rows", "blk")),
            P(("rows", "blk")),
            P(),
        ),
        check_vma=False,
    )
```
